32 devices in a mesh: section: 2 (over core), seq: 4 (over z), dp: 4 (over y, x).
Axes of the slice: x: 2, y: 2, z: 4, core: 2. Of those that a mesh axis runs over, the one named last changes fastest.
Arguments:
- tracks: bfloat16 [32, 2048, 640], P('dp', 'seq')
- species: int32 [32], P('dp'), may hold values from 0 to 1
- batch_order: int32 [8], replicated, may hold values from 0 to 7, each once
- conv_one: bfloat16 [5, 640, 768], P(None, None, 'dp'), may hold values from -0.109375 to 0.109375
- dilated_kernel: bfloat16 [3, 768, 384], P(None, 'dp'), may hold values from -0.125 to 0.125
- point_wise: bfloat16 [384, 768], P(None, 'dp'), may hold values from -0.3125 to 0.3125
- head_human: bfloat16 [768, 5313], P('dp'), may hold values from -0.21875 to 0.21875
- head_mouse: bfloat16 [768, 1643], P('dp'), may hold values from -0.21875 to 0.21875
- bias_human: float32 [5313], replicated, may hold values from -4 to 4
- bias_mouse: float32 [1643], replicated, may hold values from -4 to 4
- gain_one: float32 [640], replicated, may hold values from 0.1 to 1.9
- shift_one: float32 [640], replicated, may hold values from -3 to 3
- gain_two: float32 [768], replicated, may hold values from 0.1 to 1.9
- shift_two: float32 [768], replicated, may hold values from -3 to 3
- gain_three: float32 [384], replicated, may hold values from 0.1 to 1.9
- shift_three: float32 [384], replicated, may hold values from -3 to 3
- cotangent: bfloat16 [32, 1024, 5313], P('dp', 'seq'), may hold values from -6 to 6
Outputs:
- predicted: bfloat16 [32, 1024, 5313], P('dp', ('seq', 'section'))
- grad_input: bfloat16 [32, 2048, 640], P('dp', ('seq', 'section'))
- grad_conv_one: float32 [5, 640, 768], P(None, None, 'dp')
- grad_conv_two: float32 [3, 768, 384], P(None, 'dp')
- grad_point_wise: float32 [384, 768], P(None, 'dp')
- grad_head_human: float32 [768, 5313], P('dp')
- grad_head_mouse: float32 [768, 1643], P('dp')
- grad_bias_human: float32 [5313], replicated
- grad_bias_mouse: float32 [1643], replicated
- grad_gain_one: float32 [640], replicated
- grad_shift_one: float32 [640], replicated
- grad_gain_two: float32 [768], replicated
- grad_shift_two: float32 [768], replicated
- grad_gain_three: float32 [384], replicated
- grad_shift_three: float32 [384], replicated
The draws below stay inside these ranges and needn't reach their ends.
Inputs may be any that keep to these rules, and one draw needn't show every extreme that they name: `species`: 0 marks a human window, 1 a mouse window. `batch_order`: each of 0 to 7 exactly once.
All inputs are finite; a program needn't handle non-finite values.
Results may differ from the reference program's by a relative error of at most 0.018.
Values may be sent and summed in bfloat16 or wider, within the bound.
A program may use at most 576 MiB of HBM per device.

```python
import jax
import jax.numpy as jnp
from jax import lax

C1 = 640
C2 = 768
CB = 384
HT = 5313
MT = 1643
BINS = 1024
BRANCH_DILATION = 11
MB = 4
WIN_DEV = 8
WINDOWS = 32
IN_BINS = 2048
N_DP = 4


def draw_tracks(key, part):
    key = jax.random.fold_in(key, 11)
    key_base, key_rough, key_channel, key_centre, key_window, key_offset = jax.random.split(key, 6)
    array_shape = (WINDOWS, IN_BINS, C1)
    base = jax.random.normal(key_base, array_shape, jnp.float32)
    level = 3.0
    rough = 10.0 ** jax.random.uniform(key_rough, (WINDOWS, IN_BINS, 1), jnp.float32, -0.5, 0.5)
    channel = 10.0 ** jax.random.uniform(key_channel, (1, 1, C1), jnp.float32, -0.5, 0.5)
    centre = jax.random.normal(key_centre, (1, 1, C1), jnp.float32)
    offset = 0.7 * jax.random.normal(key_offset, (WINDOWS, 1, C1), jnp.float32)
    window_scale = 10.0 ** jax.random.uniform(key_window, (WINDOWS, 1, 1), jnp.float32, -1.0, 1.0)
    bin_pos = jnp.arange(IN_BINS, dtype=jnp.float32)[None, :, None] / IN_BINS
    scale = window_scale * 3.0 ** bin_pos / level
    return ((centre + offset + base) * channel * scale * rough).astype(jnp.bfloat16)


def set_ends(values, stream_key, low, largest):
    longest = values.shape.index(max(values.shape))
    spots = []
    for shift in (0, 1):
        where = [jax.random.randint(jax.random.fold_in(stream_key, axis), (), 0, length) for axis, length in enumerate(values.shape)]
        where[longest] = (where[longest] + shift) % values.shape[longest]
        spots.append(tuple(where))
    return values.at[spots[0]].set(low).at[spots[1]].set(largest)


def steps_of(stream_key, extent, shards, least, top_value):
    level, own = 1.0, jax.random.fold_in(stream_key, 6)
    for position, blocks in shards:
        draws = jnp.exp(jax.random.uniform(jax.random.fold_in(own, position), (blocks,), jnp.float32, least / len(shards), top_value / len(shards)))
        level = level * jnp.repeat(draws, extent[position] // blocks).reshape([-1 if axis == position else 1 for axis in range(len(extent))])
    return level


def centred(key, shape, scale, most, cuts=(), kind=jnp.bfloat16):
    values = scale * jax.random.normal(key, shape, jnp.float32)
    if cuts:
        values = values * steps_of(key, shape, cuts, -0.22, 0.18)
    return jnp.clip(values, -most, most).astype(kind)


def setup_inputs(seed: int = 0) -> dict:
    seeds = jax.random.split(jax.random.key(seed), 18)
    tracks = draw_tracks(jax.random.fold_in(seeds[17], 71), 0)
    species = set_ends(jax.random.randint(seeds[1], (WINDOWS,), 0, 2), jax.random.fold_in(seeds[1], 1), 0, 1).astype(jnp.int32)
    batch_order = jax.random.permutation(seeds[2], WIN_DEV).astype(jnp.int32)
    conv_one = centred(seeds[3], (5, C1, C2), (5 * C1) ** -0.5, 0.109375, ((2, 4),))
    dilated_kernel = centred(seeds[4], (3, C2, CB), (3 * C2) ** -0.5, 0.125, ((1, 4),))
    point_wise = centred(seeds[5], (CB, C2), CB ** -0.5, 0.3125, ((1, 4),))
    head_human = centred(seeds[6], (C2, HT), C2 ** -0.5, 0.21875, ((0, 4),))
    head_mouse = centred(seeds[7], (C2, MT), C2 ** -0.5, 0.21875, ((0, 4),))
    bias_human = centred(seeds[8], (HT,), 1.0, 4.0, (), jnp.float32)
    bias_mouse = centred(seeds[9], (MT,), 1.0, 4.0, (), jnp.float32)
    gain_one = jnp.clip(1.0 + 0.18 * jax.random.normal(seeds[10], (C1,), jnp.float32), 0.1, 1.9)
    shift_one = centred(seeds[11], (C1,), 0.5, 3.0, (), jnp.float32)
    gain_two = jnp.clip(1.0 + 0.18 * jax.random.normal(seeds[12], (C2,), jnp.float32), 0.1, 1.9)
    shift_two = centred(seeds[13], (C2,), 0.5, 3.0, (), jnp.float32)
    gain_three = jnp.clip(1.0 + 0.18 * jax.random.normal(seeds[14], (CB,), jnp.float32), 0.1, 1.9)
    shift_three = centred(seeds[15], (CB,), 0.5, 3.0, (), jnp.float32)
    cotangent = centred(seeds[16], (WINDOWS, BINS, HT), 1.0, 6.0, ((0, 4), (1, 4)))
    return dict(tracks=tracks, species=species, batch_order=batch_order, conv_one=conv_one, dilated_kernel=dilated_kernel, point_wise=point_wise, head_human=head_human, head_mouse=head_mouse, bias_human=bias_human, bias_mouse=bias_mouse, gain_one=gain_one, shift_one=shift_one, gain_two=gain_two, shift_two=shift_two, gain_three=gain_three, shift_three=shift_three, cotangent=cotangent)


EPS = 1e-05

@jax.custom_vjp
def low(v):
    return lax.optimization_barrier(v.astype(jnp.bfloat16)).astype(jnp.float32)

@jax.custom_vjp
def low_back(v):
    return v

def low_keep(v):
    return (low(v), None)

def low_pass(kept, grad):
    return (grad,)

def back_keep(v):
    return (v, None)

def back_low(kept, grad):
    return (low(grad),)
low.defvjp(low_keep, low_pass)
low_back.defvjp(back_keep, back_low)

def batch_norm(value, gain, shift):
    centre = lax.optimization_barrier(jnp.mean(value, axis=(0, 1)))
    spread = lax.optimization_barrier(jnp.mean(jnp.square(value - centre), axis=(0, 1)))
    return (value - centre) * lax.rsqrt(spread + EPS) * gain + shift

def convolve_signal(value, weight, dilation):
    taps = weight.shape[0]
    reach = taps // 2 * dilation
    padded = jnp.pad(value, ((0, 0), (reach, reach), (0, 0)))
    length = value.shape[1]
    total = jnp.zeros(value.shape[:2] + (weight.shape[2],), jnp.float32)
    for tap_index in range(taps):
        start = tap_index * dilation
        total = total + jnp.einsum('wlc,cd->wld', padded[:, start:start + length], weight[tap_index], precision=lax.Precision.HIGHEST)
    return total

def block(inputs, params, kinds):
    conv_one, dilated_kernel, point_wise, head_human, head_mouse, bias_human, bias_mouse, gain_one, shift_one, gain_two, shift_two, gain_three, shift_three = params
    act_one = low(jax.nn.gelu(batch_norm(inputs, gain_one, shift_one)))
    conv_out = convolve_signal(act_one, conv_one, 1)
    windows, length, channels = conv_out.shape
    pooled = lax.optimization_barrier(jnp.mean(conv_out.reshape(windows, length // 2, 2, channels), axis=2))
    pooled = low(low_back(pooled))
    second_activated = low(jax.nn.gelu(batch_norm(pooled, gain_two, shift_two)))
    branch_output = low_back(convolve_signal(second_activated, dilated_kernel, BRANCH_DILATION))
    act_three = low(jax.nn.gelu(batch_norm(branch_output, gain_three, shift_three)))
    lifted = low_back(jnp.einsum('wlc,cd->wld', act_three, point_wise, precision=lax.Precision.HIGHEST))
    summed = low(pooled + lifted)
    pre_human = low_back(jnp.einsum('wlc,ct->wlt', summed, head_human, precision=lax.Precision.HIGHEST) + bias_human)
    pre_mouse = low_back(jnp.einsum('wlc,ct->wlt', summed, head_mouse, precision=lax.Precision.HIGHEST) + bias_mouse)
    human = jax.nn.softplus(pre_human)
    mouse = jnp.pad(jax.nn.softplus(pre_mouse), ((0, 0), (0, 0), (0, HT - MT)))
    return jnp.where((kinds == 0)[:, None, None], human, mouse)

def reference(tracks, species, batch_order, conv_one, dilated_kernel, point_wise, head_human, head_mouse, bias_human, bias_mouse, gain_one, shift_one, gain_two, shift_two, gain_three, shift_three, cotangent):
    per_batch = WIN_DEV // MB

    def gather_batches(value):
        value = value.reshape((N_DP, WIN_DEV) + value.shape[1:])
        value = jnp.take(value, batch_order.astype(jnp.int32), axis=1)
        value = value.reshape((N_DP, MB, per_batch) + value.shape[2:])
        value = jnp.swapaxes(value, 0, 1)
        return value.reshape((MB, N_DP * per_batch) + value.shape[3:])

    def scatter_batches(value):
        value = value.reshape((MB, N_DP, per_batch) + value.shape[2:])
        value = jnp.swapaxes(value, 0, 1).reshape((N_DP, WIN_DEV) + value.shape[3:])
        inverse = jnp.argsort(batch_order).astype(jnp.int32)
        value = jnp.take(value, inverse, axis=1)
        return value.reshape((N_DP * WIN_DEV,) + value.shape[2:])
    params = tuple((p.astype(jnp.float32) for p in (conv_one, dilated_kernel, point_wise, head_human, head_mouse, bias_human, bias_mouse, gain_one, shift_one, gain_two, shift_two, gain_three, shift_three)))
    inputs = gather_batches(tracks).astype(jnp.float32)
    kinds = gather_batches(species)
    cots = gather_batches(cotangent).astype(jnp.float32)
    outputs = []
    input_grads = []
    totals = [jnp.zeros(p.shape, jnp.float32) for p in params]
    for batch_index in range(MB):

        def forward(value, *weights):
            return block(value, weights, kinds[batch_index])
        result, pull = jax.vjp(forward, inputs[batch_index], *params)
        grads = pull(cots[batch_index])
        outputs.append(result)
        input_grads.append(grads[0])
        totals = [a + b for a, b in zip(totals, grads[1:])]
    predicted = scatter_batches(jnp.stack(outputs)).astype(jnp.bfloat16)
    grad_input = scatter_batches(jnp.stack(input_grads)).astype(jnp.bfloat16)
    return (predicted, grad_input, totals[0], totals[1], totals[2], totals[3], totals[4], totals[5], totals[6], totals[7], totals[8], totals[9], totals[10], totals[11], totals[12])
```

```python
import functools
import math

import jax
import jax.numpy as jnp
from jax import lax
from jax.experimental import pallas as pl
from jax.experimental.pallas import tpu as pltpu
from jax.sharding import PartitionSpec as P

MESH = pl.DeviceIdType.MESH
DILATION = 11
MB = 4
EPS = 1e-05
EDGE = 16
BLOCK = 1792
LANES = 128
VMEM_LIMIT = 60 * 1024 * 1024
GELU_K = math.sqrt(2.0 / math.pi)
GELU_C = 0.044715
f32 = jnp.float32
bf16 = jnp.bfloat16
VM = pl.BlockSpec(memory_space=pltpu.VMEM)
HBM = pl.BlockSpec(memory_space=pl.ANY)


def params(collective_id=None, limit=VMEM_LIMIT):
    if collective_id is None:
        return pltpu.CompilerParams(vmem_limit_bytes=limit)
    return pltpu.CompilerParams(
        vmem_limit_bytes=limit, collective_id=collective_id, has_side_effects=True
    )


def gelu(u):
    t = jnp.tanh(u * (GELU_K + (GELU_K * GELU_C) * (u * u)))
    h = 0.5 * u
    return h + h * t


def gelu_slope(u):
    uu = u * u
    t = jnp.tanh(u * (GELU_K + (GELU_K * GELU_C) * uu))
    return 0.5 * (1.0 + t) + (0.5 * u) * (1.0 - t * t) * (GELU_K + (3.0 * GELU_K * GELU_C) * uu)


def dot_nn(a, b):
    return jnp.dot(a, b, preferred_element_type=f32)


def dot_nt(a, b):
    return lax.dot_general(a, b, (((1,), (1,)), ((), ())), preferred_element_type=f32)


def dot_tn(a, b):
    return lax.dot_general(a, b, (((0,), (0,)), ((), ())), preferred_element_type=f32)


class Place:
    def __init__(self, shape):
        self.n_sec, self.n_seq, self.n_dp = shape
        self.n_near = self.n_sec * self.n_dp
        self.sec = lax.axis_index("section")
        self.seq = lax.axis_index("seq")
        self.dp = lax.axis_index("dp")
        self.near = self.sec * self.n_dp + self.dp
        n_bins = self.n_seq * self.n_sec
        bins = self.seq * self.n_sec + self.sec
        self.is_first = bins == 0
        self.is_last = bins == n_bins - 1
        low = lax.rem(bins + n_bins - 1, n_bins)
        high = lax.rem(bins + 1, n_bins)
        self.low = self.bin_device(low)
        self.high = self.bin_device(high)
        across = jnp.where(self.sec == 0, low, high)
        self.across = self.bin_device(across)

    def bin_device(self, bins):
        return (lax.rem(bins, self.n_sec), lax.div(bins, self.n_sec), self.dp)

    def near_device(self, rank):
        return (lax.div(rank, self.n_dp), self.seq, lax.rem(rank, self.n_dp))

    def greet(self):
        barrier = pltpu.get_barrier_semaphore()
        for k in range(1, self.n_near):
            rank = lax.rem(self.near + k, self.n_near)
            pl.semaphore_signal(
                barrier, inc=1, device_id=self.near_device(rank), device_id_type=MESH
            )
        for k in range(1, self.n_seq):
            seq = lax.rem(self.seq + k, self.n_seq)
            pl.semaphore_signal(
                barrier, inc=1, device_id=(self.sec, seq, self.dp), device_id_type=MESH
            )
        pl.semaphore_signal(barrier, inc=1, device_id=self.across, device_id_type=MESH)

    def meet(self):
        pl.semaphore_wait(pltpu.get_barrier_semaphore(), self.n_near + self.n_seq - 1)


def halo_copies(place, from_self, arrived, sems):
    up = pltpu.make_async_remote_copy(
        src_ref=from_self[1],
        dst_ref=arrived[0],
        send_sem=sems.at[0],
        recv_sem=sems.at[1],
        device_id=place.high,
        device_id_type=MESH,
    )
    down = pltpu.make_async_remote_copy(
        src_ref=from_self[0],
        dst_ref=arrived[1],
        send_sem=sems.at[2],
        recv_sem=sems.at[3],
        device_id=place.low,
        device_id_type=MESH,
    )
    return up, down


def spread_round(buffer, mine, count, device_of, send, recv):
    copies = []
    for k in range(1, count):
        rank = lax.rem(mine + k, count)
        copy = pltpu.make_async_remote_copy(
            src_ref=buffer.at[mine],
            dst_ref=buffer.at[mine],
            send_sem=send.at[k],
            recv_sem=recv.at[mine],
            device_id=device_of(rank),
            device_id_type=MESH,
        )
        copy.start()
        copies.append((rank, copy))
    for rank, copy in copies:
        pltpu.make_async_remote_copy(
            src_ref=buffer.at[rank],
            dst_ref=buffer.at[rank],
            send_sem=send.at[0],
            recv_sem=recv.at[rank],
            device_id=device_of(rank),
            device_id_type=MESH,
        ).wait_recv()
    for rank, copy in copies:
        copy.wait_send()


def reduce_everywhere(place, value, near_buf, far_buf, sems, combine):
    near_send, near_recv, far_send, far_recv = sems
    near_buf[place.near] = value
    spread_round(
        near_buf, place.near, place.n_near, place.near_device, near_send, near_recv
    )
    far_buf[place.seq] = combine(near_buf, place.n_near, 1)
    spread_round(
        far_buf,
        place.seq,
        place.n_seq,
        lambda seq: (place.sec, seq, place.dp),
        far_send,
        far_recv,
    )
    return combine(far_buf, place.n_seq, place.n_near)


def add_up(buffer, count, weight):
    total = buffer[0]
    for i in range(1, count):
        total = total + buffer[i]
    return total


def merge_stats(rows, buffer, count, weight):
    means = [buffer[i][:MB] for i in range(count)]
    centre = means[0]
    spread = buffer[0][MB:]
    for i in range(1, count):
        centre = centre + means[i]
        spread = spread + buffer[i][MB:]
    centre = centre * (1.0 / count)
    apart = jnp.square(means[0] - centre)
    for i in range(1, count):
        apart = apart + jnp.square(means[i] - centre)
    return jnp.concatenate([centre, spread + apart * float(rows * weight)], axis=0)


def reduce_scratch(shape, rows, columns):
    n_sec, n_seq, n_dp = shape
    near = n_sec * n_dp
    return [
        pltpu.VMEM((near, rows, columns), f32),
        pltpu.VMEM((n_seq, rows, columns), f32),
        pltpu.SemaphoreType.DMA((near,)),
        pltpu.SemaphoreType.DMA((near,)),
        pltpu.SemaphoreType.DMA((n_seq,)),
        pltpu.SemaphoreType.DMA((n_seq,)),
    ]


def local_stats(value):
    count = value.shape[0]
    centre = jnp.sum(value, axis=0, keepdims=True) * (1.0 / count)
    return centre, jnp.sum(jnp.square(value - centre), axis=0, keepdims=True)


def finish_stats(stats, total):
    return jnp.concatenate(
        [stats[:MB], lax.rsqrt(stats[MB:] * (1.0 / total) + EPS)], axis=0
    )


def prepare_kernel(meta, first, second, pairs, low, high, stats, scratch):
    m = pl.program_id(0)
    half = scratch.shape[1]
    start = pl.multiple_of(meta[meta.shape[0] - 1] * half, half)
    values = []
    for i, ref in enumerate((first, second)):
        value = ref[0, pl.ds(start, half), :].astype(f32)
        values.append(value)
        lanes = scratch.shape[0]
        for c in range(lanes):
            scratch[c] = value[:, c * LANES : (c + 1) * LANES]
        both = jnp.concatenate(
            [scratch[c, pl.ds(odd, half // 2, 2), :] for odd in range(2) for c in range(lanes)],
            axis=1,
        )
        pairs[i] = both.astype(bf16)
        low[pl.ds(2 * m + i, 1), :] = both[:1]
        high[pl.ds(2 * m + i, 1), :] = both[half // 2 - 1 :]
    count = 2 * half
    centre = (
        jnp.sum(values[0], axis=0, keepdims=True) + jnp.sum(values[1], axis=0, keepdims=True)
    ) * (1.0 / count)
    spread = jnp.sum(jnp.square(values[0] - centre), axis=0, keepdims=True) + jnp.sum(
        jnp.square(values[1] - centre), axis=0, keepdims=True
    )
    stats[pl.ds(m, 1), :] = centre
    stats[pl.ds(MB + m, 1), :] = spread


def prepare(tracks, meta, half):
    windows, length, channels = tracks.shape
    whole = lambda shape: pl.BlockSpec(shape, lambda m, meta: (0,) * len(shape))
    return pl.pallas_call(
        prepare_kernel,
        grid_spec=pltpu.PrefetchScalarGridSpec(
            num_scalar_prefetch=1,
            grid=(MB,),
            in_specs=[
                pl.BlockSpec((1, length, channels), lambda m, meta: (meta[2 * m], 0, 0)),
                pl.BlockSpec((1, length, channels), lambda m, meta: (meta[2 * m + 1], 0, 0)),
            ],
            out_specs=[
                pl.BlockSpec((2, half // 2, 2 * channels), lambda m, meta: (m, 0, 0)),
                whole((windows, 2 * channels)),
                whole((windows, 2 * channels)),
                whole((2 * MB, channels)),
            ],
            scratch_shapes=[pltpu.VMEM((channels // LANES, half, LANES), f32)],
        ),
        out_shape=[
            jax.ShapeDtypeStruct((windows, half // 2, 2 * channels), bf16),
            jax.ShapeDtypeStruct((windows, 2 * channels), f32),
            jax.ShapeDtypeStruct((windows, 2 * channels), f32),
            jax.ShapeDtypeStruct((2 * MB, channels), f32),
        ],
        compiler_params=params(),
        name="prepare",
    )(meta, tracks, tracks)


def shifted_rows(value, offset, length):
    rows = value.shape[0]
    if offset:
        value = pltpu.roll(value, rows - offset, axis=0)
    return value[:length]


def forward_kernel(
    shape,
    x2,
    edge_low,
    edge_high,
    stats_in,
    gain_one,
    shift_one,
    gain_two,
    shift_two,
    gain_three,
    shift_three,
    w_one,
    w_two,
    w_point,
    u_one,
    u_two,
    pooled,
    pooled_low,
    pooled_high,
    branch,
    branch_low,
    branch_high,
    act_three,
    summed,
    bn_one,
    bn_two,
    bn_three,
    near_one,
    far_one,
    s10,
    s11,
    s12,
    s13,
    near_two,
    far_two,
    s20,
    s21,
    s22,
    s23,
    near_three,
    far_three,
    s30,
    s31,
    s32,
    s33,
    got_low,
    got_high,
    stats_two,
    stats_three,
    halo_sems,
    s_branch_edge_low,
    s_branch_edge_high,
):
    place = Place(shape)
    place.greet()
    windows, length, wide = x2.shape
    channels = wide // 2
    mid = pooled.shape[2]
    small = branch.shape[1]
    parts = shape[0] * shape[1] * shape[2]
    pair = 2 * length
    place.meet()
    up, down = halo_copies(place, (edge_low, edge_high), (got_low, got_high), halo_sems.at[0])
    up.start()
    down.start()
    stats = reduce_everywhere(
        place,
        stats_in[...],
        near_one,
        far_one,
        (s10, s11, s12, s13),
        functools.partial(merge_stats, 4 * length),
    )
    stats = finish_stats(stats, 4 * length * parts)
    bn_one[...] = jnp.concatenate([stats, stats], axis=1)
    up.wait()
    down.wait()

    @pl.loop(0, windows)
    def _(w):
        m = lax.div(w, 2)
        centre = bn_one[pl.ds(m, 1), :]
        scale = bn_one[pl.ds(MB + m, 1), :] * gain_one[...]
        move = shift_one[...]

        def act(value):
            return gelu((value - centre) * scale + move).astype(bf16).astype(f32)

        main = act(x2[w].astype(f32))
        before = jnp.where(place.is_first, 0.0, act(got_low[pl.ds(w, 1), :]))
        after = jnp.where(place.is_last, 0.0, act(got_high[pl.ds(w, 1), :]))
        even, odd = main[:, :channels], main[:, channels:]
        mean = (even + odd) * 0.5
        mean_before = (before[:, :channels] + before[:, channels:]) * 0.5
        mean_after = (after[:, :channels] + after[:, channels:]) * 0.5
        row = lax.broadcasted_iota(jnp.int32, (length, channels), 0)
        top, bottom = row == 0, row == length - 1
        odd_before = jnp.where(top, before[:, channels:], pltpu.roll(odd, 1, axis=0))
        cross = (odd_before + even) * 0.5
        cross_after = (odd[length - 1 :] + after[:, :channels]) * 0.5
        start = pl.multiple_of(w * length, length)
        taps = (
            jnp.where(top, mean_before, pltpu.roll(mean, 1, axis=0)),
            cross,
            mean,
            jnp.where(bottom, cross_after, pltpu.roll(cross, length - 1, axis=0)),
            jnp.where(bottom, mean_after, pltpu.roll(mean, length - 1, axis=0)),
        )
        for t, tap in enumerate(taps):
            u_one[pl.ds(start, length), t * channels : (t + 1) * channels] = tap.astype(bf16)

    @pl.loop(0, MB)
    def _(m):
        start = pl.multiple_of(m * pair, pair)
        value = dot_nt(u_one[pl.ds(start, pair), :], w_one[...]).astype(bf16)
        pooled[pl.ds(2 * m, 2)] = value.reshape(2, length, mid)
        centre, spread = local_stats(value.astype(f32))
        stats_two[pl.ds(m, 1), :] = centre
        stats_two[pl.ds(MB + m, 1), :] = spread

    up, down = halo_copies(
        place,
        (pooled.at[:, pl.ds(0, EDGE), :], pooled.at[:, pl.ds(length - EDGE, EDGE), :]),
        (pooled_low, pooled_high),
        halo_sems.at[1],
    )
    up.start()
    down.start()
    stats = reduce_everywhere(
        place,
        stats_two[...],
        near_two,
        far_two,
        (s20, s21, s22, s23),
        functools.partial(merge_stats, pair),
    )
    bn_two[...] = finish_stats(stats, pair * parts)
    up.wait()
    down.wait()

    @pl.loop(0, windows)
    def _(w):
        m = lax.div(w, 2)
        centre = bn_two[pl.ds(m, 1), :]
        scale = bn_two[pl.ds(MB + m, 1), :] * gain_two[...]
        move = shift_two[...]

        def act(value):
            return gelu((value.astype(f32) - centre) * scale + move)

        ext = jnp.concatenate(
            [
                jnp.where(place.is_first, 0.0, act(pooled_low[w])),
                act(pooled[w]),
                jnp.where(place.is_last, 0.0, act(pooled_high[w])),
            ],
            axis=0,
        )
        start = pl.multiple_of(w * length, length)
        for t in range(3):
            tap = shifted_rows(ext, EDGE + (t - 1) * DILATION, length)
            u_two[pl.ds(start, length), t * mid : (t + 1) * mid] = tap.astype(bf16)

    @pl.loop(0, MB)
    def _(m):
        start = pl.multiple_of(m * pair, pair)
        value = dot_nn(u_two[pl.ds(start, pair), :], w_two[...])
        branch[pl.ds(start, pair), :] = value
        centre, spread = local_stats(value)
        stats_three[pl.ds(m, 1), :] = centre
        stats_three[pl.ds(MB + m, 1), :] = spread
        for i in range(2):
            s_branch_edge_low[2 * m + i] = value[i * length : i * length + EDGE]
            s_branch_edge_high[2 * m + i] = value[(i + 1) * length - EDGE : (i + 1) * length]

    up, down = halo_copies(
        place,
        (s_branch_edge_low, s_branch_edge_high),
        (branch_low, branch_high),
        halo_sems.at[2],
    )
    up.start()
    down.start()
    stats = reduce_everywhere(
        place,
        stats_three[...],
        near_three,
        far_three,
        (s30, s31, s32, s33),
        functools.partial(merge_stats, pair),
    )
    bn_three[...] = finish_stats(stats, pair * parts)

    @pl.loop(0, MB)
    def _(m):
        centre = bn_three[pl.ds(m, 1), :]
        scale = bn_three[pl.ds(MB + m, 1), :] * gain_three[...]
        start = pl.multiple_of(m * pair, pair)
        act = gelu((branch[pl.ds(start, pair), :] - centre) * scale + shift_three[...])
        act = act.astype(bf16)
        act_three[pl.ds(start, pair), :] = act
        lifted = dot_nt(act, w_point[...])
        here = pooled[pl.ds(2 * m, 2)].reshape(pair, mid).astype(f32)
        summed[pl.ds(start, pair), :] = (here + lifted).astype(bf16)

    up.wait()
    down.wait()


def forward(shape, x2, edge_low, edge_high, stats, gains, w_one, w_two, w_point):
    windows, length, wide = x2.shape
    rows = windows * length
    mid, small = w_point.shape
    out = [
        ((rows, w_one.shape[1]), bf16),
        ((rows, w_two.shape[0]), bf16),
        ((windows, length, mid), bf16),
        ((windows, EDGE, mid), bf16),
        ((windows, EDGE, mid), bf16),
        ((rows, small), f32),
        ((windows, EDGE, small), f32),
        ((windows, EDGE, small), f32),
        ((rows, small), bf16),
        ((rows, mid), bf16),
        ((2 * MB, wide), f32),
        ((2 * MB, mid), f32),
        ((2 * MB, small), f32),
    ]
    scratch = (
        reduce_scratch(shape, 2 * MB, wide // 2)
        + reduce_scratch(shape, 2 * MB, mid)
        + reduce_scratch(shape, 2 * MB, small)
    )
    scratch += [
        pltpu.VMEM((windows, wide), f32),
        pltpu.VMEM((windows, wide), f32),
        pltpu.VMEM((2 * MB, mid), f32),
        pltpu.VMEM((2 * MB, small), f32),
        pltpu.SemaphoreType.DMA((3, 4)),
        pltpu.VMEM((windows, EDGE, small), f32),
        pltpu.VMEM((windows, EDGE, small), f32),
    ]
    return pl.pallas_call(
        functools.partial(forward_kernel, shape),
        in_specs=[VM] * 13,
        out_specs=[VM] * len(out),
        out_shape=[jax.ShapeDtypeStruct(*o) for o in out],
        scratch_shapes=scratch,
        compiler_params=params(1),
        name="forward",
    )(x2, edge_low, edge_high, stats, *gains, w_one, w_two, w_point)


def heads_kernel(
    human_tracks,
    mouse_tracks,
    meta,
    summed,
    w_human,
    w_mouse,
    b_human,
    b_mouse,
    cot,
    predicted,
    grad_summed,
    d_human,
    d_mouse,
    db_human,
    db_mouse,
    rows_sorted,
    grad_sorted,
    grad_pre,
):
    j = pl.program_id(0)
    windows, length, block = cot.shape
    pair = 2 * length
    n_pairs = windows // 2
    mid = summed.shape[1]
    n_human = meta[2 * windows]

    @pl.when(j == 0)
    def _():
        grad_sorted[...] = jnp.zeros_like(grad_sorted)

        @pl.loop(0, windows)
        def _(s):
            source = pl.multiple_of(meta[s] * length, length)
            target = pl.multiple_of(s * length, length)
            rows_sorted[pl.ds(target, length), :] = summed[pl.ds(source, length), :]

    column = lax.broadcasted_iota(jnp.int32, (1, block), 1)

    def run(weight, bias, limit, is_mouse, first_pair, last_pair):
        def body(p, carry):
            start = pl.multiple_of(p * pair, pair)
            pre = dot_nn(rows_sorted[pl.ds(start, pair), :], weight[...]) + bias[...]
            decay = jnp.exp(-jnp.abs(pre))
            whole = 1.0 + decay
            inverse = 1.0 / whole
            sigmoid = jnp.where(pre >= 0, inverse, decay * inverse)
            logs = jnp.where(decay < 2.0**-11, decay, jnp.log(whole))
            output = (jnp.maximum(pre, 0.0) + logs).astype(bf16)
            output = jnp.where(column < limit, output, jnp.zeros_like(output))
            for i in range(2):
                s = 2 * p + i
                window = meta[windows + s]
                mine = s >= n_human if is_mouse else s < n_human
                keep = (column < limit) & mine
                part = slice(i * length, (i + 1) * length)
                grad = jnp.where(keep, cot[window].astype(f32) * sigmoid[part], 0.0)
                grad_pre[pl.ds(pl.multiple_of(s * length, length), length), :] = grad.astype(bf16)

                @pl.when(mine)
                def _():
                    predicted[window] = output[part]

            grad_sorted[pl.ds(start, pair), :] += dot_nt(
                grad_pre[pl.ds(start, pair), :], weight[...]
            )
            return carry

        lax.fori_loop(first_pair, last_pair, body, 0)

    def weight_grads(count, n_used, from_end, d_weight, d_bias):
        for n in range(n_pairs + 1):

            @pl.when(n_used == n)
            def _(n=n):
                if n == 0:
                    d_weight[...] = jnp.zeros_like(d_weight)
                    d_bias[...] = jnp.zeros_like(d_bias)
                else:
                    part = slice((n_pairs - n) * pair, None) if from_end else slice(0, n * pair)
                    grad = grad_pre[part, :]
                    d_weight[...] = dot_tn(rows_sorted[part, :], grad).astype(bf16)
                    d_bias[...] = dot_nn(jnp.ones((8, n * pair), bf16), grad)[:1]

    human_pairs = lax.div(n_human + 1, 2)
    run(w_human, b_human, human_tracks - j * block, False, 0, human_pairs)
    weight_grads(n_pairs, human_pairs, False, d_human, db_human)

    @pl.when(j == 0)
    def _():
        mouse_start = lax.div(n_human, 2)
        run(w_mouse, b_mouse, mouse_tracks, True, mouse_start, n_pairs)
        weight_grads(n_pairs, n_pairs - mouse_start, True, d_mouse, db_mouse)

    @pl.when(j > 0)
    def _():
        def body(s, carry):
            predicted[meta[windows + s]] = jnp.zeros((length, block), bf16)
            return carry

        lax.fori_loop(n_human, windows, body, 0)

    @pl.when(j == pl.num_programs(0) - 1)
    def _():
        @pl.loop(0, windows)
        def _(s):
            source = pl.multiple_of(s * length, length)
            target = pl.multiple_of(meta[s] * length, length)
            grad_summed[pl.ds(target, length), :] = grad_sorted[pl.ds(source, length), :]


def heads(meta, summed, w_heads, b_human, b_mouse, cotangent, mouse_tracks, length):
    windows, _, human_tracks = cotangent.shape
    rows, mid = summed.shape
    blocks = w_heads.shape[1] // BLOCK - 1
    sec_at = 2 * windows + 1
    row_block = pl.BlockSpec((1, BLOCK), lambda j, meta: (0, j))
    row_fixed = pl.BlockSpec((1, BLOCK), lambda j, meta: (0, 0))
    fixed = pl.BlockSpec((rows, mid), lambda j, meta: (0, 0))
    return pl.pallas_call(
        functools.partial(heads_kernel, human_tracks, mouse_tracks),
        grid_spec=pltpu.PrefetchScalarGridSpec(
            num_scalar_prefetch=1,
            grid=(blocks,),
            in_specs=[
                fixed,
                pl.BlockSpec((mid, BLOCK), lambda j, meta: (0, j)),
                pl.BlockSpec((mid, BLOCK), lambda j, meta: (0, blocks), pipeline_mode=pl.Buffered(1)),
                row_block,
                row_fixed,
                pl.BlockSpec((windows, length, BLOCK), lambda j, meta: (0, meta[sec_at], j)),
            ],
            out_specs=[
                pl.BlockSpec((windows, length, BLOCK), lambda j, meta: (0, 0, j)),
                fixed,
                pl.BlockSpec((mid, BLOCK), lambda j, meta: (0, j)),
                pl.BlockSpec((mid, BLOCK), lambda j, meta: (0, 0)),
                row_block,
                row_fixed,
            ],
            scratch_shapes=[
                pltpu.VMEM((rows, mid), bf16),
                pltpu.VMEM((rows, mid), f32),
                pltpu.VMEM((rows, BLOCK), bf16),
            ],
        ),
        out_shape=[
            jax.ShapeDtypeStruct((windows, length, human_tracks), bf16),
            jax.ShapeDtypeStruct((rows, mid), f32),
            jax.ShapeDtypeStruct((mid, blocks * BLOCK), bf16),
            jax.ShapeDtypeStruct((mid, BLOCK), bf16),
            jax.ShapeDtypeStruct((1, blocks * BLOCK), f32),
            jax.ShapeDtypeStruct((1, BLOCK), f32),
        ],
        compiler_params=params(),
        name="heads",
    )(meta, summed, w_heads, w_heads, b_human, b_mouse, cotangent)


def back_three_kernel(
    shape,
    grad_summed,
    act_three,
    branch,
    bn_three,
    gain_three,
    shift_three,
    w_point,
    bias_sums,
    d_point,
    du_three,
    du_low,
    du_high,
    gs_low,
    gs_high,
    sums_three,
    bias_out,
    near,
    far,
    s0,
    s1,
    s2,
    s3,
    near_b,
    far_b,
    b0,
    b1,
    b2,
    b3,
    edge_low,
    edge_high,
    row_low,
    row_high,
    sums,
    halo_sems,
):
    place = Place(shape)
    place.greet()
    rows, mid = grad_summed.shape
    pair = rows // MB
    length = pair // 2

    @pl.loop(0, MB)
    def _(m):
        start = pl.multiple_of(m * pair, pair)
        grad = grad_summed[pl.ds(start, pair), :]
        back = dot_nn(grad.astype(bf16), w_point[...])
        centre = bn_three[pl.ds(m, 1), :]
        xhat = (branch[pl.ds(start, pair), :] - centre) * bn_three[pl.ds(MB + m, 1), :]
        du = gelu_slope(xhat * gain_three[...] + shift_three[...]) * back
        du_three[pl.ds(start, pair), :] = du
        sums[pl.ds(m, 1), :] = jnp.sum(du, axis=0, keepdims=True)
        sums[pl.ds(MB + m, 1), :] = jnp.sum(du * xhat, axis=0, keepdims=True)
        for i in range(2):
            edge_low[2 * m + i] = du[i * length : i * length + EDGE]
            edge_high[2 * m + i] = du[(i + 1) * length - EDGE : (i + 1) * length]
            row_low[pl.ds(2 * m + i, 1), :] = grad[i * length : i * length + 1]
            row_high[pl.ds(2 * m + i, 1), :] = grad[(i + 1) * length - 1 : (i + 1) * length]

    place.meet()
    moves = halo_copies(place, (edge_low, edge_high), (du_low, du_high), halo_sems.at[0])
    moves += halo_copies(place, (row_low, row_high), (gs_low, gs_high), halo_sems.at[1])
    for move in moves:
        move.start()
    bias_out[...] = reduce_everywhere(
        place, bias_sums[...], near_b, far_b, (b0, b1, b2, b3), add_up
    )
    sums_three[...] = reduce_everywhere(place, sums[...], near, far, (s0, s1, s2, s3), add_up)
    d_point[...] = dot_tn(grad_summed[...].astype(bf16), act_three[...]).astype(bf16)
    for move in moves:
        move.wait()


def back_three(shape, windows, grad_summed, act_three, branch, bn_three, gain, move, w_point, bias_sums):
    rows, mid = grad_summed.shape
    small = branch.shape[1]
    out = [
        ((mid, small), bf16),
        ((rows, small), f32),
        ((windows, EDGE, small), f32),
        ((windows, EDGE, small), f32),
        ((windows, mid), f32),
        ((windows, mid), f32),
        ((2 * MB, small), f32),
        (bias_sums.shape, f32),
    ]
    scratch = reduce_scratch(shape, 2 * MB, small) + reduce_scratch(shape, *bias_sums.shape)
    scratch += [
        pltpu.VMEM((windows, EDGE, small), f32),
        pltpu.VMEM((windows, EDGE, small), f32),
        pltpu.VMEM((windows, mid), f32),
        pltpu.VMEM((windows, mid), f32),
        pltpu.VMEM((2 * MB, small), f32),
        pltpu.SemaphoreType.DMA((2, 4)),
    ]
    return pl.pallas_call(
        functools.partial(back_three_kernel, shape),
        in_specs=[VM] * 8,
        out_specs=[VM] * len(out),
        out_shape=[jax.ShapeDtypeStruct(*o) for o in out],
        scratch_shapes=scratch,
        compiler_params=params(2),
        name="back_three",
    )(grad_summed, act_three, branch, bn_three, gain, move, w_point, bias_sums)


def back_two_kernel(
    shape,
    du_three,
    du_low,
    du_high,
    sums_three,
    branch,
    branch_low,
    branch_high,
    bn_three,
    gain_three,
    u_two,
    w_two,
    pooled,
    bn_two,
    gain_two,
    shift_two,
    d_two,
    du_two,
    row_low_out,
    row_high_out,
    sums_two,
    near,
    far,
    s0,
    s1,
    s2,
    s3,
    row_low,
    row_high,
    sums,
    grad_branch,
    halo_sems,
):
    place = Place(shape)
    place.greet()
    windows, length, mid = pooled.shape
    parts = shape[0] * shape[1] * shape[2]
    pair = 2 * length
    scale = 1.0 / (pair * parts)
    taps = w_two.shape[0] // mid

    @pl.loop(0, MB)
    def _(m):
        start = pl.multiple_of(m * pair, pair)
        centre = bn_three[pl.ds(m, 1), :]
        inverse = bn_three[pl.ds(MB + m, 1), :]
        factor = gain_three[...] * inverse
        mean_du = sums_three[pl.ds(m, 1), :] * scale
        mean_dx = sums_three[pl.ds(MB + m, 1), :] * scale

        def back(du, value):
            xhat = (value - centre) * inverse
            return factor * (du - mean_du - xhat * mean_dx)

        main = back(du_three[pl.ds(start, pair), :], branch[pl.ds(start, pair), :])
        grad_branch[pl.ds(start, pair), :] = main.astype(bf16)
        pieces = []
        for i in range(2):
            w = 2 * m + i
            low = jnp.where(place.is_first, 0.0, back(du_low[w], branch_low[w]))
            high = jnp.where(place.is_last, 0.0, back(du_high[w], branch_high[w]))
            pieces += [low, main[i * length : (i + 1) * length], high]
        ext = jnp.concatenate(pieces, axis=0).astype(bf16)
        span = length + 2 * EDGE
        through = [dot_nt(ext, w_two[t * mid : (t + 1) * mid, :]) for t in range(taps)]
        centre_two = bn_two[pl.ds(m, 1), :]
        inverse_two = bn_two[pl.ds(MB + m, 1), :]
        total_du = jnp.zeros((1, mid), f32)
        total_dx = jnp.zeros((1, mid), f32)
        for i in range(2):
            w = 2 * m + i
            grad = jnp.zeros((length, mid), f32)
            for t in range(taps):
                whole = through[t][i * span : (i + 1) * span]
                grad = grad + shifted_rows(whole, EDGE - (t - 1) * DILATION, length)
            xhat = (pooled[w].astype(f32) - centre_two) * inverse_two
            du = gelu_slope(xhat * gain_two[...] + shift_two[...]) * grad
            du_two[w] = du
            total_du = total_du + jnp.sum(du, axis=0, keepdims=True)
            total_dx = total_dx + jnp.sum(du * xhat, axis=0, keepdims=True)
            row_low[pl.ds(w, 1), :] = du[:1]
            row_high[pl.ds(w, 1), :] = du[length - 1 :]
        sums[pl.ds(m, 1), :] = total_du
        sums[pl.ds(MB + m, 1), :] = total_dx

    place.meet()
    moves = halo_copies(place, (row_low, row_high), (row_low_out, row_high_out), halo_sems)
    for move in moves:
        move.start()
    sums_two[...] = reduce_everywhere(place, sums[...], near, far, (s0, s1, s2, s3), add_up)
    d_two[...] = dot_tn(u_two[...], grad_branch[...]).astype(bf16)
    for move in moves:
        move.wait()


def back_two(shape, du, sums_three, branch, bn_three, gain_three, u_two, w_two, pooled, bn_two, gain, move):
    windows, length, mid = pooled.shape
    rows, small = branch[0].shape
    out = [
        (w_two.shape, bf16),
        ((windows, length, mid), f32),
        ((windows, mid), f32),
        ((windows, mid), f32),
        ((2 * MB, mid), f32),
    ]
    scratch = reduce_scratch(shape, 2 * MB, mid)
    scratch += [
        pltpu.VMEM((windows, mid), f32),
        pltpu.VMEM((windows, mid), f32),
        pltpu.VMEM((2 * MB, mid), f32),
        pltpu.VMEM((rows, small), bf16),
        pltpu.SemaphoreType.DMA((4,)),
    ]
    return pl.pallas_call(
        functools.partial(back_two_kernel, shape),
        in_specs=[VM] * 15,
        out_specs=[VM] * len(out),
        out_shape=[jax.ShapeDtypeStruct(*o) for o in out],
        scratch_shapes=scratch,
        compiler_params=params(3),
        name="back_two",
    )(*du, sums_three, *branch, bn_three, gain_three, u_two, w_two, pooled, bn_two, gain, move)


def pool_grad_kernel(
    shape,
    du_two,
    du_low,
    du_high,
    sums_two,
    pooled,
    pooled_low,
    pooled_high,
    bn_two,
    gain_two,
    grad_summed,
    gs_low,
    gs_high,
    u_one,
    grad_ext,
    d_one,
    grad_main,
):
    place = Place(shape)
    windows, length, mid = pooled.shape
    parts = shape[0] * shape[1] * shape[2]
    pair = 2 * length
    scale = 1.0 / (pair * parts)

    @pl.loop(0, MB)
    def _(m):
        start = pl.multiple_of(m * pair, pair)
        centre = bn_two[pl.ds(m, 1), :]
        inverse = bn_two[pl.ds(MB + m, 1), :]
        factor = gain_two[...] * inverse
        mean_du = sums_two[pl.ds(m, 1), :] * scale
        mean_dx = sums_two[pl.ds(MB + m, 1), :] * scale

        def back(du, value, extra):
            xhat = (value.astype(f32) - centre) * inverse
            return factor * (du - mean_du - xhat * mean_dx) + extra

        edges = []
        for i in range(2):
            w = 2 * m + i
            at = pl.multiple_of(w * length, length)
            value = back(du_two[w], pooled[w], grad_summed[pl.ds(at, length), :]).astype(bf16)
            grad_ext[m, i * length : (i + 1) * length, :] = value
            grad_main[pl.ds(at, length), :] = value
            low = back(
                du_low[pl.ds(w, 1), :],
                pooled_low[w].astype(f32)[EDGE - 1 :],
                gs_low[pl.ds(w, 1), :],
            )
            high = back(
                du_high[pl.ds(w, 1), :],
                pooled_high[w].astype(f32)[:1],
                gs_high[pl.ds(w, 1), :],
            )
            edges += [jnp.where(place.is_first, 0.0, low), jnp.where(place.is_last, 0.0, high)]
        row = lax.broadcasted_iota(jnp.int32, (EDGE, mid), 0)
        block = jnp.zeros((EDGE, mid), f32)
        for i, edge in enumerate(edges):
            block = jnp.where(row == i, edge, block)
        grad_ext[m, pair : pair + EDGE, :] = block.astype(bf16)

    d_one[...] = dot_tn(grad_main[...], u_one[...]).astype(bf16)


def pool_grad(shape, du, sums_two, pooled, bn_two, gain_two, grad_summed, gs, u_one):
    windows, length, mid = pooled[0].shape
    rows = windows * length
    return pl.pallas_call(
        functools.partial(pool_grad_kernel, shape),
        in_specs=[VM] * 13,
        out_specs=[VM] * 2,
        out_shape=[
            jax.ShapeDtypeStruct((MB, 2 * length + EDGE, mid), bf16),
            jax.ShapeDtypeStruct((mid, u_one.shape[1]), bf16),
        ],
        scratch_shapes=[pltpu.VMEM((rows, mid), bf16)],
        compiler_params=params(),
        name="pool_grad",
    )(*du, sums_two, *pooled, bn_two, gain_two, grad_summed, *gs, u_one)


def back_one_kernel(
    shape,
    grad_ext,
    w_one,
    x2,
    bn_one,
    gain_one,
    shift_one,
    du_one,
    sums_one,
    near,
    far,
    s0,
    s1,
    s2,
    s3,
    sums,
):
    place = Place(shape)
    place.greet()
    windows, length, wide = x2.shape
    channels = wide // 2
    pair = 2 * length

    @pl.loop(0, MB)
    def _(m):
        through = [
            dot_nn(grad_ext[m], w_one[:, t * channels : (t + 1) * channels]) for t in range(5)
        ]
        centre = bn_one[pl.ds(m, 1), :]
        inverse = bn_one[pl.ds(MB + m, 1), :]
        total_du = jnp.zeros((1, wide), f32)
        total_dx = jnp.zeros((1, wide), f32)
        row = lax.broadcasted_iota(jnp.int32, (length, channels), 0)
        top, bottom = row == 0, row == length - 1
        for i in range(2):
            w = 2 * m + i
            main = [t[i * length : (i + 1) * length] for t in through]
            low = [t[pair + 2 * i : pair + 2 * i + 1] for t in through]
            high = [t[pair + 2 * i + 1 : pair + 2 * i + 2] for t in through]
            later = lambda t: jnp.where(bottom, high[t], pltpu.roll(main[t], length - 1, axis=0))
            earlier = lambda t: jnp.where(top, low[t], pltpu.roll(main[t], 1, axis=0))
            mean = later(0) + main[2] + earlier(4)
            cross = main[1] + earlier(3)
            cross_end = high[1] + main[3][length - 1 :]
            cross_later = jnp.where(bottom, cross_end, pltpu.roll(cross, length - 1, axis=0))
            grad = jnp.concatenate([(mean + cross) * 0.5, (mean + cross_later) * 0.5], axis=1)
            xhat = (x2[w].astype(f32) - centre) * inverse
            du = gelu_slope(xhat * gain_one[...] + shift_one[...]) * grad
            du_one[w] = du
            total_du = total_du + jnp.sum(du, axis=0, keepdims=True)
            total_dx = total_dx + jnp.sum(du * xhat, axis=0, keepdims=True)
        sums[pl.ds(m, 1), :] = total_du[:, :channels] + total_du[:, channels:]
        sums[pl.ds(MB + m, 1), :] = total_dx[:, :channels] + total_dx[:, channels:]

    place.meet()
    sums_one[...] = reduce_everywhere(place, sums[...], near, far, (s0, s1, s2, s3), add_up)


def back_one(shape, grad_ext, w_one, x2, bn_one, gain, move):
    windows, length, wide = x2.shape
    out = [((windows, length, wide), f32), ((2 * MB, wide // 2), f32)]
    scratch = reduce_scratch(shape, 2 * MB, wide // 2)
    scratch += [pltpu.VMEM((2 * MB, wide // 2), f32)]
    return pl.pallas_call(
        functools.partial(back_one_kernel, shape),
        in_specs=[VM] * 6,
        out_specs=[VM] * len(out),
        out_shape=[jax.ShapeDtypeStruct(*o) for o in out],
        scratch_shapes=scratch,
        compiler_params=params(4),
        name="back_one",
    )(grad_ext, w_one, x2, bn_one, gain, move)


def input_grad_kernel(total, meta, du, x2, bn_one, sums, gain, out, scratch):
    w = pl.program_id(0)
    m = lax.div(w, 2)
    wide = x2.shape[2]
    channels = wide // 2
    length = x2.shape[1]
    twice = lambda v: jnp.concatenate([v, v], axis=1)
    mean_du = twice(sums[pl.ds(m, 1), :]) * (1.0 / total)
    mean_dx = twice(sums[pl.ds(MB + m, 1), :]) * (1.0 / total)
    centre = bn_one[pl.ds(m, 1), :]
    inverse = bn_one[pl.ds(MB + m, 1), :]
    xhat = (x2[0].astype(f32) - centre) * inverse
    grad = gain[...] * inverse * (du[0] - mean_du - xhat * mean_dx)
    lanes = scratch.shape[0]
    for odd in range(2):
        for c in range(lanes):
            at = odd * channels + c * LANES
            scratch[c, pl.ds(odd, length, 2), :] = grad[:, at : at + LANES]
    for c in range(lanes):
        out[0, :, c * LANES : (c + 1) * LANES] = scratch[c].astype(bf16)


def input_grad(shape, meta, du, x2, bn_one, sums, gain):
    windows, length, wide = x2.shape
    total = 4 * length * shape[0] * shape[1] * shape[2]
    whole = lambda s: pl.BlockSpec(s, lambda w, meta: (0,) * len(s))

    return pl.pallas_call(
        functools.partial(input_grad_kernel, total),
        grid_spec=pltpu.PrefetchScalarGridSpec(
            num_scalar_prefetch=1,
            grid=(windows,),
            in_specs=[
                pl.BlockSpec((1, length, wide), lambda w, meta: (w, 0, 0)),
                pl.BlockSpec((1, length, wide), lambda w, meta: (w, 0, 0)),
                whole(bn_one.shape),
                whole(sums.shape),
                whole(gain.shape),
            ],
            out_specs=pl.BlockSpec(
                (1, 2 * length, wide // 2), lambda w, meta: (meta[w], 0, 0)
            ),
            scratch_shapes=[pltpu.VMEM((wide // 2 // LANES, 2 * length, LANES), f32)],
        ),
        out_shape=jax.ShapeDtypeStruct((windows, 2 * length, wide // 2), bf16),
        compiler_params=params(),
        name="input_grad",
    )(meta, du, x2, bn_one, sums, gain)


def per_device(
    shape,
    tracks,
    species,
    batch_order,
    conv_one,
    dilated_kernel,
    point_wise,
    head_human,
    head_mouse,
    bias_human,
    bias_mouse,
    gain_one,
    shift_one,
    gain_two,
    shift_two,
    gain_three,
    shift_three,
    cotangent,
):
    sec = lax.axis_index("section").astype(jnp.int32)
    windows, seq_bins, channels = tracks.shape
    half = seq_bins // 2
    length = half // 2
    human_tracks, mouse_tracks = head_human.shape[1], head_mouse.shape[1]
    human_wide = -(-human_tracks // BLOCK) * BLOCK
    share = conv_one.shape[2]
    mid = share * shape[2]

    taps_one = conv_one.shape[0]
    shard_one = jnp.transpose(conv_one, (2, 0, 1)).reshape(share, taps_one * channels)
    shard_point = point_wise.T
    shard_heads = jnp.concatenate(
        [
            jnp.pad(head_human, ((0, 0), (0, human_wide - human_tracks))),
            jnp.pad(head_mouse, ((0, 0), (0, BLOCK - mouse_tracks))),
        ],
        axis=1,
    )

    def gathered(shard, axis):
        size = shard.shape[axis] // 2
        part = lax.dynamic_slice_in_dim(shard, sec * size, size, axis)
        return lax.all_gather(part, ("dp", "section"), axis=axis, tiled=True)

    w_one = gathered(shard_one, 0)
    w_two = gathered(dilated_kernel, 1).reshape(-1, dilated_kernel.shape[2])
    w_point = gathered(shard_point, 0)
    w_heads = gathered(shard_heads, 0)

    meta_one = jnp.concatenate([batch_order, sec[None]])
    x2, edge_low, edge_high, stats = prepare(tracks, meta_one, half)
    row = lambda v: v.reshape(1, -1)
    twice = lambda v: jnp.tile(v, 2).reshape(1, -1)
    gains = (
        twice(gain_one),
        twice(shift_one),
        row(gain_two),
        row(shift_two),
        row(gain_three),
        row(shift_three),
    )
    (
        u_one,
        u_two,
        pooled,
        pooled_low,
        pooled_high,
        branch,
        branch_low,
        branch_high,
        act_three,
        summed,
        bn_one,
        bn_two,
        bn_three,
    ) = forward(shape, x2, edge_low, edge_high, stats, gains, w_one, w_two, w_point)

    kinds = species[batch_order]
    is_human = kinds == 0
    n_human = jnp.sum(is_human.astype(jnp.int32))
    place_human = jnp.cumsum(is_human.astype(jnp.int32)) - 1
    place_mouse = n_human + jnp.cumsum(1 - is_human.astype(jnp.int32)) - 1
    target = jnp.where(is_human, place_human, place_mouse)
    positions = jnp.sum(
        jnp.where(target[None, :] == jnp.arange(windows)[:, None], jnp.arange(windows)[None, :], 0),
        axis=1,
    ).astype(jnp.int32)
    meta_two = jnp.concatenate(
        [positions, batch_order[positions], n_human[None], sec[None]]
    ).astype(jnp.int32)
    wide_human = jnp.pad(bias_human, (0, human_wide - human_tracks)).reshape(1, -1)
    wide_mouse = jnp.pad(bias_mouse, (0, BLOCK - mouse_tracks)).reshape(1, -1)
    predicted, grad_summed, d_human, d_mouse, db_human, db_mouse = heads(
        meta_two, summed, w_heads, wide_human, wide_mouse, cotangent, mouse_tracks, length
    )

    bias_sums = jnp.concatenate([db_human, db_mouse], axis=1).reshape(8, -1)
    d_point, du_three, du_low, du_high, gs_low, gs_high, sums_three, bias_out = back_three(
        shape, windows, grad_summed, act_three, branch, bn_three, gains[4], gains[5], w_point, bias_sums
    )
    d_two, du_two, dlow_two, dhigh_two, sums_two = back_two(
        shape,
        (du_three, du_low, du_high),
        sums_three,
        (branch, branch_low, branch_high),
        bn_three,
        gains[4],
        u_two,
        w_two,
        pooled,
        bn_two,
        gains[2],
        gains[3],
    )
    grad_ext, d_one = pool_grad(
        shape,
        (du_two, dlow_two, dhigh_two),
        sums_two,
        (pooled, pooled_low, pooled_high),
        bn_two,
        gains[2],
        grad_summed,
        (gs_low, gs_high),
        u_one,
    )
    du_one, sums_one = back_one(shape, grad_ext, w_one, x2, bn_one, gains[0], gains[1])
    grad_input = input_grad(shape, meta_one, du_one, x2, bn_one, sums_one, gains[0])

    def reduced(grad, axis):
        part = lax.psum_scatter(grad, "dp", scatter_dimension=axis, tiled=True)
        return lax.psum(part, ("section", "seq")).astype(f32)

    r_human = reduced(d_human, 0)[:, :human_tracks]
    r_mouse = reduced(d_mouse, 0)[:, :mouse_tracks]
    r_two = reduced(d_two.reshape((dilated_kernel.shape[0], mid, -1)), 1)
    r_point = reduced(d_point, 0).T
    r_one = jnp.transpose(reduced(d_one, 0).reshape(share, taps_one, channels), (1, 2, 0))
    bias = bias_out.reshape(-1)
    return (
        predicted,
        grad_input,
        r_one,
        r_two,
        r_point,
        r_human,
        r_mouse,
        bias[:human_tracks],
        bias[human_wide : human_wide + mouse_tracks],
        jnp.sum(sums_one[MB:], axis=0),
        jnp.sum(sums_one[:MB], axis=0),
        jnp.sum(sums_two[MB:], axis=0),
        jnp.sum(sums_two[:MB], axis=0),
        jnp.sum(sums_three[MB:], axis=0),
        jnp.sum(sums_three[:MB], axis=0),
    )


def solution(mesh):
    shape = (mesh.shape["section"], mesh.shape["seq"], mesh.shape["dp"])
    placed = (
        P("dp", "seq", None),
        P("dp"),
        P(),
        P(None, None, "dp"),
        P(None, "dp", None),
        P(None, "dp"),
        P("dp", None),
        P("dp", None),
    ) + (P(),) * 8 + (P("dp", "seq", None),)
    return jax.shard_map(
        functools.partial(per_device, shape),
        mesh=mesh,
        in_specs=placed,
        out_specs=(
            P("dp", ("seq", "section"), None),
            P("dp", ("seq", "section"), None),
            P(None, None, "dp"),
            P(None, "dp", None),
            P(None, "dp"),
            P("dp", None),
            P("dp", None),
        )
        + (P(),) * 8,
        check_vma=False,
    )
```

```python
import functools
import math

import jax
import jax.numpy as jnp
from jax import lax
from jax.experimental import pallas as pl
from jax.experimental.pallas import tpu as pltpu
from jax.sharding import PartitionSpec as P

MESH = pl.DeviceIdType.MESH
DILATION = 11
MB = 4
EPS = 1e-05
EDGE = 16
BLOCK = 1792
LANES = 128
VMEM_LIMIT = 60 * 1024 * 1024
GELU_K = math.sqrt(2.0 / math.pi)
GELU_C = 0.044715
f32 = jnp.float32
bf16 = jnp.bfloat16
VM = pl.BlockSpec(memory_space=pltpu.VMEM)
HBM = pl.BlockSpec(memory_space=pl.ANY)


def params(collective_id=None, limit=VMEM_LIMIT):
    if collective_id is None:
        return pltpu.CompilerParams(vmem_limit_bytes=limit)
    return pltpu.CompilerParams(
        vmem_limit_bytes=limit, collective_id=collective_id, has_side_effects=True
    )


def gelu(u):
    t = jnp.tanh(u * (GELU_K + (GELU_K * GELU_C) * (u * u)))
    h = 0.5 * u
    return h + h * t


def gelu_slope(u):
    uu = u * u
    t = jnp.tanh(u * (GELU_K + (GELU_K * GELU_C) * uu))
    return 0.5 * (1.0 + t) + (0.5 * u) * (1.0 - t * t) * (GELU_K + (3.0 * GELU_K * GELU_C) * uu)


def dot_nn(a, b):
    return jnp.dot(a, b, preferred_element_type=f32)


def dot_nt(a, b):
    return lax.dot_general(a, b, (((1,), (1,)), ((), ())), preferred_element_type=f32)


def dot_tn(a, b):
    return lax.dot_general(a, b, (((0,), (0,)), ((), ())), preferred_element_type=f32)


class Place:
    def __init__(self, shape):
        self.n_sec, self.n_seq, self.n_dp = shape
        self.n_near = self.n_sec * self.n_dp
        self.sec = lax.axis_index("section")
        self.seq = lax.axis_index("seq")
        self.dp = lax.axis_index("dp")
        self.near = self.sec * self.n_dp + self.dp
        n_bins = self.n_seq * self.n_sec
        bins = self.seq * self.n_sec + self.sec
        self.is_first = bins == 0
        self.is_last = bins == n_bins - 1
        low = lax.rem(bins + n_bins - 1, n_bins)
        high = lax.rem(bins + 1, n_bins)
        self.low = self.bin_device(low)
        self.high = self.bin_device(high)
        across = jnp.where(self.sec == 0, low, high)
        self.across = self.bin_device(across)

    def bin_device(self, bins):
        return (lax.rem(bins, self.n_sec), lax.div(bins, self.n_sec), self.dp)

    def near_device(self, rank):
        return (lax.div(rank, self.n_dp), self.seq, lax.rem(rank, self.n_dp))

    def greet(self):
        barrier = pltpu.get_barrier_semaphore()
        for k in range(1, self.n_near):
            rank = lax.rem(self.near + k, self.n_near)
            pl.semaphore_signal(
                barrier, inc=1, device_id=self.near_device(rank), device_id_type=MESH
            )
        for k in range(1, self.n_seq):
            seq = lax.rem(self.seq + k, self.n_seq)
            pl.semaphore_signal(
                barrier, inc=1, device_id=(self.sec, seq, self.dp), device_id_type=MESH
            )
        pl.semaphore_signal(barrier, inc=1, device_id=self.across, device_id_type=MESH)

    def meet(self):
        pl.semaphore_wait(pltpu.get_barrier_semaphore(), self.n_near + self.n_seq - 1)


def halo_copies(place, from_self, arrived, sems):
    up = pltpu.make_async_remote_copy(
        src_ref=from_self[1],
        dst_ref=arrived[0],
        send_sem=sems.at[0],
        recv_sem=sems.at[1],
        device_id=place.high,
        device_id_type=MESH,
    )
    down = pltpu.make_async_remote_copy(
        src_ref=from_self[0],
        dst_ref=arrived[1],
        send_sem=sems.at[2],
        recv_sem=sems.at[3],
        device_id=place.low,
        device_id_type=MESH,
    )
    return up, down


def spread_round(buffer, mine, count, device_of, send, recv):
    copies = []
    for k in range(1, count):
        rank = lax.rem(mine + k, count)
        copy = pltpu.make_async_remote_copy(
            src_ref=buffer.at[mine],
            dst_ref=buffer.at[mine],
            send_sem=send.at[k],
            recv_sem=recv.at[mine],
            device_id=device_of(rank),
            device_id_type=MESH,
        )
        copy.start()
        copies.append((rank, copy))
    for rank, copy in copies:
        pltpu.make_async_remote_copy(
            src_ref=buffer.at[rank],
            dst_ref=buffer.at[rank],
            send_sem=send.at[0],
            recv_sem=recv.at[rank],
            device_id=device_of(rank),
            device_id_type=MESH,
        ).wait_recv()
    for rank, copy in copies:
        copy.wait_send()


def reduce_everywhere(place, value, near_buf, far_buf, sems, combine):
    near_send, near_recv, far_send, far_recv = sems
    near_buf[place.near] = value
    spread_round(
        near_buf, place.near, place.n_near, place.near_device, near_send, near_recv
    )
    far_buf[place.seq] = combine(near_buf, place.n_near, 1)
    spread_round(
        far_buf,
        place.seq,
        place.n_seq,
        lambda seq: (place.sec, seq, place.dp),
        far_send,
        far_recv,
    )
    return combine(far_buf, place.n_seq, place.n_near)


def add_up(buffer, count, weight):
    total = buffer[0]
    for i in range(1, count):
        total = total + buffer[i]
    return total


def merge_stats(rows, buffer, count, weight):
    means = [buffer[i][:MB] for i in range(count)]
    centre = means[0]
    spread = buffer[0][MB:]
    for i in range(1, count):
        centre = centre + means[i]
        spread = spread + buffer[i][MB:]
    centre = centre * (1.0 / count)
    apart = jnp.square(means[0] - centre)
    for i in range(1, count):
        apart = apart + jnp.square(means[i] - centre)
    return jnp.concatenate([centre, spread + apart * float(rows * weight)], axis=0)


def reduce_scratch(shape, rows, columns):
    n_sec, n_seq, n_dp = shape
    near = n_sec * n_dp
    return [
        pltpu.VMEM((near, rows, columns), f32),
        pltpu.VMEM((n_seq, rows, columns), f32),
        pltpu.SemaphoreType.DMA((near,)),
        pltpu.SemaphoreType.DMA((near,)),
        pltpu.SemaphoreType.DMA((n_seq,)),
        pltpu.SemaphoreType.DMA((n_seq,)),
    ]


def local_stats(value):
    count = value.shape[0]
    centre = jnp.sum(value, axis=0, keepdims=True) * (1.0 / count)
    return centre, jnp.sum(jnp.square(value - centre), axis=0, keepdims=True)


def finish_stats(stats, total):
    return jnp.concatenate(
        [stats[:MB], lax.rsqrt(stats[MB:] * (1.0 / total) + EPS)], axis=0
    )


def prepare_kernel(meta, first, second, pairs, low, high, stats, scratch):
    m = pl.program_id(0)
    half = scratch.shape[1]
    start = pl.multiple_of(meta[meta.shape[0] - 1] * half, half)
    values = []
    for i, ref in enumerate((first, second)):
        value = ref[0, pl.ds(start, half), :].astype(f32)
        values.append(value)
        lanes = scratch.shape[0]
        for c in range(lanes):
            scratch[c] = value[:, c * LANES : (c + 1) * LANES]
        both = jnp.concatenate(
            [scratch[c, pl.ds(odd, half // 2, 2), :] for odd in range(2) for c in range(lanes)],
            axis=1,
        )
        pairs[i] = both.astype(bf16)
        low[pl.ds(2 * m + i, 1), :] = both[:1]
        high[pl.ds(2 * m + i, 1), :] = both[half // 2 - 1 :]
    count = 2 * half
    centre = (
        jnp.sum(values[0], axis=0, keepdims=True) + jnp.sum(values[1], axis=0, keepdims=True)
    ) * (1.0 / count)
    spread = jnp.sum(jnp.square(values[0] - centre), axis=0, keepdims=True) + jnp.sum(
        jnp.square(values[1] - centre), axis=0, keepdims=True
    )
    stats[pl.ds(m, 1), :] = centre
    stats[pl.ds(MB + m, 1), :] = spread


def prepare(tracks, meta, half):
    windows, length, channels = tracks.shape
    whole = lambda shape: pl.BlockSpec(shape, lambda m, meta: (0,) * len(shape))
    return pl.pallas_call(
        prepare_kernel,
        grid_spec=pltpu.PrefetchScalarGridSpec(
            num_scalar_prefetch=1,
            grid=(MB,),
            in_specs=[
                pl.BlockSpec((1, length, channels), lambda m, meta: (meta[2 * m], 0, 0)),
                pl.BlockSpec((1, length, channels), lambda m, meta: (meta[2 * m + 1], 0, 0)),
            ],
            out_specs=[
                pl.BlockSpec((2, half // 2, 2 * channels), lambda m, meta: (m, 0, 0)),
                whole((windows, 2 * channels)),
                whole((windows, 2 * channels)),
                whole((2 * MB, channels)),
            ],
            scratch_shapes=[pltpu.VMEM((channels // LANES, half, LANES), f32)],
        ),
        out_shape=[
            jax.ShapeDtypeStruct((windows, half // 2, 2 * channels), bf16),
            jax.ShapeDtypeStruct((windows, 2 * channels), f32),
            jax.ShapeDtypeStruct((windows, 2 * channels), f32),
            jax.ShapeDtypeStruct((2 * MB, channels), f32),
        ],
        compiler_params=params(),
        name="prepare",
    )(meta, tracks, tracks)


class Gathering:
    STAGES = 5

    def __init__(self, place, shard, full, rows_at, sems):
        self.place, self.shard, self.full, self.rows_at, self.sems = place, shard, full, rows_at, sems
        p = place
        x, y, z = lax.rem(p.dp, 2), lax.div(p.dp, 2), lax.rem(p.seq, 2)
        self.share = shard.shape[rows_at]
        self.group = self.share // 6
        g = self.group
        self.dp_x, self.dp_y = p.dp + 1 - 2 * x, p.dp + 2 - 4 * y
        self.dp_xy = 3 - p.dp
        self.sibling = (1 - p.sec, p.seq, p.dp)
        self.over_x, self.over_y = (p.sec, p.seq, self.dp_x), (p.sec, p.seq, self.dp_y)
        self.over_z = (p.sec, p.seq + 1 - 2 * z, p.dp)
        base = p.sec * 3 * g
        self.near, self.middle, self.edge, self.far, self.half = (
            (base + z * g, 2 * g),
            (base + g, g),
            (base + 2 * z * g, g),
            (base + 2 * (1 - z) * g, g),
            (base, 3 * g),
        )

    def at(self, ref, dp, span):
        start, rows = span
        index = pl.ds(pl.multiple_of(dp * self.share + start, self.group), rows)
        return ref.at[:, index] if self.rows_at else ref.at[index]

    def remote(self, dp, span, sem, device, source=None):
        source = self.at(self.full, dp, span) if source is None else source
        return pltpu.make_async_remote_copy(
            src_ref=source,
            dst_ref=self.at(self.full, dp, span),
            send_sem=self.sems.at[2 * sem],
            recv_sem=self.sems.at[2 * sem + 1],
            device_id=device,
            device_id_type=MESH,
        )

    def own_copy(self):
        target = self.at(self.full, self.place.dp, (0, self.share))
        return pltpu.make_async_copy(self.shard, target, self.sems.at[26])

    def copies(self, stage):
        me = self.place.dp
        if stage == 0:
            own = self.at(self.shard, 0, self.near)
            return [
                self.remote(me, self.near, 0, self.over_x, own),
                self.remote(me, self.near, 1, self.over_y, own),
            ]
        if stage == 1:
            return [
                self.remote(self.dp_x, self.middle, 2, self.over_y),
                self.remote(self.dp_y, self.edge, 3, self.over_x),
                self.remote(self.dp_x, self.edge, 4, self.over_z),
                self.remote(self.dp_y, self.edge, 5, self.over_z),
                self.remote(self.dp_x, self.near, 6, self.sibling),
                self.remote(self.dp_y, self.near, 7, self.sibling),
            ]
        if stage == 2:
            return [
                self.remote(self.dp_xy, self.edge, 8, self.over_z),
                self.remote(self.dp_xy, self.near, 9, self.sibling),
            ]
        if stage == 3:
            return [
                self.remote(self.dp_x, self.far, 10, self.sibling),
                self.remote(self.dp_y, self.far, 11, self.sibling),
                self.remote(self.dp_xy, self.far, 12, self.sibling),
            ]
        return []

    def start(self, stage):
        for copy in self.copies(stage):
            copy.start()

    def arrived(self, stage, which, dp, span):
        copy = self.copies(stage)[which]
        pltpu.make_async_remote_copy(
            src_ref=self.at(self.full, dp, span),
            dst_ref=self.at(self.full, dp, span),
            send_sem=self.sems.at[0],
            recv_sem=self.sems.at[2 * {0: 0, 1: 2, 2: 8, 3: 10}[stage] + 2 * which + 1],
            device_id=self.sibling,
            device_id_type=MESH,
        ).wait_recv()

    def advance(self, stage):
        if stage == 0:
            self.own_copy().start()
        elif stage == 1:
            self.arrived(0, 0, self.dp_x, self.near)
            self.arrived(0, 1, self.dp_y, self.near)
        elif stage == 2:
            self.arrived(1, 0, self.dp_xy, self.middle)
            self.arrived(1, 1, self.dp_xy, self.edge)
        elif stage == 3:
            self.arrived(1, 2, self.dp_x, self.far)
            self.arrived(1, 3, self.dp_y, self.far)
            self.arrived(2, 0, self.dp_xy, self.far)
        if stage < 4:
            self.start(stage)
            return
        base = (1 - self.place.sec) * 3 * self.group
        z = lax.rem(self.place.seq, 2)
        near = (base + z * self.group, 2 * self.group)
        far = (base + 2 * (1 - z) * self.group, self.group)
        self.arrived(1, 4, self.dp_x, near)
        self.arrived(1, 5, self.dp_y, near)
        self.arrived(2, 1, self.dp_xy, near)
        self.arrived(3, 0, self.dp_x, far)
        self.arrived(3, 1, self.dp_y, far)
        self.arrived(3, 2, self.dp_xy, far)
        self.own_copy().wait()
        for stage in range(4):
            for copy in self.copies(stage):
                copy.wait_send()


def shifted_rows(value, offset, length):
    rows = value.shape[0]
    if offset:
        value = pltpu.roll(value, rows - offset, axis=0)
    return value[:length]


def forward_kernel(shape, *refs):
    (
        x2,
        edge_low,
        edge_high,
        stats_in,
        gain_one,
        shift_one,
        gain_two,
        shift_two,
        gain_three,
        shift_three,
        in_one,
        in_two,
        in_point,
    ) = refs[:13]
    refs = refs[13:]
    (
        out_u_one,
        out_u_two,
        pooled,
        pooled_low,
        pooled_high,
        branch,
        branch_low,
        branch_high,
        act_three,
        summed,
        bn_one,
        bn_two,
        bn_three,
        out_one,
        out_two,
        out_point,
    ) = refs[:16]
    refs = refs[16:]
    (
        near_one,
        far_one,
        s10,
        s11,
        s12,
        s13,
        near_two,
        far_two,
        s20,
        s21,
        s22,
        s23,
        near_three,
        far_three,
        s30,
        s31,
        s32,
        s33,
        got_low,
        got_high,
        stats_two,
        stats_three,
        halo_sems,
        s_branch_edge_low,
        s_branch_edge_high,
        u_one,
        u_two,
        w_one,
        w_two,
        w_point,
        weight_sems,
        save_sems,
    ) = refs
    place = Place(shape)
    place.greet()
    windows, length, wide = x2.shape
    channels = wide // 2
    mid = pooled.shape[2]
    small = branch.shape[1]
    parts = shape[0] * shape[1] * shape[2]
    pair = 2 * length
    saves = [
        pltpu.make_async_copy(source, target, save_sems.at[i])
        for i, (source, target) in enumerate(
            ((u_one, out_u_one), (u_two, out_u_two), (w_one, out_one), (w_two, out_two), (w_point, out_point))
        )
    ]
    gathers = []
    if in_one.shape[0] < w_one.shape[0]:
        pieces = [(in_one, w_one, 0), (in_two, w_two, 1), (in_point, w_point, 0)]
        gathers = [
            Gathering(place, *piece, weight_sems.at[i]) for i, piece in enumerate(pieces)
        ]
    else:
        loads = [
            pltpu.make_async_copy(source, target, weight_sems.at[i, 0])
            for i, (source, target) in enumerate(
                ((in_one, w_one), (in_two, w_two), (in_point, w_point))
            )
        ]
        for load in loads:
            load.start()
        for load in loads:
            load.wait()

    def advance(*steps):
        for index, stage in steps:
            if index < len(gathers):
                gathers[index].advance(stage)

    place.meet()
    advance((0, 0))
    up, down = halo_copies(place, (edge_low, edge_high), (got_low, got_high), halo_sems.at[0])
    up.start()
    down.start()
    stats = reduce_everywhere(
        place,
        stats_in[...],
        near_one,
        far_one,
        (s10, s11, s12, s13),
        functools.partial(merge_stats, 4 * length),
    )
    stats = finish_stats(stats, 4 * length * parts)
    bn_one[...] = jnp.concatenate([stats, stats], axis=1)
    up.wait()
    down.wait()
    advance((0, 1), (1, 0), (2, 0))

    @pl.loop(0, windows)
    def _(w):
        m = lax.div(w, 2)
        centre = bn_one[pl.ds(m, 1), :]
        scale = bn_one[pl.ds(MB + m, 1), :] * gain_one[...]
        move = shift_one[...]

        def act(value):
            return gelu((value - centre) * scale + move).astype(bf16).astype(f32)

        main = act(x2[w].astype(f32))
        before = jnp.where(place.is_first, 0.0, act(got_low[pl.ds(w, 1), :]))
        after = jnp.where(place.is_last, 0.0, act(got_high[pl.ds(w, 1), :]))
        even, odd = main[:, :channels], main[:, channels:]
        mean = (even + odd) * 0.5
        mean_before = (before[:, :channels] + before[:, channels:]) * 0.5
        mean_after = (after[:, :channels] + after[:, channels:]) * 0.5
        row = lax.broadcasted_iota(jnp.int32, (length, channels), 0)
        top, bottom = row == 0, row == length - 1
        odd_before = jnp.where(top, before[:, channels:], pltpu.roll(odd, 1, axis=0))
        cross = (odd_before + even) * 0.5
        cross_after = (odd[length - 1 :] + after[:, :channels]) * 0.5
        start = pl.multiple_of(w * length, length)
        taps = (
            jnp.where(top, mean_before, pltpu.roll(mean, 1, axis=0)),
            cross,
            mean,
            jnp.where(bottom, cross_after, pltpu.roll(cross, length - 1, axis=0)),
            jnp.where(bottom, mean_after, pltpu.roll(mean, length - 1, axis=0)),
        )
        for t, tap in enumerate(taps):
            u_one[pl.ds(start, length), t * channels : (t + 1) * channels] = tap.astype(bf16)

    saves[0].start()
    advance((0, 2), (1, 1), (2, 1), (0, 3), (1, 2), (2, 2), (0, 4))
    saves[2].start()

    @pl.loop(0, MB)
    def _(m):
        start = pl.multiple_of(m * pair, pair)
        value = dot_nt(u_one[pl.ds(start, pair), :], w_one[...]).astype(bf16)
        pooled[pl.ds(2 * m, 2)] = value.reshape(2, length, mid)
        centre, spread = local_stats(value.astype(f32))
        stats_two[pl.ds(m, 1), :] = centre
        stats_two[pl.ds(MB + m, 1), :] = spread

    up, down = halo_copies(
        place,
        (pooled.at[:, pl.ds(0, EDGE), :], pooled.at[:, pl.ds(length - EDGE, EDGE), :]),
        (pooled_low, pooled_high),
        halo_sems.at[1],
    )
    up.start()
    down.start()
    stats = reduce_everywhere(
        place,
        stats_two[...],
        near_two,
        far_two,
        (s20, s21, s22, s23),
        functools.partial(merge_stats, pair),
    )
    bn_two[...] = finish_stats(stats, pair * parts)
    up.wait()
    down.wait()
    advance((1, 3), (2, 3))

    @pl.loop(0, windows)
    def _(w):
        m = lax.div(w, 2)
        centre = bn_two[pl.ds(m, 1), :]
        scale = bn_two[pl.ds(MB + m, 1), :] * gain_two[...]
        move = shift_two[...]

        def act(value):
            return gelu((value.astype(f32) - centre) * scale + move)

        ext = jnp.concatenate(
            [
                jnp.where(place.is_first, 0.0, act(pooled_low[w])),
                act(pooled[w]),
                jnp.where(place.is_last, 0.0, act(pooled_high[w])),
            ],
            axis=0,
        )
        start = pl.multiple_of(w * length, length)
        for t in range(3):
            tap = shifted_rows(ext, EDGE + (t - 1) * DILATION, length)
            u_two[pl.ds(start, length), t * mid : (t + 1) * mid] = tap.astype(bf16)

    saves[1].start()
    advance((1, 4), (2, 4))
    saves[3].start()
    saves[4].start()

    @pl.loop(0, MB)
    def _(m):
        start = pl.multiple_of(m * pair, pair)
        value = jnp.zeros((pair, small), f32)
        for t in range(w_two.shape[0]):
            value = value + dot_nn(
                u_two[pl.ds(start, pair), t * mid : (t + 1) * mid], w_two[t]
            )
        branch[pl.ds(start, pair), :] = value
        centre, spread = local_stats(value)
        stats_three[pl.ds(m, 1), :] = centre
        stats_three[pl.ds(MB + m, 1), :] = spread
        for i in range(2):
            s_branch_edge_low[2 * m + i] = value[i * length : i * length + EDGE]
            s_branch_edge_high[2 * m + i] = value[(i + 1) * length - EDGE : (i + 1) * length]

    up, down = halo_copies(
        place,
        (s_branch_edge_low, s_branch_edge_high),
        (branch_low, branch_high),
        halo_sems.at[2],
    )
    up.start()
    down.start()
    stats = reduce_everywhere(
        place,
        stats_three[...],
        near_three,
        far_three,
        (s30, s31, s32, s33),
        functools.partial(merge_stats, pair),
    )
    bn_three[...] = finish_stats(stats, pair * parts)

    @pl.loop(0, MB)
    def _(m):
        centre = bn_three[pl.ds(m, 1), :]
        scale = bn_three[pl.ds(MB + m, 1), :] * gain_three[...]
        start = pl.multiple_of(m * pair, pair)
        act = gelu((branch[pl.ds(start, pair), :] - centre) * scale + shift_three[...])
        act = act.astype(bf16)
        act_three[pl.ds(start, pair), :] = act
        lifted = dot_nt(act, w_point[...])
        here = pooled[pl.ds(2 * m, 2)].reshape(pair, mid).astype(f32)
        summed[pl.ds(start, pair), :] = (here + lifted).astype(bf16)

    up.wait()
    down.wait()
    for save in saves:
        save.wait()


def forward(shape, mid, x2, edge_low, edge_high, stats, gains, w_one, w_two, w_point):
    windows, length, wide = x2.shape
    rows = windows * length
    taps_two, _, small = w_two.shape
    big = [
        ((mid, w_one.shape[1]), bf16),
        ((taps_two, mid, small), bf16),
        ((mid, small), bf16),
    ]
    out = [
        ((rows, w_one.shape[1]), bf16),
        ((rows, taps_two * mid), bf16),
        ((windows, length, mid), bf16),
        ((windows, EDGE, mid), bf16),
        ((windows, EDGE, mid), bf16),
        ((rows, small), f32),
        ((windows, EDGE, small), f32),
        ((windows, EDGE, small), f32),
        ((rows, small), bf16),
        ((rows, mid), bf16),
        ((2 * MB, wide), f32),
        ((2 * MB, mid), f32),
        ((2 * MB, small), f32),
    ]
    out_specs = [HBM] * 2 + [VM] * 11 + [HBM] * 3
    out += big
    scratch = (
        reduce_scratch(shape, 2 * MB, wide // 2)
        + reduce_scratch(shape, 2 * MB, mid)
        + reduce_scratch(shape, 2 * MB, small)
    )
    scratch += [
        pltpu.VMEM((windows, wide), f32),
        pltpu.VMEM((windows, wide), f32),
        pltpu.VMEM((2 * MB, mid), f32),
        pltpu.VMEM((2 * MB, small), f32),
        pltpu.SemaphoreType.DMA((3, 4)),
        pltpu.VMEM((windows, EDGE, small), f32),
        pltpu.VMEM((windows, EDGE, small), f32),
        pltpu.VMEM(*out[0]),
        pltpu.VMEM(*out[1]),
    ]
    scratch += [pltpu.VMEM(*b) for b in big]
    scratch += [
        pltpu.SemaphoreType.DMA((3, 27)),
        pltpu.SemaphoreType.DMA((5,)),
    ]
    return pl.pallas_call(
        functools.partial(forward_kernel, shape),
        in_specs=[VM] * 10 + [HBM] * 3,
        out_specs=out_specs,
        out_shape=[jax.ShapeDtypeStruct(*o) for o in out],
        scratch_shapes=scratch,
        compiler_params=params(1),
        name="forward",
    )(x2, edge_low, edge_high, stats, *gains, w_one, w_two, w_point)


def heads_kernel(
    human_tracks,
    mouse_tracks,
    meta,
    summed,
    w_human,
    w_mouse,
    b_human,
    b_mouse,
    cot,
    predicted,
    grad_summed,
    d_human,
    d_mouse,
    db_human,
    db_mouse,
    rows_sorted,
    grad_sorted,
    grad_pre,
):
    j = pl.program_id(0)
    windows, length, block = cot.shape
    pair = 2 * length
    n_pairs = windows // 2
    mid = summed.shape[1]
    n_human = meta[2 * windows]

    @pl.when(j == 0)
    def _():
        grad_sorted[...] = jnp.zeros_like(grad_sorted)

        @pl.loop(0, windows)
        def _(s):
            source = pl.multiple_of(meta[s] * length, length)
            target = pl.multiple_of(s * length, length)
            rows_sorted[pl.ds(target, length), :] = summed[pl.ds(source, length), :]

    column = lax.broadcasted_iota(jnp.int32, (1, block), 1)

    def run(weight, bias, limit, is_mouse, first_pair, last_pair):
        def body(p, carry):
            start = pl.multiple_of(p * pair, pair)
            pre = dot_nn(rows_sorted[pl.ds(start, pair), :], weight[...]) + bias[...]
            decay = jnp.exp(-jnp.abs(pre))
            whole = 1.0 + decay
            inverse = 1.0 / whole
            sigmoid = jnp.where(pre >= 0, inverse, decay * inverse)
            logs = jnp.where(decay < 2.0**-11, decay, jnp.log(whole))
            output = (jnp.maximum(pre, 0.0) + logs).astype(bf16)
            output = jnp.where(column < limit, output, jnp.zeros_like(output))
            for i in range(2):
                s = 2 * p + i
                window = meta[windows + s]
                mine = s >= n_human if is_mouse else s < n_human
                keep = (column < limit) & mine
                part = slice(i * length, (i + 1) * length)
                grad = jnp.where(keep, cot[window].astype(f32) * sigmoid[part], 0.0)
                grad_pre[pl.ds(pl.multiple_of(s * length, length), length), :] = grad.astype(bf16)

                @pl.when(mine)
                def _():
                    predicted[window] = output[part]

            grad_sorted[pl.ds(start, pair), :] += dot_nt(
                grad_pre[pl.ds(start, pair), :], weight[...]
            )
            return carry

        lax.fori_loop(first_pair, last_pair, body, 0)

    def weight_grads(count, n_used, from_end, d_weight, d_bias):
        for n in range(n_pairs + 1):

            @pl.when(n_used == n)
            def _(n=n):
                if n == 0:
                    d_weight[...] = jnp.zeros_like(d_weight)
                    d_bias[...] = jnp.zeros_like(d_bias)
                else:
                    part = slice((n_pairs - n) * pair, None) if from_end else slice(0, n * pair)
                    grad = grad_pre[part, :]
                    d_weight[...] = dot_tn(rows_sorted[part, :], grad).astype(bf16)
                    d_bias[...] = dot_nn(jnp.ones((8, n * pair), bf16), grad)[:1]

    human_pairs = lax.div(n_human + 1, 2)
    run(w_human, b_human, human_tracks - j * block, False, 0, human_pairs)
    weight_grads(n_pairs, human_pairs, False, d_human, db_human)

    @pl.when(j == 0)
    def _():
        mouse_start = lax.div(n_human, 2)
        run(w_mouse, b_mouse, mouse_tracks, True, mouse_start, n_pairs)
        weight_grads(n_pairs, n_pairs - mouse_start, True, d_mouse, db_mouse)

    @pl.when(j > 0)
    def _():
        def body(s, carry):
            predicted[meta[windows + s]] = jnp.zeros((length, block), bf16)
            return carry

        lax.fori_loop(n_human, windows, body, 0)

    @pl.when(j == pl.num_programs(0) - 1)
    def _():
        @pl.loop(0, windows)
        def _(s):
            source = pl.multiple_of(s * length, length)
            target = pl.multiple_of(meta[s] * length, length)
            grad_summed[pl.ds(target, length), :] = grad_sorted[pl.ds(source, length), :]


def heads(meta, summed, w_heads, b_human, b_mouse, cotangent, mouse_tracks, length):
    windows, _, human_tracks = cotangent.shape
    rows, mid = summed.shape
    blocks = w_heads.shape[1] // BLOCK - 1
    row_block = pl.BlockSpec((1, BLOCK), lambda j, meta: (0, j))
    row_fixed = pl.BlockSpec((1, BLOCK), lambda j, meta: (0, 0))
    fixed = pl.BlockSpec((rows, mid), lambda j, meta: (0, 0))
    return pl.pallas_call(
        functools.partial(heads_kernel, human_tracks, mouse_tracks),
        grid_spec=pltpu.PrefetchScalarGridSpec(
            num_scalar_prefetch=1,
            grid=(blocks,),
            in_specs=[
                fixed,
                pl.BlockSpec((mid, BLOCK), lambda j, meta: (0, j)),
                pl.BlockSpec(
                    (mid, BLOCK), lambda j, meta: (0, blocks), pipeline_mode=pl.Buffered(1)
                ),
                row_block,
                row_fixed,
                pl.BlockSpec((windows, length, BLOCK), lambda j, meta: (0, 0, j)),
            ],
            out_specs=[
                pl.BlockSpec((windows, length, BLOCK), lambda j, meta: (0, 0, j)),
                fixed,
                pl.BlockSpec((mid, BLOCK), lambda j, meta: (0, j)),
                pl.BlockSpec((mid, BLOCK), lambda j, meta: (0, 0)),
                row_block,
                row_fixed,
            ],
            scratch_shapes=[
                pltpu.VMEM((rows, mid), bf16),
                pltpu.VMEM((rows, mid), f32),
                pltpu.VMEM((rows, BLOCK), bf16),
            ],
        ),
        out_shape=[
            jax.ShapeDtypeStruct((windows, length, human_tracks), bf16),
            jax.ShapeDtypeStruct((rows, mid), f32),
            jax.ShapeDtypeStruct((mid, blocks * BLOCK), bf16),
            jax.ShapeDtypeStruct((mid, BLOCK), bf16),
            jax.ShapeDtypeStruct((1, blocks * BLOCK), f32),
            jax.ShapeDtypeStruct((1, BLOCK), f32),
        ],
        compiler_params=params(),
        name="heads",
    )(meta, summed, w_heads, w_heads, b_human, b_mouse, cotangent)


def back_three_kernel(
    shape,
    grad_summed,
    act_three,
    branch,
    bn_three,
    gain_three,
    shift_three,
    w_point,
    bias_sums,
    d_point,
    du_three,
    du_low,
    du_high,
    gs_low,
    gs_high,
    sums_three,
    bias_out,
    near,
    far,
    s0,
    s1,
    s2,
    s3,
    near_b,
    far_b,
    b0,
    b1,
    b2,
    b3,
    edge_low,
    edge_high,
    row_low,
    row_high,
    sums,
    halo_sems,
):
    place = Place(shape)
    place.greet()
    rows, mid = grad_summed.shape
    pair = rows // MB
    length = pair // 2

    @pl.loop(0, MB)
    def _(m):
        start = pl.multiple_of(m * pair, pair)
        grad = grad_summed[pl.ds(start, pair), :]
        back = dot_nn(grad.astype(bf16), w_point[...])
        centre = bn_three[pl.ds(m, 1), :]
        xhat = (branch[pl.ds(start, pair), :] - centre) * bn_three[pl.ds(MB + m, 1), :]
        du = gelu_slope(xhat * gain_three[...] + shift_three[...]) * back
        du_three[pl.ds(start, pair), :] = du
        sums[pl.ds(m, 1), :] = jnp.sum(du, axis=0, keepdims=True)
        sums[pl.ds(MB + m, 1), :] = jnp.sum(du * xhat, axis=0, keepdims=True)
        for i in range(2):
            edge_low[2 * m + i] = du[i * length : i * length + EDGE]
            edge_high[2 * m + i] = du[(i + 1) * length - EDGE : (i + 1) * length]
            row_low[pl.ds(2 * m + i, 1), :] = grad[i * length : i * length + 1]
            row_high[pl.ds(2 * m + i, 1), :] = grad[(i + 1) * length - 1 : (i + 1) * length]

    place.meet()
    moves = halo_copies(place, (edge_low, edge_high), (du_low, du_high), halo_sems.at[0])
    moves += halo_copies(place, (row_low, row_high), (gs_low, gs_high), halo_sems.at[1])
    for move in moves:
        move.start()
    bias_out[...] = reduce_everywhere(
        place, bias_sums[...], near_b, far_b, (b0, b1, b2, b3), add_up
    )
    sums_three[...] = reduce_everywhere(place, sums[...], near, far, (s0, s1, s2, s3), add_up)
    d_point[...] = dot_tn(grad_summed[...].astype(bf16), act_three[...]).astype(bf16)
    for move in moves:
        move.wait()


def back_three(shape, windows, grad_summed, act_three, branch, bn_three, gain, move, w_point, bias_sums):
    rows, mid = grad_summed.shape
    small = branch.shape[1]
    out = [
        ((mid, small), bf16),
        ((rows, small), f32),
        ((windows, EDGE, small), f32),
        ((windows, EDGE, small), f32),
        ((windows, mid), f32),
        ((windows, mid), f32),
        ((2 * MB, small), f32),
        (bias_sums.shape, f32),
    ]
    scratch = reduce_scratch(shape, 2 * MB, small) + reduce_scratch(shape, *bias_sums.shape)
    scratch += [
        pltpu.VMEM((windows, EDGE, small), f32),
        pltpu.VMEM((windows, EDGE, small), f32),
        pltpu.VMEM((windows, mid), f32),
        pltpu.VMEM((windows, mid), f32),
        pltpu.VMEM((2 * MB, small), f32),
        pltpu.SemaphoreType.DMA((2, 4)),
    ]
    return pl.pallas_call(
        functools.partial(back_three_kernel, shape),
        in_specs=[VM] * 8,
        out_specs=[VM] * len(out),
        out_shape=[jax.ShapeDtypeStruct(*o) for o in out],
        scratch_shapes=scratch,
        compiler_params=params(2),
        name="back_three",
    )(grad_summed, act_three, branch, bn_three, gain, move, w_point, bias_sums)


def back_two_kernel(
    shape,
    du_three,
    du_low,
    du_high,
    sums_three,
    branch,
    branch_low,
    branch_high,
    bn_three,
    gain_three,
    u_two,
    w_two,
    pooled,
    bn_two,
    gain_two,
    shift_two,
    d_two,
    du_two,
    row_low_out,
    row_high_out,
    sums_two,
    near,
    far,
    s0,
    s1,
    s2,
    s3,
    row_low,
    row_high,
    sums,
    grad_branch,
    halo_sems,
):
    place = Place(shape)
    place.greet()
    windows, length, mid = pooled.shape
    parts = shape[0] * shape[1] * shape[2]
    pair = 2 * length
    scale = 1.0 / (pair * parts)
    taps = w_two.shape[0] // mid

    @pl.loop(0, MB)
    def _(m):
        start = pl.multiple_of(m * pair, pair)
        centre = bn_three[pl.ds(m, 1), :]
        inverse = bn_three[pl.ds(MB + m, 1), :]
        factor = gain_three[...] * inverse
        mean_du = sums_three[pl.ds(m, 1), :] * scale
        mean_dx = sums_three[pl.ds(MB + m, 1), :] * scale

        def back(du, value):
            xhat = (value - centre) * inverse
            return factor * (du - mean_du - xhat * mean_dx)

        main = back(du_three[pl.ds(start, pair), :], branch[pl.ds(start, pair), :])
        grad_branch[pl.ds(start, pair), :] = main.astype(bf16)
        pieces = []
        for i in range(2):
            w = 2 * m + i
            low = jnp.where(place.is_first, 0.0, back(du_low[w], branch_low[w]))
            high = jnp.where(place.is_last, 0.0, back(du_high[w], branch_high[w]))
            pieces += [low, main[i * length : (i + 1) * length], high]
        ext = jnp.concatenate(pieces, axis=0).astype(bf16)
        span = length + 2 * EDGE
        through = [dot_nt(ext, w_two[t * mid : (t + 1) * mid, :]) for t in range(taps)]
        centre_two = bn_two[pl.ds(m, 1), :]
        inverse_two = bn_two[pl.ds(MB + m, 1), :]
        total_du = jnp.zeros((1, mid), f32)
        total_dx = jnp.zeros((1, mid), f32)
        for i in range(2):
            w = 2 * m + i
            grad = jnp.zeros((length, mid), f32)
            for t in range(taps):
                whole = through[t][i * span : (i + 1) * span]
                grad = grad + shifted_rows(whole, EDGE - (t - 1) * DILATION, length)
            xhat = (pooled[w].astype(f32) - centre_two) * inverse_two
            du = gelu_slope(xhat * gain_two[...] + shift_two[...]) * grad
            du_two[w] = du
            total_du = total_du + jnp.sum(du, axis=0, keepdims=True)
            total_dx = total_dx + jnp.sum(du * xhat, axis=0, keepdims=True)
            row_low[pl.ds(w, 1), :] = du[:1]
            row_high[pl.ds(w, 1), :] = du[length - 1 :]
        sums[pl.ds(m, 1), :] = total_du
        sums[pl.ds(MB + m, 1), :] = total_dx

    place.meet()
    moves = halo_copies(place, (row_low, row_high), (row_low_out, row_high_out), halo_sems)
    for move in moves:
        move.start()
    sums_two[...] = reduce_everywhere(place, sums[...], near, far, (s0, s1, s2, s3), add_up)
    small = grad_branch.shape[1]
    for t in range(taps):
        part = dot_tn(u_two[:, t * mid : (t + 1) * mid], grad_branch[...])
        d_two[:, t * small : (t + 1) * small] = part.astype(bf16)
    for move in moves:
        move.wait()


def back_two(shape, du, sums_three, branch, bn_three, gain_three, u_two, w_two, pooled, bn_two, gain, move):
    windows, length, mid = pooled.shape
    rows, small = branch[0].shape
    out = [
        ((mid, w_two.shape[0] // mid * small), bf16),
        ((windows, length, mid), f32),
        ((windows, mid), f32),
        ((windows, mid), f32),
        ((2 * MB, mid), f32),
    ]
    scratch = reduce_scratch(shape, 2 * MB, mid)
    scratch += [
        pltpu.VMEM((windows, mid), f32),
        pltpu.VMEM((windows, mid), f32),
        pltpu.VMEM((2 * MB, mid), f32),
        pltpu.VMEM((rows, small), bf16),
        pltpu.SemaphoreType.DMA((4,)),
    ]
    return pl.pallas_call(
        functools.partial(back_two_kernel, shape),
        in_specs=[VM] * 15,
        out_specs=[VM] * len(out),
        out_shape=[jax.ShapeDtypeStruct(*o) for o in out],
        scratch_shapes=scratch,
        compiler_params=params(3),
        name="back_two",
    )(*du, sums_three, *branch, bn_three, gain_three, u_two, w_two, pooled, bn_two, gain, move)


def pool_grad_kernel(
    shape,
    du_two,
    du_low,
    du_high,
    sums_two,
    pooled,
    pooled_low,
    pooled_high,
    bn_two,
    gain_two,
    grad_summed,
    gs_low,
    gs_high,
    u_one,
    grad_ext,
    d_one,
    grad_main,
):
    place = Place(shape)
    windows, length, mid = pooled.shape
    parts = shape[0] * shape[1] * shape[2]
    pair = 2 * length
    scale = 1.0 / (pair * parts)

    @pl.loop(0, MB)
    def _(m):
        start = pl.multiple_of(m * pair, pair)
        centre = bn_two[pl.ds(m, 1), :]
        inverse = bn_two[pl.ds(MB + m, 1), :]
        factor = gain_two[...] * inverse
        mean_du = sums_two[pl.ds(m, 1), :] * scale
        mean_dx = sums_two[pl.ds(MB + m, 1), :] * scale

        def back(du, value, extra):
            xhat = (value.astype(f32) - centre) * inverse
            return factor * (du - mean_du - xhat * mean_dx) + extra

        edges = []
        for i in range(2):
            w = 2 * m + i
            at = pl.multiple_of(w * length, length)
            value = back(du_two[w], pooled[w], grad_summed[pl.ds(at, length), :]).astype(bf16)
            grad_ext[m, i * length : (i + 1) * length, :] = value
            grad_main[pl.ds(at, length), :] = value
            low = back(
                du_low[pl.ds(w, 1), :],
                pooled_low[w].astype(f32)[EDGE - 1 :],
                gs_low[pl.ds(w, 1), :],
            )
            high = back(
                du_high[pl.ds(w, 1), :],
                pooled_high[w].astype(f32)[:1],
                gs_high[pl.ds(w, 1), :],
            )
            edges += [jnp.where(place.is_first, 0.0, low), jnp.where(place.is_last, 0.0, high)]
        row = lax.broadcasted_iota(jnp.int32, (EDGE, mid), 0)
        block = jnp.zeros((EDGE, mid), f32)
        for i, edge in enumerate(edges):
            block = jnp.where(row == i, edge, block)
        grad_ext[m, pair : pair + EDGE, :] = block.astype(bf16)

    d_one[...] = dot_tn(grad_main[...], u_one[...]).astype(bf16)


def pool_grad(shape, du, sums_two, pooled, bn_two, gain_two, grad_summed, gs, u_one):
    windows, length, mid = pooled[0].shape
    rows = windows * length
    return pl.pallas_call(
        functools.partial(pool_grad_kernel, shape),
        in_specs=[VM] * 13,
        out_specs=[VM] * 2,
        out_shape=[
            jax.ShapeDtypeStruct((MB, 2 * length + EDGE, mid), bf16),
            jax.ShapeDtypeStruct((mid, u_one.shape[1]), bf16),
        ],
        scratch_shapes=[pltpu.VMEM((rows, mid), bf16)],
        compiler_params=params(),
        name="pool_grad",
    )(*du, sums_two, *pooled, bn_two, gain_two, grad_summed, *gs, u_one)


def back_one_kernel(
    shape,
    grad_ext,
    w_one,
    x2,
    bn_one,
    gain_one,
    shift_one,
    du_one,
    sums_one,
    near,
    far,
    s0,
    s1,
    s2,
    s3,
    sums,
):
    place = Place(shape)
    place.greet()
    windows, length, wide = x2.shape
    channels = wide // 2
    pair = 2 * length

    @pl.loop(0, MB)
    def _(m):
        through = [
            dot_nn(grad_ext[m], w_one[:, t * channels : (t + 1) * channels]) for t in range(5)
        ]
        centre = bn_one[pl.ds(m, 1), :]
        inverse = bn_one[pl.ds(MB + m, 1), :]
        total_du = jnp.zeros((1, wide), f32)
        total_dx = jnp.zeros((1, wide), f32)
        row = lax.broadcasted_iota(jnp.int32, (length, channels), 0)
        top, bottom = row == 0, row == length - 1
        for i in range(2):
            w = 2 * m + i
            main = [t[i * length : (i + 1) * length] for t in through]
            low = [t[pair + 2 * i : pair + 2 * i + 1] for t in through]
            high = [t[pair + 2 * i + 1 : pair + 2 * i + 2] for t in through]
            later = lambda t: jnp.where(bottom, high[t], pltpu.roll(main[t], length - 1, axis=0))
            earlier = lambda t: jnp.where(top, low[t], pltpu.roll(main[t], 1, axis=0))
            mean = later(0) + main[2] + earlier(4)
            cross = main[1] + earlier(3)
            cross_end = high[1] + main[3][length - 1 :]
            cross_later = jnp.where(bottom, cross_end, pltpu.roll(cross, length - 1, axis=0))
            grad = jnp.concatenate([(mean + cross) * 0.5, (mean + cross_later) * 0.5], axis=1)
            xhat = (x2[w].astype(f32) - centre) * inverse
            du = gelu_slope(xhat * gain_one[...] + shift_one[...]) * grad
            du_one[w] = du
            total_du = total_du + jnp.sum(du, axis=0, keepdims=True)
            total_dx = total_dx + jnp.sum(du * xhat, axis=0, keepdims=True)
        sums[pl.ds(m, 1), :] = total_du[:, :channels] + total_du[:, channels:]
        sums[pl.ds(MB + m, 1), :] = total_dx[:, :channels] + total_dx[:, channels:]

    place.meet()
    sums_one[...] = reduce_everywhere(place, sums[...], near, far, (s0, s1, s2, s3), add_up)


def back_one(shape, grad_ext, w_one, x2, bn_one, gain, move):
    windows, length, wide = x2.shape
    out = [((windows, length, wide), f32), ((2 * MB, wide // 2), f32)]
    scratch = reduce_scratch(shape, 2 * MB, wide // 2)
    scratch += [pltpu.VMEM((2 * MB, wide // 2), f32)]
    return pl.pallas_call(
        functools.partial(back_one_kernel, shape),
        in_specs=[VM] * 6,
        out_specs=[VM] * len(out),
        out_shape=[jax.ShapeDtypeStruct(*o) for o in out],
        scratch_shapes=scratch,
        compiler_params=params(4),
        name="back_one",
    )(grad_ext, w_one, x2, bn_one, gain, move)


def input_grad_kernel(total, meta, du, x2, bn_one, sums, gain, out, scratch):
    w = pl.program_id(0)
    m = lax.div(w, 2)
    wide = x2.shape[2]
    channels = wide // 2
    length = x2.shape[1]
    twice = lambda v: jnp.concatenate([v, v], axis=1)
    mean_du = twice(sums[pl.ds(m, 1), :]) * (1.0 / total)
    mean_dx = twice(sums[pl.ds(MB + m, 1), :]) * (1.0 / total)
    centre = bn_one[pl.ds(m, 1), :]
    inverse = bn_one[pl.ds(MB + m, 1), :]
    xhat = (x2[0].astype(f32) - centre) * inverse
    grad = gain[...] * inverse * (du[0] - mean_du - xhat * mean_dx)
    lanes = scratch.shape[0]
    for odd in range(2):
        for c in range(lanes):
            at = odd * channels + c * LANES
            scratch[c, pl.ds(odd, length, 2), :] = grad[:, at : at + LANES]
    for c in range(lanes):
        out[0, :, c * LANES : (c + 1) * LANES] = scratch[c].astype(bf16)


def input_grad(shape, meta, du, x2, bn_one, sums, gain):
    windows, length, wide = x2.shape
    total = 4 * length * shape[0] * shape[1] * shape[2]
    whole = lambda s: pl.BlockSpec(s, lambda w, meta: (0,) * len(s))

    return pl.pallas_call(
        functools.partial(input_grad_kernel, total),
        grid_spec=pltpu.PrefetchScalarGridSpec(
            num_scalar_prefetch=1,
            grid=(windows,),
            in_specs=[
                pl.BlockSpec((1, length, wide), lambda w, meta: (w, 0, 0)),
                pl.BlockSpec((1, length, wide), lambda w, meta: (w, 0, 0)),
                whole(bn_one.shape),
                whole(sums.shape),
                whole(gain.shape),
            ],
            out_specs=pl.BlockSpec(
                (1, 2 * length, wide // 2), lambda w, meta: (meta[w], 0, 0)
            ),
            scratch_shapes=[pltpu.VMEM((wide // 2 // LANES, 2 * length, LANES), f32)],
        ),
        out_shape=jax.ShapeDtypeStruct((windows, 2 * length, wide // 2), bf16),
        compiler_params=params(),
        name="input_grad",
    )(meta, du, x2, bn_one, sums, gain)


class Summing:
    STAGES = 7

    def __init__(self, place, source, columns, own, buffers, sems, emit):
        self.place, self.source, self.columns, self.own = place, source, columns, own
        self.core, self.side_a, self.side_b, self.end_a, self.end_b = buffers[:5]
        self.z_near, self.z_far, self.z_back, self.mate = buffers[5:]
        self.sems, self.emit = sems, emit
        half = own.shape[2]
        self.half, self.part = half, half // 2
        self.mine = pl.ds(pl.multiple_of(place.sec * half, half), half)
        self.other = pl.ds(pl.multiple_of((1 - place.sec) * half, half), half)
        self.x, self.y = lax.rem(place.dp, 2), lax.div(place.dp, 2)
        self.z = lax.rem(place.seq, 2)
        self.top, self.bottom = pl.ds(0, self.part), pl.ds(self.part, self.part)
        self.keep = pl.ds(pl.multiple_of(self.z * self.part, self.part), self.part)
        self.give = pl.ds(pl.multiple_of((1 - self.z) * self.part, self.part), self.part)

    def remote(self, source, target, sem, device):
        return pltpu.make_async_remote_copy(
            src_ref=source,
            dst_ref=target,
            send_sem=self.sems.at[2 * sem],
            recv_sem=self.sems.at[2 * sem + 1],
            device_id=device,
            device_id_type=MESH,
        )

    def copies(self, stage):
        p, own, x, y = self.place, self.own, self.x, self.y
        sibling = (1 - p.sec, p.seq, p.dp)
        over_x = (p.sec, p.seq, p.dp + 1 - 2 * x)
        over_y = (p.sec, p.seq, p.dp + 2 - 4 * y)
        over_z = (p.sec, p.seq + 1 - 2 * self.z, p.dp)
        z_pair = lax.div(p.seq, 2)
        beyond = (p.sec, p.seq + 2 - 4 * z_pair, p.dp)
        if stage == 0:
            return [
                pltpu.make_async_copy(
                    self.source.at[:, :, self.mine, self.columns], own, self.sems.at[20]
                ),
                self.remote(
                    self.source.at[:, :, self.other, self.columns], self.core, 0, sibling
                ),
            ]
        if stage == 1:
            return [
                self.remote(own.at[:, 1 - x, self.top], self.side_a, 1, over_x),
                self.remote(own.at[1 - y, :, self.bottom], self.side_b, 2, over_y),
            ]
        if stage == 2:
            return [
                self.remote(own.at[1 - y, x, self.top], self.end_a, 3, over_y),
                self.remote(own.at[y, 1 - x, self.bottom], self.end_b, 4, over_x),
            ]
        if stage == 3:
            return [self.remote(own.at[y, x, self.give], self.z_near, 5, over_z)]
        if stage == 4:
            return [self.remote(own.at[y, x, self.keep], self.z_far, 6, beyond)]
        if stage == 5:
            return [self.remote(own.at[y, x, self.keep], self.z_back, 7, over_z)]
        return [
            self.remote(own.at[y, x, self.keep], self.mate.at[self.keep], 8, sibling),
            self.remote(self.z_back, self.mate.at[self.give], 9, sibling),
        ]

    def start(self, stage):
        for copy in self.copies(stage):
            copy.start()

    def finish(self, stage):
        for copy in self.copies(stage):
            copy.wait()
        own, x, y = self.own, self.x, self.y

        def add(at, other):
            own[at] = (own[at].astype(f32) + other.astype(f32)).astype(bf16)

        if stage == 0:

            @pl.loop(0, 4)
            def _(i):
                a, b = lax.div(i, 2), lax.rem(i, 2)
                add((a, b), self.core[a, b])

        elif stage == 1:
            for i in range(2):
                add((i, x, self.top), self.side_a[i])
                add((y, i, self.bottom), self.side_b[i])
        elif stage == 2:
            add((y, x, self.top), self.end_a[...])
            add((y, x, self.bottom), self.end_b[...])
        elif stage == 3:
            add((y, x, self.keep), self.z_near[...])
        elif stage == 4:
            add((y, x, self.keep), self.z_far[...])
        elif stage == 6:
            base = self.place.sec * self.half
            there = (1 - self.place.sec) * self.half
            first = pl.multiple_of(base + self.z * self.part, self.part)
            second = pl.multiple_of(base + (1 - self.z) * self.part, self.part)
            self.emit(first, self.part, own[y, x, self.keep].astype(f32))
            self.emit(second, self.part, self.z_back[...].astype(f32))
            self.emit(pl.multiple_of(there, self.half), self.half, self.mate[...].astype(f32))

    @staticmethod
    def scratch(share, width):
        half = share // 2
        part = half // 2
        return [
            pltpu.VMEM((2, 2, half, width), bf16),
            pltpu.VMEM((2, 2, half, width), bf16),
            pltpu.VMEM((2, part, width), bf16),
            pltpu.VMEM((2, part, width), bf16),
            pltpu.VMEM((part, width), bf16),
            pltpu.VMEM((part, width), bf16),
            pltpu.VMEM((part, width), bf16),
            pltpu.VMEM((part, width), bf16),
            pltpu.VMEM((part, width), bf16),
            pltpu.VMEM((half, width), bf16),
            pltpu.SemaphoreType.DMA((21,)),
        ]


def grad_chunks(human_tracks, mouse_tracks, channels, mid, small):
    chunks = []
    for start in range(0, human_tracks, BLOCK):
        width = min(BLOCK, human_tracks - start)
        chunks.append((0, start, BLOCK, [(0, None, start, 0, width)]))
    chunks.append((1, 0, BLOCK, [(1, None, 0, 0, mouse_tracks)]))
    chunks.append((2, 0, small, [(2, None, 0, 0, small)]))
    chunks.append((3, 0, 3 * small, [(3, t, 0, t * small, small) for t in range(3)]))
    for taps in ((0, 1, 2), (3, 4)):
        chunks.append(
            (
                4,
                taps[0] * channels,
                len(taps) * channels,
                [(4, t, 0, i * channels, channels) for i, t in enumerate(taps)],
            )
        )
    return chunks


def sum_kernel(shape, chunks, n_in, *refs):
    sources, refs = refs[:n_in], refs[n_in:]
    outs, refs = refs[:n_in], refs[n_in:]
    place = Place(shape)
    place.greet()
    place.meet()
    sums = []
    for index, (source, start, width, targets) in enumerate(chunks):
        scratch, refs = refs[:11], refs[11:]

        def emit(row, rows, value, targets=targets):
            for out, tap, to, at, columns in targets:
                piece = value[:, at : at + columns]
                if tap is None:
                    outs[out][pl.ds(row, rows), to : to + columns] = piece
                else:
                    outs[out][tap, pl.ds(row, rows), to : to + columns] = piece

        sums.append(
            Summing(
                place,
                sources[source],
                pl.ds(start, width),
                scratch[0],
                scratch[1:10],
                scratch[10],
                emit,
            )
        )
    count = len(sums)
    lag = [-2, -1, 0, 1, 2, 3, 4]
    for tick in range(-2, count + Summing.STAGES):
        for stage in range(Summing.STAGES + 1):
            k = tick - lag[stage] if stage < Summing.STAGES else tick - lag[-1] - 1
            if 0 <= k < count:
                if stage > 0:
                    sums[k].finish(stage - 1)
                if stage < Summing.STAGES:
                    sums[k].start(stage)


def sum_grads(shape, grads, human_tracks, mouse_tracks, channels):
    mid = grads[0].shape[0]
    small = grads[2].shape[1]
    share = mid // shape[2]
    taps_one = grads[4].shape[1] // channels
    chunks = grad_chunks(human_tracks, mouse_tracks, channels, mid, small)
    scratch = []
    for chunk in chunks:
        scratch += Summing.scratch(share, chunk[2])
    return pl.pallas_call(
        functools.partial(sum_kernel, shape, chunks, len(grads)),
        in_specs=[HBM] * len(grads),
        out_specs=[VM] * len(grads),
        out_shape=[
            jax.ShapeDtypeStruct((share, human_tracks), f32),
            jax.ShapeDtypeStruct((share, mouse_tracks), f32),
            jax.ShapeDtypeStruct((share, small), f32),
            jax.ShapeDtypeStruct((3, share, small), f32),
            jax.ShapeDtypeStruct((taps_one, share, channels), f32),
        ],
        scratch_shapes=scratch,
        compiler_params=params(5),
        name="sum_grads",
    )(*[g.reshape(2, 2, share, g.shape[1]) for g in grads])


def per_device(
    shape,
    tracks,
    species,
    batch_order,
    conv_one,
    dilated_kernel,
    point_wise,
    head_human,
    head_mouse,
    bias_human,
    bias_mouse,
    gain_one,
    shift_one,
    gain_two,
    shift_two,
    gain_three,
    shift_three,
    cotangent,
):
    sec = lax.axis_index("section").astype(jnp.int32)
    windows, seq_bins, channels = tracks.shape
    half = seq_bins // 2
    length = half // 2
    human_tracks, mouse_tracks = head_human.shape[1], head_mouse.shape[1]
    human_wide = -(-human_tracks // BLOCK) * BLOCK
    share = conv_one.shape[2]
    mid = share * shape[2]

    taps_one = conv_one.shape[0]
    shard_one = jnp.transpose(conv_one, (2, 0, 1)).reshape(share, taps_one * channels)
    shard_point = point_wise.T
    shard_heads = jnp.concatenate(
        [
            jnp.pad(head_human, ((0, 0), (0, human_wide - human_tracks))),
            jnp.pad(head_mouse, ((0, 0), (0, BLOCK - mouse_tracks))),
        ],
        axis=1,
    )
    half_rows = share // shape[0]
    half_heads = lax.dynamic_slice_in_dim(shard_heads, sec * half_rows, half_rows, 0)
    w_heads = lax.all_gather(half_heads, ("dp", "section"), axis=0, tiled=True)
    weights = [shard_one, dilated_kernel, shard_point]
    if shape != (2, 4, 4):
        weights = [lax.all_gather(w, "dp", axis=w.ndim - 2, tiled=True) for w in weights]

    meta_one = jnp.concatenate([batch_order, sec[None]])
    x2, edge_low, edge_high, stats = prepare(tracks, meta_one, half)
    row = lambda v: v.reshape(1, -1)
    twice = lambda v: jnp.tile(v, 2).reshape(1, -1)
    gains = (
        twice(gain_one),
        twice(shift_one),
        row(gain_two),
        row(shift_two),
        row(gain_three),
        row(shift_three),
    )
    (
        u_one,
        u_two,
        pooled,
        pooled_low,
        pooled_high,
        branch,
        branch_low,
        branch_high,
        act_three,
        summed,
        bn_one,
        bn_two,
        bn_three,
        w_one,
        w_two,
        w_point,
    ) = forward(shape, mid, x2, edge_low, edge_high, stats, gains, *weights)
    w_two = w_two.reshape(-1, w_two.shape[2])

    kinds = species[batch_order]
    is_human = kinds == 0
    n_human = jnp.sum(is_human.astype(jnp.int32))
    place_human = jnp.cumsum(is_human.astype(jnp.int32)) - 1
    place_mouse = n_human + jnp.cumsum(1 - is_human.astype(jnp.int32)) - 1
    target = jnp.where(is_human, place_human, place_mouse)
    positions = jnp.sum(
        jnp.where(target[None, :] == jnp.arange(windows)[:, None], jnp.arange(windows)[None, :], 0),
        axis=1,
    ).astype(jnp.int32)
    meta_two = jnp.concatenate(
        [positions, batch_order[positions], n_human[None], sec[None]]
    ).astype(jnp.int32)
    wide_human = jnp.pad(bias_human, (0, human_wide - human_tracks)).reshape(1, -1)
    wide_mouse = jnp.pad(bias_mouse, (0, BLOCK - mouse_tracks)).reshape(1, -1)
    cot_half = lax.dynamic_slice_in_dim(cotangent, sec * length, length, 1)
    predicted, grad_summed, d_human, d_mouse, db_human, db_mouse = heads(
        meta_two, summed, w_heads, wide_human, wide_mouse, cot_half, mouse_tracks, length
    )

    bias_sums = jnp.concatenate([db_human, db_mouse], axis=1).reshape(8, -1)
    d_point, du_three, du_low, du_high, gs_low, gs_high, sums_three, bias_out = back_three(
        shape, windows, grad_summed, act_three, branch, bn_three, gains[4], gains[5], w_point, bias_sums
    )
    d_two, du_two, dlow_two, dhigh_two, sums_two = back_two(
        shape,
        (du_three, du_low, du_high),
        sums_three,
        (branch, branch_low, branch_high),
        bn_three,
        gains[4],
        u_two,
        w_two,
        pooled,
        bn_two,
        gains[2],
        gains[3],
    )
    grad_ext, d_one = pool_grad(
        shape,
        (du_two, dlow_two, dhigh_two),
        sums_two,
        (pooled, pooled_low, pooled_high),
        bn_two,
        gains[2],
        grad_summed,
        (gs_low, gs_high),
        u_one,
    )
    du_one, sums_one = back_one(shape, grad_ext, w_one, x2, bn_one, gains[0], gains[1])
    grad_input = input_grad(shape, meta_one, du_one, x2, bn_one, sums_one, gains[0])

    grads = (d_human, d_mouse, d_point, d_two, d_one)
    if shape == (2, 4, 4):
        r_human, r_mouse, r_point, r_two, r_one = sum_grads(
            shape, grads, human_tracks, mouse_tracks, channels
        )
    else:

        def reduced(grad):
            part = lax.psum_scatter(grad, "dp", scatter_dimension=0, tiled=True)
            return lax.psum(part, ("section", "seq")).astype(f32)

        r_human, r_mouse, r_point, r_two, r_one = [reduced(grad) for grad in grads]
        r_human, r_mouse = r_human[:, :human_tracks], r_mouse[:, :mouse_tracks]
        r_two = jnp.transpose(r_two.reshape(share, -1, dilated_kernel.shape[2]), (1, 0, 2))
        r_one = jnp.transpose(r_one.reshape(share, taps_one, channels), (1, 0, 2))
    r_point = r_point.T
    r_one = jnp.transpose(r_one, (0, 2, 1))
    bias = bias_out.reshape(-1)
    return (
        predicted,
        grad_input,
        r_one,
        r_two,
        r_point,
        r_human,
        r_mouse,
        bias[:human_tracks],
        bias[human_wide : human_wide + mouse_tracks],
        jnp.sum(sums_one[MB:], axis=0),
        jnp.sum(sums_one[:MB], axis=0),
        jnp.sum(sums_two[MB:], axis=0),
        jnp.sum(sums_two[:MB], axis=0),
        jnp.sum(sums_three[MB:], axis=0),
        jnp.sum(sums_three[:MB], axis=0),
    )


def solution(mesh):
    shape = (mesh.shape["section"], mesh.shape["seq"], mesh.shape["dp"])
    placed = (
        P("dp", "seq", None),
        P("dp"),
        P(),
        P(None, None, "dp"),
        P(None, "dp", None),
        P(None, "dp"),
        P("dp", None),
        P("dp", None),
    ) + (P(),) * 8 + (P("dp", "seq", None),)
    return jax.shard_map(
        functools.partial(per_device, shape),
        mesh=mesh,
        in_specs=placed,
        out_specs=(
            P("dp", ("seq", "section"), None),
            P("dp", ("seq", "section"), None),
            P(None, None, "dp"),
            P(None, "dp", None),
            P(None, "dp"),
            P("dp", None),
            P("dp", None),
        )
        + (P(),) * 8,
        check_vma=False,
    )
```

```python
import functools
import math

import jax
import jax.numpy as jnp
from jax import lax
from jax.experimental import pallas as pl
from jax.experimental.pallas import tpu as pltpu
from jax.sharding import PartitionSpec as P

MESH = pl.DeviceIdType.MESH
DILATION = 11
MB = 4
EPS = 1e-05
EDGE = 16
BLOCK = 1792
LANES = 128
VMEM_LIMIT = 60 * 1024 * 1024
GELU_K = math.sqrt(2.0 / math.pi)
GELU_C = 0.044715
f32 = jnp.float32
bf16 = jnp.bfloat16
VM = pl.BlockSpec(memory_space=pltpu.VMEM)
HBM = pl.BlockSpec(memory_space=pl.ANY)


def params(collective_id=None, limit=VMEM_LIMIT):
    if collective_id is None:
        return pltpu.CompilerParams(vmem_limit_bytes=limit)
    return pltpu.CompilerParams(
        vmem_limit_bytes=limit, collective_id=collective_id, has_side_effects=True
    )


def gelu(u):
    t = jnp.tanh(u * (GELU_K + (GELU_K * GELU_C) * (u * u)))
    h = 0.5 * u
    return h + h * t


def gelu_slope(u):
    uu = u * u
    t = jnp.tanh(u * (GELU_K + (GELU_K * GELU_C) * uu))
    return 0.5 * (1.0 + t) + (0.5 * u) * (1.0 - t * t) * (GELU_K + (3.0 * GELU_K * GELU_C) * uu)


def dot_nn(a, b):
    return jnp.dot(a, b, preferred_element_type=f32)


def dot_nt(a, b):
    return lax.dot_general(a, b, (((1,), (1,)), ((), ())), preferred_element_type=f32)


def dot_tn(a, b):
    return lax.dot_general(a, b, (((0,), (0,)), ((), ())), preferred_element_type=f32)


class Place:
    def __init__(self, shape):
        self.n_sec, self.n_seq, self.n_dp = shape
        self.n_near = self.n_sec * self.n_dp
        self.sec = lax.axis_index("section")
        self.seq = lax.axis_index("seq")
        self.dp = lax.axis_index("dp")
        self.near = self.sec * self.n_dp + self.dp
        n_bins = self.n_seq * self.n_sec
        bins = self.seq * self.n_sec + self.sec
        self.is_first = bins == 0
        self.is_last = bins == n_bins - 1
        low = lax.rem(bins + n_bins - 1, n_bins)
        high = lax.rem(bins + 1, n_bins)
        self.low = self.bin_device(low)
        self.high = self.bin_device(high)
        across = jnp.where(self.sec == 0, low, high)
        self.across = self.bin_device(across)

    def bin_device(self, bins):
        return (lax.rem(bins, self.n_sec), lax.div(bins, self.n_sec), self.dp)

    def near_device(self, rank):
        return (lax.div(rank, self.n_dp), self.seq, lax.rem(rank, self.n_dp))

    def greet(self):
        barrier = pltpu.get_barrier_semaphore()
        for k in range(1, self.n_near):
            rank = lax.rem(self.near + k, self.n_near)
            pl.semaphore_signal(
                barrier, inc=1, device_id=self.near_device(rank), device_id_type=MESH
            )
        for k in range(1, self.n_seq):
            seq = lax.rem(self.seq + k, self.n_seq)
            pl.semaphore_signal(
                barrier, inc=1, device_id=(self.sec, seq, self.dp), device_id_type=MESH
            )
        pl.semaphore_signal(barrier, inc=1, device_id=self.across, device_id_type=MESH)

    def meet(self):
        pl.semaphore_wait(pltpu.get_barrier_semaphore(), self.n_near + self.n_seq - 1)


def halo_copies(place, from_self, arrived, sems):
    up = pltpu.make_async_remote_copy(
        src_ref=from_self[1],
        dst_ref=arrived[0],
        send_sem=sems.at[0],
        recv_sem=sems.at[1],
        device_id=place.high,
        device_id_type=MESH,
    )
    down = pltpu.make_async_remote_copy(
        src_ref=from_self[0],
        dst_ref=arrived[1],
        send_sem=sems.at[2],
        recv_sem=sems.at[3],
        device_id=place.low,
        device_id_type=MESH,
    )
    return up, down


def nothing():
    pass


def spread_round(buffer, mine, count, device_of, send, recv, meanwhile=nothing):
    copies = []
    for k in range(1, count):
        rank = lax.rem(mine + k, count)
        copy = pltpu.make_async_remote_copy(
            src_ref=buffer.at[mine],
            dst_ref=buffer.at[mine],
            send_sem=send.at[k],
            recv_sem=recv.at[mine],
            device_id=device_of(rank),
            device_id_type=MESH,
        )
        copy.start()
        copies.append((rank, copy))
    meanwhile()
    for rank, copy in copies:
        pltpu.make_async_remote_copy(
            src_ref=buffer.at[rank],
            dst_ref=buffer.at[rank],
            send_sem=send.at[0],
            recv_sem=recv.at[rank],
            device_id=device_of(rank),
            device_id_type=MESH,
        ).wait_recv()
    for rank, copy in copies:
        copy.wait_send()


def reduce_everywhere(place, value, near_buf, far_buf, sems, combine, meanwhile=nothing):
    near_send, near_recv, far_send, far_recv = sems
    near_buf[place.near] = value
    spread_round(
        near_buf, place.near, place.n_near, place.near_device, near_send, near_recv, meanwhile
    )
    far_buf[place.seq] = combine(near_buf, place.n_near, 1)
    spread_round(
        far_buf,
        place.seq,
        place.n_seq,
        lambda seq: (place.sec, seq, place.dp),
        far_send,
        far_recv,
        meanwhile,
    )
    return combine(far_buf, place.n_seq, place.n_near)


def add_up(buffer, count, weight):
    total = buffer[0]
    for i in range(1, count):
        total = total + buffer[i]
    return total


def merge_stats(rows, buffer, count, weight):
    means = [buffer[i][:MB] for i in range(count)]
    centre = means[0]
    spread = buffer[0][MB:]
    for i in range(1, count):
        centre = centre + means[i]
        spread = spread + buffer[i][MB:]
    centre = centre * (1.0 / count)
    apart = jnp.square(means[0] - centre)
    for i in range(1, count):
        apart = apart + jnp.square(means[i] - centre)
    return jnp.concatenate([centre, spread + apart * float(rows * weight)], axis=0)


def reduce_scratch(shape, rows, columns):
    n_sec, n_seq, n_dp = shape
    near = n_sec * n_dp
    return [
        pltpu.VMEM((near, rows, columns), f32),
        pltpu.VMEM((n_seq, rows, columns), f32),
        pltpu.SemaphoreType.DMA((near,)),
        pltpu.SemaphoreType.DMA((near,)),
        pltpu.SemaphoreType.DMA((n_seq,)),
        pltpu.SemaphoreType.DMA((n_seq,)),
    ]


def local_stats(value):
    count = value.shape[0]
    centre = jnp.sum(value, axis=0, keepdims=True) * (1.0 / count)
    return centre, jnp.sum(jnp.square(value - centre), axis=0, keepdims=True)


def finish_stats(stats, total):
    return jnp.concatenate(
        [stats[:MB], lax.rsqrt(stats[MB:] * (1.0 / total) + EPS)], axis=0
    )


def prepare_kernel(meta, first, second, pairs, low, high, stats, scratch):
    m = pl.program_id(0)
    half = scratch.shape[1]
    start = pl.multiple_of(meta[meta.shape[0] - 1] * half, half)
    values = []
    for i, ref in enumerate((first, second)):
        value = ref[0, pl.ds(start, half), :].astype(f32)
        values.append(value)
        lanes = scratch.shape[0]
        for c in range(lanes):
            scratch[c] = value[:, c * LANES : (c + 1) * LANES]
        both = jnp.concatenate(
            [scratch[c, pl.ds(odd, half // 2, 2), :] for odd in range(2) for c in range(lanes)],
            axis=1,
        )
        pairs[i] = both.astype(bf16)
        low[pl.ds(2 * m + i, 1), :] = both[:1]
        high[pl.ds(2 * m + i, 1), :] = both[half // 2 - 1 :]
    count = 2 * half
    centre = (
        jnp.sum(values[0], axis=0, keepdims=True) + jnp.sum(values[1], axis=0, keepdims=True)
    ) * (1.0 / count)
    spread = jnp.sum(jnp.square(values[0] - centre), axis=0, keepdims=True) + jnp.sum(
        jnp.square(values[1] - centre), axis=0, keepdims=True
    )
    stats[pl.ds(m, 1), :] = centre
    stats[pl.ds(MB + m, 1), :] = spread


def prepare(tracks, meta, half):
    windows, length, channels = tracks.shape
    whole = lambda shape: pl.BlockSpec(shape, lambda m, meta: (0,) * len(shape))
    return pl.pallas_call(
        prepare_kernel,
        grid_spec=pltpu.PrefetchScalarGridSpec(
            num_scalar_prefetch=1,
            grid=(MB,),
            in_specs=[
                pl.BlockSpec((1, length, channels), lambda m, meta: (meta[2 * m], 0, 0)),
                pl.BlockSpec((1, length, channels), lambda m, meta: (meta[2 * m + 1], 0, 0)),
            ],
            out_specs=[
                pl.BlockSpec((2, half // 2, 2 * channels), lambda m, meta: (m, 0, 0)),
                whole((windows, 2 * channels)),
                whole((windows, 2 * channels)),
                whole((2 * MB, channels)),
            ],
            scratch_shapes=[pltpu.VMEM((channels // LANES, half, LANES), f32)],
        ),
        out_shape=[
            jax.ShapeDtypeStruct((windows, half // 2, 2 * channels), bf16),
            jax.ShapeDtypeStruct((windows, 2 * channels), f32),
            jax.ShapeDtypeStruct((windows, 2 * channels), f32),
            jax.ShapeDtypeStruct((2 * MB, channels), f32),
        ],
        compiler_params=params(),
        name="prepare",
    )(meta, tracks, tracks)


class Gathering:
    STAGES = 5

    def __init__(self, place, shard, full, rows_at, sems):
        self.place, self.shard, self.full, self.rows_at, self.sems = place, shard, full, rows_at, sems
        p = place
        x, y, z = lax.rem(p.dp, 2), lax.div(p.dp, 2), lax.rem(p.seq, 2)
        self.share = shard.shape[rows_at]
        self.group = self.share // 6
        g = self.group
        self.dp_x, self.dp_y = p.dp + 1 - 2 * x, p.dp + 2 - 4 * y
        self.dp_xy = 3 - p.dp
        self.sibling = (1 - p.sec, p.seq, p.dp)
        self.over_x, self.over_y = (p.sec, p.seq, self.dp_x), (p.sec, p.seq, self.dp_y)
        self.over_z = (p.sec, p.seq + 1 - 2 * z, p.dp)
        base = p.sec * 3 * g
        self.near, self.middle, self.edge, self.far, self.half = (
            (base + z * g, 2 * g),
            (base + g, g),
            (base + 2 * z * g, g),
            (base + 2 * (1 - z) * g, g),
            (base, 3 * g),
        )

    def at(self, ref, dp, span):
        start, rows = span
        index = pl.ds(pl.multiple_of(dp * self.share + start, self.group), rows)
        return ref.at[:, index] if self.rows_at else ref.at[index]

    def remote(self, dp, span, sem, device, source=None):
        source = self.at(self.full, dp, span) if source is None else source
        return pltpu.make_async_remote_copy(
            src_ref=source,
            dst_ref=self.at(self.full, dp, span),
            send_sem=self.sems.at[2 * sem],
            recv_sem=self.sems.at[2 * sem + 1],
            device_id=device,
            device_id_type=MESH,
        )

    def own_copy(self):
        target = self.at(self.full, self.place.dp, (0, self.share))
        return pltpu.make_async_copy(self.shard, target, self.sems.at[26])

    def copies(self, stage):
        me = self.place.dp
        if stage == 0:
            own = self.at(self.shard, 0, self.near)
            return [
                self.remote(me, self.near, 0, self.over_x, own),
                self.remote(me, self.near, 1, self.over_y, own),
            ]
        if stage == 1:
            return [
                self.remote(self.dp_x, self.middle, 2, self.over_y),
                self.remote(self.dp_y, self.edge, 3, self.over_x),
                self.remote(self.dp_x, self.edge, 4, self.over_z),
                self.remote(self.dp_y, self.edge, 5, self.over_z),
                self.remote(self.dp_x, self.near, 6, self.sibling),
                self.remote(self.dp_y, self.near, 7, self.sibling),
            ]
        if stage == 2:
            return [
                self.remote(self.dp_xy, self.edge, 8, self.over_z),
                self.remote(self.dp_xy, self.near, 9, self.sibling),
            ]
        if stage == 3:
            return [
                self.remote(self.dp_x, self.far, 10, self.sibling),
                self.remote(self.dp_y, self.far, 11, self.sibling),
                self.remote(self.dp_xy, self.far, 12, self.sibling),
            ]
        return []

    def start(self, stage):
        for copy in self.copies(stage):
            copy.start()

    def arrived(self, stage, which, dp, span):
        copy = self.copies(stage)[which]
        pltpu.make_async_remote_copy(
            src_ref=self.at(self.full, dp, span),
            dst_ref=self.at(self.full, dp, span),
            send_sem=self.sems.at[0],
            recv_sem=self.sems.at[2 * {0: 0, 1: 2, 2: 8, 3: 10}[stage] + 2 * which + 1],
            device_id=self.sibling,
            device_id_type=MESH,
        ).wait_recv()

    def advance(self, stage):
        if stage == 0:
            self.own_copy().start()
        elif stage == 1:
            self.arrived(0, 0, self.dp_x, self.near)
            self.arrived(0, 1, self.dp_y, self.near)
        elif stage == 2:
            self.arrived(1, 0, self.dp_xy, self.middle)
            self.arrived(1, 1, self.dp_xy, self.edge)
        elif stage == 3:
            self.arrived(1, 2, self.dp_x, self.far)
            self.arrived(1, 3, self.dp_y, self.far)
            self.arrived(2, 0, self.dp_xy, self.far)
        if stage < 4:
            self.start(stage)
            return
        base = (1 - self.place.sec) * 3 * self.group
        z = lax.rem(self.place.seq, 2)
        near = (base + z * self.group, 2 * self.group)
        far = (base + 2 * (1 - z) * self.group, self.group)
        self.arrived(1, 4, self.dp_x, near)
        self.arrived(1, 5, self.dp_y, near)
        self.arrived(2, 1, self.dp_xy, near)
        self.arrived(3, 0, self.dp_x, far)
        self.arrived(3, 1, self.dp_y, far)
        self.arrived(3, 2, self.dp_xy, far)
        self.own_copy().wait()
        for stage in range(4):
            for copy in self.copies(stage):
                copy.wait_send()


def shifted_rows(value, offset, length):
    rows = value.shape[0]
    if offset:
        value = pltpu.roll(value, rows - offset, axis=0)
    return value[:length]


def forward_kernel(shape, *refs):
    (
        x2,
        edge_low,
        edge_high,
        stats_in,
        gain_one,
        shift_one,
        gain_two,
        shift_two,
        gain_three,
        shift_three,
        in_one,
        in_two,
        in_point,
    ) = refs[:13]
    refs = refs[13:]
    (
        out_u_one,
        out_u_two,
        pooled,
        pooled_low,
        pooled_high,
        branch,
        branch_low,
        branch_high,
        act_three,
        summed,
        bn_one,
        bn_two,
        bn_three,
        out_one,
        out_two,
        out_point,
    ) = refs[:16]
    refs = refs[16:]
    (
        near_one,
        far_one,
        s10,
        s11,
        s12,
        s13,
        near_two,
        far_two,
        s20,
        s21,
        s22,
        s23,
        near_three,
        far_three,
        s30,
        s31,
        s32,
        s33,
        got_low,
        got_high,
        stats_two,
        stats_three,
        halo_sems,
        s_branch_edge_low,
        s_branch_edge_high,
        u_one,
        u_two,
        w_one,
        w_two,
        w_point,
        weight_sems,
        save_sems,
    ) = refs
    place = Place(shape)
    place.greet()
    windows, length, wide = x2.shape
    channels = wide // 2
    mid = pooled.shape[2]
    small = branch.shape[1]
    parts = shape[0] * shape[1] * shape[2]
    pair = 2 * length
    saves = [
        pltpu.make_async_copy(source, target, save_sems.at[i])
        for i, (source, target) in enumerate(
            ((u_one, out_u_one), (u_two, out_u_two), (w_one, out_one), (w_two, out_two), (w_point, out_point))
        )
    ]
    gathers = []
    if in_one.shape[0] < w_one.shape[0]:
        pieces = [(in_one, w_one, 0), (in_two, w_two, 1), (in_point, w_point, 0)]
        gathers = [
            Gathering(place, *piece, weight_sems.at[i]) for i, piece in enumerate(pieces)
        ]
    else:
        loads = [
            pltpu.make_async_copy(source, target, weight_sems.at[i, 0])
            for i, (source, target) in enumerate(
                ((in_one, w_one), (in_two, w_two), (in_point, w_point))
            )
        ]
        for load in loads:
            load.start()
        for load in loads:
            load.wait()

    def advance(*steps):
        for index, stage in steps:
            if index < len(gathers):
                gathers[index].advance(stage)

    place.meet()
    advance((0, 0))
    up, down = halo_copies(place, (edge_low, edge_high), (got_low, got_high), halo_sems.at[0])
    up.start()
    down.start()
    stats = reduce_everywhere(
        place,
        stats_in[...],
        near_one,
        far_one,
        (s10, s11, s12, s13),
        functools.partial(merge_stats, 4 * length),
    )
    stats = finish_stats(stats, 4 * length * parts)
    bn_one[...] = jnp.concatenate([stats, stats], axis=1)
    up.wait()
    down.wait()
    advance((0, 1), (1, 0), (2, 0))

    @pl.loop(0, windows)
    def _(w):
        m = lax.div(w, 2)
        centre = bn_one[pl.ds(m, 1), :]
        scale = bn_one[pl.ds(MB + m, 1), :] * gain_one[...]
        move = shift_one[...]

        def act(value):
            return gelu((value - centre) * scale + move).astype(bf16).astype(f32)

        main = act(x2[w].astype(f32))
        before = jnp.where(place.is_first, 0.0, act(got_low[pl.ds(w, 1), :]))
        after = jnp.where(place.is_last, 0.0, act(got_high[pl.ds(w, 1), :]))
        even, odd = main[:, :channels], main[:, channels:]
        mean = (even + odd) * 0.5
        mean_before = (before[:, :channels] + before[:, channels:]) * 0.5
        mean_after = (after[:, :channels] + after[:, channels:]) * 0.5
        row = lax.broadcasted_iota(jnp.int32, (length, channels), 0)
        top, bottom = row == 0, row == length - 1
        odd_before = jnp.where(top, before[:, channels:], pltpu.roll(odd, 1, axis=0))
        cross = (odd_before + even) * 0.5
        cross_after = (odd[length - 1 :] + after[:, :channels]) * 0.5
        start = pl.multiple_of(w * length, length)
        taps = (
            jnp.where(top, mean_before, pltpu.roll(mean, 1, axis=0)),
            cross,
            mean,
            jnp.where(bottom, cross_after, pltpu.roll(cross, length - 1, axis=0)),
            jnp.where(bottom, mean_after, pltpu.roll(mean, length - 1, axis=0)),
        )
        for t, tap in enumerate(taps):
            u_one[pl.ds(start, length), t * channels : (t + 1) * channels] = tap.astype(bf16)

    saves[0].start()
    advance((0, 2), (1, 1), (2, 1), (0, 3), (1, 2), (2, 2), (0, 4))
    saves[2].start()

    @pl.loop(0, MB)
    def _(m):
        start = pl.multiple_of(m * pair, pair)
        value = dot_nt(u_one[pl.ds(start, pair), :], w_one[...]).astype(bf16)
        pooled[pl.ds(2 * m, 2)] = value.reshape(2, length, mid)
        centre, spread = local_stats(value.astype(f32))
        stats_two[pl.ds(m, 1), :] = centre
        stats_two[pl.ds(MB + m, 1), :] = spread

    up, down = halo_copies(
        place,
        (pooled.at[:, pl.ds(0, EDGE), :], pooled.at[:, pl.ds(length - EDGE, EDGE), :]),
        (pooled_low, pooled_high),
        halo_sems.at[1],
    )
    up.start()
    down.start()
    stats = reduce_everywhere(
        place,
        stats_two[...],
        near_two,
        far_two,
        (s20, s21, s22, s23),
        functools.partial(merge_stats, pair),
    )
    bn_two[...] = finish_stats(stats, pair * parts)
    up.wait()
    down.wait()
    advance((1, 3), (2, 3))

    @pl.loop(0, windows)
    def _(w):
        m = lax.div(w, 2)
        centre = bn_two[pl.ds(m, 1), :]
        scale = bn_two[pl.ds(MB + m, 1), :] * gain_two[...]
        move = shift_two[...]

        def act(value):
            return gelu((value.astype(f32) - centre) * scale + move)

        ext = jnp.concatenate(
            [
                jnp.where(place.is_first, 0.0, act(pooled_low[w])),
                act(pooled[w]),
                jnp.where(place.is_last, 0.0, act(pooled_high[w])),
            ],
            axis=0,
        )
        start = pl.multiple_of(w * length, length)
        for t in range(3):
            tap = shifted_rows(ext, EDGE + (t - 1) * DILATION, length)
            u_two[pl.ds(start, length), t * mid : (t + 1) * mid] = tap.astype(bf16)

    saves[1].start()
    advance((1, 4), (2, 4))
    saves[3].start()
    saves[4].start()

    @pl.loop(0, MB)
    def _(m):
        start = pl.multiple_of(m * pair, pair)
        value = jnp.zeros((pair, small), f32)
        for t in range(w_two.shape[0]):
            value = value + dot_nn(
                u_two[pl.ds(start, pair), t * mid : (t + 1) * mid], w_two[t]
            )
        branch[pl.ds(start, pair), :] = value
        centre, spread = local_stats(value)
        stats_three[pl.ds(m, 1), :] = centre
        stats_three[pl.ds(MB + m, 1), :] = spread
        for i in range(2):
            s_branch_edge_low[2 * m + i] = value[i * length : i * length + EDGE]
            s_branch_edge_high[2 * m + i] = value[(i + 1) * length - EDGE : (i + 1) * length]

    up, down = halo_copies(
        place,
        (s_branch_edge_low, s_branch_edge_high),
        (branch_low, branch_high),
        halo_sems.at[2],
    )
    up.start()
    down.start()
    stats = reduce_everywhere(
        place,
        stats_three[...],
        near_three,
        far_three,
        (s30, s31, s32, s33),
        functools.partial(merge_stats, pair),
    )
    bn_three[...] = finish_stats(stats, pair * parts)

    @pl.loop(0, MB)
    def _(m):
        centre = bn_three[pl.ds(m, 1), :]
        scale = bn_three[pl.ds(MB + m, 1), :] * gain_three[...]
        start = pl.multiple_of(m * pair, pair)
        act = gelu((branch[pl.ds(start, pair), :] - centre) * scale + shift_three[...])
        act = act.astype(bf16)
        act_three[pl.ds(start, pair), :] = act
        lifted = dot_nt(act, w_point[...])
        here = pooled[pl.ds(2 * m, 2)].reshape(pair, mid).astype(f32)
        summed[pl.ds(start, pair), :] = (here + lifted).astype(bf16)

    up.wait()
    down.wait()
    for save in saves:
        save.wait()


def forward(shape, mid, x2, edge_low, edge_high, stats, gains, w_one, w_two, w_point):
    windows, length, wide = x2.shape
    rows = windows * length
    taps_two, _, small = w_two.shape
    big = [
        ((mid, w_one.shape[1]), bf16),
        ((taps_two, mid, small), bf16),
        ((mid, small), bf16),
    ]
    out = [
        ((rows, w_one.shape[1]), bf16),
        ((rows, taps_two * mid), bf16),
        ((windows, length, mid), bf16),
        ((windows, EDGE, mid), bf16),
        ((windows, EDGE, mid), bf16),
        ((rows, small), f32),
        ((windows, EDGE, small), f32),
        ((windows, EDGE, small), f32),
        ((rows, small), bf16),
        ((rows, mid), bf16),
        ((2 * MB, wide), f32),
        ((2 * MB, mid), f32),
        ((2 * MB, small), f32),
    ]
    out_specs = [HBM] * 2 + [VM] * 11 + [HBM] * 3
    out += big
    scratch = (
        reduce_scratch(shape, 2 * MB, wide // 2)
        + reduce_scratch(shape, 2 * MB, mid)
        + reduce_scratch(shape, 2 * MB, small)
    )
    scratch += [
        pltpu.VMEM((windows, wide), f32),
        pltpu.VMEM((windows, wide), f32),
        pltpu.VMEM((2 * MB, mid), f32),
        pltpu.VMEM((2 * MB, small), f32),
        pltpu.SemaphoreType.DMA((3, 4)),
        pltpu.VMEM((windows, EDGE, small), f32),
        pltpu.VMEM((windows, EDGE, small), f32),
        pltpu.VMEM(*out[0]),
        pltpu.VMEM(*out[1]),
    ]
    scratch += [pltpu.VMEM(*b) for b in big]
    scratch += [
        pltpu.SemaphoreType.DMA((3, 27)),
        pltpu.SemaphoreType.DMA((5,)),
    ]
    return pl.pallas_call(
        functools.partial(forward_kernel, shape),
        in_specs=[VM] * 10 + [HBM] * 3,
        out_specs=out_specs,
        out_shape=[jax.ShapeDtypeStruct(*o) for o in out],
        scratch_shapes=scratch,
        compiler_params=params(1),
        name="forward",
    )(x2, edge_low, edge_high, stats, *gains, w_one, w_two, w_point)


def heads_kernel(
    human_tracks,
    mouse_tracks,
    meta,
    summed,
    w_human,
    w_mouse,
    b_human,
    b_mouse,
    cot,
    predicted,
    grad_summed,
    d_human,
    d_mouse,
    db_human,
    db_mouse,
    rows_sorted,
    grad_sorted,
    grad_pre,
):
    j = pl.program_id(0)
    windows, length, block = cot.shape
    pair = 2 * length
    n_pairs = windows // 2
    mid = summed.shape[1]
    n_human = meta[2 * windows]

    @pl.when(j == 0)
    def _():
        grad_sorted[...] = jnp.zeros_like(grad_sorted)

        @pl.loop(0, windows)
        def _(s):
            source = pl.multiple_of(meta[s] * length, length)
            target = pl.multiple_of(s * length, length)
            rows_sorted[pl.ds(target, length), :] = summed[pl.ds(source, length), :]

    column = lax.broadcasted_iota(jnp.int32, (1, block), 1)

    def run(weight, bias, limit, is_mouse, first_pair, last_pair):
        def body(p, carry):
            start = pl.multiple_of(p * pair, pair)
            pre = dot_nn(rows_sorted[pl.ds(start, pair), :], weight[...]) + bias[...]
            decay = jnp.exp(-jnp.abs(pre))
            whole = 1.0 + decay
            inverse = 1.0 / whole
            sigmoid = jnp.where(pre >= 0, inverse, decay * inverse)
            logs = jnp.where(decay < 2.0**-11, decay, jnp.log(whole))
            output = (jnp.maximum(pre, 0.0) + logs).astype(bf16)
            output = jnp.where(column < limit, output, jnp.zeros_like(output))
            for i in range(2):
                s = 2 * p + i
                window = meta[windows + s]
                mine = s >= n_human if is_mouse else s < n_human
                keep = (column < limit) & mine
                part = slice(i * length, (i + 1) * length)
                grad = jnp.where(keep, cot[window].astype(f32) * sigmoid[part], 0.0)
                grad_pre[pl.ds(pl.multiple_of(s * length, length), length), :] = grad.astype(bf16)

                @pl.when(mine)
                def _():
                    predicted[window] = output[part]

            grad_sorted[pl.ds(start, pair), :] += dot_nt(
                grad_pre[pl.ds(start, pair), :], weight[...]
            )
            return carry

        lax.fori_loop(first_pair, last_pair, body, 0)

    def weight_grads(count, n_used, from_end, d_weight, d_bias):
        for n in range(n_pairs + 1):

            @pl.when(n_used == n)
            def _(n=n):
                if n == 0:
                    d_weight[...] = jnp.zeros_like(d_weight)
                    d_bias[...] = jnp.zeros_like(d_bias)
                else:
                    part = slice((n_pairs - n) * pair, None) if from_end else slice(0, n * pair)
                    grad = grad_pre[part, :]
                    d_weight[...] = dot_tn(rows_sorted[part, :], grad).astype(bf16)
                    d_bias[...] = dot_nn(jnp.ones((8, n * pair), bf16), grad)[:1]

    human_pairs = lax.div(n_human + 1, 2)
    run(w_human, b_human, human_tracks - j * block, False, 0, human_pairs)
    weight_grads(n_pairs, human_pairs, False, d_human, db_human)

    @pl.when(j == 0)
    def _():
        mouse_start = lax.div(n_human, 2)
        run(w_mouse, b_mouse, mouse_tracks, True, mouse_start, n_pairs)
        weight_grads(n_pairs, n_pairs - mouse_start, True, d_mouse, db_mouse)

    @pl.when(j > 0)
    def _():
        def body(s, carry):
            predicted[meta[windows + s]] = jnp.zeros((length, block), bf16)
            return carry

        lax.fori_loop(n_human, windows, body, 0)

    @pl.when(j == pl.num_programs(0) - 1)
    def _():
        @pl.loop(0, windows)
        def _(s):
            source = pl.multiple_of(s * length, length)
            target = pl.multiple_of(meta[s] * length, length)
            grad_summed[pl.ds(target, length), :] = grad_sorted[pl.ds(source, length), :]


def heads(meta, summed, w_heads, b_human, b_mouse, cotangent, mouse_tracks, length):
    windows, _, human_tracks = cotangent.shape
    rows, mid = summed.shape
    blocks = w_heads.shape[1] // BLOCK - 1
    row_block = pl.BlockSpec((1, BLOCK), lambda j, meta: (0, j))
    row_fixed = pl.BlockSpec((1, BLOCK), lambda j, meta: (0, 0))
    fixed = pl.BlockSpec((rows, mid), lambda j, meta: (0, 0))
    return pl.pallas_call(
        functools.partial(heads_kernel, human_tracks, mouse_tracks),
        grid_spec=pltpu.PrefetchScalarGridSpec(
            num_scalar_prefetch=1,
            grid=(blocks,),
            in_specs=[
                fixed,
                pl.BlockSpec((mid, BLOCK), lambda j, meta: (0, j)),
                pl.BlockSpec(
                    (mid, BLOCK), lambda j, meta: (0, blocks), pipeline_mode=pl.Buffered(1)
                ),
                row_block,
                row_fixed,
                pl.BlockSpec((windows, length, BLOCK), lambda j, meta: (0, 0, j)),
            ],
            out_specs=[
                pl.BlockSpec((windows, length, BLOCK), lambda j, meta: (0, 0, j)),
                fixed,
                pl.BlockSpec((mid, BLOCK), lambda j, meta: (0, j)),
                pl.BlockSpec((mid, BLOCK), lambda j, meta: (0, 0)),
                row_block,
                row_fixed,
            ],
            scratch_shapes=[
                pltpu.VMEM((rows, mid), bf16),
                pltpu.VMEM((rows, mid), f32),
                pltpu.VMEM((rows, BLOCK), bf16),
            ],
        ),
        out_shape=[
            jax.ShapeDtypeStruct((windows, length, human_tracks), bf16),
            jax.ShapeDtypeStruct((rows, mid), f32),
            jax.ShapeDtypeStruct((mid, blocks * BLOCK), bf16),
            jax.ShapeDtypeStruct((mid, BLOCK), bf16),
            jax.ShapeDtypeStruct((1, blocks * BLOCK), f32),
            jax.ShapeDtypeStruct((1, BLOCK), f32),
        ],
        compiler_params=params(),
        name="heads",
    )(meta, summed, w_heads, w_heads, b_human, b_mouse, cotangent)


class Summing:
    STAGES = 7

    def __init__(self, place, source, target, columns, scratch):
        self.place, self.source, self.target, self.columns = place, source, target, columns
        self.own, self.core, self.side_a, self.side_b, self.end_a, self.end_b = scratch[:6]
        self.z_near, self.z_far, self.z_back, self.mate, self.sems = scratch[6:]
        half = self.own.shape[2]
        self.half, self.part = half, half // 2
        self.mine = pl.ds(pl.multiple_of(place.sec * half, half), half)
        self.other = pl.ds(pl.multiple_of((1 - place.sec) * half, half), half)
        self.x, self.y = lax.rem(place.dp, 2), lax.div(place.dp, 2)
        self.z = lax.rem(place.seq, 2)
        self.top, self.bottom = pl.ds(0, self.part), pl.ds(self.part, self.part)
        self.keep = pl.ds(pl.multiple_of(self.z * self.part, self.part), self.part)
        self.give = pl.ds(pl.multiple_of((1 - self.z) * self.part, self.part), self.part)

    def remote(self, source, target, sem, device):
        return pltpu.make_async_remote_copy(
            src_ref=source,
            dst_ref=target,
            send_sem=self.sems.at[2 * sem],
            recv_sem=self.sems.at[2 * sem + 1],
            device_id=device,
            device_id_type=MESH,
        )

    def copies(self, stage):
        p, own, x, y = self.place, self.own, self.x, self.y
        sibling = (1 - p.sec, p.seq, p.dp)
        over_x = (p.sec, p.seq, p.dp + 1 - 2 * x)
        over_y = (p.sec, p.seq, p.dp + 2 - 4 * y)
        over_z = (p.sec, p.seq + 1 - 2 * self.z, p.dp)
        z_pair = lax.div(p.seq, 2)
        beyond = (p.sec, p.seq + 2 - 4 * z_pair, p.dp)
        if stage == 0:
            return [
                pltpu.make_async_copy(
                    self.source.at[:, :, self.mine, self.columns], own, self.sems.at[20]
                ),
                self.remote(
                    self.source.at[:, :, self.other, self.columns], self.core, 0, sibling
                ),
            ]
        if stage == 1:
            return [
                self.remote(own.at[:, 1 - x, self.top], self.side_a, 1, over_x),
                self.remote(own.at[1 - y, :, self.bottom], self.side_b, 2, over_y),
            ]
        if stage == 2:
            return [
                self.remote(own.at[1 - y, x, self.top], self.end_a, 3, over_y),
                self.remote(own.at[y, 1 - x, self.bottom], self.end_b, 4, over_x),
            ]
        if stage == 3:
            return [self.remote(own.at[y, x, self.give], self.z_near, 5, over_z)]
        if stage == 4:
            return [self.remote(own.at[y, x, self.keep], self.z_far, 6, beyond)]
        if stage == 5:
            return [self.remote(own.at[y, x, self.keep], self.z_back, 7, over_z)]
        return [
            self.remote(own.at[y, x, self.keep], self.mate.at[self.keep], 8, sibling),
            self.remote(self.z_back, self.mate.at[self.give], 9, sibling),
        ]

    def start(self, stage):
        for copy in self.copies(stage):
            copy.start()

    def finish(self, stage):
        for copy in self.copies(stage):
            copy.wait()
        own, x, y = self.own, self.x, self.y

        def add(at, other):
            own[at] = (own[at].astype(f32) + other.astype(f32)).astype(bf16)

        if stage == 0:

            @pl.loop(0, 4)
            def _(i):
                a, b = lax.div(i, 2), lax.rem(i, 2)
                add((a, b), self.core[a, b])

        elif stage == 1:
            for i in range(2):
                add((i, x, self.top), self.side_a[i])
                add((y, i, self.bottom), self.side_b[i])
        elif stage == 2:
            add((y, x, self.top), self.end_a[...])
            add((y, x, self.bottom), self.end_b[...])
        elif stage == 3:
            add((y, x, self.keep), self.z_near[...])
        elif stage == 4:
            add((y, x, self.keep), self.z_far[...])
        elif stage == 6:
            for copy in self.results():
                copy.start()

    def results(self):
        there = pl.ds(pl.multiple_of((1 - self.place.sec) * self.half, self.half), self.half)
        base = self.place.sec * self.half
        first = pl.ds(pl.multiple_of(base + self.z * self.part, self.part), self.part)
        second = pl.ds(pl.multiple_of(base + (1 - self.z) * self.part, self.part), self.part)
        kept = self.own.at[self.y, self.x, self.keep]
        return [
            pltpu.make_async_copy(source, self.target.at[rows, self.columns], self.sems.at[21 + i])
            for i, (source, rows) in enumerate(
                ((kept, first), (self.z_back, second), (self.mate, there))
            )
        ]

    def close(self):
        for copy in self.results():
            copy.wait()

    @staticmethod
    def scratch(share, width):
        half = share // 2
        part = half // 2
        return [
            pltpu.VMEM((2, 2, half, width), bf16),
            pltpu.VMEM((2, 2, half, width), bf16),
            pltpu.VMEM((2, part, width), bf16),
            pltpu.VMEM((2, part, width), bf16),
            pltpu.VMEM((part, width), bf16),
            pltpu.VMEM((part, width), bf16),
            pltpu.VMEM((part, width), bf16),
            pltpu.VMEM((part, width), bf16),
            pltpu.VMEM((part, width), bf16),
            pltpu.VMEM((half, width), bf16),
            pltpu.SemaphoreType.DMA((24,)),
        ]


class Sums:
    LAG = (-2, -1, 0, 1, 2, 3, 4, 5)

    def __init__(self, place, sources, targets, chunks, scratch):
        self.parts = [
            Summing(
                place,
                sources[source],
                targets[source],
                pl.ds(start, width),
                scratch[11 * i : 11 * (i + 1)],
            )
            for i, (source, start, width) in enumerate(chunks)
        ]
        self.begun = 0
        self.tick = min(self.LAG)

    def step(self, ready=None):
        count = len(self.parts)
        if self.tick > count + self.LAG[-1]:
            return
        if ready is not None and self.tick - self.LAG[0] >= ready and self.tick - self.LAG[0] < count:
            return
        for stage, lag in enumerate(self.LAG):
            k = self.tick - lag
            if 0 <= k < count:
                if stage > 0:
                    self.parts[k].finish(stage - 1)
                if stage < Summing.STAGES:
                    self.parts[k].start(stage)
        self.tick += 1

    def finish(self):
        while self.tick <= len(self.parts) + self.LAG[-1]:
            self.step()
        for part in self.parts:
            part.close()


def cut(widths, most):
    chunks = []
    for source, width in enumerate(widths):
        pieces = -(-width // most)
        size = -(-width // (pieces * LANES)) * LANES
        chunks += [(source, at, min(size, width - at)) for at in range(0, width, size)]
    return chunks


def sums_scratch(share, chunks):
    return [ref for chunk in chunks for ref in Summing.scratch(share, chunk[2])]


def split_refs(refs, *counts):
    groups = []
    for count in counts:
        groups.append(refs[:count])
        refs = refs[count:]
    assert not refs
    return groups


def back_high_kernel(shape, n_sums, chunks, *refs):
    (sources, big_in, small_in, targets, d_outs, outs, fixed, sum_refs) = split_refs(
        refs, n_sums, 3, 16, n_sums, 3, 4, 43, 11 * len(chunks)
    )
    in_grad, in_u_one, in_u_two = big_in
    (
        act_three,
        branch,
        branch_low,
        branch_high,
        bn_three,
        gain_three,
        shift_three,
        w_point,
        bias_sums,
        w_two,
        pooled,
        pooled_low,
        pooled_high,
        bn_two,
        gain_two,
        shift_two,
    ) = small_in
    grad_ext, sums_three, sums_two, bias_out = outs
    reduce_b, reduce_three, reduce_two, fixed = fixed[:6], fixed[6:12], fixed[12:18], fixed[18:]
    (
        grad_summed,
        u_any,
        du_three,
        edge_low,
        edge_high,
        du_low,
        du_high,
        row_low,
        row_high,
        gs_low,
        gs_high,
        local_three,
        grad_branch,
        du_two,
        row_low_two,
        row_high_two,
        dlow_two,
        dhigh_two,
        local_two,
        grad_main,
        d_point,
        d_two,
        d_one,
        halo_sems,
        copy_sems,
    ) = fixed
    place = Place(shape)
    place.greet()
    windows, length, mid = pooled.shape
    small = branch.shape[1]
    pair = 2 * length
    taps = w_two.shape[0] // mid
    scale = 1.0 / (pair * shape[0] * shape[1] * shape[2])
    u_two = u_any.at[:, : taps * mid]
    load_grad = pltpu.make_async_copy(in_grad, grad_summed, copy_sems.at[0])
    load_two = pltpu.make_async_copy(in_u_two, u_two, copy_sems.at[1])
    load_one = pltpu.make_async_copy(in_u_one, u_any, copy_sems.at[2])
    save_point, save_two, save_one = [
        pltpu.make_async_copy(a, b, copy_sems.at[3 + i])
        for i, (a, b) in enumerate(((d_point, d_outs[0]), (d_two, d_outs[1]), (d_one, d_outs[2])))
    ]
    load_grad.start()
    load_two.start()
    sums = Sums(place, sources, targets, chunks, sum_refs)
    place.meet()
    sums.step()
    load_grad.wait()

    for m in range(MB):
        at = slice(m * pair, (m + 1) * pair)
        grad = grad_summed[at, :]
        back = dot_nn(grad.astype(bf16), w_point[...])
        xhat = (branch[at, :] - bn_three[m : m + 1, :]) * bn_three[MB + m : MB + m + 1, :]
        du = gelu_slope(xhat * gain_three[...] + shift_three[...]) * back
        du_three[at, :] = du
        local_three[m : m + 1, :] = jnp.sum(du, axis=0, keepdims=True)
        local_three[MB + m : MB + m + 1, :] = jnp.sum(du * xhat, axis=0, keepdims=True)
        for i in range(2):
            w = 2 * m + i
            edge_low[w] = du[i * length : i * length + EDGE]
            edge_high[w] = du[(i + 1) * length - EDGE : (i + 1) * length]
            row_low[w : w + 1, :] = grad[i * length : i * length + 1]
            row_high[w : w + 1, :] = grad[(i + 1) * length - 1 : (i + 1) * length]
        if m == 1:
            sums.step()

    moves = halo_copies(place, (edge_low, edge_high), (du_low, du_high), halo_sems.at[0])
    moves += halo_copies(place, (row_low, row_high), (gs_low, gs_high), halo_sems.at[1])
    for move in moves:
        move.start()
    sums_three[...] = reduce_everywhere(
        place, local_three[...], *reduce_three[:2], reduce_three[2:], add_up, sums.step
    )
    d_point[...] = dot_tn(grad_summed[...].astype(bf16), act_three[...]).astype(bf16)
    save_point.start()
    for move in moves:
        move.wait()
    sums.step()

    for m in range(MB):
        at = slice(m * pair, (m + 1) * pair)
        centre, inverse = bn_three[m : m + 1, :], bn_three[MB + m : MB + m + 1, :]
        factor = gain_three[...] * inverse
        mean_du = sums_three[m : m + 1, :] * scale
        mean_dx = sums_three[MB + m : MB + m + 1, :] * scale

        def back(du, value):
            xhat = (value - centre) * inverse
            return factor * (du - mean_du - xhat * mean_dx)

        main = back(du_three[at, :], branch[at, :])
        grad_branch[at, :] = main.astype(bf16)
        pieces = []
        for i in range(2):
            w = 2 * m + i
            low = jnp.where(place.is_first, 0.0, back(du_low[w], branch_low[w]))
            high = jnp.where(place.is_last, 0.0, back(du_high[w], branch_high[w]))
            pieces += [low, main[i * length : (i + 1) * length], high]
        ext = jnp.concatenate(pieces, axis=0).astype(bf16)
        span = length + 2 * EDGE
        through = [dot_nt(ext, w_two[t * mid : (t + 1) * mid, :]) for t in range(taps)]
        centre_two, inverse_two = bn_two[m : m + 1, :], bn_two[MB + m : MB + m + 1, :]
        total_du = jnp.zeros((1, mid), f32)
        total_dx = jnp.zeros((1, mid), f32)
        for i in range(2):
            w = 2 * m + i
            grad = jnp.zeros((length, mid), f32)
            for t in range(taps):
                whole = through[t][i * span : (i + 1) * span]
                grad = grad + shifted_rows(whole, EDGE - (t - 1) * DILATION, length)
            xhat = (pooled[w].astype(f32) - centre_two) * inverse_two
            du = gelu_slope(xhat * gain_two[...] + shift_two[...]) * grad
            du_two[w] = du
            total_du = total_du + jnp.sum(du, axis=0, keepdims=True)
            total_dx = total_dx + jnp.sum(du * xhat, axis=0, keepdims=True)
            row_low_two[w : w + 1, :] = du[:1]
            row_high_two[w : w + 1, :] = du[length - 1 :]
        local_two[m : m + 1, :] = total_du
        local_two[MB + m : MB + m + 1, :] = total_dx
        sums.step()

    moves = halo_copies(
        place, (row_low_two, row_high_two), (dlow_two, dhigh_two), halo_sems.at[2]
    )
    for move in moves:
        move.start()
    sums_two[...] = reduce_everywhere(
        place, local_two[...], *reduce_two[:2], reduce_two[2:], add_up, sums.step
    )
    load_two.wait()
    for t in range(taps):
        part = dot_tn(u_two[:, t * mid : (t + 1) * mid], grad_branch[...])
        d_two[:, t * small : (t + 1) * small] = part.astype(bf16)
    save_two.start()
    load_one.start()
    for move in moves:
        move.wait()
    sums.step()

    for m in range(MB):
        centre, inverse = bn_two[m : m + 1, :], bn_two[MB + m : MB + m + 1, :]
        factor = gain_two[...] * inverse
        mean_du = sums_two[m : m + 1, :] * scale
        mean_dx = sums_two[MB + m : MB + m + 1, :] * scale

        def back(du, value, extra):
            xhat = (value.astype(f32) - centre) * inverse
            return factor * (du - mean_du - xhat * mean_dx) + extra

        edges = []
        for i in range(2):
            w = 2 * m + i
            at = slice(w * length, (w + 1) * length)
            value = back(du_two[w], pooled[w], grad_summed[at, :]).astype(bf16)
            grad_ext[m, i * length : (i + 1) * length, :] = value
            grad_main[at, :] = value
            row = slice(w, w + 1)
            low = back(dlow_two[row, :], pooled_low[w].astype(f32)[EDGE - 1 :], gs_low[row, :])
            high = back(dhigh_two[row, :], pooled_high[w].astype(f32)[:1], gs_high[row, :])
            edges += [jnp.where(place.is_first, 0.0, low), jnp.where(place.is_last, 0.0, high)]
        row = lax.broadcasted_iota(jnp.int32, (EDGE, mid), 0)
        block = jnp.zeros((EDGE, mid), f32)
        for i, edge in enumerate(edges):
            block = jnp.where(row == i, edge, block)
        grad_ext[m, pair : pair + EDGE, :] = block.astype(bf16)
    sums.step()
    load_one.wait()
    columns = d_one.shape[1] // 5
    for t in range(5):
        part = slice(t * columns, (t + 1) * columns)
        d_one[:, part] = dot_tn(grad_main[...], u_any[:, part]).astype(bf16)
        if t in (1, 3):
            sums.step()
    save_one.start()
    bias_out[...] = reduce_everywhere(
        place, bias_sums[...], *reduce_b[:2], reduce_b[2:], add_up, sums.step
    )
    sums.finish()
    save_point.wait()
    save_two.wait()
    save_one.wait()


def back_high(shape, sources, grad_summed, u_one, u_two, three, bias_sums, two):
    branch, w_point = three[1], three[-1]
    w_two, pooled = two[0], two[1]
    windows, length, mid = pooled.shape
    rows, small = branch.shape
    share = mid // shape[2]
    chunks = cut([g.shape[3] for g in sources], BLOCK // 2)
    taps = w_two.shape[0] // mid
    targets = [((share, g.shape[3]), bf16) for g in sources]
    d_shapes = [((mid, small), bf16), ((mid, taps * small), bf16), ((mid, u_one.shape[1]), bf16)]
    outs = [
        ((MB, 2 * length + EDGE, mid), bf16),
        ((2 * MB, small), f32),
        ((2 * MB, mid), f32),
        (bias_sums.shape, f32),
    ]
    fixed = (
        reduce_scratch(shape, *bias_sums.shape)
        + reduce_scratch(shape, 2 * MB, small)
        + reduce_scratch(shape, 2 * MB, mid)
    )
    fixed += [
        pltpu.VMEM(*a)
        for a in [
            ((rows, mid), f32),
            (u_one.shape, bf16),
            ((rows, small), f32),
            ((windows, EDGE, small), f32),
            ((windows, EDGE, small), f32),
            ((windows, EDGE, small), f32),
            ((windows, EDGE, small), f32),
            ((windows, mid), f32),
            ((windows, mid), f32),
            ((windows, mid), f32),
            ((windows, mid), f32),
            ((2 * MB, small), f32),
            ((rows, small), bf16),
            ((windows, length, mid), f32),
            ((windows, mid), f32),
            ((windows, mid), f32),
            ((windows, mid), f32),
            ((windows, mid), f32),
            ((2 * MB, mid), f32),
            ((rows, mid), bf16),
            *d_shapes,
        ]
    ]
    fixed += [pltpu.SemaphoreType.DMA((3, 4)), pltpu.SemaphoreType.DMA((6,))]
    return pl.pallas_call(
        functools.partial(back_high_kernel, shape, len(sources), chunks),
        in_specs=[HBM] * (3 + len(sources)) + [VM] * 16,
        out_specs=[HBM] * (3 + len(sources)) + [VM] * 4,
        out_shape=[jax.ShapeDtypeStruct(*o) for o in targets + d_shapes + outs],
        scratch_shapes=fixed + sums_scratch(share, chunks),
        compiler_params=params(2),
        name="back_high",
    )(*sources, grad_summed, u_one, u_two, *three, bias_sums, *two)


def back_low_kernel(shape, n_sums, chunks, *refs):
    (sources, ins, targets, outs, reduce_one, fixed, sum_refs) = split_refs(
        refs, n_sums, 7, n_sums, 2, 6, 5, 11 * len(chunks)
    )
    inverse_order, in_one, grad_ext, x2, bn_one, gain_one, shift_one = ins
    grad_input, sums_one = outs
    w_one, du_one, local, lanes_buffer, load_sem = fixed
    place = Place(shape)
    place.greet()
    windows, length, wide = x2.shape
    channels = wide // 2
    pair = 2 * length
    load_one = pltpu.make_async_copy(in_one, w_one, load_sem)
    load_one.start()
    sums = Sums(place, sources, targets, chunks, sum_refs)
    place.meet()
    sums.step()
    load_one.wait()

    for m in range(MB):
        through = [
            dot_nn(grad_ext[m], w_one[:, t * channels : (t + 1) * channels]) for t in range(5)
        ]
        centre, inverse = bn_one[m : m + 1, :], bn_one[MB + m : MB + m + 1, :]
        total_du = jnp.zeros((1, wide), f32)
        total_dx = jnp.zeros((1, wide), f32)
        row = lax.broadcasted_iota(jnp.int32, (length, channels), 0)
        top, bottom = row == 0, row == length - 1
        for i in range(2):
            w = 2 * m + i
            main = [t[i * length : (i + 1) * length] for t in through]
            low = [t[pair + 2 * i : pair + 2 * i + 1] for t in through]
            high = [t[pair + 2 * i + 1 : pair + 2 * i + 2] for t in through]
            later = lambda t: jnp.where(bottom, high[t], pltpu.roll(main[t], length - 1, axis=0))
            earlier = lambda t: jnp.where(top, low[t], pltpu.roll(main[t], 1, axis=0))
            mean = later(0) + main[2] + earlier(4)
            cross = main[1] + earlier(3)
            cross_end = high[1] + main[3][length - 1 :]
            cross_later = jnp.where(bottom, cross_end, pltpu.roll(cross, length - 1, axis=0))
            grad = jnp.concatenate([(mean + cross) * 0.5, (mean + cross_later) * 0.5], axis=1)
            xhat = (x2[w].astype(f32) - centre) * inverse
            du = gelu_slope(xhat * gain_one[...] + shift_one[...]) * grad
            du_one[w] = du
            total_du = total_du + jnp.sum(du, axis=0, keepdims=True)
            total_dx = total_dx + jnp.sum(du * xhat, axis=0, keepdims=True)
        local[m : m + 1, :] = total_du[:, :channels] + total_du[:, channels:]
        local[MB + m : MB + m + 1, :] = total_dx[:, :channels] + total_dx[:, channels:]
        sums.step()

    sums_one[...] = reduce_everywhere(
        place, local[...], *reduce_one[:2], reduce_one[2:], add_up, sums.step
    )
    scale = 1.0 / (4 * length * shape[0] * shape[1] * shape[2])
    lanes = lanes_buffer.shape[0]
    twice = lambda v: jnp.concatenate([v, v], axis=1)

    def write(window):
        w = inverse_order[window]
        m = lax.div(w, 2)
        mean_du = twice(sums_one[pl.ds(m, 1), :]) * scale
        mean_dx = twice(sums_one[pl.ds(MB + m, 1), :]) * scale
        inverse = bn_one[pl.ds(MB + m, 1), :]
        xhat = (x2[w].astype(f32) - bn_one[pl.ds(m, 1), :]) * inverse
        grad = gain_one[...] * inverse * (du_one[w] - mean_du - xhat * mean_dx)
        for odd in range(2):
            for c in range(lanes):
                at = odd * channels + c * LANES
                lanes_buffer[c, pl.ds(odd, length, 2), :] = grad[:, at : at + LANES]
        for c in range(lanes):
            grad_input[window, :, c * LANES : (c + 1) * LANES] = lanes_buffer[c].astype(bf16)

    for half in range(2):
        sums.step()

        @pl.loop(half * windows // 2, (half + 1) * windows // 2)
        def _(window):
            write(window)

    sums.finish()


def back_low(shape, sources, inverse_order, w_one, grad_ext, x2, bn_one, gain, move):
    windows, length, wide = x2.shape
    channels = wide // 2
    share = grad_ext.shape[2] // shape[2]
    chunks = cut([g.shape[3] for g in sources], 1152)
    targets = [((share, g.shape[3]), bf16) for g in sources]
    outs = [((windows, 2 * length, channels), bf16), ((2 * MB, channels), f32)]
    scratch = reduce_scratch(shape, 2 * MB, channels)
    scratch += [
        pltpu.VMEM(w_one.shape, bf16),
        pltpu.VMEM((windows, length, wide), f32),
        pltpu.VMEM((2 * MB, channels), f32),
        pltpu.VMEM((channels // LANES, 2 * length, LANES), f32),
        pltpu.SemaphoreType.DMA,
    ]
    smem = pl.BlockSpec(memory_space=pltpu.SMEM)
    return pl.pallas_call(
        functools.partial(back_low_kernel, shape, len(sources), chunks),
        in_specs=[HBM] * len(sources) + [smem, HBM] + [VM] * 5,
        out_specs=[HBM] * len(sources) + [VM] * 2,
        out_shape=[jax.ShapeDtypeStruct(*o) for o in targets + outs],
        scratch_shapes=scratch + sums_scratch(share, chunks),
        compiler_params=params(3),
        name="back_low",
    )(*sources, inverse_order, w_one, grad_ext, x2, bn_one, gain, move)


def per_device(
    shape,
    tracks,
    species,
    batch_order,
    conv_one,
    dilated_kernel,
    point_wise,
    head_human,
    head_mouse,
    bias_human,
    bias_mouse,
    gain_one,
    shift_one,
    gain_two,
    shift_two,
    gain_three,
    shift_three,
    cotangent,
):
    sec = lax.axis_index("section").astype(jnp.int32)
    windows, seq_bins, channels = tracks.shape
    half = seq_bins // 2
    length = half // 2
    human_tracks, mouse_tracks = head_human.shape[1], head_mouse.shape[1]
    human_wide = -(-human_tracks // BLOCK) * BLOCK
    share = conv_one.shape[2]
    mid = share * shape[2]

    taps_one = conv_one.shape[0]
    shard_one = jnp.transpose(conv_one, (2, 0, 1)).reshape(share, taps_one * channels)
    shard_point = point_wise.T
    shard_heads = jnp.concatenate(
        [
            jnp.pad(head_human, ((0, 0), (0, human_wide - human_tracks))),
            jnp.pad(head_mouse, ((0, 0), (0, BLOCK - mouse_tracks))),
        ],
        axis=1,
    )
    half_rows = share // shape[0]
    half_heads = lax.dynamic_slice_in_dim(shard_heads, sec * half_rows, half_rows, 0)
    w_heads = lax.all_gather(half_heads, ("dp", "section"), axis=0, tiled=True)
    weights = [shard_one, dilated_kernel, shard_point]
    if shape != (2, 4, 4):
        weights = [lax.all_gather(w, "dp", axis=w.ndim - 2, tiled=True) for w in weights]

    meta_one = jnp.concatenate([batch_order, sec[None]])
    x2, edge_low, edge_high, stats = prepare(tracks, meta_one, half)
    row = lambda v: v.reshape(1, -1)
    twice = lambda v: jnp.tile(v, 2).reshape(1, -1)
    gains = (
        twice(gain_one),
        twice(shift_one),
        row(gain_two),
        row(shift_two),
        row(gain_three),
        row(shift_three),
    )
    (
        u_one,
        u_two,
        pooled,
        pooled_low,
        pooled_high,
        branch,
        branch_low,
        branch_high,
        act_three,
        summed,
        bn_one,
        bn_two,
        bn_three,
        w_one,
        w_two,
        w_point,
    ) = forward(shape, mid, x2, edge_low, edge_high, stats, gains, *weights)
    w_two = w_two.reshape(-1, w_two.shape[2])

    kinds = species[batch_order]
    is_human = kinds == 0
    n_human = jnp.sum(is_human.astype(jnp.int32))
    place_human = jnp.cumsum(is_human.astype(jnp.int32)) - 1
    place_mouse = n_human + jnp.cumsum(1 - is_human.astype(jnp.int32)) - 1
    target = jnp.where(is_human, place_human, place_mouse)
    positions = jnp.sum(
        jnp.where(target[None, :] == jnp.arange(windows)[:, None], jnp.arange(windows)[None, :], 0),
        axis=1,
    ).astype(jnp.int32)
    meta_two = jnp.concatenate(
        [positions, batch_order[positions], n_human[None], sec[None]]
    ).astype(jnp.int32)
    wide_human = jnp.pad(bias_human, (0, human_wide - human_tracks)).reshape(1, -1)
    wide_mouse = jnp.pad(bias_mouse, (0, BLOCK - mouse_tracks)).reshape(1, -1)
    cot_half = lax.dynamic_slice_in_dim(cotangent, sec * length, length, 1)
    predicted, grad_summed, d_human, d_mouse, db_human, db_mouse = heads(
        meta_two, summed, w_heads, wide_human, wide_mouse, cot_half, mouse_tracks, length
    )

    bias_sums = jnp.concatenate([db_human, db_mouse], axis=1).reshape(8, -1)

    def in_kernel(*grads):
        if shape != (2, 4, 4):
            return []
        return [g.reshape(2, 2, -1, g.shape[1]) for g in grads]

    def summed_up(given, *grads):
        if given:
            return given
        parts = [lax.psum_scatter(g, "dp", scatter_dimension=0, tiled=True) for g in grads]
        return [lax.psum(part, ("section", "seq")) for part in parts]

    *sums_high, d_point, d_two, d_one, grad_ext, sums_three, sums_two, bias_out = back_high(
        shape,
        in_kernel(d_human, d_mouse),
        grad_summed,
        u_one,
        u_two,
        (act_three, branch, branch_low, branch_high, bn_three, gains[4], gains[5], w_point),
        bias_sums,
        (w_two, pooled, pooled_low, pooled_high, bn_two, gains[2], gains[3]),
    )
    inverse_order = jnp.sum(
        jnp.where(
            batch_order[None, :] == jnp.arange(windows)[:, None], jnp.arange(windows)[None, :], 0
        ),
        axis=1,
    ).astype(jnp.int32)
    *sums_low, grad_input, sums_one = back_low(
        shape,
        in_kernel(d_point, d_two, d_one),
        inverse_order,
        w_one,
        grad_ext,
        x2,
        bn_one,
        gains[0],
        gains[1],
    )
    r_human, r_mouse = summed_up(sums_high, d_human, d_mouse)
    r_point, r_two, r_one = summed_up(sums_low, d_point, d_two, d_one)
    r_human = r_human.astype(f32)[:, :human_tracks]
    r_mouse = r_mouse.astype(f32)[:, :mouse_tracks]
    r_point = r_point.astype(f32)
    r_two = jnp.transpose(
        r_two.astype(f32).reshape(share, -1, dilated_kernel.shape[2]), (1, 0, 2)
    )
    r_one = jnp.transpose(r_one.astype(f32).reshape(share, taps_one, channels), (1, 0, 2))
    r_point = r_point.T
    r_one = jnp.transpose(r_one, (0, 2, 1))
    bias = bias_out.reshape(-1)
    return (
        predicted,
        grad_input,
        r_one,
        r_two,
        r_point,
        r_human,
        r_mouse,
        bias[:human_tracks],
        bias[human_wide : human_wide + mouse_tracks],
        jnp.sum(sums_one[MB:], axis=0),
        jnp.sum(sums_one[:MB], axis=0),
        jnp.sum(sums_two[MB:], axis=0),
        jnp.sum(sums_two[:MB], axis=0),
        jnp.sum(sums_three[MB:], axis=0),
        jnp.sum(sums_three[:MB], axis=0),
    )


def solution(mesh):
    shape = (mesh.shape["section"], mesh.shape["seq"], mesh.shape["dp"])
    placed = (
        P("dp", "seq", None),
        P("dp"),
        P(),
        P(None, None, "dp"),
        P(None, "dp", None),
        P(None, "dp"),
        P("dp", None),
        P("dp", None),
    ) + (P(),) * 8 + (P("dp", "seq", None),)
    return jax.shard_map(
        functools.partial(per_device, shape),
        mesh=mesh,
        in_specs=placed,
        out_specs=(
            P("dp", ("seq", "section"), None),
            P("dp", ("seq", "section"), None),
            P(None, None, "dp"),
            P(None, "dp", None),
            P(None, "dp"),
            P("dp", None),
            P("dp", None),
        )
        + (P(),) * 8,
        check_vma=False,
    )
```

```python
import functools
import math

import jax
import jax.numpy as jnp
from jax import lax
from jax.experimental import pallas as pl
from jax.experimental.pallas import tpu as pltpu
from jax.sharding import PartitionSpec as P

MESH = pl.DeviceIdType.MESH
DILATION = 11
MB = 4
EPS = 1e-05
EDGE = 16
BLOCK = 1792
LANES = 128
VMEM_LIMIT = 60 * 1024 * 1024
GELU_K = math.sqrt(2.0 / math.pi)
GELU_C = 0.044715
f32 = jnp.float32
bf16 = jnp.bfloat16
VM = pl.BlockSpec(memory_space=pltpu.VMEM)
HBM = pl.BlockSpec(memory_space=pl.ANY)


def params(collective_id=None, limit=VMEM_LIMIT):
    if collective_id is None:
        return pltpu.CompilerParams(vmem_limit_bytes=limit)
    return pltpu.CompilerParams(
        vmem_limit_bytes=limit, collective_id=collective_id, has_side_effects=True
    )


def gelu(u):
    t = jnp.tanh(u * (GELU_K + (GELU_K * GELU_C) * (u * u)))
    h = 0.5 * u
    return h + h * t


def gelu_slope(u):
    uu = u * u
    t = jnp.tanh(u * (GELU_K + (GELU_K * GELU_C) * uu))
    return 0.5 * (1.0 + t) + (0.5 * u) * (1.0 - t * t) * (GELU_K + (3.0 * GELU_K * GELU_C) * uu)


def dot_nn(a, b):
    return jnp.dot(a, b, preferred_element_type=f32)


def dot_nt(a, b):
    return lax.dot_general(a, b, (((1,), (1,)), ((), ())), preferred_element_type=f32)


def dot_tn(a, b):
    return lax.dot_general(a, b, (((0,), (0,)), ((), ())), preferred_element_type=f32)


class Place:
    def __init__(self, shape):
        self.n_sec, self.n_seq, self.n_dp = shape
        self.n_near = self.n_sec * self.n_dp
        self.sec = lax.axis_index("section")
        self.seq = lax.axis_index("seq")
        self.dp = lax.axis_index("dp")
        self.near = self.sec * self.n_dp + self.dp
        n_bins = self.n_seq * self.n_sec
        bins = self.seq * self.n_sec + self.sec
        self.is_first = bins == 0
        self.is_last = bins == n_bins - 1
        low = lax.rem(bins + n_bins - 1, n_bins)
        high = lax.rem(bins + 1, n_bins)
        self.low = self.bin_device(low)
        self.high = self.bin_device(high)
        across = jnp.where(self.sec == 0, low, high)
        self.across = self.bin_device(across)

    def halos(self, moves, action):
        for up, down in zip(moves[::2], moves[1::2]):
            if action == 0:
                pl.when(jnp.logical_not(self.is_last))(up.start)
                pl.when(jnp.logical_not(self.is_first))(down.start)
            else:
                for first, last in ((up.wait_send, up.wait_recv), (down.wait_recv, down.wait_send)):
                    pl.when(jnp.logical_not(self.is_last))(first)
                    pl.when(jnp.logical_not(self.is_first))(last)

    def bin_device(self, bins):
        return (lax.rem(bins, self.n_sec), lax.div(bins, self.n_sec), self.dp)

    def near_device(self, rank):
        return (lax.div(rank, self.n_dp), self.seq, lax.rem(rank, self.n_dp))

    def greet(self):
        barrier = pltpu.get_barrier_semaphore()
        for k in range(1, self.n_near):
            rank = lax.rem(self.near + k, self.n_near)
            pl.semaphore_signal(
                barrier, inc=1, device_id=self.near_device(rank), device_id_type=MESH
            )
        for k in range(1, self.n_seq):
            seq = lax.rem(self.seq + k, self.n_seq)
            pl.semaphore_signal(
                barrier, inc=1, device_id=(self.sec, seq, self.dp), device_id_type=MESH
            )
        pl.semaphore_signal(barrier, inc=1, device_id=self.across, device_id_type=MESH)

    def meet(self):
        pl.semaphore_wait(pltpu.get_barrier_semaphore(), self.n_near + self.n_seq - 1)


def halo_copies(place, from_self, arrived, sems):
    up = pltpu.make_async_remote_copy(
        src_ref=from_self[1],
        dst_ref=arrived[0],
        send_sem=sems.at[0],
        recv_sem=sems.at[1],
        device_id=place.high,
        device_id_type=MESH,
    )
    down = pltpu.make_async_remote_copy(
        src_ref=from_self[0],
        dst_ref=arrived[1],
        send_sem=sems.at[2],
        recv_sem=sems.at[3],
        device_id=place.low,
        device_id_type=MESH,
    )
    return up, down


def nothing():
    pass


def spread_round(buffer, mine, count, device_of, send, recv, meanwhile=nothing):
    copies = []
    for k in range(1, count):
        rank = lax.rem(mine + k, count)
        copy = pltpu.make_async_remote_copy(
            src_ref=buffer.at[mine],
            dst_ref=buffer.at[mine],
            send_sem=send.at[k],
            recv_sem=recv.at[mine],
            device_id=device_of(rank),
            device_id_type=MESH,
        )
        copy.start()
        copies.append((rank, copy))
    meanwhile()
    for rank, copy in copies:
        pltpu.make_async_remote_copy(
            src_ref=buffer.at[rank],
            dst_ref=buffer.at[rank],
            send_sem=send.at[0],
            recv_sem=recv.at[rank],
            device_id=device_of(rank),
            device_id_type=MESH,
        ).wait_recv()
    for rank, copy in copies:
        copy.wait_send()


def reduce_everywhere(
    place, value, near_buf, far_buf, sems, combine, meanwhile=nothing, then=None
):
    then = meanwhile if then is None else then
    near_send, near_recv, far_send, far_recv = sems
    far_buf[place.seq] = value
    spread_round(
        far_buf,
        place.seq,
        place.n_seq,
        lambda seq: (place.sec, seq, place.dp),
        far_send,
        far_recv,
        meanwhile,
    )
    near_buf[place.near] = combine(far_buf, place.n_seq, 1)
    spread_round(
        near_buf, place.near, place.n_near, place.near_device, near_send, near_recv, then
    )
    return combine(near_buf, place.n_near, place.n_seq)


def add_up(buffer, count, weight):
    total = buffer[0]
    for i in range(1, count):
        total = total + buffer[i]
    return total


def merge_stats(rows, buffer, count, weight):
    means = [buffer[i][:MB] for i in range(count)]
    centre = means[0]
    spread = buffer[0][MB:]
    for i in range(1, count):
        centre = centre + means[i]
        spread = spread + buffer[i][MB:]
    centre = centre * (1.0 / count)
    apart = jnp.square(means[0] - centre)
    for i in range(1, count):
        apart = apart + jnp.square(means[i] - centre)
    return jnp.concatenate([centre, spread + apart * float(rows * weight)], axis=0)


def reduce_scratch(shape, rows, columns):
    n_sec, n_seq, n_dp = shape
    near = n_sec * n_dp
    return [
        pltpu.VMEM((near, rows, columns), f32),
        pltpu.VMEM((n_seq, rows, columns), f32),
        pltpu.SemaphoreType.DMA((near,)),
        pltpu.SemaphoreType.DMA((near,)),
        pltpu.SemaphoreType.DMA((n_seq,)),
        pltpu.SemaphoreType.DMA((n_seq,)),
    ]


def local_stats(value):
    count = value.shape[0]
    centre = jnp.sum(value, axis=0, keepdims=True) * (1.0 / count)
    return centre, jnp.sum(jnp.square(value - centre), axis=0, keepdims=True)


def finish_stats(stats, total):
    return jnp.concatenate(
        [stats[:MB], lax.rsqrt(stats[MB:] * (1.0 / total) + EPS)], axis=0
    )


def prepare(place, order, tracks, pairs, low, high, stats, scratch):
    lanes, half, _ = scratch.shape
    start = pl.multiple_of(place.sec * half, half)

    @pl.loop(0, MB)
    def _(m):
        values = []
        for i in range(2):
            value = tracks[order[2 * m + i], pl.ds(start, half), :].astype(f32)
            values.append(value)
            for c in range(lanes):
                scratch[c] = value[:, c * LANES : (c + 1) * LANES]
            both = jnp.concatenate(
                [scratch[c, pl.ds(odd, half // 2, 2), :] for odd in range(2) for c in range(lanes)],
                axis=1,
            )
            pairs[2 * m + i] = both.astype(bf16)
            low[pl.ds(2 * m + i, 1), :] = both[:1]
            high[pl.ds(2 * m + i, 1), :] = both[half // 2 - 1 :]
        count = 2 * half
        centre = (
            jnp.sum(values[0], axis=0, keepdims=True) + jnp.sum(values[1], axis=0, keepdims=True)
        ) * (1.0 / count)
        spread = jnp.sum(jnp.square(values[0] - centre), axis=0, keepdims=True) + jnp.sum(
            jnp.square(values[1] - centre), axis=0, keepdims=True
        )
        stats[pl.ds(m, 1), :] = centre
        stats[pl.ds(MB + m, 1), :] = spread


class Gathering:
    STAGES = 5

    def __init__(self, place, shard, full, rows_at, sems):
        self.place, self.shard, self.full, self.rows_at, self.sems = place, shard, full, rows_at, sems
        p = place
        x, y, z = lax.rem(p.dp, 2), lax.div(p.dp, 2), lax.rem(p.seq, 2)
        self.share = shard.shape[rows_at]
        self.group = self.share // 6
        g = self.group
        self.dp_x, self.dp_y = p.dp + 1 - 2 * x, p.dp + 2 - 4 * y
        self.dp_xy = 3 - p.dp
        self.sibling = (1 - p.sec, p.seq, p.dp)
        self.over_x, self.over_y = (p.sec, p.seq, self.dp_x), (p.sec, p.seq, self.dp_y)
        self.over_z = (p.sec, p.seq + 1 - 2 * z, p.dp)
        base = p.sec * 3 * g
        self.near, self.middle, self.edge, self.far, self.half = (
            (base + z * g, 2 * g),
            (base + g, g),
            (base + 2 * z * g, g),
            (base + 2 * (1 - z) * g, g),
            (base, 3 * g),
        )

    def at(self, ref, dp, span):
        start, rows = span
        index = pl.ds(pl.multiple_of(dp * self.share + start, self.group), rows)
        return ref.at[:, index] if self.rows_at else ref.at[index]

    def remote(self, dp, span, sem, device, source=None):
        source = self.at(self.full, dp, span) if source is None else source
        return pltpu.make_async_remote_copy(
            src_ref=source,
            dst_ref=self.at(self.full, dp, span),
            send_sem=self.sems.at[2 * sem],
            recv_sem=self.sems.at[2 * sem + 1],
            device_id=device,
            device_id_type=MESH,
        )

    def own_copy(self):
        target = self.at(self.full, self.place.dp, (0, self.share))
        return pltpu.make_async_copy(self.shard, target, self.sems.at[26])

    def copies(self, stage):
        me = self.place.dp
        if stage == 0:
            own = self.at(self.shard, 0, self.near)
            return [
                self.remote(me, self.near, 0, self.over_x, own),
                self.remote(me, self.near, 1, self.over_y, own),
            ]
        if stage == 1:
            return [
                self.remote(self.dp_x, self.middle, 2, self.over_y),
                self.remote(self.dp_y, self.edge, 3, self.over_x),
                self.remote(self.dp_x, self.edge, 4, self.over_z),
                self.remote(self.dp_y, self.edge, 5, self.over_z),
                self.remote(self.dp_x, self.near, 6, self.sibling),
                self.remote(self.dp_y, self.near, 7, self.sibling),
            ]
        if stage == 2:
            return [
                self.remote(self.dp_xy, self.edge, 8, self.over_z),
                self.remote(self.dp_xy, self.near, 9, self.sibling),
            ]
        if stage == 3:
            return [
                self.remote(self.dp_x, self.far, 10, self.sibling),
                self.remote(self.dp_y, self.far, 11, self.sibling),
                self.remote(self.dp_xy, self.far, 12, self.sibling),
            ]
        return []

    def start(self, stage):
        for copy in self.copies(stage):
            copy.start()

    def arrived(self, stage, which, dp, span):
        copy = self.copies(stage)[which]
        pltpu.make_async_remote_copy(
            src_ref=self.at(self.full, dp, span),
            dst_ref=self.at(self.full, dp, span),
            send_sem=self.sems.at[0],
            recv_sem=self.sems.at[2 * {0: 0, 1: 2, 2: 8, 3: 10}[stage] + 2 * which + 1],
            device_id=self.sibling,
            device_id_type=MESH,
        ).wait_recv()

    def advance(self, stage):
        if stage == 0:
            self.own_copy().start()
        elif stage == 1:
            self.arrived(0, 0, self.dp_x, self.near)
            self.arrived(0, 1, self.dp_y, self.near)
        elif stage == 2:
            self.arrived(1, 0, self.dp_xy, self.middle)
            self.arrived(1, 1, self.dp_xy, self.edge)
        elif stage == 3:
            self.arrived(1, 2, self.dp_x, self.far)
            self.arrived(1, 3, self.dp_y, self.far)
            self.arrived(2, 0, self.dp_xy, self.far)
        if stage < 4:
            self.start(stage)
            return
        base = (1 - self.place.sec) * 3 * self.group
        z = lax.rem(self.place.seq, 2)
        near = (base + z * self.group, 2 * self.group)
        far = (base + 2 * (1 - z) * self.group, self.group)
        self.arrived(1, 4, self.dp_x, near)
        self.arrived(1, 5, self.dp_y, near)
        self.arrived(2, 1, self.dp_xy, near)
        self.arrived(3, 0, self.dp_x, far)
        self.arrived(3, 1, self.dp_y, far)
        self.arrived(3, 2, self.dp_xy, far)
        self.own_copy().wait()
        for stage in range(4):
            for copy in self.copies(stage):
                copy.wait_send()


class Relay:
    TRACKS = 512

    def __init__(self, source, target, first_bin, refs):
        self.source, self.target, self.first = source, target, first_bin
        self.got, self.rows, self.made, self.sems = refs
        self.length = target.shape[1]
        self.count = -(-source.shape[0] // self.TRACKS)
        self.at = 0

    def width(self, i):
        return min(self.TRACKS, self.source.shape[0] - i * self.TRACKS)

    def load(self, i):
        width = self.width(i)
        bins = pl.ds(pl.multiple_of(self.first, self.length), self.length)
        return pltpu.make_async_copy(
            self.source.at[pl.ds(i * self.TRACKS, width), :, bins],
            self.got.at[i % 2, pl.ds(0, width)],
            self.sems.at[i % 2],
        )

    def store(self, i):
        width = min(self.TRACKS, self.target.shape[2] - i * self.TRACKS)
        return pltpu.make_async_copy(
            self.made.at[i % 2, :, :, pl.ds(0, width)],
            self.target.at[:, :, pl.ds(i * self.TRACKS, width)],
            self.sems.at[2 + i % 2],
        )

    def begin(self):
        self.load(0).start()

    def step(self):
        i = self.at
        if i == self.count:
            return
        self.at += 1
        slot, width = i % 2, self.width(i)
        windows = self.got.shape[2]
        self.load(i).wait()
        if i + 1 < self.count:
            self.load(i + 1).start()
        if i > 1:
            self.store(i - 2).wait()
        if width < self.TRACKS:
            self.got[slot, width:] = jnp.zeros((self.TRACKS - width, *self.got.shape[2:]), bf16)
        value = self.got[slot].astype(f32)
        self.rows[...] = value.reshape(self.TRACKS * windows, self.length)
        for w in range(windows):
            self.made[slot, w] = self.rows[pl.ds(w, self.TRACKS, windows), :].astype(bf16).T
        self.store(i).start()

    def finish(self):
        while self.at < self.count:
            self.step()
        for i in range(max(0, self.count - 2), self.count):
            self.store(i).wait()

    @staticmethod
    def scratch(windows, length):
        tracks = Relay.TRACKS
        return [
            pltpu.VMEM((2, tracks, windows, length), bf16),
            pltpu.VMEM((tracks * windows, length), f32),
            pltpu.VMEM((2, windows, length, tracks), bf16),
            pltpu.SemaphoreType.DMA((4,)),
        ]


def shifted_rows(value, offset, length):
    rows = value.shape[0]
    if offset:
        value = pltpu.roll(value, rows - offset, axis=0)
    return value[:length]


def forward_kernel(shape, n_relay, *refs):
    (
        order,
        tracks,
        vectors,
        in_one,
        in_two,
        in_point,
    ) = refs[:6]
    refs = refs[6:]
    in_cot, refs = refs[:n_relay], refs[n_relay:]
    (
        out_u_one,
        out_u_two,
        pooled,
        pooled_low,
        pooled_high,
        branch,
        branch_low,
        branch_high,
        act_three,
        summed,
        bn_one,
        bn_two,
        bn_three,
        out_one,
        out_two,
        out_point,
        x2,
    ) = refs[:17]
    refs = refs[17:]
    out_cot, refs = refs[:n_relay], refs[n_relay:]
    (
        near_one,
        far_one,
        s10,
        s11,
        s12,
        s13,
        near_two,
        far_two,
        s20,
        s21,
        s22,
        s23,
        near_three,
        far_three,
        s30,
        s31,
        s32,
        s33,
        got_low,
        got_high,
        stats_two,
        stats_three,
        halo_sems,
        s_branch_edge_low,
        s_branch_edge_high,
        u_one,
        u_two,
        w_one,
        w_two,
        w_point,
        weight_sems,
        save_sems,
        edge_low,
        edge_high,
        stats_in,
        lanes_buffer,
    ) = refs[:36]
    relay_refs = refs[36:]
    place = Place(shape)
    place.greet()
    windows, length, wide = x2.shape
    channels = wide // 2
    mid = pooled.shape[2]
    small = branch.shape[1]
    parts = shape[0] * shape[1] * shape[2]
    pair = 2 * length
    saves = [
        pltpu.make_async_copy(source, target, save_sems.at[i])
        for i, (source, target) in enumerate(
            ((u_one, out_u_one), (u_two, out_u_two), (w_one, out_one), (w_two, out_two), (w_point, out_point))
        )
    ]
    gathers = []
    if in_one.shape[0] < w_one.shape[0]:
        columns = w_one.shape[1]
        first = columns // (2 * LANES) * LANES
        pieces = [
            (in_one.at[:, part], w_one.at[:, part], 0)
            for part in (pl.ds(0, first), pl.ds(first, columns - first))
        ]
        pieces += [(in_two, w_two, 1), (in_point, w_point, 0)]
        gathers = [
            Gathering(place, *piece, weight_sems.at[i]) for i, piece in enumerate(pieces)
        ]
    else:
        loads = [
            pltpu.make_async_copy(source, target, weight_sems.at[i, 0])
            for i, (source, target) in enumerate(
                ((in_one, w_one), (in_two, w_two), (in_point, w_point))
            )
        ]
        for load in loads:
            load.start()
        for load in loads:
            load.wait()

    def advance(*steps):
        for index, stage in steps:
            if index < len(gathers):
                gathers[index].advance(stage)

    mid_rows = lambda index, width: vectors.at[index : index + 1, :width]
    gain_one, shift_one = mid_rows(0, wide), mid_rows(1, wide)
    gain_two, shift_two = mid_rows(2, mid), mid_rows(3, mid)
    gain_three, shift_three = mid_rows(4, small), mid_rows(5, small)
    relay = None
    if n_relay:
        relay = Relay(in_cot[0], out_cot[0], place.sec * length, relay_refs)
        relay.begin()

    def fill(count=1):
        for _ in range(count if relay else 0):
            relay.step()

    prepare(place, order, tracks, x2, edge_low, edge_high, stats_in, lanes_buffer)
    place.meet()
    advance((0, 0), (1, 0))
    up, down = halo_copies(place, (edge_low, edge_high), (got_low, got_high), halo_sems.at[0])
    place.halos((up, down), 0)
    stats = reduce_everywhere(
        place,
        stats_in[...],
        near_one,
        far_one,
        (s10, s11, s12, s13),
        functools.partial(merge_stats, 4 * length),
        fill,
        lambda: advance((0, 1)),
    )
    stats = finish_stats(stats, 4 * length * parts)
    bn_one[...] = jnp.concatenate([stats, stats], axis=1)
    place.halos((up, down), 1)
    advance((1, 1), (0, 2), (2, 0), (3, 0))

    @pl.loop(0, windows)
    def _(w):
        m = lax.div(w, 2)
        centre = bn_one[pl.ds(m, 1), :]
        scale = bn_one[pl.ds(MB + m, 1), :] * gain_one[...]
        move = shift_one[...]

        def act(value):
            return gelu((value - centre) * scale + move).astype(bf16).astype(f32)

        main = act(x2[w].astype(f32))
        before = jnp.where(place.is_first, 0.0, act(got_low[pl.ds(w, 1), :]))
        after = jnp.where(place.is_last, 0.0, act(got_high[pl.ds(w, 1), :]))
        even, odd = main[:, :channels], main[:, channels:]
        mean = (even + odd) * 0.5
        mean_before = (before[:, :channels] + before[:, channels:]) * 0.5
        mean_after = (after[:, :channels] + after[:, channels:]) * 0.5
        row = lax.broadcasted_iota(jnp.int32, (length, channels), 0)
        top, bottom = row == 0, row == length - 1
        odd_before = jnp.where(top, before[:, channels:], pltpu.roll(odd, 1, axis=0))
        cross = (odd_before + even) * 0.5
        cross_after = (odd[length - 1 :] + after[:, :channels]) * 0.5
        start = pl.multiple_of(w * length, length)
        taps = (
            jnp.where(top, mean_before, pltpu.roll(mean, 1, axis=0)),
            cross,
            mean,
            jnp.where(bottom, cross_after, pltpu.roll(cross, length - 1, axis=0)),
            jnp.where(bottom, mean_after, pltpu.roll(mean, length - 1, axis=0)),
        )
        for t, tap in enumerate(taps):
            u_one[pl.ds(start, length), t * channels : (t + 1) * channels] = tap.astype(bf16)

    saves[0].start()
    advance((1, 2), (0, 3))
    fill(2)
    advance((1, 3), (0, 4))
    fill()
    advance((1, 4), (2, 1), (3, 1))
    saves[2].start()

    @pl.loop(0, MB)
    def _(m):
        start = pl.multiple_of(m * pair, pair)
        value = dot_nt(u_one[pl.ds(start, pair), :], w_one[...]).astype(bf16)
        pooled[pl.ds(2 * m, 2)] = value.reshape(2, length, mid)
        centre, spread = local_stats(value.astype(f32))
        stats_two[pl.ds(m, 1), :] = centre
        stats_two[pl.ds(MB + m, 1), :] = spread

    advance((2, 2), (3, 2))
    up, down = halo_copies(
        place,
        (pooled.at[:, pl.ds(0, EDGE), :], pooled.at[:, pl.ds(length - EDGE, EDGE), :]),
        (pooled_low, pooled_high),
        halo_sems.at[1],
    )
    place.halos((up, down), 0)
    stats = reduce_everywhere(
        place,
        stats_two[...],
        near_two,
        far_two,
        (s20, s21, s22, s23),
        functools.partial(merge_stats, pair),
        fill,
    )
    bn_two[...] = finish_stats(stats, pair * parts)
    place.halos((up, down), 1)
    advance((2, 3), (3, 3))

    @pl.loop(0, windows)
    def _(w):
        m = lax.div(w, 2)
        centre = bn_two[pl.ds(m, 1), :]
        scale = bn_two[pl.ds(MB + m, 1), :] * gain_two[...]
        move = shift_two[...]

        def act(value):
            return gelu((value.astype(f32) - centre) * scale + move)

        ext = jnp.concatenate(
            [
                jnp.where(place.is_first, 0.0, act(pooled_low[w])),
                act(pooled[w]),
                jnp.where(place.is_last, 0.0, act(pooled_high[w])),
            ],
            axis=0,
        )
        start = pl.multiple_of(w * length, length)
        for t in range(3):
            tap = shifted_rows(ext, EDGE + (t - 1) * DILATION, length)
            u_two[pl.ds(start, length), t * mid : (t + 1) * mid] = tap.astype(bf16)

    saves[1].start()
    advance((2, 4), (3, 4))
    saves[3].start()
    saves[4].start()

    @pl.loop(0, MB)
    def _(m):
        start = pl.multiple_of(m * pair, pair)
        value = jnp.zeros((pair, small), f32)
        for t in range(w_two.shape[0]):
            value = value + dot_nn(
                u_two[pl.ds(start, pair), t * mid : (t + 1) * mid], w_two[t]
            )
        branch[pl.ds(start, pair), :] = value
        centre, spread = local_stats(value)
        stats_three[pl.ds(m, 1), :] = centre
        stats_three[pl.ds(MB + m, 1), :] = spread
        for i in range(2):
            s_branch_edge_low[2 * m + i] = value[i * length : i * length + EDGE]
            s_branch_edge_high[2 * m + i] = value[(i + 1) * length - EDGE : (i + 1) * length]

    up, down = halo_copies(
        place,
        (s_branch_edge_low, s_branch_edge_high),
        (branch_low, branch_high),
        halo_sems.at[2],
    )
    place.halos((up, down), 0)
    stats = reduce_everywhere(
        place,
        stats_three[...],
        near_three,
        far_three,
        (s30, s31, s32, s33),
        functools.partial(merge_stats, pair),
        fill,
    )
    bn_three[...] = finish_stats(stats, pair * parts)

    @pl.loop(0, MB)
    def _(m):
        centre = bn_three[pl.ds(m, 1), :]
        scale = bn_three[pl.ds(MB + m, 1), :] * gain_three[...]
        start = pl.multiple_of(m * pair, pair)
        act = gelu((branch[pl.ds(start, pair), :] - centre) * scale + shift_three[...])
        act = act.astype(bf16)
        act_three[pl.ds(start, pair), :] = act
        lifted = dot_nt(act, w_point[...])
        here = pooled[pl.ds(2 * m, 2)].reshape(pair, mid).astype(f32)
        summed[pl.ds(start, pair), :] = (here + lifted).astype(bf16)

    place.halos((up, down), 1)
    if relay:
        relay.finish()
    for save in saves:
        save.wait()


def forward(shape, mid, order, tracks, vectors, w_one, w_two, w_point, cot):
    windows, seq_bins, channels = tracks.shape
    half = seq_bins // shape[0]
    length, wide = half // 2, 2 * channels
    rows = windows * length
    taps_two, _, small = w_two.shape
    big = [
        ((mid, w_one.shape[1]), bf16),
        ((taps_two, mid, small), bf16),
        ((mid, small), bf16),
    ]
    out = [
        ((rows, w_one.shape[1]), bf16),
        ((rows, taps_two * mid), bf16),
        ((windows, length, mid), bf16),
        ((windows, EDGE, mid), bf16),
        ((windows, EDGE, mid), bf16),
        ((rows, small), f32),
        ((windows, EDGE, small), f32),
        ((windows, EDGE, small), f32),
        ((rows, small), bf16),
        ((rows, mid), bf16),
        ((2 * MB, wide), f32),
        ((2 * MB, mid), f32),
        ((2 * MB, small), f32),
    ]
    out_specs = [HBM] * 2 + [VM] * 11 + [HBM] * 3 + [VM] + [HBM] * len(cot)
    out += big + [((windows, length, wide), bf16)]
    out += [((windows, length, -(-c.shape[0] // BLOCK) * BLOCK), bf16) for c in cot]
    scratch = (
        reduce_scratch(shape, 2 * MB, wide // 2)
        + reduce_scratch(shape, 2 * MB, mid)
        + reduce_scratch(shape, 2 * MB, small)
    )
    scratch += [
        pltpu.VMEM((windows, wide), f32),
        pltpu.VMEM((windows, wide), f32),
        pltpu.VMEM((2 * MB, mid), f32),
        pltpu.VMEM((2 * MB, small), f32),
        pltpu.SemaphoreType.DMA((3, 4)),
        pltpu.VMEM((windows, EDGE, small), f32),
        pltpu.VMEM((windows, EDGE, small), f32),
        pltpu.VMEM(*out[0]),
        pltpu.VMEM(*out[1]),
    ]
    scratch += [pltpu.VMEM(*b) for b in big]
    scratch += [
        pltpu.SemaphoreType.DMA((4, 27)),
        pltpu.SemaphoreType.DMA((5,)),
        pltpu.VMEM((windows, wide), f32),
        pltpu.VMEM((windows, wide), f32),
        pltpu.VMEM((2 * MB, channels), f32),
        pltpu.VMEM((channels // LANES, half, LANES), f32),
        *(Relay.scratch(windows, length) if cot else []),
    ]
    return pl.pallas_call(
        functools.partial(forward_kernel, shape, len(cot)),
        in_specs=[pl.BlockSpec(memory_space=pltpu.SMEM), VM, VM] + [HBM] * (3 + len(cot)),
        out_specs=out_specs,
        out_shape=[jax.ShapeDtypeStruct(*o) for o in out],
        scratch_shapes=scratch,
        compiler_params=params(1),
        name="forward",
    )(order, tracks, vectors, w_one, w_two, w_point, *cot)


def heads_kernel(
    human_tracks,
    mouse_tracks,
    species,
    order,
    summed,
    w_human,
    w_mouse,
    b_human,
    b_mouse,
    cot,
    predicted,
    grad_summed,
    d_human,
    d_mouse,
    db,
    rows_sorted,
    grad_sorted,
    grad_pre,
    meta,
):
    j = pl.program_id(0)
    windows, length, block = cot.shape
    pair = 2 * length
    n_pairs = windows // 2
    mid = summed.shape[1]

    @pl.when(j == 0)
    def _():
        grad_sorted[...] = jnp.zeros_like(grad_sorted)
        db[...] = jnp.zeros_like(db)
        found = 0
        for kind in range(2):
            for p in range(windows):
                window = order[p]
                mine = species[window] == kind

                @pl.when(mine)
                def _(found=found, p=p, window=window):
                    meta[found] = p
                    meta[windows + found] = window

                found = found + mine.astype(jnp.int32)
            if kind == 0:
                meta[2 * windows] = found

        @pl.loop(0, windows)
        def _(s):
            source = pl.multiple_of(meta[s] * length, length)
            target = pl.multiple_of(s * length, length)
            rows_sorted[pl.ds(target, length), :] = summed[pl.ds(source, length), :]

    n_human = meta[2 * windows]
    column = lax.broadcasted_iota(jnp.int32, (1, block), 1)

    def run(weight, bias, limit, is_mouse, first_pair, last_pair):
        def body(p, carry):
            start = pl.multiple_of(p * pair, pair)
            pre = dot_nn(rows_sorted[pl.ds(start, pair), :], weight[...]) + bias[...]
            decay = jnp.exp(-jnp.abs(pre))
            whole = 1.0 + decay
            inverse = 1.0 / whole
            sigmoid = jnp.where(pre >= 0, inverse, decay * inverse)
            logs = jnp.where(decay < 2.0**-11, decay, jnp.log(whole))
            output = (jnp.maximum(pre, 0.0) + logs).astype(bf16)
            output = jnp.where(column < limit, output, jnp.zeros_like(output))
            for i in range(2):
                s = 2 * p + i
                window = meta[windows + s]
                mine = s >= n_human if is_mouse else s < n_human
                keep = (column < limit) & mine
                part = slice(i * length, (i + 1) * length)
                grad = jnp.where(keep, cot[window].astype(f32) * sigmoid[part], 0.0)
                grad_pre[pl.ds(pl.multiple_of(s * length, length), length), :] = grad.astype(bf16)

                @pl.when(mine)
                def _():
                    predicted[window] = output[part]

            grad_sorted[pl.ds(start, pair), :] += dot_nt(
                grad_pre[pl.ds(start, pair), :], weight[...]
            )
            return carry

        lax.fori_loop(first_pair, last_pair, body, 0)

    def weight_grads(n_used, from_end, d_weight, bias_row):
        for n in range(n_pairs + 1):

            @pl.when(n_used == n)
            def _(n=n):
                if n == 0:
                    d_weight[...] = jnp.zeros_like(d_weight)
                else:
                    part = slice((n_pairs - n) * pair, None) if from_end else slice(0, n * pair)
                    grad = grad_pre[part, :]
                    d_weight[...] = dot_tn(rows_sorted[part, :], grad).astype(bf16)
                    total = dot_nn(jnp.ones((8, n * pair), bf16), grad)[:1]
                    db[pl.ds(bias_row, 1), :] = total

    human_pairs = lax.div(n_human + 1, 2)
    run(w_human, b_human, human_tracks - j * block, False, 0, human_pairs)
    weight_grads(human_pairs, False, d_human, j)

    @pl.when(j == 0)
    def _():
        mouse_start = lax.div(n_human, 2)
        run(w_mouse, b_mouse, mouse_tracks, True, mouse_start, n_pairs)
        weight_grads(n_pairs - mouse_start, True, d_mouse, pl.num_programs(0))

    @pl.when(j > 0)
    def _():
        def body(s, carry):
            predicted[meta[windows + s]] = jnp.zeros((length, block), bf16)
            return carry

        lax.fori_loop(n_human, windows, body, 0)

    @pl.when(j == pl.num_programs(0) - 1)
    def _():
        @pl.loop(0, windows)
        def _(s):
            source = pl.multiple_of(s * length, length)
            target = pl.multiple_of(meta[s] * length, length)
            grad_summed[pl.ds(target, length), :] = grad_sorted[pl.ds(source, length), :]


def heads(species, order, summed, w_heads, bias, cot, human_tracks, mouse_tracks):
    windows, length, _ = cot.shape
    rows, mid = summed.shape
    blocks = w_heads.shape[1] // BLOCK - 1
    smem = pl.BlockSpec(memory_space=pltpu.SMEM)
    fixed = lambda shape, at=0: pl.BlockSpec(
        shape, lambda j: (0, at), pipeline_mode=pl.Buffered(1)
    )
    return pl.pallas_call(
        functools.partial(heads_kernel, human_tracks, mouse_tracks),
        grid=(blocks,),
        in_specs=[
            smem,
            smem,
            fixed((rows, mid)),
            pl.BlockSpec((mid, BLOCK), lambda j: (0, j)),
            fixed((mid, BLOCK), blocks),
            pl.BlockSpec((1, BLOCK), lambda j: (0, j)),
            fixed((1, BLOCK), blocks),
            pl.BlockSpec((windows, length, BLOCK), lambda j: (0, 0, j)),
        ],
        out_specs=[
            pl.BlockSpec((windows, length, BLOCK), lambda j: (0, 0, j)),
            pl.BlockSpec((rows, mid), lambda j: (0, 0)),
            pl.BlockSpec((mid, BLOCK), lambda j: (0, j)),
            pl.BlockSpec((mid, BLOCK), lambda j: (0, 0)),
            pl.BlockSpec((8, BLOCK), lambda j: (0, 0)),
        ],
        scratch_shapes=[
            pltpu.VMEM((rows, mid), bf16),
            pltpu.VMEM((rows, mid), f32),
            pltpu.VMEM((rows, BLOCK), bf16),
            pltpu.SMEM((2 * windows + 1,), jnp.int32),
        ],
        out_shape=[
            jax.ShapeDtypeStruct((windows, length, human_tracks), bf16),
            jax.ShapeDtypeStruct((rows, mid), f32),
            jax.ShapeDtypeStruct((mid, blocks * BLOCK), bf16),
            jax.ShapeDtypeStruct((mid, BLOCK), bf16),
            jax.ShapeDtypeStruct((8, BLOCK), f32),
        ],
        compiler_params=params(),
        name="heads",
    )(species, order, summed, w_heads, w_heads, bias, bias, cot)


HAND, LOAD = 7, 8
WHOLE = (0, 1, 2, 3, 4, 5, 6)
PLANE = (0, 1, 2, HAND)
ALONG = (LOAD, 3, 4, 5, 6)


class Summing:
    def __init__(self, place, plan, source, start, width, target, to, scratch):
        self.place, self.plan, self.source, self.target = place, plan, source, target
        self.columns = pl.ds(start, width)
        self.width, self.to = width, to
        for name, ref in zip(self.names(plan), scratch):
            setattr(self, name, ref)
        half = self.own.shape[2]
        self.half, self.part = half, half // 2
        self.mine = pl.ds(pl.multiple_of(place.sec * half, half), half)
        self.other = pl.ds(pl.multiple_of((1 - place.sec) * half, half), half)
        self.x, self.y = lax.rem(place.dp, 2), lax.div(place.dp, 2)
        self.cell = (self.y, self.x) if 0 in plan else (0, 0)
        self.top, self.bottom = pl.ds(0, self.part), pl.ds(self.part, self.part)
        self.at_end = (place.seq == 0) | (place.seq == place.n_seq - 1)
        self.between = jnp.logical_not(self.at_end)

    @staticmethod
    def names(plan):
        names = ["own"]
        if 0 in plan:
            names += ["core", "side_a", "side_b", "end_a", "end_b"]
        if 6 in plan:
            names += ["z_one", "z_far", "mate"]
        return names + ["sems"]

    @staticmethod
    def scratch(plan, share, width):
        half = share // 2
        part = half // 2
        cells = 2 if 0 in plan else 1
        shapes = dict(
            own=(cells, cells, half, width),
            core=(2, 2, half, width),
            side_a=(2, part, width),
            side_b=(2, part, width),
            end_a=(part, width),
            end_b=(part, width),
            z_one=(half, width),
            z_far=(half, width),
            mate=(half, width),
        )
        refs = [pltpu.VMEM(shapes[name], bf16) for name in Summing.names(plan)[:-1]]
        return refs + [pltpu.SemaphoreType.DMA((23,))]

    def remote(self, source, target, sem, device):
        return pltpu.make_async_remote_copy(
            src_ref=source,
            dst_ref=target,
            send_sem=self.sems.at[2 * sem],
            recv_sem=self.sems.at[2 * sem + 1],
            device_id=device,
            device_id_type=MESH,
        )

    def copies(self, stage):
        p, own, x, y = self.place, self.own, self.x, self.y
        sibling = (1 - p.sec, p.seq, p.dp)
        over_x = (p.sec, p.seq, p.dp + 1 - 2 * x)
        over_y = (p.sec, p.seq, p.dp + 2 - 4 * y)
        over_z = (p.sec, p.seq + 1 - 2 * lax.rem(p.seq, 2), p.dp)
        if stage == 0:
            return [
                pltpu.make_async_copy(
                    self.source.at[:, :, self.mine, self.columns], own, self.sems.at[16]
                ),
                self.remote(
                    self.source.at[:, :, self.other, self.columns], self.core, 0, sibling
                ),
            ]
        if stage == 1:
            return [
                self.remote(own.at[:, 1 - x, self.top], self.side_a, 1, over_x),
                self.remote(own.at[1 - y, :, self.bottom], self.side_b, 2, over_y),
            ]
        if stage == 2:
            return [
                self.remote(own.at[1 - y, x, self.top], self.end_a, 3, over_y),
                self.remote(own.at[y, 1 - x, self.bottom], self.end_b, 4, over_x),
            ]
        if stage == HAND:
            columns = pl.ds(self.to, self.width)
            return [
                pltpu.make_async_copy(
                    own.at[self.cell], self.target.at[:, columns], self.sems.at[17]
                )
            ]
        if stage == LOAD:
            return [
                pltpu.make_async_copy(
                    self.source.at[:, self.columns], own.at[self.cell], self.sems.at[17]
                )
            ]
        if stage == 3:
            return [self.remote(own.at[self.cell], self.z_one, 5, over_z)]
        if stage == 4:
            opposite = (p.sec, p.n_seq - 1 - p.seq, p.dp)
            return [self.remote(own.at[self.cell], self.z_far, 6, opposite)]
        if stage == 5:
            return [self.remote(own.at[self.cell], self.z_one, 5, over_z)]
        return [
            self.remote(source, self.mate, 7, sibling) for source in (own.at[self.cell], self.z_one)
        ]

    def start(self, stage):
        copies = self.copies(stage)
        if stage == 3:
            pl.when(self.at_end)(copies[0].start)
        elif stage in (4, 5):
            pl.when(self.between)(copies[0].start)
        elif stage == 6:
            pl.when(self.between)(copies[0].start)
            pl.when(self.at_end)(copies[1].start)
        else:
            for copy in copies:
                copy.start()

    def add(self, at, other):
        self.own[at] = (self.own[at].astype(f32) + other.astype(f32)).astype(bf16)

    def finish(self, stage):
        copies = self.copies(stage)
        x, y = self.x, self.y
        if stage == 3:
            pl.when(self.at_end)(copies[0].wait_send)

            @pl.when(self.between)
            def _():
                copies[0].wait_recv()
                self.add(self.cell, self.z_one[...])

        elif stage == 4:

            @pl.when(self.between)
            def _():
                copies[0].wait()
                self.add(self.cell, self.z_far[...])

        elif stage == 5:
            pl.when(self.between)(copies[0].wait_send)
            pl.when(self.at_end)(copies[0].wait_recv)
        elif stage == 6:
            copies[0].wait()
            pl.when(self.between)(self.results(self.own.at[self.cell])[0].start)
            pl.when(self.at_end)(self.results(self.z_one)[0].start)
            self.results(self.z_one)[1].start()
        elif stage != HAND:
            for copy in copies:
                copy.wait()
        if stage == 0:

            @pl.loop(0, 4)
            def _(i):
                a, b = lax.div(i, 2), lax.rem(i, 2)
                self.add((a, b), self.core[a, b])

        elif stage == 1:
            for i in range(2):
                self.add((i, x, self.top), self.side_a[i])
                self.add((y, i, self.bottom), self.side_b[i])
        elif stage == 2:
            self.add((y, x, self.top), self.end_a[...])
            self.add((y, x, self.bottom), self.end_b[...])

    def results(self, source):
        copies = []
        for i, (ref, rows) in enumerate(((source, self.mine), (self.mate, self.other))):
            if len(self.target.shape) == 3:
                target = self.target.at[self.to, rows]
            else:
                target = self.target.at[rows, pl.ds(self.to, self.width)]
            copies.append(pltpu.make_async_copy(ref, target, self.sems.at[18 + i]))
        return copies

    def close(self):
        copies = self.results(self.mate) if 6 in self.plan else self.copies(HAND)
        for copy in copies:
            copy.wait()


class Sums:
    def __init__(self, place, sources, targets, chunks, refs):
        self.parts = []
        for plan, begin, source, start, width, target, to in chunks:
            count = len(Summing.names(plan))
            part = Summing(
                place, plan, sources[source], start, width, targets[target], to, refs[:count]
            )
            refs = refs[count:]
            self.parts.append((begin, part))
        self.parts.sort(key=lambda item: -item[0])
        self.last = max([begin + len(part.plan) for begin, part in self.parts], default=-1)
        self.tick = 0

    def step(self):
        if self.tick > self.last:
            return
        for begin, part in self.parts:
            i = self.tick - begin
            if 0 < i <= len(part.plan):
                part.finish(part.plan[i - 1])
            if 0 <= i < len(part.plan):
                part.start(part.plan[i])
        self.tick += 1

    def finish(self):
        while self.tick <= self.last:
            self.step()
        for _, part in self.parts:
            part.close()


def sums_scratch(share, chunks):
    return [ref for chunk in chunks for ref in Summing.scratch(chunk[0], share, chunk[4])]


def count_refs(chunks):
    return sum(len(Summing.names(chunk[0])) for chunk in chunks)


def head_chunks(human_wide):
    size = BLOCK // 2
    pieces = [(0, at) for at in range(0, human_wide, size)] + [(1, 0), (1, size)]
    n_whole = len(pieces) // 2
    chunks = []
    for k, (source, at) in enumerate(pieces):
        whole = k < n_whole
        to = (k if whole else k - n_whole) * size
        chunks.append((WHOLE if whole else PLANE, k, source, at, size, 0 if whole else 1, to))
    return chunks, n_whole * size, (len(pieces) - n_whole) * size


def split_refs(refs, *counts):
    groups = []
    for count in counts:
        groups.append(refs[:count])
        refs = refs[count:]
    assert not refs
    return groups


def back_high_kernel(shape, n_sums, chunks, *refs):
    (sources, big_in, small_in, targets, d_outs, outs, fixed, sum_refs) = split_refs(
        refs, n_sums, 3, 13, n_sums, 3, 4, 43, count_refs(chunks)
    )
    in_grad, in_u_one, in_u_two = big_in
    (
        act_three,
        branch,
        branch_low,
        branch_high,
        bn_three,
        w_point,
        bias_sums,
        w_two,
        pooled,
        pooled_low,
        pooled_high,
        bn_two,
        vectors,
    ) = small_in
    grad_ext, sums_three, sums_two, bias_out = outs
    reduce_b, reduce_three, reduce_two, fixed = fixed[:6], fixed[6:12], fixed[12:18], fixed[18:]
    (
        grad_summed,
        u_any,
        du_three,
        edge_low,
        edge_high,
        du_low,
        du_high,
        row_low,
        row_high,
        gs_low,
        gs_high,
        local_three,
        grad_branch,
        du_two,
        row_low_two,
        row_high_two,
        dlow_two,
        dhigh_two,
        local_two,
        grad_main,
        d_point,
        d_two,
        d_one,
        halo_sems,
        copy_sems,
    ) = fixed
    place = Place(shape)
    place.greet()
    windows, length, mid = pooled.shape
    small = branch.shape[1]
    pair = 2 * length
    taps = w_two.shape[0] // mid
    scale = 1.0 / (pair * shape[0] * shape[1] * shape[2])
    row = lambda index, width: vectors.at[index : index + 1, :width]
    gain_two, shift_two = row(2, mid), row(3, mid)
    gain_three, shift_three = row(4, small), row(5, small)
    u_two = u_any.at[:, : taps * mid]
    load_grad = pltpu.make_async_copy(in_grad, grad_summed, copy_sems.at[0])
    load_two = pltpu.make_async_copy(in_u_two, u_two, copy_sems.at[1])
    load_one = pltpu.make_async_copy(in_u_one, u_any, copy_sems.at[2])
    save_point, save_two, save_one = [
        pltpu.make_async_copy(a, b, copy_sems.at[3 + i])
        for i, (a, b) in enumerate(((d_point, d_outs[0]), (d_two, d_outs[1]), (d_one, d_outs[2])))
    ]
    load_grad.start()
    load_two.start()
    sums = Sums(place, sources, targets, chunks, sum_refs)
    place.meet()
    sums.step()
    load_grad.wait()

    for m in range(MB):
        at = slice(m * pair, (m + 1) * pair)
        grad = grad_summed[at, :]
        back = dot_nn(grad.astype(bf16), w_point[...])
        xhat = (branch[at, :] - bn_three[m : m + 1, :]) * bn_three[MB + m : MB + m + 1, :]
        du = gelu_slope(xhat * gain_three[...] + shift_three[...]) * back
        du_three[at, :] = du
        local_three[m : m + 1, :] = jnp.sum(du, axis=0, keepdims=True)
        local_three[MB + m : MB + m + 1, :] = jnp.sum(du * xhat, axis=0, keepdims=True)
        for i in range(2):
            w = 2 * m + i
            edge_low[w] = du[i * length : i * length + EDGE]
            edge_high[w] = du[(i + 1) * length - EDGE : (i + 1) * length]
            row_low[w : w + 1, :] = grad[i * length : i * length + 1]
            row_high[w : w + 1, :] = grad[(i + 1) * length - 1 : (i + 1) * length]
        if m == 1:
            sums.step()

    moves = halo_copies(place, (edge_low, edge_high), (du_low, du_high), halo_sems.at[0])
    moves += halo_copies(place, (row_low, row_high), (gs_low, gs_high), halo_sems.at[1])
    place.halos(moves, 0)
    sums_three[...] = reduce_everywhere(
        place, local_three[...], *reduce_three[:2], reduce_three[2:], add_up, sums.step
    )
    d_point[...] = dot_tn(grad_summed[...].astype(bf16), act_three[...]).astype(bf16)
    save_point.start()
    place.halos(moves, 1)
    sums.step()

    for m in range(MB):
        at = slice(m * pair, (m + 1) * pair)
        centre, inverse = bn_three[m : m + 1, :], bn_three[MB + m : MB + m + 1, :]
        factor = gain_three[...] * inverse
        mean_du = sums_three[m : m + 1, :] * scale
        mean_dx = sums_three[MB + m : MB + m + 1, :] * scale

        def back(du, value):
            xhat = (value - centre) * inverse
            return factor * (du - mean_du - xhat * mean_dx)

        main = back(du_three[at, :], branch[at, :])
        grad_branch[at, :] = main.astype(bf16)
        pieces = []
        for i in range(2):
            w = 2 * m + i
            low = jnp.where(place.is_first, 0.0, back(du_low[w], branch_low[w]))
            high = jnp.where(place.is_last, 0.0, back(du_high[w], branch_high[w]))
            pieces += [low, main[i * length : (i + 1) * length], high]
        ext = jnp.concatenate(pieces, axis=0).astype(bf16)
        span = length + 2 * EDGE
        through = [dot_nt(ext, w_two[t * mid : (t + 1) * mid, :]) for t in range(taps)]
        centre_two, inverse_two = bn_two[m : m + 1, :], bn_two[MB + m : MB + m + 1, :]
        total_du = jnp.zeros((1, mid), f32)
        total_dx = jnp.zeros((1, mid), f32)
        for i in range(2):
            w = 2 * m + i
            grad = jnp.zeros((length, mid), f32)
            for t in range(taps):
                whole = through[t][i * span : (i + 1) * span]
                grad = grad + shifted_rows(whole, EDGE - (t - 1) * DILATION, length)
            xhat = (pooled[w].astype(f32) - centre_two) * inverse_two
            du = gelu_slope(xhat * gain_two[...] + shift_two[...]) * grad
            du_two[w] = du
            total_du = total_du + jnp.sum(du, axis=0, keepdims=True)
            total_dx = total_dx + jnp.sum(du * xhat, axis=0, keepdims=True)
            row_low_two[w : w + 1, :] = du[:1]
            row_high_two[w : w + 1, :] = du[length - 1 :]
        local_two[m : m + 1, :] = total_du
        local_two[MB + m : MB + m + 1, :] = total_dx
        sums.step()

    moves = halo_copies(
        place, (row_low_two, row_high_two), (dlow_two, dhigh_two), halo_sems.at[2]
    )
    place.halos(moves, 0)
    sums_two[...] = reduce_everywhere(
        place, local_two[...], *reduce_two[:2], reduce_two[2:], add_up, sums.step
    )
    load_two.wait()
    for t in range(taps):
        part = dot_tn(u_two[:, t * mid : (t + 1) * mid], grad_branch[...])
        d_two[:, t * small : (t + 1) * small] = part.astype(bf16)
    save_two.start()
    load_one.start()
    place.halos(moves, 1)
    sums.step()

    for m in range(MB):
        centre, inverse = bn_two[m : m + 1, :], bn_two[MB + m : MB + m + 1, :]
        factor = gain_two[...] * inverse
        mean_du = sums_two[m : m + 1, :] * scale
        mean_dx = sums_two[MB + m : MB + m + 1, :] * scale

        def back(du, value, extra):
            xhat = (value.astype(f32) - centre) * inverse
            return factor * (du - mean_du - xhat * mean_dx) + extra

        edges = []
        for i in range(2):
            w = 2 * m + i
            at = slice(w * length, (w + 1) * length)
            value = back(du_two[w], pooled[w], grad_summed[at, :]).astype(bf16)
            grad_ext[m, i * length : (i + 1) * length, :] = value
            grad_main[at, :] = value
            row = slice(w, w + 1)
            low = back(dlow_two[row, :], pooled_low[w].astype(f32)[EDGE - 1 :], gs_low[row, :])
            high = back(dhigh_two[row, :], pooled_high[w].astype(f32)[:1], gs_high[row, :])
            edges += [jnp.where(place.is_first, 0.0, low), jnp.where(place.is_last, 0.0, high)]
        row = lax.broadcasted_iota(jnp.int32, (EDGE, mid), 0)
        block = jnp.zeros((EDGE, mid), f32)
        for i, edge in enumerate(edges):
            block = jnp.where(row == i, edge, block)
        grad_ext[m, pair : pair + EDGE, :] = block.astype(bf16)
    sums.step()
    load_one.wait()
    columns = d_one.shape[1] // 5
    for t in range(5):
        part = slice(t * columns, (t + 1) * columns)
        d_one[:, part] = dot_tn(grad_main[...], u_any[:, part]).astype(bf16)
        if t in (1, 3):
            sums.step()
    save_one.start()
    bias_out[...] = reduce_everywhere(
        place, bias_sums[...], *reduce_b[:2], reduce_b[2:], add_up, sums.step
    )
    sums.finish()
    save_point.wait()
    save_two.wait()
    save_one.wait()


def back_high(shape, sources, grad_summed, u_one, u_two, three, bias_sums, two):
    branch = three[1]
    w_two, pooled = two[0], two[1]
    windows, length, mid = pooled.shape
    rows, small = branch.shape
    share = mid // shape[2]
    chunks, targets = [], []
    if sources:
        chunks, n_whole, n_plane = head_chunks(sources[0].shape[3])
        targets = [((share, n_whole), bf16), ((share // 2, n_plane), bf16)]
    taps = w_two.shape[0] // mid
    d_shapes = [((mid, small), bf16), ((mid, taps * small), bf16), ((mid, u_one.shape[1]), bf16)]
    outs = [
        ((MB, 2 * length + EDGE, mid), bf16),
        ((2 * MB, small), f32),
        ((2 * MB, mid), f32),
        (bias_sums.shape, f32),
    ]
    fixed = (
        reduce_scratch(shape, *bias_sums.shape)
        + reduce_scratch(shape, 2 * MB, small)
        + reduce_scratch(shape, 2 * MB, mid)
    )
    fixed += [
        pltpu.VMEM(*a)
        for a in [
            ((rows, mid), f32),
            (u_one.shape, bf16),
            ((rows, small), f32),
            ((windows, EDGE, small), f32),
            ((windows, EDGE, small), f32),
            ((windows, EDGE, small), f32),
            ((windows, EDGE, small), f32),
            ((windows, mid), f32),
            ((windows, mid), f32),
            ((windows, mid), f32),
            ((windows, mid), f32),
            ((2 * MB, small), f32),
            ((rows, small), bf16),
            ((windows, length, mid), f32),
            ((windows, mid), f32),
            ((windows, mid), f32),
            ((windows, mid), f32),
            ((windows, mid), f32),
            ((2 * MB, mid), f32),
            ((rows, mid), bf16),
            *d_shapes,
        ]
    ]
    fixed += [pltpu.SemaphoreType.DMA((3, 4)), pltpu.SemaphoreType.DMA((6,))]
    return pl.pallas_call(
        functools.partial(back_high_kernel, shape, len(sources), chunks),
        in_specs=[HBM] * (3 + len(sources)) + [VM] * 13,
        out_specs=[HBM] * (3 + len(sources)) + [VM] * 4,
        out_shape=[jax.ShapeDtypeStruct(*o) for o in targets + d_shapes + outs],
        scratch_shapes=fixed + sums_scratch(share, chunks),
        compiler_params=params(2),
        name="back_high",
    )(*sources, grad_summed, u_one, u_two, *three, bias_sums, *two)


def back_low_kernel(shape, n_sums, chunks, *refs):
    (sources, ins, targets, outs, reduce_one, fixed, sum_refs) = split_refs(
        refs, n_sums, 6, n_sums, 2, 6, 5, count_refs(chunks)
    )
    order, in_one, grad_ext, x2, bn_one, vectors = ins
    grad_input, sums_one = outs
    w_one, du_one, local, lanes_buffer, load_sem = fixed
    place = Place(shape)
    place.greet()
    windows, length, wide = x2.shape
    channels = wide // 2
    pair = 2 * length
    gain_one, shift_one = vectors.at[0:1, :wide], vectors.at[1:2, :wide]
    load_one = pltpu.make_async_copy(in_one, w_one, load_sem)
    load_one.start()
    sums = Sums(place, sources, targets, chunks, sum_refs)
    place.meet()
    sums.step()
    load_one.wait()

    for m in range(MB):
        through = [
            dot_nn(grad_ext[m], w_one[:, t * channels : (t + 1) * channels]) for t in range(5)
        ]
        centre, inverse = bn_one[m : m + 1, :], bn_one[MB + m : MB + m + 1, :]
        total_du = jnp.zeros((1, wide), f32)
        total_dx = jnp.zeros((1, wide), f32)
        row = lax.broadcasted_iota(jnp.int32, (length, channels), 0)
        top, bottom = row == 0, row == length - 1
        for i in range(2):
            w = 2 * m + i
            main = [t[i * length : (i + 1) * length] for t in through]
            low = [t[pair + 2 * i : pair + 2 * i + 1] for t in through]
            high = [t[pair + 2 * i + 1 : pair + 2 * i + 2] for t in through]
            later = lambda t: jnp.where(bottom, high[t], pltpu.roll(main[t], length - 1, axis=0))
            earlier = lambda t: jnp.where(top, low[t], pltpu.roll(main[t], 1, axis=0))
            mean = later(0) + main[2] + earlier(4)
            cross = main[1] + earlier(3)
            cross_end = high[1] + main[3][length - 1 :]
            cross_later = jnp.where(bottom, cross_end, pltpu.roll(cross, length - 1, axis=0))
            grad = jnp.concatenate([(mean + cross) * 0.5, (mean + cross_later) * 0.5], axis=1)
            xhat = (x2[w].astype(f32) - centre) * inverse
            du = gelu_slope(xhat * gain_one[...] + shift_one[...]) * grad
            du_one[w] = du
            total_du = total_du + jnp.sum(du, axis=0, keepdims=True)
            total_dx = total_dx + jnp.sum(du * xhat, axis=0, keepdims=True)
        local[m : m + 1, :] = total_du[:, :channels] + total_du[:, channels:]
        local[MB + m : MB + m + 1, :] = total_dx[:, :channels] + total_dx[:, channels:]
        sums.step()

    sums_one[...] = reduce_everywhere(
        place, local[...], *reduce_one[:2], reduce_one[2:], add_up, sums.step
    )
    scale = 1.0 / (4 * length * shape[0] * shape[1] * shape[2])
    lanes = lanes_buffer.shape[0]
    twice = lambda v: jnp.concatenate([v, v], axis=1)

    def write(window):
        w = 0
        for p in range(1, windows):
            w = jnp.where(order[p] == window, p, w)
        m = lax.div(w, 2)
        mean_du = twice(sums_one[pl.ds(m, 1), :]) * scale
        mean_dx = twice(sums_one[pl.ds(MB + m, 1), :]) * scale
        inverse = bn_one[pl.ds(MB + m, 1), :]
        xhat = (x2[w].astype(f32) - bn_one[pl.ds(m, 1), :]) * inverse
        grad = gain_one[...] * inverse * (du_one[w] - mean_du - xhat * mean_dx)
        for odd in range(2):
            for c in range(lanes):
                at = odd * channels + c * LANES
                lanes_buffer[c, pl.ds(odd, length, 2), :] = grad[:, at : at + LANES]
        for c in range(lanes):
            grad_input[window, :, c * LANES : (c + 1) * LANES] = lanes_buffer[c].astype(bf16)

    for half in range(2):
        sums.step()

        @pl.loop(half * windows // 2, (half + 1) * windows // 2)
        def _(window):
            write(window)

    sums.finish()


def back_low(shape, sources, order, w_one, grad_ext, x2, bn_one, vectors):
    windows, length, wide = x2.shape
    channels = wide // 2
    share = grad_ext.shape[2] // shape[2]
    chunks, targets = [], []
    if sources:
        columns = sources[0].shape[1]
        size = BLOCK // 2
        chunks = [(ALONG, i, 0, i * size, size, 0, i * size) for i in range(columns // size)]
        targets = [((share, columns), bf16)]
        begin = 0
        for i, taps in enumerate((1, 3, w_one.shape[1] // channels), 1):
            width = sources[i].shape[3] // taps
            chunks += [(WHOLE, begin + t, i, t * width, width, i, t) for t in range(taps)]
            targets.append(((taps, share, width), bf16))
            begin += taps
    outs = [((windows, 2 * length, channels), bf16), ((2 * MB, channels), f32)]
    scratch = reduce_scratch(shape, 2 * MB, channels)
    scratch += [
        pltpu.VMEM(w_one.shape, bf16),
        pltpu.VMEM((windows, length, wide), f32),
        pltpu.VMEM((2 * MB, channels), f32),
        pltpu.VMEM((channels // LANES, 2 * length, LANES), f32),
        pltpu.SemaphoreType.DMA,
    ]
    smem = pl.BlockSpec(memory_space=pltpu.SMEM)
    return pl.pallas_call(
        functools.partial(back_low_kernel, shape, len(sources), chunks),
        in_specs=[HBM] * len(sources) + [smem, HBM] + [VM] * 4,
        out_specs=[HBM] * len(sources) + [VM] * 2,
        out_shape=[jax.ShapeDtypeStruct(*o) for o in targets + outs],
        scratch_shapes=scratch + sums_scratch(share, chunks),
        compiler_params=params(3),
        name="back_low",
    )(*sources, order, w_one, grad_ext, x2, bn_one, vectors)


def per_device(
    shape,
    tracks,
    species,
    batch_order,
    conv_one,
    dilated_kernel,
    point_wise,
    head_human,
    head_mouse,
    bias_human,
    bias_mouse,
    gain_one,
    shift_one,
    gain_two,
    shift_two,
    gain_three,
    shift_three,
    cotangent,
):
    sec = lax.axis_index("section").astype(jnp.int32)
    windows, seq_bins, channels = tracks.shape
    half = seq_bins // 2
    length = half // 2
    human_tracks, mouse_tracks = head_human.shape[1], head_mouse.shape[1]
    human_wide = -(-human_tracks // BLOCK) * BLOCK
    share = conv_one.shape[2]
    mid = share * shape[2]

    taps_one = conv_one.shape[0]
    shard_one = jnp.transpose(conv_one, (2, 0, 1)).reshape(share, taps_one * channels)
    shard_point = point_wise.T
    shard_heads = jnp.concatenate(
        [
            jnp.pad(head_human, ((0, 0), (0, human_wide - human_tracks))),
            jnp.pad(head_mouse, ((0, 0), (0, BLOCK - mouse_tracks))),
        ],
        axis=1,
    )
    half_rows = share // shape[0]
    half_heads = lax.dynamic_slice_in_dim(shard_heads, sec * half_rows, half_rows, 0)
    w_heads = lax.all_gather(half_heads, ("dp", "section"), axis=0, tiled=True)
    weights = [shard_one, dilated_kernel, shard_point]
    if shape != (2, 4, 4):
        weights = [lax.all_gather(w, "dp", axis=w.ndim - 2, tiled=True) for w in weights]

    wide = 2 * channels
    vectors = jnp.stack(
        [
            jnp.pad(v, (0, wide - v.shape[0]))
            for v in (
                jnp.tile(gain_one, 2),
                jnp.tile(shift_one, 2),
                gain_two,
                shift_two,
                gain_three,
                shift_three,
            )
        ]
    )
    native = jnp.transpose(cotangent, (2, 0, 1))
    relay = [native] if length % LANES == 0 else []
    (
        u_one,
        u_two,
        pooled,
        pooled_low,
        pooled_high,
        branch,
        branch_low,
        branch_high,
        act_three,
        summed,
        bn_one,
        bn_two,
        bn_three,
        w_one,
        w_two,
        w_point,
        x2,
        *cot,
    ) = forward(shape, mid, batch_order, tracks, vectors, *weights, relay)
    if not cot:
        half_cot = lax.dynamic_slice_in_dim(cotangent, sec * length, length, 1)
        cot = [jnp.pad(half_cot, ((0, 0), (0, 0), (0, human_wide - human_tracks)))]
    w_two = w_two.reshape(-1, w_two.shape[2])

    wide_bias = jnp.concatenate(
        [
            jnp.pad(bias_human, (0, human_wide - human_tracks)),
            jnp.pad(bias_mouse, (0, BLOCK - mouse_tracks)),
        ]
    ).reshape(1, -1)
    predicted, grad_summed, d_human, d_mouse, bias_sums = heads(
        species, batch_order, summed, w_heads, wide_bias, cot[0], human_tracks, mouse_tracks
    )


    def in_kernel(*grads):
        if shape != (2, 4, 4):
            return []
        return [g.reshape(2, 2, -1, g.shape[1]) for g in grads]

    def summed_up(*grads):
        parts = [lax.psum_scatter(g, "dp", scatter_dimension=0, tiled=True) for g in grads]
        return [lax.psum(part, ("section", "seq")) for part in parts]

    def by_tap(grad, taps):
        grad = grad.astype(f32)
        if grad.ndim == 2:
            grad = jnp.transpose(grad.reshape(share, taps, -1), (1, 0, 2))
        return grad

    *heads_summed, d_point, d_two, d_one, grad_ext, sums_three, sums_two, bias_out = back_high(
        shape,
        in_kernel(d_human, d_mouse),
        grad_summed,
        u_one,
        u_two,
        (act_three, branch, branch_low, branch_high, bn_three, w_point),
        bias_sums,
        (w_two, pooled, pooled_low, pooled_high, bn_two, vectors),
    )
    *sums_low, grad_input, sums_one = back_low(
        shape,
        heads_summed[1:] + in_kernel(d_point, d_two, d_one),
        batch_order,
        w_one,
        grad_ext,
        x2,
        bn_one,
        vectors,
    )
    if sums_low:
        rest, r_point, r_two, r_one = sums_low
        all_heads = jnp.concatenate([heads_summed[0], rest], axis=1)
        r_human, r_mouse = all_heads[:, :human_wide], all_heads[:, human_wide:]
    else:
        r_human, r_mouse, r_point, r_two, r_one = summed_up(d_human, d_mouse, d_point, d_two, d_one)
    r_human = r_human[:, :human_tracks].astype(f32)
    r_mouse = r_mouse[:, :mouse_tracks].astype(f32)
    r_point = by_tap(r_point, 1)[0]
    r_two = by_tap(r_two, dilated_kernel.shape[0])
    r_one = by_tap(r_one, taps_one)
    r_point = r_point.T
    r_one = jnp.transpose(r_one, (0, 2, 1))
    bias_human_grad = bias_out[: human_wide // BLOCK].reshape(-1)[:human_tracks]
    bias_mouse_grad = bias_out[human_wide // BLOCK, :mouse_tracks]
    return (
        predicted,
        grad_input,
        r_one,
        r_two,
        r_point,
        r_human,
        r_mouse,
        bias_human_grad,
        bias_mouse_grad,
        jnp.sum(sums_one[MB:], axis=0),
        jnp.sum(sums_one[:MB], axis=0),
        jnp.sum(sums_two[MB:], axis=0),
        jnp.sum(sums_two[:MB], axis=0),
        jnp.sum(sums_three[MB:], axis=0),
        jnp.sum(sums_three[:MB], axis=0),
    )


def solution(mesh):
    shape = (mesh.shape["section"], mesh.shape["seq"], mesh.shape["dp"])
    placed = (
        P("dp", "seq", None),
        P("dp"),
        P(),
        P(None, None, "dp"),
        P(None, "dp", None),
        P(None, "dp"),
        P("dp", None),
        P("dp", None),
    ) + (P(),) * 8 + (P("dp", "seq", None),)
    return jax.shard_map(
        functools.partial(per_device, shape),
        mesh=mesh,
        in_specs=placed,
        out_specs=(
            P("dp", ("seq", "section"), None),
            P("dp", ("seq", "section"), None),
            P(None, None, "dp"),
            P(None, "dp", None),
            P(None, "dp"),
            P("dp", None),
            P("dp", None),
        )
        + (P(),) * 8,
        check_vma=False,
    )
```

```python
import functools
import math

import jax
import jax.numpy as jnp
from jax import lax
from jax.experimental import pallas as pl
from jax.experimental.pallas import tpu as pltpu
from jax.sharding import PartitionSpec as P

MESH = pl.DeviceIdType.MESH
DILATION = 11
MB = 4
EPS = 1e-05
EDGE = 16
BLOCK = 1792
SPLIT = 512
LANES = 128
VMEM_LIMIT = 60 * 1024 * 1024
GELU_K = math.sqrt(2.0 / math.pi)
GELU_C = 0.044715
f32 = jnp.float32
bf16 = jnp.bfloat16
VM = pl.BlockSpec(memory_space=pltpu.VMEM)
HBM = pl.BlockSpec(memory_space=pl.ANY)


def params(collective_id=None, limit=VMEM_LIMIT):
    if collective_id is None:
        return pltpu.CompilerParams(vmem_limit_bytes=limit)
    return pltpu.CompilerParams(
        vmem_limit_bytes=limit, collective_id=collective_id, has_side_effects=True
    )


def gelu(u):
    t = jnp.tanh(u * (GELU_K + (GELU_K * GELU_C) * (u * u)))
    h = 0.5 * u
    return h + h * t


def gelu_slope(u):
    uu = u * u
    t = jnp.tanh(u * (GELU_K + (GELU_K * GELU_C) * uu))
    return 0.5 * (1.0 + t) + (0.5 * u) * (1.0 - t * t) * (GELU_K + (3.0 * GELU_K * GELU_C) * uu)


def dot_nn(a, b):
    return jnp.dot(a, b, preferred_element_type=f32)


def dot_nt(a, b):
    return lax.dot_general(a, b, (((1,), (1,)), ((), ())), preferred_element_type=f32)


def dot_tn(a, b):
    return lax.dot_general(a, b, (((0,), (0,)), ((), ())), preferred_element_type=f32)


class Place:
    def __init__(self, shape):
        self.n_sec, self.n_seq, self.n_dp = shape
        self.n_near = self.n_sec * self.n_dp
        self.sec = lax.axis_index("section")
        self.seq = lax.axis_index("seq")
        self.dp = lax.axis_index("dp")
        self.near = self.sec * self.n_dp + self.dp
        n_bins = self.n_seq * self.n_sec
        bins = self.seq * self.n_sec + self.sec
        self.is_first = bins == 0
        self.is_last = bins == n_bins - 1
        low = lax.rem(bins + n_bins - 1, n_bins)
        high = lax.rem(bins + 1, n_bins)
        self.low = self.bin_device(low)
        self.high = self.bin_device(high)
        across = jnp.where(self.sec == 0, low, high)
        self.across = self.bin_device(across)

    def halos(self, moves, action):
        for up, down in zip(moves[::2], moves[1::2]):
            if action == 0:
                pl.when(jnp.logical_not(self.is_last))(up.start)
                pl.when(jnp.logical_not(self.is_first))(down.start)
            else:
                for first, last in ((up.wait_send, up.wait_recv), (down.wait_recv, down.wait_send)):
                    pl.when(jnp.logical_not(self.is_last))(first)
                    pl.when(jnp.logical_not(self.is_first))(last)

    def bin_device(self, bins):
        return (lax.rem(bins, self.n_sec), lax.div(bins, self.n_sec), self.dp)

    def near_device(self, rank):
        return (lax.div(rank, self.n_dp), self.seq, lax.rem(rank, self.n_dp))

    def greet(self):
        barrier = pltpu.get_barrier_semaphore()
        for k in range(1, self.n_near):
            rank = lax.rem(self.near + k, self.n_near)
            pl.semaphore_signal(
                barrier, inc=1, device_id=self.near_device(rank), device_id_type=MESH
            )
        for k in range(1, self.n_seq):
            seq = lax.rem(self.seq + k, self.n_seq)
            pl.semaphore_signal(
                barrier, inc=1, device_id=(self.sec, seq, self.dp), device_id_type=MESH
            )
        pl.semaphore_signal(barrier, inc=1, device_id=self.across, device_id_type=MESH)

    def meet(self):
        pl.semaphore_wait(pltpu.get_barrier_semaphore(), self.n_near + self.n_seq - 1)


def halo_copies(place, from_self, arrived, sems):
    up = pltpu.make_async_remote_copy(
        src_ref=from_self[1],
        dst_ref=arrived[0],
        send_sem=sems.at[0],
        recv_sem=sems.at[1],
        device_id=place.high,
        device_id_type=MESH,
    )
    down = pltpu.make_async_remote_copy(
        src_ref=from_self[0],
        dst_ref=arrived[1],
        send_sem=sems.at[2],
        recv_sem=sems.at[3],
        device_id=place.low,
        device_id_type=MESH,
    )
    return up, down


def nothing():
    pass


def spread_round(buffer, mine, count, device_of, send, recv, meanwhile=nothing):
    copies = []
    for k in range(1, count):
        rank = lax.rem(mine + k, count)
        copy = pltpu.make_async_remote_copy(
            src_ref=buffer.at[mine],
            dst_ref=buffer.at[mine],
            send_sem=send.at[k],
            recv_sem=recv.at[mine],
            device_id=device_of(rank),
            device_id_type=MESH,
        )
        copy.start()
        copies.append((rank, copy))
    meanwhile()
    for rank, copy in copies:
        pltpu.make_async_remote_copy(
            src_ref=buffer.at[rank],
            dst_ref=buffer.at[rank],
            send_sem=send.at[0],
            recv_sem=recv.at[rank],
            device_id=device_of(rank),
            device_id_type=MESH,
        ).wait_recv()
    for rank, copy in copies:
        copy.wait_send()


def reduce_everywhere(
    place, value, near_buf, far_buf, sems, combine, meanwhile=nothing, then=None
):
    then = meanwhile if then is None else then
    near_send, near_recv, far_send, far_recv = sems
    far_buf[place.seq] = value
    spread_round(
        far_buf,
        place.seq,
        place.n_seq,
        lambda seq: (place.sec, seq, place.dp),
        far_send,
        far_recv,
        meanwhile,
    )
    near_buf[place.near] = combine(far_buf, place.n_seq, 1)
    spread_round(
        near_buf, place.near, place.n_near, place.near_device, near_send, near_recv, then
    )
    return combine(near_buf, place.n_near, place.n_seq)


def add_up(buffer, count, weight):
    total = buffer[0]
    for i in range(1, count):
        total = total + buffer[i]
    return total


def merge_stats(rows, buffer, count, weight):
    means = [buffer[i][:MB] for i in range(count)]
    centre = means[0]
    spread = buffer[0][MB:]
    for i in range(1, count):
        centre = centre + means[i]
        spread = spread + buffer[i][MB:]
    centre = centre * (1.0 / count)
    apart = jnp.square(means[0] - centre)
    for i in range(1, count):
        apart = apart + jnp.square(means[i] - centre)
    return jnp.concatenate([centre, spread + apart * float(rows * weight)], axis=0)


def reduce_scratch(shape, rows, columns):
    n_sec, n_seq, n_dp = shape
    near = n_sec * n_dp
    return [
        pltpu.VMEM((near, rows, columns), f32),
        pltpu.VMEM((n_seq, rows, columns), f32),
        pltpu.SemaphoreType.DMA((near,)),
        pltpu.SemaphoreType.DMA((near,)),
        pltpu.SemaphoreType.DMA((n_seq,)),
        pltpu.SemaphoreType.DMA((n_seq,)),
    ]


def local_stats(value):
    count = value.shape[0]
    centre = jnp.sum(value, axis=0, keepdims=True) * (1.0 / count)
    return centre, jnp.sum(jnp.square(value - centre), axis=0, keepdims=True)


def finish_stats(stats, total):
    return jnp.concatenate(
        [stats[:MB], lax.rsqrt(stats[MB:] * (1.0 / total) + EPS)], axis=0
    )


def prepare(place, order, tracks, pairs, low, high, stats, scratch):
    lanes, half, _ = scratch.shape
    start = pl.multiple_of(place.sec * half, half)

    @pl.loop(0, MB)
    def _(m):
        values = []
        for i in range(2):
            value = tracks[order[2 * m + i], pl.ds(start, half), :].astype(f32)
            values.append(value)
            for c in range(lanes):
                scratch[c] = value[:, c * LANES : (c + 1) * LANES]
            both = jnp.concatenate(
                [scratch[c, pl.ds(odd, half // 2, 2), :] for odd in range(2) for c in range(lanes)],
                axis=1,
            )
            pairs[2 * m + i] = both.astype(bf16)
            low[pl.ds(2 * m + i, 1), :] = both[:1]
            high[pl.ds(2 * m + i, 1), :] = both[half // 2 - 1 :]
        count = 2 * half
        centre = (
            jnp.sum(values[0], axis=0, keepdims=True) + jnp.sum(values[1], axis=0, keepdims=True)
        ) * (1.0 / count)
        spread = jnp.sum(jnp.square(values[0] - centre), axis=0, keepdims=True) + jnp.sum(
            jnp.square(values[1] - centre), axis=0, keepdims=True
        )
        stats[pl.ds(m, 1), :] = centre
        stats[pl.ds(MB + m, 1), :] = spread


class Gathering:
    STAGES = 5

    def __init__(self, place, shard, full, rows_at, sems):
        self.place, self.shard, self.full, self.rows_at, self.sems = place, shard, full, rows_at, sems
        p = place
        x, y, z = lax.rem(p.dp, 2), lax.div(p.dp, 2), lax.rem(p.seq, 2)
        self.share = full.shape[rows_at] // p.n_dp
        self.group = self.share // 6
        g = self.group
        self.dp_x, self.dp_y = p.dp + 1 - 2 * x, p.dp + 2 - 4 * y
        self.dp_xy = 3 - p.dp
        self.sibling = (1 - p.sec, p.seq, p.dp)
        self.over_x, self.over_y = (p.sec, p.seq, self.dp_x), (p.sec, p.seq, self.dp_y)
        self.over_z = (p.sec, p.seq + 1 - 2 * z, p.dp)
        base = p.sec * 3 * g
        self.near, self.middle, self.edge, self.far, self.half = (
            (base + z * g, 2 * g),
            (base + g, g),
            (base + 2 * z * g, g),
            (base + 2 * (1 - z) * g, g),
            (base, 3 * g),
        )

    def at(self, ref, dp, span):
        start, rows = span
        index = pl.ds(pl.multiple_of(dp * self.share + start, self.group), rows)
        return ref.at[:, index] if self.rows_at else ref.at[index]

    def remote(self, dp, span, sem, device, source=None):
        source = self.at(self.full, dp, span) if source is None else source
        return pltpu.make_async_remote_copy(
            src_ref=source,
            dst_ref=self.at(self.full, dp, span),
            send_sem=self.sems.at[2 * sem],
            recv_sem=self.sems.at[2 * sem + 1],
            device_id=device,
            device_id_type=MESH,
        )

    def own_copy(self):
        target = self.at(self.full, self.place.dp, (0, self.share))
        return pltpu.make_async_copy(self.shard, target, self.sems.at[26])

    def copies(self, stage):
        me = self.place.dp
        if stage == 0:
            own = None if self.shard is None else self.at(self.shard, 0, self.near)
            return [
                self.remote(me, self.near, 0, self.over_x, own),
                self.remote(me, self.near, 1, self.over_y, own),
            ]
        if stage == 1:
            return [
                self.remote(self.dp_x, self.middle, 2, self.over_y),
                self.remote(self.dp_y, self.edge, 3, self.over_x),
                self.remote(self.dp_x, self.edge, 4, self.over_z),
                self.remote(self.dp_y, self.edge, 5, self.over_z),
                self.remote(self.dp_x, self.near, 6, self.sibling),
                self.remote(self.dp_y, self.near, 7, self.sibling),
            ]
        if stage == 2:
            return [
                self.remote(self.dp_xy, self.edge, 8, self.over_z),
                self.remote(self.dp_xy, self.near, 9, self.sibling),
            ]
        if stage == 3:
            return [
                self.remote(self.dp_x, self.far, 10, self.sibling),
                self.remote(self.dp_y, self.far, 11, self.sibling),
                self.remote(self.dp_xy, self.far, 12, self.sibling),
            ]
        return []

    def start(self, stage):
        for copy in self.copies(stage):
            copy.start()

    def arrived(self, stage, which, dp, span):
        copy = self.copies(stage)[which]
        pltpu.make_async_remote_copy(
            src_ref=self.at(self.full, dp, span),
            dst_ref=self.at(self.full, dp, span),
            send_sem=self.sems.at[0],
            recv_sem=self.sems.at[2 * {0: 0, 1: 2, 2: 8, 3: 10}[stage] + 2 * which + 1],
            device_id=self.sibling,
            device_id_type=MESH,
        ).wait_recv()

    def advance(self, stage):
        if stage == 0:
            if self.shard is not None:
                self.own_copy().start()
        elif stage == 1:
            self.arrived(0, 0, self.dp_x, self.near)
            self.arrived(0, 1, self.dp_y, self.near)
        elif stage == 2:
            self.arrived(1, 0, self.dp_xy, self.middle)
            self.arrived(1, 1, self.dp_xy, self.edge)
        elif stage == 3:
            self.arrived(1, 2, self.dp_x, self.far)
            self.arrived(1, 3, self.dp_y, self.far)
            self.arrived(2, 0, self.dp_xy, self.far)
        if stage < 4:
            self.start(stage)
            return
        base = (1 - self.place.sec) * 3 * self.group
        z = lax.rem(self.place.seq, 2)
        near = (base + z * self.group, 2 * self.group)
        far = (base + 2 * (1 - z) * self.group, self.group)
        self.arrived(1, 4, self.dp_x, near)
        self.arrived(1, 5, self.dp_y, near)
        self.arrived(2, 1, self.dp_xy, near)
        self.arrived(3, 0, self.dp_x, far)
        self.arrived(3, 1, self.dp_y, far)
        self.arrived(3, 2, self.dp_xy, far)
        if self.shard is not None:
            self.own_copy().wait()
        for stage in range(4):
            for copy in self.copies(stage):
                copy.wait_send()


class Relay:
    TRACKS = 512

    def __init__(self, source, target, first_bin, refs):
        self.source, self.target, self.first = source, target, first_bin
        self.got, self.rows, self.made, self.sems = refs
        self.length = target.shape[1]
        self.count = -(-source.shape[0] // self.TRACKS)
        self.at = 0

    def width(self, i):
        return min(self.TRACKS, self.source.shape[0] - i * self.TRACKS)

    def load(self, i):
        width = self.width(i)
        bins = pl.ds(pl.multiple_of(self.first, self.length), self.length)
        return pltpu.make_async_copy(
            self.source.at[pl.ds(i * self.TRACKS, width), :, bins],
            self.got.at[i % 2, pl.ds(0, width)],
            self.sems.at[i % 2],
        )

    def store(self, i):
        width = min(self.TRACKS, self.target.shape[2] - i * self.TRACKS)
        return pltpu.make_async_copy(
            self.made.at[i % 2, :, :, pl.ds(0, width)],
            self.target.at[:, :, pl.ds(i * self.TRACKS, width)],
            self.sems.at[2 + i % 2],
        )

    def begin(self):
        self.load(0).start()

    def step(self):
        i = self.at
        if i == self.count:
            return
        self.at += 1
        slot, width = i % 2, self.width(i)
        windows = self.got.shape[2]
        self.load(i).wait()
        if i + 1 < self.count:
            self.load(i + 1).start()
        if i > 1:
            self.store(i - 2).wait()
        if width < self.TRACKS:
            self.got[slot, width:] = jnp.zeros((self.TRACKS - width, *self.got.shape[2:]), bf16)
        value = self.got[slot].astype(f32)
        self.rows[...] = value.reshape(self.TRACKS * windows, self.length)
        for w in range(windows):
            self.made[slot, w] = self.rows[pl.ds(w, self.TRACKS, windows), :].astype(bf16).T
        self.store(i).start()

    def finish(self):
        while self.at < self.count:
            self.step()
        for i in range(max(0, self.count - 2), self.count):
            self.store(i).wait()

    @staticmethod
    def scratch(windows, length):
        tracks = Relay.TRACKS
        return [
            pltpu.VMEM((2, tracks, windows, length), bf16),
            pltpu.VMEM((tracks * windows, length), f32),
            pltpu.VMEM((2, windows, length, tracks), bf16),
            pltpu.SemaphoreType.DMA((4,)),
        ]


def shifted_rows(value, offset, length):
    rows = value.shape[0]
    if offset:
        value = pltpu.roll(value, rows - offset, axis=0)
    return value[:length]


def forward_kernel(shape, n_relay, *refs):
    (
        order,
        tracks,
        vectors,
        in_one,
        in_two,
        in_point,
    ) = refs[:6]
    refs = refs[6:]
    in_cot, refs = refs[:n_relay], refs[n_relay:]
    (
        out_u_one,
        out_u_two,
        pooled,
        pooled_low,
        pooled_high,
        branch,
        branch_low,
        branch_high,
        act_three,
        summed,
        bn_one,
        bn_two,
        bn_three,
        out_one,
        out_two,
        out_point,
        x2,
    ) = refs[:17]
    refs = refs[17:]
    out_cot, refs = refs[:n_relay], refs[n_relay:]
    (
        near_one,
        far_one,
        s10,
        s11,
        s12,
        s13,
        near_two,
        far_two,
        s20,
        s21,
        s22,
        s23,
        near_three,
        far_three,
        s30,
        s31,
        s32,
        s33,
        got_low,
        got_high,
        stats_two,
        stats_three,
        halo_sems,
        s_branch_edge_low,
        s_branch_edge_high,
        u_one,
        u_two,
        w_one,
        w_two,
        w_point,
        weight_sems,
        save_sems,
        edge_low,
        edge_high,
        stats_in,
        lanes_buffer,
    ) = refs[:36]
    relay_refs = refs[36:]
    place = Place(shape)
    place.greet()
    windows, length, wide = x2.shape
    channels = wide // 2
    mid = pooled.shape[2]
    small = branch.shape[1]
    parts = shape[0] * shape[1] * shape[2]
    pair = 2 * length
    saves = [
        pltpu.make_async_copy(source, target, save_sems.at[i])
        for i, (source, target) in enumerate(
            ((u_one, out_u_one), (u_two, out_u_two), (w_one, out_one), (w_two, out_two), (w_point, out_point))
        )
    ]
    gathers = []
    own_taps = []
    if len(in_one.shape) == 3:
        taps, share, columns = in_one.shape
        own_rows = pl.ds(pl.multiple_of(place.dp * share, share), share)
        own_taps = [
            pltpu.make_async_copy(
                in_one.at[t],
                w_one.at[own_rows, pl.ds(t * columns, columns)],
                weight_sems.at[0, 27 + t],
            )
            for t in range(taps)
        ]
        for tap in own_taps:
            tap.start()
        columns = w_one.shape[1]
        first = columns // (2 * LANES) * LANES
        pieces = [
            (None, w_one.at[:, part], 0)
            for part in (pl.ds(0, first), pl.ds(first, columns - first))
        ]
        pieces += [(in_two, w_two, 1), (in_point, w_point, 0)]
        gathers = [
            Gathering(place, *piece, weight_sems.at[i]) for i, piece in enumerate(pieces)
        ]
    else:
        loads = [
            pltpu.make_async_copy(source, target, weight_sems.at[i, 0])
            for i, (source, target) in enumerate(
                ((in_one, w_one), (in_two, w_two), (in_point, w_point))
            )
        ]
        for load in loads:
            load.start()
        for load in loads:
            load.wait()

    def advance(*steps):
        for index, stage in steps:
            if index < len(gathers):
                gathers[index].advance(stage)

    mid_rows = lambda index, width: vectors.at[index : index + 1, :width]
    gain_one, shift_one = mid_rows(0, wide), mid_rows(1, wide)
    gain_two, shift_two = mid_rows(2, mid), mid_rows(3, mid)
    gain_three, shift_three = mid_rows(4, small), mid_rows(5, small)
    relay = None
    if n_relay:
        relay = Relay(in_cot[0], out_cot[0], place.sec * length, relay_refs)
        relay.begin()

    def fill(count=1):
        for _ in range(count if relay else 0):
            relay.step()

    prepare(place, order, tracks, x2, edge_low, edge_high, stats_in, lanes_buffer)
    for tap in own_taps:
        tap.wait()
    place.meet()
    advance((0, 0), (1, 0))
    up, down = halo_copies(place, (edge_low, edge_high), (got_low, got_high), halo_sems.at[0])
    place.halos((up, down), 0)
    stats = reduce_everywhere(
        place,
        stats_in[...],
        near_one,
        far_one,
        (s10, s11, s12, s13),
        functools.partial(merge_stats, 4 * length),
        fill,
        lambda: advance((0, 1)),
    )
    stats = finish_stats(stats, 4 * length * parts)
    bn_one[...] = jnp.concatenate([stats, stats], axis=1)
    place.halos((up, down), 1)
    advance((1, 1), (0, 2), (2, 0), (3, 0))

    @pl.loop(0, windows)
    def _(w):
        m = lax.div(w, 2)
        centre = bn_one[pl.ds(m, 1), :]
        scale = bn_one[pl.ds(MB + m, 1), :] * gain_one[...]
        move = shift_one[...]

        def act(value):
            return gelu((value - centre) * scale + move).astype(bf16).astype(f32)

        main = act(x2[w].astype(f32))
        before = jnp.where(place.is_first, 0.0, act(got_low[pl.ds(w, 1), :]))
        after = jnp.where(place.is_last, 0.0, act(got_high[pl.ds(w, 1), :]))
        even, odd = main[:, :channels], main[:, channels:]
        mean = (even + odd) * 0.5
        mean_before = (before[:, :channels] + before[:, channels:]) * 0.5
        mean_after = (after[:, :channels] + after[:, channels:]) * 0.5
        row = lax.broadcasted_iota(jnp.int32, (length, channels), 0)
        top, bottom = row == 0, row == length - 1
        odd_before = jnp.where(top, before[:, channels:], pltpu.roll(odd, 1, axis=0))
        cross = (odd_before + even) * 0.5
        cross_after = (odd[length - 1 :] + after[:, :channels]) * 0.5
        start = pl.multiple_of(w * length, length)
        taps = (
            jnp.where(top, mean_before, pltpu.roll(mean, 1, axis=0)),
            cross,
            mean,
            jnp.where(bottom, cross_after, pltpu.roll(cross, length - 1, axis=0)),
            jnp.where(bottom, mean_after, pltpu.roll(mean, length - 1, axis=0)),
        )
        for t, tap in enumerate(taps):
            u_one[pl.ds(start, length), t * channels : (t + 1) * channels] = tap.astype(bf16)

    saves[0].start()
    advance((1, 2), (0, 3))
    fill(2)
    advance((1, 3), (0, 4))
    fill()
    advance((1, 4), (2, 1), (3, 1))
    saves[2].start()

    @pl.loop(0, MB)
    def _(m):
        start = pl.multiple_of(m * pair, pair)
        value = dot_nt(u_one[pl.ds(start, pair), :], w_one[...]).astype(bf16)
        pooled[pl.ds(2 * m, 2)] = value.reshape(2, length, mid)
        centre, spread = local_stats(value.astype(f32))
        stats_two[pl.ds(m, 1), :] = centre
        stats_two[pl.ds(MB + m, 1), :] = spread

    advance((2, 2), (3, 2))
    up, down = halo_copies(
        place,
        (pooled.at[:, pl.ds(0, EDGE), :], pooled.at[:, pl.ds(length - EDGE, EDGE), :]),
        (pooled_low, pooled_high),
        halo_sems.at[1],
    )
    place.halos((up, down), 0)
    stats = reduce_everywhere(
        place,
        stats_two[...],
        near_two,
        far_two,
        (s20, s21, s22, s23),
        functools.partial(merge_stats, pair),
        fill,
    )
    bn_two[...] = finish_stats(stats, pair * parts)
    place.halos((up, down), 1)
    advance((2, 3), (3, 3))

    @pl.loop(0, windows)
    def _(w):
        m = lax.div(w, 2)
        centre = bn_two[pl.ds(m, 1), :]
        scale = bn_two[pl.ds(MB + m, 1), :] * gain_two[...]
        move = shift_two[...]

        def act(value):
            return gelu((value.astype(f32) - centre) * scale + move)

        ext = jnp.concatenate(
            [
                jnp.where(place.is_first, 0.0, act(pooled_low[w])),
                act(pooled[w]),
                jnp.where(place.is_last, 0.0, act(pooled_high[w])),
            ],
            axis=0,
        )
        start = pl.multiple_of(w * length, length)
        for t in range(3):
            tap = shifted_rows(ext, EDGE + (t - 1) * DILATION, length)
            u_two[pl.ds(start, length), t * mid : (t + 1) * mid] = tap.astype(bf16)

    saves[1].start()
    advance((2, 4), (3, 4))
    saves[3].start()
    saves[4].start()

    @pl.loop(0, MB)
    def _(m):
        start = pl.multiple_of(m * pair, pair)
        value = jnp.zeros((pair, small), f32)
        for t in range(w_two.shape[0]):
            value = value + dot_nn(
                u_two[pl.ds(start, pair), t * mid : (t + 1) * mid], w_two[t]
            )
        branch[pl.ds(start, pair), :] = value
        centre, spread = local_stats(value)
        stats_three[pl.ds(m, 1), :] = centre
        stats_three[pl.ds(MB + m, 1), :] = spread
        for i in range(2):
            s_branch_edge_low[2 * m + i] = value[i * length : i * length + EDGE]
            s_branch_edge_high[2 * m + i] = value[(i + 1) * length - EDGE : (i + 1) * length]

    up, down = halo_copies(
        place,
        (s_branch_edge_low, s_branch_edge_high),
        (branch_low, branch_high),
        halo_sems.at[2],
    )
    place.halos((up, down), 0)
    stats = reduce_everywhere(
        place,
        stats_three[...],
        near_three,
        far_three,
        (s30, s31, s32, s33),
        functools.partial(merge_stats, pair),
        fill,
    )
    bn_three[...] = finish_stats(stats, pair * parts)

    @pl.loop(0, MB)
    def _(m):
        centre = bn_three[pl.ds(m, 1), :]
        scale = bn_three[pl.ds(MB + m, 1), :] * gain_three[...]
        start = pl.multiple_of(m * pair, pair)
        act = gelu((branch[pl.ds(start, pair), :] - centre) * scale + shift_three[...])
        act = act.astype(bf16)
        act_three[pl.ds(start, pair), :] = act
        lifted = dot_nt(act, w_point[...])
        here = pooled[pl.ds(2 * m, 2)].reshape(pair, mid).astype(f32)
        summed[pl.ds(start, pair), :] = (here + lifted).astype(bf16)

    place.halos((up, down), 1)
    if relay:
        relay.finish()
    for save in saves:
        save.wait()


def forward(shape, mid, order, tracks, vectors, w_one, w_two, w_point, cot):
    windows, seq_bins, channels = tracks.shape
    half = seq_bins // shape[0]
    length, wide = half // 2, 2 * channels
    rows = windows * length
    taps_two, _, small = w_two.shape
    big = [
        ((mid, w_one.shape[-1] * (w_one.shape[0] if w_one.ndim == 3 else 1)), bf16),
        ((taps_two, mid, small), bf16),
        ((mid, small), bf16),
    ]
    out = [
        ((rows, big[0][0][1]), bf16),
        ((rows, taps_two * mid), bf16),
        ((windows, length, mid), bf16),
        ((windows, EDGE, mid), bf16),
        ((windows, EDGE, mid), bf16),
        ((rows, small), f32),
        ((windows, EDGE, small), f32),
        ((windows, EDGE, small), f32),
        ((rows, small), bf16),
        ((rows, mid), bf16),
        ((2 * MB, wide), f32),
        ((2 * MB, mid), f32),
        ((2 * MB, small), f32),
    ]
    out_specs = [HBM] * 2 + [VM] * 11 + [HBM] * 3 + [VM] + [HBM] * len(cot)
    out += big + [((windows, length, wide), bf16)]
    out += [((windows, length, -(-c.shape[0] // BLOCK) * BLOCK), bf16) for c in cot]
    scratch = (
        reduce_scratch(shape, 2 * MB, wide // 2)
        + reduce_scratch(shape, 2 * MB, mid)
        + reduce_scratch(shape, 2 * MB, small)
    )
    scratch += [
        pltpu.VMEM((windows, wide), f32),
        pltpu.VMEM((windows, wide), f32),
        pltpu.VMEM((2 * MB, mid), f32),
        pltpu.VMEM((2 * MB, small), f32),
        pltpu.SemaphoreType.DMA((3, 4)),
        pltpu.VMEM((windows, EDGE, small), f32),
        pltpu.VMEM((windows, EDGE, small), f32),
        pltpu.VMEM(*out[0]),
        pltpu.VMEM(*out[1]),
    ]
    scratch += [pltpu.VMEM(*b) for b in big]
    scratch += [
        pltpu.SemaphoreType.DMA((4, 32)),
        pltpu.SemaphoreType.DMA((5,)),
        pltpu.VMEM((windows, wide), f32),
        pltpu.VMEM((windows, wide), f32),
        pltpu.VMEM((2 * MB, channels), f32),
        pltpu.VMEM((channels // LANES, half, LANES), f32),
        *(Relay.scratch(windows, length) if cot else []),
    ]
    return pl.pallas_call(
        functools.partial(forward_kernel, shape, len(cot)),
        in_specs=[pl.BlockSpec(memory_space=pltpu.SMEM), VM, VM] + [HBM] * (3 + len(cot)),
        out_specs=out_specs,
        out_shape=[jax.ShapeDtypeStruct(*o) for o in out],
        scratch_shapes=scratch,
        compiler_params=params(1),
        name="forward",
    )(order, tracks, vectors, w_one, w_two, w_point, *cot)


def heads_kernel(
    human_tracks,
    mouse_tracks,
    species,
    order,
    summed,
    w_human,
    w_mouse,
    b_human,
    b_mouse,
    cot,
    predicted,
    grad_summed,
    d_human,
    d_mouse,
    db,
    rows_sorted,
    grad_sorted,
    grad_pre,
    by_track,
    meta,
):
    j = pl.program_id(0)
    windows, length, block = cot.shape
    pair = 2 * length
    n_pairs = windows // 2
    mid = summed.shape[1]

    @pl.when(j == 0)
    def _():
        grad_sorted[...] = jnp.zeros_like(grad_sorted)
        db[...] = jnp.zeros_like(db)
        found = 0
        for kind in range(2):
            for p in range(windows):
                window = order[p]
                mine = species[window] == kind

                @pl.when(mine)
                def _(found=found, p=p, window=window):
                    meta[found] = p
                    meta[windows + found] = window

                found = found + mine.astype(jnp.int32)
            if kind == 0:
                meta[2 * windows] = found

        @pl.loop(0, windows)
        def _(s):
            source = pl.multiple_of(meta[s] * length, length)
            target = pl.multiple_of(s * length, length)
            rows_sorted[pl.ds(target, length), :] = summed[pl.ds(source, length), :]

    n_human = meta[2 * windows]
    column = lax.broadcasted_iota(jnp.int32, (1, block), 1)

    cuts = [slice(at, min(at + SPLIT, block)) for at in range(0, block, SPLIT)]

    def run(weight, bias, limit, is_mouse, first_pair, last_pair):
        def body(p, carry):
            start = pl.multiple_of(p * pair, pair)
            rows = rows_sorted[pl.ds(start, pair), :]
            mine = [s >= n_human if is_mouse else s < n_human for s in (2 * p, 2 * p + 1)]
            window = [meta[windows + 2 * p], meta[windows + 2 * p + 1]]
            pres = [dot_nn(rows, weight[:, cut]) + bias[:, cut] for cut in cuts]
            back = jnp.zeros((pair, mid), f32)
            for cut, pre in zip(cuts, pres):
                inside = column[:, cut] < limit
                decay = jnp.exp(-jnp.abs(pre))
                whole = 1.0 + decay
                inverse = 1.0 / whole
                sigmoid = jnp.where(pre >= 0, inverse, decay * inverse)
                logs = jnp.where(decay < 2.0**-11, decay, jnp.log(whole))
                output = jnp.where(inside, jnp.maximum(pre, 0.0) + logs, 0.0)
                grads = []
                for i in range(2):
                    part = slice(i * length, (i + 1) * length)
                    grad = cot[window[i], :, cut].astype(f32) * sigmoid[part]
                    grads.append(jnp.where(inside & mine[i], grad, 0.0))
                    here = output[part].T
                    spots = pl.ds(cut.start * windows + window[i], cut.stop - cut.start, windows)
                    if is_mouse:
                        here = jnp.where(mine[i], here, by_track[spots, :])
                    by_track[spots, :] = here
                grad = jnp.concatenate(grads, axis=0).astype(bf16)
                grad_pre[pl.ds(start, pair), cut] = grad
                back = back + dot_nt(grad, weight[:, cut])
            grad_sorted[pl.ds(start, pair), :] += back
            return carry

        lax.fori_loop(first_pair, last_pair, body, 0)

    def weight_grads(n_used, from_end, d_weight, bias_row):
        for n in range(n_pairs + 1):

            @pl.when(n_used == n)
            def _(n=n):
                if n == 0:
                    d_weight[...] = jnp.zeros_like(d_weight)
                else:
                    part = slice((n_pairs - n) * pair, None) if from_end else slice(0, n * pair)
                    grad = grad_pre[part, :]
                    d_weight[...] = dot_tn(rows_sorted[part, :], grad).astype(bf16)
                    total = dot_nn(jnp.ones((8, n * pair), bf16), grad)[:1]
                    db[pl.ds(bias_row, 1), :] = total

    human_pairs = lax.div(n_human + 1, 2)
    run(w_human, b_human, human_tracks - j * block, False, 0, human_pairs)
    weight_grads(human_pairs, False, d_human, j)

    @pl.when(j == 0)
    def _():
        mouse_start = lax.div(n_human, 2)
        run(w_mouse, b_mouse, mouse_tracks, True, mouse_start, n_pairs)
        weight_grads(n_pairs - mouse_start, True, d_mouse, pl.num_programs(0))

    @pl.when(j > 0)
    def _():
        def body(s, carry):
            by_track[pl.ds(meta[windows + s], block, windows), :] = jnp.zeros((block, length), f32)
            return carry

        lax.fori_loop(n_human, windows, body, 0)

    predicted[...] = by_track[...].reshape(block, windows, length).astype(bf16)

    @pl.when(j == pl.num_programs(0) - 1)
    def _():
        @pl.loop(0, windows)
        def _(s):
            source = pl.multiple_of(s * length, length)
            target = pl.multiple_of(meta[s] * length, length)
            grad_summed[pl.ds(target, length), :] = grad_sorted[pl.ds(source, length), :]


def heads(species, order, summed, w_heads, bias, cot, human_tracks, mouse_tracks):
    windows, length, _ = cot.shape
    rows, mid = summed.shape
    blocks = w_heads.shape[1] // BLOCK - 1
    smem = pl.BlockSpec(memory_space=pltpu.SMEM)
    fixed = lambda shape, at=0: pl.BlockSpec(
        shape, lambda j: (0, at), pipeline_mode=pl.Buffered(1)
    )
    return pl.pallas_call(
        functools.partial(heads_kernel, human_tracks, mouse_tracks),
        grid=(blocks,),
        in_specs=[
            smem,
            smem,
            fixed((rows, mid)),
            pl.BlockSpec((mid, BLOCK), lambda j: (0, j)),
            fixed((mid, BLOCK), blocks),
            pl.BlockSpec((1, BLOCK), lambda j: (0, j)),
            fixed((1, BLOCK), blocks),
            pl.BlockSpec((windows, length, BLOCK), lambda j: (0, 0, j)),
        ],
        out_specs=[
            pl.BlockSpec((BLOCK, windows, length), lambda j: (j, 0, 0)),
            pl.BlockSpec((rows, mid), lambda j: (0, 0)),
            pl.BlockSpec((mid, BLOCK), lambda j: (0, j)),
            pl.BlockSpec((mid, BLOCK), lambda j: (0, 0)),
            pl.BlockSpec((8, BLOCK), lambda j: (0, 0)),
        ],
        scratch_shapes=[
            pltpu.VMEM((rows, mid), bf16),
            pltpu.VMEM((rows, mid), f32),
            pltpu.VMEM((rows, BLOCK), bf16),
            pltpu.VMEM((BLOCK * windows, length), f32),
            pltpu.SMEM((2 * windows + 1,), jnp.int32),
        ],
        out_shape=[
            jax.ShapeDtypeStruct((human_tracks, windows, length), bf16),
            jax.ShapeDtypeStruct((rows, mid), f32),
            jax.ShapeDtypeStruct((mid, blocks * BLOCK), bf16),
            jax.ShapeDtypeStruct((mid, BLOCK), bf16),
            jax.ShapeDtypeStruct((8, BLOCK), f32),
        ],
        compiler_params=params(),
        name="heads",
    )(species, order, summed, w_heads, w_heads, bias, bias, cot)


HAND, LOAD = 7, 8
WHOLE = (0, 1, 2, 3, 4, 5, 6)
PLANE = (0, 1, 2, HAND)
ALONG = (LOAD, 3, 4, 5, 6)


class Summing:
    def __init__(self, place, plan, source, start, width, target, to, scratch):
        self.place, self.plan, self.source, self.target = place, plan, source, target
        self.columns = pl.ds(start, width)
        self.width, self.to = width, to
        for name, ref in zip(self.names(plan), scratch):
            setattr(self, name, ref)
        half = self.own.shape[2]
        self.half, self.part = half, half // 2
        self.mine = pl.ds(pl.multiple_of(place.sec * half, half), half)
        self.other = pl.ds(pl.multiple_of((1 - place.sec) * half, half), half)
        self.x, self.y = lax.rem(place.dp, 2), lax.div(place.dp, 2)
        self.cell = (self.y, self.x) if 0 in plan else (0, 0)
        self.top, self.bottom = pl.ds(0, self.part), pl.ds(self.part, self.part)
        self.at_end = (place.seq == 0) | (place.seq == place.n_seq - 1)
        self.between = jnp.logical_not(self.at_end)

    @staticmethod
    def names(plan):
        names = ["own"]
        if 0 in plan:
            names += ["core", "side_a", "side_b", "end_a", "end_b"]
        if 6 in plan:
            names += ["z_one", "z_far", "mate"]
        return names + ["sems"]

    @staticmethod
    def scratch(plan, share, width):
        half = share // 2
        part = half // 2
        cells = 2 if 0 in plan else 1
        shapes = dict(
            own=(cells, cells, half, width),
            core=(2, 2, half, width),
            side_a=(2, part, width),
            side_b=(2, part, width),
            end_a=(part, width),
            end_b=(part, width),
            z_one=(half, width),
            z_far=(half, width),
            mate=(half, width),
        )
        refs = [pltpu.VMEM(shapes[name], bf16) for name in Summing.names(plan)[:-1]]
        return refs + [pltpu.SemaphoreType.DMA((23,))]

    def remote(self, source, target, sem, device):
        return pltpu.make_async_remote_copy(
            src_ref=source,
            dst_ref=target,
            send_sem=self.sems.at[2 * sem],
            recv_sem=self.sems.at[2 * sem + 1],
            device_id=device,
            device_id_type=MESH,
        )

    def copies(self, stage):
        p, own, x, y = self.place, self.own, self.x, self.y
        sibling = (1 - p.sec, p.seq, p.dp)
        over_x = (p.sec, p.seq, p.dp + 1 - 2 * x)
        over_y = (p.sec, p.seq, p.dp + 2 - 4 * y)
        over_z = (p.sec, p.seq + 1 - 2 * lax.rem(p.seq, 2), p.dp)
        if stage == 0:
            return [
                pltpu.make_async_copy(
                    self.source.at[:, :, self.mine, self.columns], own, self.sems.at[16]
                ),
                self.remote(
                    self.source.at[:, :, self.other, self.columns], self.core, 0, sibling
                ),
            ]
        if stage == 1:
            return [
                self.remote(own.at[:, 1 - x, self.top], self.side_a, 1, over_x),
                self.remote(own.at[1 - y, :, self.bottom], self.side_b, 2, over_y),
            ]
        if stage == 2:
            return [
                self.remote(own.at[1 - y, x, self.top], self.end_a, 3, over_y),
                self.remote(own.at[y, 1 - x, self.bottom], self.end_b, 4, over_x),
            ]
        if stage == HAND:
            columns = pl.ds(self.to, self.width)
            return [
                pltpu.make_async_copy(
                    own.at[self.cell], self.target.at[:, columns], self.sems.at[17]
                )
            ]
        if stage == LOAD:
            return [
                pltpu.make_async_copy(
                    self.source.at[:, self.columns], own.at[self.cell], self.sems.at[17]
                )
            ]
        if stage == 3:
            return [self.remote(own.at[self.cell], self.z_one, 5, over_z)]
        if stage == 4:
            opposite = (p.sec, p.n_seq - 1 - p.seq, p.dp)
            return [self.remote(own.at[self.cell], self.z_far, 6, opposite)]
        if stage == 5:
            return [self.remote(own.at[self.cell], self.z_one, 5, over_z)]
        return [
            self.remote(source, self.mate, 7, sibling) for source in (own.at[self.cell], self.z_one)
        ]

    def start(self, stage):
        copies = self.copies(stage)
        if stage == 3:
            pl.when(self.at_end)(copies[0].start)
        elif stage in (4, 5):
            pl.when(self.between)(copies[0].start)
        elif stage == 6:
            pl.when(self.between)(copies[0].start)
            pl.when(self.at_end)(copies[1].start)
        else:
            for copy in copies:
                copy.start()

    def add(self, at, other):
        self.own[at] = (self.own[at].astype(f32) + other.astype(f32)).astype(bf16)

    def finish(self, stage):
        copies = self.copies(stage)
        x, y = self.x, self.y
        if stage == 3:
            pl.when(self.at_end)(copies[0].wait_send)

            @pl.when(self.between)
            def _():
                copies[0].wait_recv()
                self.add(self.cell, self.z_one[...])

        elif stage == 4:

            @pl.when(self.between)
            def _():
                copies[0].wait()
                self.add(self.cell, self.z_far[...])

        elif stage == 5:
            pl.when(self.between)(copies[0].wait_send)
            pl.when(self.at_end)(copies[0].wait_recv)
        elif stage == 6:
            copies[0].wait()
            pl.when(self.between)(self.results(self.own.at[self.cell])[0].start)
            pl.when(self.at_end)(self.results(self.z_one)[0].start)
            self.results(self.z_one)[1].start()
        elif stage != HAND:
            for copy in copies:
                copy.wait()
        if stage == 0:

            @pl.loop(0, 4)
            def _(i):
                a, b = lax.div(i, 2), lax.rem(i, 2)
                self.add((a, b), self.core[a, b])

        elif stage == 1:
            for i in range(2):
                self.add((i, x, self.top), self.side_a[i])
                self.add((y, i, self.bottom), self.side_b[i])
        elif stage == 2:
            self.add((y, x, self.top), self.end_a[...])
            self.add((y, x, self.bottom), self.end_b[...])

    def results(self, source):
        copies = []
        for i, (ref, rows) in enumerate(((source, self.mine), (self.mate, self.other))):
            if len(self.target.shape) == 3:
                target = self.target.at[self.to, rows]
            else:
                target = self.target.at[rows, pl.ds(self.to, self.width)]
            copies.append(pltpu.make_async_copy(ref, target, self.sems.at[18 + i]))
        return copies

    def close(self):
        copies = self.results(self.mate) if 6 in self.plan else self.copies(HAND)
        for copy in copies:
            copy.wait()


class Sums:
    def __init__(self, place, sources, targets, chunks, refs):
        self.parts = []
        for plan, begin, source, start, width, target, to in chunks:
            count = len(Summing.names(plan))
            part = Summing(
                place, plan, sources[source], start, width, targets[target], to, refs[:count]
            )
            refs = refs[count:]
            self.parts.append((begin, part))
        self.parts.sort(key=lambda item: -item[0])
        self.last = max([begin + len(part.plan) for begin, part in self.parts], default=-1)
        self.tick = 0

    def step(self):
        if self.tick > self.last:
            return
        for begin, part in self.parts:
            i = self.tick - begin
            if 0 < i <= len(part.plan):
                part.finish(part.plan[i - 1])
            if 0 <= i < len(part.plan):
                part.start(part.plan[i])
        self.tick += 1

    def finish(self):
        while self.tick <= self.last:
            self.step()
        for _, part in self.parts:
            part.close()


def sums_scratch(share, chunks):
    return [ref for chunk in chunks for ref in Summing.scratch(chunk[0], share, chunk[4])]


def count_refs(chunks):
    return sum(len(Summing.names(chunk[0])) for chunk in chunks)


def head_chunks(human_wide):
    size = BLOCK // 2
    pieces = [(0, at) for at in range(0, human_wide, size)] + [(1, 0), (1, size)]
    n_whole = len(pieces) // 2
    chunks = []
    for k, (source, at) in enumerate(pieces):
        whole = k < n_whole
        to = (k if whole else k - n_whole) * size
        chunks.append((WHOLE if whole else PLANE, k, source, at, size, 0 if whole else 1, to))
    return chunks, n_whole * size, (len(pieces) - n_whole) * size


def split_refs(refs, *counts):
    groups = []
    for count in counts:
        groups.append(refs[:count])
        refs = refs[count:]
    assert not refs
    return groups


def back_high_kernel(shape, n_sums, chunks, *refs):
    (sources, big_in, small_in, targets, d_outs, outs, fixed, sum_refs) = split_refs(
        refs, n_sums, 3, 12, n_sums, 3, 3, 37, count_refs(chunks)
    )
    in_grad, in_u_one, in_u_two = big_in
    (
        act_three,
        branch,
        branch_low,
        branch_high,
        bn_three,
        w_point,
        w_two,
        pooled,
        pooled_low,
        pooled_high,
        bn_two,
        vectors,
    ) = small_in
    grad_ext, sums_three, sums_two = outs
    reduce_three, reduce_two, fixed = fixed[:6], fixed[6:12], fixed[12:]
    (
        grad_summed,
        u_any,
        du_three,
        edge_low,
        edge_high,
        du_low,
        du_high,
        row_low,
        row_high,
        gs_low,
        gs_high,
        local_three,
        grad_branch,
        du_two,
        row_low_two,
        row_high_two,
        dlow_two,
        dhigh_two,
        local_two,
        grad_main,
        d_point,
        d_two,
        d_one,
        halo_sems,
        copy_sems,
    ) = fixed
    place = Place(shape)
    place.greet()
    windows, length, mid = pooled.shape
    small = branch.shape[1]
    pair = 2 * length
    taps = w_two.shape[0] // mid
    scale = 1.0 / (pair * shape[0] * shape[1] * shape[2])
    row = lambda index, width: vectors.at[index : index + 1, :width]
    gain_two, shift_two = row(2, mid), row(3, mid)
    gain_three, shift_three = row(4, small), row(5, small)
    u_two = u_any.at[:, : taps * mid]
    load_grad = pltpu.make_async_copy(in_grad, grad_summed, copy_sems.at[0])
    load_two = pltpu.make_async_copy(in_u_two, u_two, copy_sems.at[1])
    load_one = pltpu.make_async_copy(in_u_one, u_any, copy_sems.at[2])
    save_point, save_two, save_one = [
        pltpu.make_async_copy(a, b, copy_sems.at[3 + i])
        for i, (a, b) in enumerate(((d_point, d_outs[0]), (d_two, d_outs[1]), (d_one, d_outs[2])))
    ]
    load_grad.start()
    load_two.start()
    sums = Sums(place, sources, targets, chunks, sum_refs)
    place.meet()
    sums.step()
    load_grad.wait()

    for m in range(MB):
        at = slice(m * pair, (m + 1) * pair)
        grad = grad_summed[at, :]
        back = dot_nn(grad.astype(bf16), w_point[...])
        xhat = (branch[at, :] - bn_three[m : m + 1, :]) * bn_three[MB + m : MB + m + 1, :]
        du = gelu_slope(xhat * gain_three[...] + shift_three[...]) * back
        du_three[at, :] = du
        local_three[m : m + 1, :] = jnp.sum(du, axis=0, keepdims=True)
        local_three[MB + m : MB + m + 1, :] = jnp.sum(du * xhat, axis=0, keepdims=True)
        for i in range(2):
            w = 2 * m + i
            edge_low[w] = du[i * length : i * length + EDGE]
            edge_high[w] = du[(i + 1) * length - EDGE : (i + 1) * length]
            row_low[w : w + 1, :] = grad[i * length : i * length + 1]
            row_high[w : w + 1, :] = grad[(i + 1) * length - 1 : (i + 1) * length]

    moves = halo_copies(place, (edge_low, edge_high), (du_low, du_high), halo_sems.at[0])
    moves += halo_copies(place, (row_low, row_high), (gs_low, gs_high), halo_sems.at[1])
    place.halos(moves, 0)
    sums_three[...] = reduce_everywhere(
        place, local_three[...], *reduce_three[:2], reduce_three[2:], add_up, sums.step, nothing
    )
    d_point[...] = dot_tn(grad_summed[...].astype(bf16), act_three[...]).astype(bf16)
    save_point.start()
    place.halos(moves, 1)
    sums.step()

    for m in range(MB):
        at = slice(m * pair, (m + 1) * pair)
        centre, inverse = bn_three[m : m + 1, :], bn_three[MB + m : MB + m + 1, :]
        factor = gain_three[...] * inverse
        mean_du = sums_three[m : m + 1, :] * scale
        mean_dx = sums_three[MB + m : MB + m + 1, :] * scale

        def back(du, value):
            xhat = (value - centre) * inverse
            return factor * (du - mean_du - xhat * mean_dx)

        main = back(du_three[at, :], branch[at, :])
        grad_branch[at, :] = main.astype(bf16)
        pieces = []
        for i in range(2):
            w = 2 * m + i
            low = jnp.where(place.is_first, 0.0, back(du_low[w], branch_low[w]))
            high = jnp.where(place.is_last, 0.0, back(du_high[w], branch_high[w]))
            pieces += [low, main[i * length : (i + 1) * length], high]
        ext = jnp.concatenate(pieces, axis=0).astype(bf16)
        span = length + 2 * EDGE
        through = [dot_nt(ext, w_two[t * mid : (t + 1) * mid, :]) for t in range(taps)]
        centre_two, inverse_two = bn_two[m : m + 1, :], bn_two[MB + m : MB + m + 1, :]
        total_du = jnp.zeros((1, mid), f32)
        total_dx = jnp.zeros((1, mid), f32)
        for i in range(2):
            w = 2 * m + i
            grad = jnp.zeros((length, mid), f32)
            for t in range(taps):
                whole = through[t][i * span : (i + 1) * span]
                grad = grad + shifted_rows(whole, EDGE - (t - 1) * DILATION, length)
            xhat = (pooled[w].astype(f32) - centre_two) * inverse_two
            du = gelu_slope(xhat * gain_two[...] + shift_two[...]) * grad
            du_two[w] = du
            total_du = total_du + jnp.sum(du, axis=0, keepdims=True)
            total_dx = total_dx + jnp.sum(du * xhat, axis=0, keepdims=True)
            row_low_two[w : w + 1, :] = du[:1]
            row_high_two[w : w + 1, :] = du[length - 1 :]
        local_two[m : m + 1, :] = total_du
        local_two[MB + m : MB + m + 1, :] = total_dx
        if m % 2:
            sums.step()

    moves = halo_copies(
        place, (row_low_two, row_high_two), (dlow_two, dhigh_two), halo_sems.at[2]
    )
    place.halos(moves, 0)
    sums_two[...] = reduce_everywhere(
        place, local_two[...], *reduce_two[:2], reduce_two[2:], add_up, sums.step, nothing
    )
    load_two.wait()
    for t in range(taps):
        part = dot_tn(u_two[:, t * mid : (t + 1) * mid], grad_branch[...])
        d_two[:, t * small : (t + 1) * small] = part.astype(bf16)
    save_two.start()
    load_one.start()
    place.halos(moves, 1)
    sums.step()

    for m in range(MB):
        centre, inverse = bn_two[m : m + 1, :], bn_two[MB + m : MB + m + 1, :]
        factor = gain_two[...] * inverse
        mean_du = sums_two[m : m + 1, :] * scale
        mean_dx = sums_two[MB + m : MB + m + 1, :] * scale

        def back(du, value, extra):
            xhat = (value.astype(f32) - centre) * inverse
            return factor * (du - mean_du - xhat * mean_dx) + extra

        edges = []
        for i in range(2):
            w = 2 * m + i
            at = slice(w * length, (w + 1) * length)
            value = back(du_two[w], pooled[w], grad_summed[at, :]).astype(bf16)
            grad_ext[m, i * length : (i + 1) * length, :] = value
            grad_main[at, :] = value
            row = slice(w, w + 1)
            low = back(dlow_two[row, :], pooled_low[w].astype(f32)[EDGE - 1 :], gs_low[row, :])
            high = back(dhigh_two[row, :], pooled_high[w].astype(f32)[:1], gs_high[row, :])
            edges += [jnp.where(place.is_first, 0.0, low), jnp.where(place.is_last, 0.0, high)]
        row = lax.broadcasted_iota(jnp.int32, (EDGE, mid), 0)
        block = jnp.zeros((EDGE, mid), f32)
        for i, edge in enumerate(edges):
            block = jnp.where(row == i, edge, block)
        grad_ext[m, pair : pair + EDGE, :] = block.astype(bf16)
    sums.step()
    load_one.wait()
    columns = d_one.shape[1] // 5
    for t in range(5):
        part = slice(t * columns, (t + 1) * columns)
        d_one[:, part] = dot_tn(grad_main[...], u_any[:, part]).astype(bf16)
        if t in (1, 3):
            sums.step()
    save_one.start()
    sums.finish()
    save_point.wait()
    save_two.wait()
    save_one.wait()


def back_high(shape, sources, grad_summed, u_one, u_two, three, two):
    branch = three[1]
    w_two, pooled = two[0], two[1]
    windows, length, mid = pooled.shape
    rows, small = branch.shape
    share = mid // shape[2]
    chunks, targets = [], []
    if sources:
        chunks, n_whole, n_plane = head_chunks(sources[0].shape[3])
        targets = [((share, n_whole), bf16), ((share // 2, n_plane), bf16)]
    taps = w_two.shape[0] // mid
    d_shapes = [((mid, small), bf16), ((mid, taps * small), bf16), ((mid, u_one.shape[1]), bf16)]
    outs = [
        ((MB, 2 * length + EDGE, mid), bf16),
        ((2 * MB, small), f32),
        ((2 * MB, mid), f32),
    ]
    fixed = reduce_scratch(shape, 2 * MB, small) + reduce_scratch(shape, 2 * MB, mid)
    fixed += [
        pltpu.VMEM(*a)
        for a in [
            ((rows, mid), f32),
            (u_one.shape, bf16),
            ((rows, small), f32),
            ((windows, EDGE, small), f32),
            ((windows, EDGE, small), f32),
            ((windows, EDGE, small), f32),
            ((windows, EDGE, small), f32),
            ((windows, mid), f32),
            ((windows, mid), f32),
            ((windows, mid), f32),
            ((windows, mid), f32),
            ((2 * MB, small), f32),
            ((rows, small), bf16),
            ((windows, length, mid), f32),
            ((windows, mid), f32),
            ((windows, mid), f32),
            ((windows, mid), f32),
            ((windows, mid), f32),
            ((2 * MB, mid), f32),
            ((rows, mid), bf16),
            *d_shapes,
        ]
    ]
    fixed += [pltpu.SemaphoreType.DMA((3, 4)), pltpu.SemaphoreType.DMA((6,))]
    return pl.pallas_call(
        functools.partial(back_high_kernel, shape, len(sources), chunks),
        in_specs=[HBM] * (3 + len(sources)) + [VM] * 12,
        out_specs=[HBM] * (3 + len(sources)) + [VM] * 3,
        out_shape=[jax.ShapeDtypeStruct(*o) for o in targets + d_shapes + outs],
        scratch_shapes=fixed + sums_scratch(share, chunks),
        compiler_params=params(2),
        name="back_high",
    )(*sources, grad_summed, u_one, u_two, *three, *two)


def back_low_kernel(shape, n_sums, chunks, *refs):
    (sources, ins, targets, outs, reduce_one, reduce_b, fixed, sum_refs) = split_refs(
        refs, n_sums, 7, n_sums, 3, 6, 6, 5, count_refs(chunks)
    )
    order, in_one, grad_ext, x2, bn_one, vectors, bias_sums = ins
    grad_input, sums_one, bias_out = outs
    w_one, du_one, local, lanes_buffer, load_sem = fixed
    place = Place(shape)
    place.greet()
    windows, length, wide = x2.shape
    channels = wide // 2
    pair = 2 * length
    gain_one, shift_one = vectors.at[0:1, :wide], vectors.at[1:2, :wide]
    load_one = pltpu.make_async_copy(in_one, w_one, load_sem)
    load_one.start()
    sums = Sums(place, sources, targets, chunks, sum_refs)
    place.meet()
    sums.step()
    load_one.wait()

    for m in range(MB):
        through = [
            dot_nn(grad_ext[m], w_one[:, t * channels : (t + 1) * channels]) for t in range(5)
        ]
        centre, inverse = bn_one[m : m + 1, :], bn_one[MB + m : MB + m + 1, :]
        total_du = jnp.zeros((1, wide), f32)
        total_dx = jnp.zeros((1, wide), f32)
        row = lax.broadcasted_iota(jnp.int32, (length, channels), 0)
        top, bottom = row == 0, row == length - 1
        for i in range(2):
            w = 2 * m + i
            main = [t[i * length : (i + 1) * length] for t in through]
            low = [t[pair + 2 * i : pair + 2 * i + 1] for t in through]
            high = [t[pair + 2 * i + 1 : pair + 2 * i + 2] for t in through]
            later = lambda t: jnp.where(bottom, high[t], pltpu.roll(main[t], length - 1, axis=0))
            earlier = lambda t: jnp.where(top, low[t], pltpu.roll(main[t], 1, axis=0))
            mean = later(0) + main[2] + earlier(4)
            cross = main[1] + earlier(3)
            cross_end = high[1] + main[3][length - 1 :]
            cross_later = jnp.where(bottom, cross_end, pltpu.roll(cross, length - 1, axis=0))
            grad = jnp.concatenate([(mean + cross) * 0.5, (mean + cross_later) * 0.5], axis=1)
            xhat = (x2[w].astype(f32) - centre) * inverse
            du = gelu_slope(xhat * gain_one[...] + shift_one[...]) * grad
            du_one[w] = du
            total_du = total_du + jnp.sum(du, axis=0, keepdims=True)
            total_dx = total_dx + jnp.sum(du * xhat, axis=0, keepdims=True)
        local[m : m + 1, :] = total_du[:, :channels] + total_du[:, channels:]
        local[MB + m : MB + m + 1, :] = total_dx[:, :channels] + total_dx[:, channels:]
        sums.step()

    sums_one[...] = reduce_everywhere(
        place, local[...], *reduce_one[:2], reduce_one[2:], add_up, sums.step
    )
    scale = 1.0 / (4 * length * shape[0] * shape[1] * shape[2])
    lanes = lanes_buffer.shape[0]
    twice = lambda v: jnp.concatenate([v, v], axis=1)

    def write(window):
        w = 0
        for p in range(1, windows):
            w = jnp.where(order[p] == window, p, w)
        m = lax.div(w, 2)
        mean_du = twice(sums_one[pl.ds(m, 1), :]) * scale
        mean_dx = twice(sums_one[pl.ds(MB + m, 1), :]) * scale
        inverse = bn_one[pl.ds(MB + m, 1), :]
        xhat = (x2[w].astype(f32) - bn_one[pl.ds(m, 1), :]) * inverse
        grad = gain_one[...] * inverse * (du_one[w] - mean_du - xhat * mean_dx)
        for odd in range(2):
            for c in range(lanes):
                at = odd * channels + c * LANES
                lanes_buffer[c, pl.ds(odd, length, 2), :] = grad[:, at : at + LANES]
        for c in range(lanes):
            grad_input[window, :, c * LANES : (c + 1) * LANES] = lanes_buffer[c].astype(bf16)

    for half in range(2):
        sums.step()

        @pl.loop(half * windows // 2, (half + 1) * windows // 2)
        def _(window):
            write(window)

    bias_out[...] = reduce_everywhere(
        place, bias_sums[...], *reduce_b[:2], reduce_b[2:], add_up, sums.step
    )
    sums.finish()


def back_low(shape, sources, order, w_one, grad_ext, x2, bn_one, vectors, bias_sums):
    windows, length, wide = x2.shape
    channels = wide // 2
    share = grad_ext.shape[2] // shape[2]
    chunks, targets = [], []
    if sources:
        columns = sources[0].shape[1]
        size = BLOCK // 2
        chunks = [(ALONG, i // 2, 0, i * size, size, 0, i * size) for i in range(columns // size)]
        targets = [((share, columns), bf16)]
        begin = 0
        for i, taps in enumerate((1, 3, w_one.shape[1] // channels), 1):
            width = sources[i].shape[3] // taps
            for t in range(taps):
                begin += width > share * 2
                chunks.append((WHOLE, begin, i, t * width, width, i, t))
            targets.append(((taps, share, width), bf16))
    outs = [((windows, 2 * length, channels), bf16), ((2 * MB, channels), f32)]
    outs += [(bias_sums.shape, f32)]
    scratch = reduce_scratch(shape, 2 * MB, channels) + reduce_scratch(shape, *bias_sums.shape)
    scratch += [
        pltpu.VMEM(w_one.shape, bf16),
        pltpu.VMEM((windows, length, wide), f32),
        pltpu.VMEM((2 * MB, channels), f32),
        pltpu.VMEM((channels // LANES, 2 * length, LANES), f32),
        pltpu.SemaphoreType.DMA,
    ]
    smem = pl.BlockSpec(memory_space=pltpu.SMEM)
    return pl.pallas_call(
        functools.partial(back_low_kernel, shape, len(sources), chunks),
        in_specs=[HBM] * len(sources) + [smem, HBM] + [VM] * 5,
        out_specs=[HBM] * len(sources) + [VM] * 3,
        out_shape=[jax.ShapeDtypeStruct(*o) for o in targets + outs],
        scratch_shapes=scratch + sums_scratch(share, chunks),
        compiler_params=params(3),
        name="back_low",
    )(*sources, order, w_one, grad_ext, x2, bn_one, vectors, bias_sums)


def per_device(
    shape,
    tracks,
    species,
    batch_order,
    conv_one,
    dilated_kernel,
    point_wise,
    head_human,
    head_mouse,
    bias_human,
    bias_mouse,
    gain_one,
    shift_one,
    gain_two,
    shift_two,
    gain_three,
    shift_three,
    cotangent,
):
    sec = lax.axis_index("section").astype(jnp.int32)
    windows, seq_bins, channels = tracks.shape
    half = seq_bins // 2
    length = half // 2
    human_tracks, mouse_tracks = head_human.shape[1], head_mouse.shape[1]
    human_wide = -(-human_tracks // BLOCK) * BLOCK
    share = conv_one.shape[2]
    mid = share * shape[2]

    taps_one = conv_one.shape[0]
    shard_one = jnp.transpose(conv_one, (0, 2, 1))
    shard_point = point_wise.T
    shard_heads = jnp.concatenate(
        [
            jnp.pad(head_human, ((0, 0), (0, human_wide - human_tracks))),
            jnp.pad(head_mouse, ((0, 0), (0, BLOCK - mouse_tracks))),
        ],
        axis=1,
    )
    half_rows = share // shape[0]
    half_heads = lax.dynamic_slice_in_dim(shard_heads, sec * half_rows, half_rows, 0)
    w_heads = lax.all_gather(half_heads, ("dp", "section"), axis=0, tiled=True)
    weights = [shard_one, dilated_kernel, shard_point]
    if shape != (2, 4, 4):
        weights[0] = jnp.transpose(conv_one, (2, 0, 1)).reshape(share, taps_one * channels)
        weights = [lax.all_gather(w, "dp", axis=w.ndim - 2, tiled=True) for w in weights]

    wide = 2 * channels
    vectors = jnp.stack(
        [
            jnp.pad(v, (0, wide - v.shape[0]))
            for v in (
                jnp.tile(gain_one, 2),
                jnp.tile(shift_one, 2),
                gain_two,
                shift_two,
                gain_three,
                shift_three,
            )
        ]
    )
    native = jnp.transpose(cotangent, (2, 0, 1))
    relay = [native] if length % LANES == 0 else []
    (
        u_one,
        u_two,
        pooled,
        pooled_low,
        pooled_high,
        branch,
        branch_low,
        branch_high,
        act_three,
        summed,
        bn_one,
        bn_two,
        bn_three,
        w_one,
        w_two,
        w_point,
        x2,
        *cot,
    ) = forward(shape, mid, batch_order, tracks, vectors, *weights, relay)
    if not cot:
        half_cot = lax.dynamic_slice_in_dim(cotangent, sec * length, length, 1)
        cot = [jnp.pad(half_cot, ((0, 0), (0, 0), (0, human_wide - human_tracks)))]
    w_two = w_two.reshape(-1, w_two.shape[2])

    wide_bias = jnp.concatenate(
        [
            jnp.pad(bias_human, (0, human_wide - human_tracks)),
            jnp.pad(bias_mouse, (0, BLOCK - mouse_tracks)),
        ]
    ).reshape(1, -1)
    predicted, grad_summed, d_human, d_mouse, bias_sums = heads(
        species, batch_order, summed, w_heads, wide_bias, cot[0], human_tracks, mouse_tracks
    )


    def in_kernel(*grads):
        if shape != (2, 4, 4):
            return []
        return [g.reshape(2, 2, -1, g.shape[1]) for g in grads]

    def summed_up(*grads):
        parts = [lax.psum_scatter(g, "dp", scatter_dimension=0, tiled=True) for g in grads]
        return [lax.psum(part, ("section", "seq")) for part in parts]

    def by_tap(grad, taps):
        grad = grad.astype(f32)
        if grad.ndim == 2:
            grad = jnp.transpose(grad.reshape(share, taps, -1), (1, 0, 2))
        return grad

    *heads_summed, d_point, d_two, d_one, grad_ext, sums_three, sums_two = back_high(
        shape,
        in_kernel(d_human, d_mouse),
        grad_summed,
        u_one,
        u_two,
        (act_three, branch, branch_low, branch_high, bn_three, w_point),
        (w_two, pooled, pooled_low, pooled_high, bn_two, vectors),
    )
    *sums_low, grad_input, sums_one, bias_out = back_low(
        shape,
        heads_summed[1:] + in_kernel(d_point, d_two, d_one),
        batch_order,
        w_one,
        grad_ext,
        x2,
        bn_one,
        vectors,
        bias_sums,
    )
    if sums_low:
        rest, r_point, r_two, r_one = sums_low
        all_heads = jnp.concatenate([heads_summed[0], rest], axis=1)
        r_human, r_mouse = all_heads[:, :human_wide], all_heads[:, human_wide:]
    else:
        r_human, r_mouse, r_point, r_two, r_one = summed_up(d_human, d_mouse, d_point, d_two, d_one)
    r_human = r_human[:, :human_tracks].astype(f32)
    r_mouse = r_mouse[:, :mouse_tracks].astype(f32)
    r_point = by_tap(r_point, 1)[0]
    r_two = by_tap(r_two, dilated_kernel.shape[0])
    r_one = by_tap(r_one, taps_one)
    r_point = r_point.T
    r_one = jnp.transpose(r_one, (0, 2, 1))
    bias_human_grad = bias_out[: human_wide // BLOCK].reshape(-1)[:human_tracks]
    bias_mouse_grad = bias_out[human_wide // BLOCK, :mouse_tracks]
    return (
        jnp.transpose(predicted, (1, 2, 0)),
        grad_input,
        r_one,
        r_two,
        r_point,
        r_human,
        r_mouse,
        bias_human_grad,
        bias_mouse_grad,
        jnp.sum(sums_one[MB:], axis=0),
        jnp.sum(sums_one[:MB], axis=0),
        jnp.sum(sums_two[MB:], axis=0),
        jnp.sum(sums_two[:MB], axis=0),
        jnp.sum(sums_three[MB:], axis=0),
        jnp.sum(sums_three[:MB], axis=0),
    )


def solution(mesh):
    shape = (mesh.shape["section"], mesh.shape["seq"], mesh.shape["dp"])
    placed = (
        P("dp", "seq", None),
        P("dp"),
        P(),
        P(None, None, "dp"),
        P(None, "dp", None),
        P(None, "dp"),
        P("dp", None),
        P("dp", None),
    ) + (P(),) * 8 + (P("dp", "seq", None),)
    return jax.shard_map(
        functools.partial(per_device, shape),
        mesh=mesh,
        in_specs=placed,
        out_specs=(
            P("dp", ("seq", "section"), None),
            P("dp", ("seq", "section"), None),
            P(None, None, "dp"),
            P(None, "dp", None),
            P(None, "dp"),
            P("dp", None),
            P("dp", None),
        )
        + (P(),) * 8,
        check_vma=False,
    )
```

```python
import functools
import math

import jax
import jax.numpy as jnp
from jax import lax
from jax.experimental import pallas as pl
from jax.experimental.pallas import tpu as pltpu
from jax.sharding import PartitionSpec as P

MESH = pl.DeviceIdType.MESH
DILATION = 11
MB = 4
EPS = 1e-05
EDGE = 16
BLOCK = 1792
SPLIT = 512
LANES = 128
VMEM_LIMIT = 60 * 1024 * 1024
GELU_K = math.sqrt(2.0 / math.pi)
GELU_C = 0.044715
f32 = jnp.float32
bf16 = jnp.bfloat16
VM = pl.BlockSpec(memory_space=pltpu.VMEM)
HBM = pl.BlockSpec(memory_space=pl.ANY)


def params(collective_id=None, limit=VMEM_LIMIT):
    if collective_id is None:
        return pltpu.CompilerParams(vmem_limit_bytes=limit)
    return pltpu.CompilerParams(
        vmem_limit_bytes=limit, collective_id=collective_id, has_side_effects=True
    )


def gelu(u):
    t = jnp.tanh(u * (GELU_K + (GELU_K * GELU_C) * (u * u)))
    h = 0.5 * u
    return h + h * t


def gelu_slope(u):
    uu = u * u
    t = jnp.tanh(u * (GELU_K + (GELU_K * GELU_C) * uu))
    return 0.5 * (1.0 + t) + (0.5 * u) * (1.0 - t * t) * (GELU_K + (3.0 * GELU_K * GELU_C) * uu)


def dot_nn(a, b):
    return jnp.dot(a, b, preferred_element_type=f32)


def dot_nt(a, b):
    return lax.dot_general(a, b, (((1,), (1,)), ((), ())), preferred_element_type=f32)


def dot_tn(a, b):
    return lax.dot_general(a, b, (((0,), (0,)), ((), ())), preferred_element_type=f32)


class Place:
    def __init__(self, shape):
        self.n_sec, self.n_seq, self.n_dp = shape
        self.n_near = self.n_sec * self.n_dp
        self.sec = lax.axis_index("section")
        self.seq = lax.axis_index("seq")
        self.dp = lax.axis_index("dp")
        self.near = self.sec * self.n_dp + self.dp
        n_bins = self.n_seq * self.n_sec
        bins = self.seq * self.n_sec + self.sec
        self.is_first = bins == 0
        self.is_last = bins == n_bins - 1
        low = lax.rem(bins + n_bins - 1, n_bins)
        high = lax.rem(bins + 1, n_bins)
        self.low = self.bin_device(low)
        self.high = self.bin_device(high)
        across = jnp.where(self.sec == 0, low, high)
        self.across = self.bin_device(across)

    def halos(self, moves, action):
        for up, down in zip(moves[::2], moves[1::2]):
            if action == 0:
                pl.when(jnp.logical_not(self.is_last))(up.start)
                pl.when(jnp.logical_not(self.is_first))(down.start)
            else:
                for first, last in ((up.wait_send, up.wait_recv), (down.wait_recv, down.wait_send)):
                    pl.when(jnp.logical_not(self.is_last))(first)
                    pl.when(jnp.logical_not(self.is_first))(last)

    def bin_device(self, bins):
        return (lax.rem(bins, self.n_sec), lax.div(bins, self.n_sec), self.dp)

    def near_device(self, rank):
        return (lax.div(rank, self.n_dp), self.seq, lax.rem(rank, self.n_dp))

    def greet(self):
        barrier = pltpu.get_barrier_semaphore()
        for k in range(1, self.n_near):
            rank = lax.rem(self.near + k, self.n_near)
            pl.semaphore_signal(
                barrier, inc=1, device_id=self.near_device(rank), device_id_type=MESH
            )
        for k in range(1, self.n_seq):
            seq = lax.rem(self.seq + k, self.n_seq)
            pl.semaphore_signal(
                barrier, inc=1, device_id=(self.sec, seq, self.dp), device_id_type=MESH
            )
        pl.semaphore_signal(barrier, inc=1, device_id=self.across, device_id_type=MESH)

    def meet(self):
        pl.semaphore_wait(pltpu.get_barrier_semaphore(), self.n_near + self.n_seq - 1)


def halo_copies(place, from_self, arrived, sems):
    up = pltpu.make_async_remote_copy(
        src_ref=from_self[1],
        dst_ref=arrived[0],
        send_sem=sems.at[0],
        recv_sem=sems.at[1],
        device_id=place.high,
        device_id_type=MESH,
    )
    down = pltpu.make_async_remote_copy(
        src_ref=from_self[0],
        dst_ref=arrived[1],
        send_sem=sems.at[2],
        recv_sem=sems.at[3],
        device_id=place.low,
        device_id_type=MESH,
    )
    return up, down


def nothing():
    pass


def spread_round(buffer, mine, count, device_of, send, recv, meanwhile=nothing):
    copies = []
    for k in range(1, count):
        rank = lax.rem(mine + k, count)
        copy = pltpu.make_async_remote_copy(
            src_ref=buffer.at[mine],
            dst_ref=buffer.at[mine],
            send_sem=send.at[k],
            recv_sem=recv.at[mine],
            device_id=device_of(rank),
            device_id_type=MESH,
        )
        copy.start()
        copies.append((rank, copy))
    meanwhile()
    for rank, copy in copies:
        pltpu.make_async_remote_copy(
            src_ref=buffer.at[rank],
            dst_ref=buffer.at[rank],
            send_sem=send.at[0],
            recv_sem=recv.at[rank],
            device_id=device_of(rank),
            device_id_type=MESH,
        ).wait_recv()
    for rank, copy in copies:
        copy.wait_send()


def reduce_everywhere(
    place, value, near_buf, far_buf, sems, combine, meanwhile=nothing, then=None
):
    then = meanwhile if then is None else then
    near_send, near_recv, far_send, far_recv = sems
    far_buf[place.seq] = value
    spread_round(
        far_buf,
        place.seq,
        place.n_seq,
        lambda seq: (place.sec, seq, place.dp),
        far_send,
        far_recv,
        meanwhile,
    )
    near_buf[place.near] = combine(far_buf, place.n_seq, 1)
    spread_round(
        near_buf, place.near, place.n_near, place.near_device, near_send, near_recv, then
    )
    return combine(near_buf, place.n_near, place.n_seq)


def add_up(buffer, count, weight):
    total = buffer[0]
    for i in range(1, count):
        total = total + buffer[i]
    return total


def merge_stats(rows, buffer, count, weight):
    means = [buffer[i][:MB] for i in range(count)]
    centre = means[0]
    spread = buffer[0][MB:]
    for i in range(1, count):
        centre = centre + means[i]
        spread = spread + buffer[i][MB:]
    centre = centre * (1.0 / count)
    apart = jnp.square(means[0] - centre)
    for i in range(1, count):
        apart = apart + jnp.square(means[i] - centre)
    return jnp.concatenate([centre, spread + apart * float(rows * weight)], axis=0)


def reduce_scratch(shape, rows, columns):
    n_sec, n_seq, n_dp = shape
    near = n_sec * n_dp
    return [
        pltpu.VMEM((near, rows, columns), f32),
        pltpu.VMEM((n_seq, rows, columns), f32),
        pltpu.SemaphoreType.DMA((near,)),
        pltpu.SemaphoreType.DMA((near,)),
        pltpu.SemaphoreType.DMA((n_seq,)),
        pltpu.SemaphoreType.DMA((n_seq,)),
    ]


def local_stats(value):
    count = value.shape[0]
    centre = jnp.sum(value, axis=0, keepdims=True) * (1.0 / count)
    return centre, jnp.sum(jnp.square(value - centre), axis=0, keepdims=True)


def finish_stats(stats, total):
    return jnp.concatenate(
        [stats[:MB], lax.rsqrt(stats[MB:] * (1.0 / total) + EPS)], axis=0
    )


def prepare(place, order, tracks, pairs, low, high, stats, scratch):
    lanes, half, _ = scratch.shape
    start = pl.multiple_of(place.sec * half, half)

    @pl.loop(0, MB)
    def _(m):
        values = []
        for i in range(2):
            value = tracks[order[2 * m + i], pl.ds(start, half), :].astype(f32)
            values.append(value)
            for c in range(lanes):
                scratch[c] = value[:, c * LANES : (c + 1) * LANES]
            both = jnp.concatenate(
                [scratch[c, pl.ds(odd, half // 2, 2), :] for odd in range(2) for c in range(lanes)],
                axis=1,
            )
            pairs[2 * m + i] = both.astype(bf16)
            low[pl.ds(2 * m + i, 1), :] = both[:1]
            high[pl.ds(2 * m + i, 1), :] = both[half // 2 - 1 :]
        count = 2 * half
        centre = (
            jnp.sum(values[0], axis=0, keepdims=True) + jnp.sum(values[1], axis=0, keepdims=True)
        ) * (1.0 / count)
        spread = jnp.sum(jnp.square(values[0] - centre), axis=0, keepdims=True) + jnp.sum(
            jnp.square(values[1] - centre), axis=0, keepdims=True
        )
        stats[pl.ds(m, 1), :] = centre
        stats[pl.ds(MB + m, 1), :] = spread


class Gathering:
    STAGES = 5

    def __init__(self, place, shard, full, rows_at, sems):
        self.place, self.shard, self.full, self.rows_at, self.sems = place, shard, full, rows_at, sems
        p = place
        x, y, z = lax.rem(p.dp, 2), lax.div(p.dp, 2), lax.rem(p.seq, 2)
        self.share = full.shape[rows_at] // p.n_dp
        self.group = self.share // 6
        g = self.group
        self.dp_x, self.dp_y = p.dp + 1 - 2 * x, p.dp + 2 - 4 * y
        self.dp_xy = 3 - p.dp
        self.sibling = (1 - p.sec, p.seq, p.dp)
        self.over_x, self.over_y = (p.sec, p.seq, self.dp_x), (p.sec, p.seq, self.dp_y)
        self.over_z = (p.sec, p.seq + 1 - 2 * z, p.dp)
        base = p.sec * 3 * g
        self.near, self.middle, self.edge, self.far, self.half = (
            (base + z * g, 2 * g),
            (base + g, g),
            (base + 2 * z * g, g),
            (base + 2 * (1 - z) * g, g),
            (base, 3 * g),
        )

    def at(self, ref, dp, span):
        start, rows = span
        index = pl.ds(pl.multiple_of(dp * self.share + start, self.group), rows)
        return ref.at[:, index] if self.rows_at else ref.at[index]

    def remote(self, dp, span, sem, device, source=None):
        source = self.at(self.full, dp, span) if source is None else source
        return pltpu.make_async_remote_copy(
            src_ref=source,
            dst_ref=self.at(self.full, dp, span),
            send_sem=self.sems.at[2 * sem],
            recv_sem=self.sems.at[2 * sem + 1],
            device_id=device,
            device_id_type=MESH,
        )

    def own_copy(self):
        target = self.at(self.full, self.place.dp, (0, self.share))
        return pltpu.make_async_copy(self.shard, target, self.sems.at[26])

    def copies(self, stage):
        me = self.place.dp
        if stage == 0:
            own = None if self.shard is None else self.at(self.shard, 0, self.near)
            return [
                self.remote(me, self.near, 0, self.over_x, own),
                self.remote(me, self.near, 1, self.over_y, own),
            ]
        if stage == 1:
            return [
                self.remote(self.dp_x, self.middle, 2, self.over_y),
                self.remote(self.dp_y, self.edge, 3, self.over_x),
                self.remote(self.dp_x, self.edge, 4, self.over_z),
                self.remote(self.dp_y, self.edge, 5, self.over_z),
                self.remote(self.dp_x, self.near, 6, self.sibling),
                self.remote(self.dp_y, self.near, 7, self.sibling),
            ]
        if stage == 2:
            return [
                self.remote(self.dp_xy, self.edge, 8, self.over_z),
                self.remote(self.dp_xy, self.near, 9, self.sibling),
            ]
        if stage == 3:
            return [
                self.remote(self.dp_x, self.far, 10, self.sibling),
                self.remote(self.dp_y, self.far, 11, self.sibling),
                self.remote(self.dp_xy, self.far, 12, self.sibling),
            ]
        return []

    def start(self, stage):
        for copy in self.copies(stage):
            copy.start()

    def arrived(self, stage, which, dp, span):
        copy = self.copies(stage)[which]
        pltpu.make_async_remote_copy(
            src_ref=self.at(self.full, dp, span),
            dst_ref=self.at(self.full, dp, span),
            send_sem=self.sems.at[0],
            recv_sem=self.sems.at[2 * {0: 0, 1: 2, 2: 8, 3: 10}[stage] + 2 * which + 1],
            device_id=self.sibling,
            device_id_type=MESH,
        ).wait_recv()

    def advance(self, stage):
        if stage == 0:
            if self.shard is not None:
                self.own_copy().start()
        elif stage == 1:
            self.arrived(0, 0, self.dp_x, self.near)
            self.arrived(0, 1, self.dp_y, self.near)
        elif stage == 2:
            self.arrived(1, 0, self.dp_xy, self.middle)
            self.arrived(1, 1, self.dp_xy, self.edge)
        elif stage == 3:
            self.arrived(1, 2, self.dp_x, self.far)
            self.arrived(1, 3, self.dp_y, self.far)
            self.arrived(2, 0, self.dp_xy, self.far)
        if stage < 4:
            self.start(stage)
            return
        base = (1 - self.place.sec) * 3 * self.group
        z = lax.rem(self.place.seq, 2)
        near = (base + z * self.group, 2 * self.group)
        far = (base + 2 * (1 - z) * self.group, self.group)
        self.arrived(1, 4, self.dp_x, near)
        self.arrived(1, 5, self.dp_y, near)
        self.arrived(2, 1, self.dp_xy, near)
        self.arrived(3, 0, self.dp_x, far)
        self.arrived(3, 1, self.dp_y, far)
        self.arrived(3, 2, self.dp_xy, far)
        if self.shard is not None:
            self.own_copy().wait()
        for stage in range(4):
            for copy in self.copies(stage):
                copy.wait_send()


class Relay:
    TRACKS = 512

    def __init__(self, source, target, first_bin, refs):
        self.source, self.target, self.first = source, target, first_bin
        self.got, self.rows, self.made, self.sems = refs
        self.length = target.shape[1]
        self.count = -(-source.shape[0] // self.TRACKS)
        self.at = 0

    def width(self, i):
        return min(self.TRACKS, self.source.shape[0] - i * self.TRACKS)

    def load(self, i):
        width = self.width(i)
        bins = pl.ds(pl.multiple_of(self.first, self.length), self.length)
        return pltpu.make_async_copy(
            self.source.at[pl.ds(i * self.TRACKS, width), :, bins],
            self.got.at[i % 2, pl.ds(0, width)],
            self.sems.at[i % 2],
        )

    def store(self, i):
        width = min(self.TRACKS, self.target.shape[2] - i * self.TRACKS)
        return pltpu.make_async_copy(
            self.made.at[i % 2, :, :, pl.ds(0, width)],
            self.target.at[:, :, pl.ds(i * self.TRACKS, width)],
            self.sems.at[2 + i % 2],
        )

    def begin(self):
        self.load(0).start()

    def step(self):
        i = self.at
        if i == self.count:
            return
        self.at += 1
        slot, width = i % 2, self.width(i)
        windows = self.got.shape[2]
        self.load(i).wait()
        if i + 1 < self.count:
            self.load(i + 1).start()
        if i > 1:
            self.store(i - 2).wait()
        if width < self.TRACKS:
            self.got[slot, width:] = jnp.zeros((self.TRACKS - width, *self.got.shape[2:]), bf16)
        value = self.got[slot].astype(f32)
        self.rows[...] = value.reshape(self.TRACKS * windows, self.length)
        for w in range(windows):
            self.made[slot, w] = self.rows[pl.ds(w, self.TRACKS, windows), :].astype(bf16).T
        self.store(i).start()

    def finish(self):
        while self.at < self.count:
            self.step()
        for i in range(max(0, self.count - 2), self.count):
            self.store(i).wait()

    @staticmethod
    def scratch(windows, length):
        tracks = Relay.TRACKS
        return [
            pltpu.VMEM((2, tracks, windows, length), bf16),
            pltpu.VMEM((tracks * windows, length), f32),
            pltpu.VMEM((2, windows, length, tracks), bf16),
            pltpu.SemaphoreType.DMA((4,)),
        ]


def shifted_rows(value, offset, length):
    rows = value.shape[0]
    if offset:
        value = pltpu.roll(value, rows - offset, axis=0)
    return value[:length]


def forward_kernel(shape, n_relay, *refs):
    (
        order,
        tracks,
        vectors,
        in_one,
        in_two,
        in_point,
    ) = refs[:6]
    refs = refs[6:]
    in_cot, refs = refs[:n_relay], refs[n_relay:]
    (
        out_u_one,
        out_u_two,
        pooled,
        pooled_low,
        pooled_high,
        branch,
        branch_low,
        branch_high,
        act_three,
        summed,
        bn_one,
        bn_two,
        bn_three,
        out_one,
        out_two,
        out_point,
        x2,
    ) = refs[:17]
    refs = refs[17:]
    out_cot, refs = refs[:n_relay], refs[n_relay:]
    (
        near_one,
        far_one,
        s10,
        s11,
        s12,
        s13,
        near_two,
        far_two,
        s20,
        s21,
        s22,
        s23,
        near_three,
        far_three,
        s30,
        s31,
        s32,
        s33,
        got_low,
        got_high,
        stats_two,
        stats_three,
        halo_sems,
        s_branch_edge_low,
        s_branch_edge_high,
        u_one,
        u_two,
        w_one,
        w_two,
        w_point,
        weight_sems,
        save_sems,
        edge_low,
        edge_high,
        stats_in,
        lanes_buffer,
    ) = refs[:36]
    relay_refs = refs[36:]
    place = Place(shape)
    place.greet()
    windows, length, wide = x2.shape
    channels = wide // 2
    mid = pooled.shape[2]
    small = branch.shape[1]
    parts = shape[0] * shape[1] * shape[2]
    pair = 2 * length
    saves = [
        pltpu.make_async_copy(source, target, save_sems.at[i])
        for i, (source, target) in enumerate(
            ((u_one, out_u_one), (u_two, out_u_two), (w_one, out_one), (w_two, out_two), (w_point, out_point))
        )
    ]
    gathers = []
    own_taps = []
    if len(in_one.shape) == 3:
        taps, share, columns = in_one.shape
        own_rows = pl.ds(pl.multiple_of(place.dp * share, share), share)
        own_taps = [
            pltpu.make_async_copy(
                in_one.at[t],
                w_one.at[own_rows, pl.ds(t * columns, columns)],
                weight_sems.at[0, 27 + t],
            )
            for t in range(taps)
        ]
        for tap in own_taps:
            tap.start()
        columns = w_one.shape[1]
        first = columns // (2 * LANES) * LANES
        pieces = [
            (None, w_one.at[:, part], 0)
            for part in (pl.ds(0, first), pl.ds(first, columns - first))
        ]
        pieces += [(in_two, w_two, 1), (in_point, w_point, 0)]
        gathers = [
            Gathering(place, *piece, weight_sems.at[i]) for i, piece in enumerate(pieces)
        ]
    else:
        loads = [
            pltpu.make_async_copy(source, target, weight_sems.at[i, 0])
            for i, (source, target) in enumerate(
                ((in_one, w_one), (in_two, w_two), (in_point, w_point))
            )
        ]
        for load in loads:
            load.start()
        for load in loads:
            load.wait()

    def advance(*steps):
        for index, stage in steps:
            if index < len(gathers):
                gathers[index].advance(stage)

    mid_rows = lambda index, width: vectors.at[index : index + 1, :width]
    gain_one, shift_one = mid_rows(0, wide), mid_rows(1, wide)
    gain_two, shift_two = mid_rows(2, mid), mid_rows(3, mid)
    gain_three, shift_three = mid_rows(4, small), mid_rows(5, small)
    relay = None
    if n_relay:
        relay = Relay(in_cot[0], out_cot[0], place.sec * length, relay_refs)
        relay.begin()

    def fill(count=1):
        for _ in range(count if relay else 0):
            relay.step()

    prepare(place, order, tracks, x2, edge_low, edge_high, stats_in, lanes_buffer)
    for tap in own_taps:
        tap.wait()
    place.meet()
    advance((0, 0), (1, 0))
    up, down = halo_copies(place, (edge_low, edge_high), (got_low, got_high), halo_sems.at[0])
    place.halos((up, down), 0)
    stats = reduce_everywhere(
        place,
        stats_in[...],
        near_one,
        far_one,
        (s10, s11, s12, s13),
        functools.partial(merge_stats, 4 * length),
        fill,
        lambda: advance((0, 1)),
    )
    stats = finish_stats(stats, 4 * length * parts)
    bn_one[...] = jnp.concatenate([stats, stats], axis=1)
    place.halos((up, down), 1)
    advance((1, 1), (0, 2), (2, 0), (3, 0))

    @pl.loop(0, windows)
    def _(w):
        m = lax.div(w, 2)
        centre = bn_one[pl.ds(m, 1), :]
        scale = bn_one[pl.ds(MB + m, 1), :] * gain_one[...]
        move = shift_one[...]

        def act(value):
            return gelu((value - centre) * scale + move).astype(bf16).astype(f32)

        main = act(x2[w].astype(f32))
        before = jnp.where(place.is_first, 0.0, act(got_low[pl.ds(w, 1), :]))
        after = jnp.where(place.is_last, 0.0, act(got_high[pl.ds(w, 1), :]))
        even, odd = main[:, :channels], main[:, channels:]
        mean = (even + odd) * 0.5
        mean_before = (before[:, :channels] + before[:, channels:]) * 0.5
        mean_after = (after[:, :channels] + after[:, channels:]) * 0.5
        row = lax.broadcasted_iota(jnp.int32, (length, channels), 0)
        top, bottom = row == 0, row == length - 1
        odd_before = jnp.where(top, before[:, channels:], pltpu.roll(odd, 1, axis=0))
        cross = (odd_before + even) * 0.5
        cross_after = (odd[length - 1 :] + after[:, :channels]) * 0.5
        start = pl.multiple_of(w * length, length)
        taps = (
            jnp.where(top, mean_before, pltpu.roll(mean, 1, axis=0)),
            cross,
            mean,
            jnp.where(bottom, cross_after, pltpu.roll(cross, length - 1, axis=0)),
            jnp.where(bottom, mean_after, pltpu.roll(mean, length - 1, axis=0)),
        )
        for t, tap in enumerate(taps):
            u_one[pl.ds(start, length), t * channels : (t + 1) * channels] = tap.astype(bf16)

    saves[0].start()
    advance((1, 2), (0, 3))
    fill(2)
    advance((1, 3), (0, 4))
    fill()
    advance((1, 4), (2, 1), (3, 1))
    saves[2].start()

    @pl.loop(0, MB)
    def _(m):
        start = pl.multiple_of(m * pair, pair)
        value = dot_nt(u_one[pl.ds(start, pair), :], w_one[...]).astype(bf16)
        pooled[pl.ds(2 * m, 2)] = value.reshape(2, length, mid)
        centre, spread = local_stats(value.astype(f32))
        stats_two[pl.ds(m, 1), :] = centre
        stats_two[pl.ds(MB + m, 1), :] = spread

    advance((2, 2), (3, 2))
    up, down = halo_copies(
        place,
        (pooled.at[:, pl.ds(0, EDGE), :], pooled.at[:, pl.ds(length - EDGE, EDGE), :]),
        (pooled_low, pooled_high),
        halo_sems.at[1],
    )
    place.halos((up, down), 0)
    stats = reduce_everywhere(
        place,
        stats_two[...],
        near_two,
        far_two,
        (s20, s21, s22, s23),
        functools.partial(merge_stats, pair),
        fill,
    )
    bn_two[...] = finish_stats(stats, pair * parts)
    place.halos((up, down), 1)
    advance((2, 3), (3, 3))

    @pl.loop(0, windows)
    def _(w):
        m = lax.div(w, 2)
        centre = bn_two[pl.ds(m, 1), :]
        scale = bn_two[pl.ds(MB + m, 1), :] * gain_two[...]
        move = shift_two[...]

        def act(value):
            return gelu((value.astype(f32) - centre) * scale + move)

        ext = jnp.concatenate(
            [
                jnp.where(place.is_first, 0.0, act(pooled_low[w])),
                act(pooled[w]),
                jnp.where(place.is_last, 0.0, act(pooled_high[w])),
            ],
            axis=0,
        )
        start = pl.multiple_of(w * length, length)
        for t in range(3):
            tap = shifted_rows(ext, EDGE + (t - 1) * DILATION, length)
            u_two[pl.ds(start, length), t * mid : (t + 1) * mid] = tap.astype(bf16)

    saves[1].start()
    advance((2, 4), (3, 4))
    saves[3].start()
    saves[4].start()

    @pl.loop(0, MB)
    def _(m):
        start = pl.multiple_of(m * pair, pair)
        value = jnp.zeros((pair, small), f32)
        for t in range(w_two.shape[0]):
            value = value + dot_nn(
                u_two[pl.ds(start, pair), t * mid : (t + 1) * mid], w_two[t]
            )
        branch[pl.ds(start, pair), :] = value
        centre, spread = local_stats(value)
        stats_three[pl.ds(m, 1), :] = centre
        stats_three[pl.ds(MB + m, 1), :] = spread
        for i in range(2):
            s_branch_edge_low[2 * m + i] = value[i * length : i * length + EDGE]
            s_branch_edge_high[2 * m + i] = value[(i + 1) * length - EDGE : (i + 1) * length]

    up, down = halo_copies(
        place,
        (s_branch_edge_low, s_branch_edge_high),
        (branch_low, branch_high),
        halo_sems.at[2],
    )
    place.halos((up, down), 0)
    stats = reduce_everywhere(
        place,
        stats_three[...],
        near_three,
        far_three,
        (s30, s31, s32, s33),
        functools.partial(merge_stats, pair),
        fill,
    )
    bn_three[...] = finish_stats(stats, pair * parts)

    @pl.loop(0, MB)
    def _(m):
        centre = bn_three[pl.ds(m, 1), :]
        scale = bn_three[pl.ds(MB + m, 1), :] * gain_three[...]
        start = pl.multiple_of(m * pair, pair)
        act = gelu((branch[pl.ds(start, pair), :] - centre) * scale + shift_three[...])
        act = act.astype(bf16)
        act_three[pl.ds(start, pair), :] = act
        lifted = dot_nt(act, w_point[...])
        here = pooled[pl.ds(2 * m, 2)].reshape(pair, mid).astype(f32)
        summed[pl.ds(start, pair), :] = (here + lifted).astype(bf16)

    place.halos((up, down), 1)
    if relay:
        relay.finish()
    for save in saves:
        save.wait()


def forward(shape, mid, order, tracks, vectors, w_one, w_two, w_point, cot):
    windows, seq_bins, channels = tracks.shape
    half = seq_bins // shape[0]
    length, wide = half // 2, 2 * channels
    rows = windows * length
    taps_two, _, small = w_two.shape
    big = [
        ((mid, w_one.shape[-1] * (w_one.shape[0] if w_one.ndim == 3 else 1)), bf16),
        ((taps_two, mid, small), bf16),
        ((mid, small), bf16),
    ]
    out = [
        ((rows, big[0][0][1]), bf16),
        ((rows, taps_two * mid), bf16),
        ((windows, length, mid), bf16),
        ((windows, EDGE, mid), bf16),
        ((windows, EDGE, mid), bf16),
        ((rows, small), f32),
        ((windows, EDGE, small), f32),
        ((windows, EDGE, small), f32),
        ((rows, small), bf16),
        ((rows, mid), bf16),
        ((2 * MB, wide), f32),
        ((2 * MB, mid), f32),
        ((2 * MB, small), f32),
    ]
    out_specs = [HBM] * 2 + [VM] * 11 + [HBM] * 3 + [VM] + [HBM] * len(cot)
    out += big + [((windows, length, wide), bf16)]
    out += [((windows, length, -(-c.shape[0] // BLOCK) * BLOCK), bf16) for c in cot]
    scratch = (
        reduce_scratch(shape, 2 * MB, wide // 2)
        + reduce_scratch(shape, 2 * MB, mid)
        + reduce_scratch(shape, 2 * MB, small)
    )
    scratch += [
        pltpu.VMEM((windows, wide), f32),
        pltpu.VMEM((windows, wide), f32),
        pltpu.VMEM((2 * MB, mid), f32),
        pltpu.VMEM((2 * MB, small), f32),
        pltpu.SemaphoreType.DMA((3, 4)),
        pltpu.VMEM((windows, EDGE, small), f32),
        pltpu.VMEM((windows, EDGE, small), f32),
        pltpu.VMEM(*out[0]),
        pltpu.VMEM(*out[1]),
    ]
    scratch += [pltpu.VMEM(*b) for b in big]
    scratch += [
        pltpu.SemaphoreType.DMA((4, 32)),
        pltpu.SemaphoreType.DMA((5,)),
        pltpu.VMEM((windows, wide), f32),
        pltpu.VMEM((windows, wide), f32),
        pltpu.VMEM((2 * MB, channels), f32),
        pltpu.VMEM((channels // LANES, half, LANES), f32),
        *(Relay.scratch(windows, length) if cot else []),
    ]
    return pl.pallas_call(
        functools.partial(forward_kernel, shape, len(cot)),
        in_specs=[pl.BlockSpec(memory_space=pltpu.SMEM), VM, VM] + [HBM] * (3 + len(cot)),
        out_specs=out_specs,
        out_shape=[jax.ShapeDtypeStruct(*o) for o in out],
        scratch_shapes=scratch,
        compiler_params=params(1),
        name="forward",
    )(order, tracks, vectors, w_one, w_two, w_point, *cot)


def heads_kernel(
    human_tracks,
    mouse_tracks,
    species,
    order,
    summed,
    w_human,
    w_mouse,
    b_human,
    b_mouse,
    cot,
    predicted,
    grad_summed,
    d_human,
    d_mouse,
    db,
    rows_sorted,
    grad_sorted,
    grad_pre,
    by_track,
    meta,
):
    j = pl.program_id(0)
    windows, length, block = cot.shape
    pair = 2 * length
    n_pairs = windows // 2
    mid = summed.shape[1]

    @pl.when(j == 0)
    def _():
        grad_sorted[...] = jnp.zeros_like(grad_sorted)
        db[...] = jnp.zeros_like(db)
        found = 0
        for kind in range(2):
            for p in range(windows):
                window = order[p]
                mine = species[window] == kind

                @pl.when(mine)
                def _(found=found, p=p, window=window):
                    meta[found] = p
                    meta[windows + found] = window

                found = found + mine.astype(jnp.int32)
            if kind == 0:
                meta[2 * windows] = found

        @pl.loop(0, windows)
        def _(s):
            source = pl.multiple_of(meta[s] * length, length)
            target = pl.multiple_of(s * length, length)
            rows_sorted[pl.ds(target, length), :] = summed[pl.ds(source, length), :]

    n_human = meta[2 * windows]
    column = lax.broadcasted_iota(jnp.int32, (1, block), 1)

    cuts = [slice(at, min(at + SPLIT, block)) for at in range(0, block, SPLIT)]

    def run(weight, bias, limit, is_mouse, first_pair, last_pair):
        def body(p, carry):
            start = pl.multiple_of(p * pair, pair)
            rows = rows_sorted[pl.ds(start, pair), :]
            mine = [s >= n_human if is_mouse else s < n_human for s in (2 * p, 2 * p + 1)]
            window = [meta[windows + 2 * p], meta[windows + 2 * p + 1]]
            pres = [dot_nn(rows, weight[:, cut]) + bias[:, cut] for cut in cuts]
            back = jnp.zeros((pair, mid), f32)
            for cut, pre in zip(cuts, pres):
                inside = column[:, cut] < limit
                decay = jnp.exp(-jnp.abs(pre))
                whole = 1.0 + decay
                inverse = 1.0 / whole
                sigmoid = jnp.where(pre >= 0, inverse, decay * inverse)
                logs = jnp.where(decay < 2.0**-11, decay, jnp.log(whole))
                output = jnp.where(inside, jnp.maximum(pre, 0.0) + logs, 0.0)
                grads = []
                for i in range(2):
                    part = slice(i * length, (i + 1) * length)
                    grad = cot[window[i], :, cut].astype(f32) * sigmoid[part]
                    grads.append(jnp.where(inside & mine[i], grad, 0.0))
                    here = output[part].T
                    spots = pl.ds(cut.start * windows + window[i], cut.stop - cut.start, windows)
                    if is_mouse:
                        here = jnp.where(mine[i], here, by_track[spots, :])
                    by_track[spots, :] = here
                grad = jnp.concatenate(grads, axis=0).astype(bf16)
                grad_pre[pl.ds(start, pair), cut] = grad
                back = back + dot_nt(grad, weight[:, cut])
            grad_sorted[pl.ds(start, pair), :] += back
            return carry

        lax.fori_loop(first_pair, last_pair, body, 0)

    def weight_grads(n_used, from_end, d_weight, bias_row):
        for n in range(n_pairs + 1):

            @pl.when(n_used == n)
            def _(n=n):
                if n == 0:
                    d_weight[...] = jnp.zeros_like(d_weight)
                else:
                    part = slice((n_pairs - n) * pair, None) if from_end else slice(0, n * pair)
                    grad = grad_pre[part, :]
                    d_weight[...] = dot_tn(rows_sorted[part, :], grad).astype(bf16)
                    total = dot_nn(jnp.ones((8, n * pair), bf16), grad)[:1]
                    db[pl.ds(bias_row, 1), :] = total

    human_pairs = lax.div(n_human + 1, 2)
    run(w_human, b_human, human_tracks - j * block, False, 0, human_pairs)
    weight_grads(human_pairs, False, d_human, j)

    @pl.when(j == 0)
    def _():
        mouse_start = lax.div(n_human, 2)
        run(w_mouse, b_mouse, mouse_tracks, True, mouse_start, n_pairs)
        weight_grads(n_pairs - mouse_start, True, d_mouse, pl.num_programs(0))

    @pl.when(j > 0)
    def _():
        def body(s, carry):
            by_track[pl.ds(meta[windows + s], block, windows), :] = jnp.zeros((block, length), f32)
            return carry

        lax.fori_loop(n_human, windows, body, 0)

    predicted[...] = by_track[...].reshape(block, windows, length).astype(bf16)

    @pl.when(j == pl.num_programs(0) - 1)
    def _():
        @pl.loop(0, windows)
        def _(s):
            source = pl.multiple_of(s * length, length)
            target = pl.multiple_of(meta[s] * length, length)
            grad_summed[pl.ds(target, length), :] = grad_sorted[pl.ds(source, length), :]


def heads(species, order, summed, w_heads, bias, cot, human_tracks, mouse_tracks):
    windows, length, _ = cot.shape
    rows, mid = summed.shape
    blocks = w_heads.shape[1] // BLOCK - 1
    smem = pl.BlockSpec(memory_space=pltpu.SMEM)
    fixed = lambda shape, at=0: pl.BlockSpec(
        shape, lambda j: (0, at), pipeline_mode=pl.Buffered(1)
    )
    return pl.pallas_call(
        functools.partial(heads_kernel, human_tracks, mouse_tracks),
        grid=(blocks,),
        in_specs=[
            smem,
            smem,
            fixed((rows, mid)),
            pl.BlockSpec((mid, BLOCK), lambda j: (0, j)),
            fixed((mid, BLOCK), blocks),
            pl.BlockSpec((1, BLOCK), lambda j: (0, j)),
            fixed((1, BLOCK), blocks),
            pl.BlockSpec((windows, length, BLOCK), lambda j: (0, 0, j)),
        ],
        out_specs=[
            pl.BlockSpec((BLOCK, windows, length), lambda j: (j, 0, 0)),
            pl.BlockSpec((rows, mid), lambda j: (0, 0)),
            pl.BlockSpec((mid, BLOCK), lambda j: (0, j)),
            pl.BlockSpec((mid, BLOCK), lambda j: (0, 0)),
            pl.BlockSpec((8, BLOCK), lambda j: (0, 0)),
        ],
        scratch_shapes=[
            pltpu.VMEM((rows, mid), bf16),
            pltpu.VMEM((rows, mid), f32),
            pltpu.VMEM((rows, BLOCK), bf16),
            pltpu.VMEM((BLOCK * windows, length), f32),
            pltpu.SMEM((2 * windows + 1,), jnp.int32),
        ],
        out_shape=[
            jax.ShapeDtypeStruct((human_tracks, windows, length), bf16),
            jax.ShapeDtypeStruct((rows, mid), f32),
            jax.ShapeDtypeStruct((mid, blocks * BLOCK), bf16),
            jax.ShapeDtypeStruct((mid, BLOCK), bf16),
            jax.ShapeDtypeStruct((8, BLOCK), f32),
        ],
        compiler_params=params(),
        name="heads",
    )(species, order, summed, w_heads, w_heads, bias, bias, cot)


HAND, LOAD = 7, 8
WHOLE = (0, 1, 2, 3, 4, 5, 6)
PLANE = (0, 1, 2, HAND)
ALONG = (LOAD, 3, 4, 5, 6)


class Summing:
    def __init__(self, place, plan, source, start, width, target, to, scratch):
        self.place, self.plan, self.source, self.target = place, plan, source, target
        self.columns = pl.ds(start, width)
        self.width, self.to = width, to
        for name, ref in zip(self.names(plan), scratch):
            setattr(self, name, ref)
        half = self.own.shape[2]
        self.half, self.part = half, half // 2
        self.mine = pl.ds(pl.multiple_of(place.sec * half, half), half)
        self.other = pl.ds(pl.multiple_of((1 - place.sec) * half, half), half)
        self.x, self.y = lax.rem(place.dp, 2), lax.div(place.dp, 2)
        self.cell = (self.y, self.x) if 0 in plan else (0, 0)
        self.top, self.bottom = pl.ds(0, self.part), pl.ds(self.part, self.part)
        self.at_end = (place.seq == 0) | (place.seq == place.n_seq - 1)
        self.between = jnp.logical_not(self.at_end)

    @staticmethod
    def names(plan):
        names = ["own"]
        if 0 in plan:
            names += ["core", "side_a", "side_b", "end_a", "end_b"]
        if 6 in plan:
            names += ["z_one", "z_far", "mate"]
        return names + ["sems"]

    @staticmethod
    def scratch(plan, share, width):
        half = share // 2
        part = half // 2
        cells = 2 if 0 in plan else 1
        shapes = dict(
            own=(cells, cells, half, width),
            core=(2, 2, half, width),
            side_a=(2, part, width),
            side_b=(2, part, width),
            end_a=(part, width),
            end_b=(part, width),
            z_one=(half, width),
            z_far=(half, width),
            mate=(half, width),
        )
        refs = [pltpu.VMEM(shapes[name], bf16) for name in Summing.names(plan)[:-1]]
        return refs + [pltpu.SemaphoreType.DMA((23,))]

    def remote(self, source, target, sem, device):
        return pltpu.make_async_remote_copy(
            src_ref=source,
            dst_ref=target,
            send_sem=self.sems.at[2 * sem],
            recv_sem=self.sems.at[2 * sem + 1],
            device_id=device,
            device_id_type=MESH,
        )

    def copies(self, stage):
        p, own, x, y = self.place, self.own, self.x, self.y
        sibling = (1 - p.sec, p.seq, p.dp)
        over_x = (p.sec, p.seq, p.dp + 1 - 2 * x)
        over_y = (p.sec, p.seq, p.dp + 2 - 4 * y)
        over_z = (p.sec, p.seq + 1 - 2 * lax.rem(p.seq, 2), p.dp)
        if stage == 0:
            return [
                pltpu.make_async_copy(
                    self.source.at[:, :, self.mine, self.columns], own, self.sems.at[16]
                ),
                self.remote(
                    self.source.at[:, :, self.other, self.columns], self.core, 0, sibling
                ),
            ]
        if stage == 1:
            return [
                self.remote(own.at[:, 1 - x, self.top], self.side_a, 1, over_x),
                self.remote(own.at[1 - y, :, self.bottom], self.side_b, 2, over_y),
            ]
        if stage == 2:
            return [
                self.remote(own.at[1 - y, x, self.top], self.end_a, 3, over_y),
                self.remote(own.at[y, 1 - x, self.bottom], self.end_b, 4, over_x),
            ]
        if stage == HAND:
            columns = pl.ds(self.to, self.width)
            return [
                pltpu.make_async_copy(
                    own.at[self.cell], self.target.at[:, columns], self.sems.at[17]
                )
            ]
        if stage == LOAD:
            return [
                pltpu.make_async_copy(
                    self.source.at[:, self.columns], own.at[self.cell], self.sems.at[17]
                )
            ]
        if stage == 3:
            return [self.remote(own.at[self.cell], self.z_one, 5, over_z)]
        if stage == 4:
            opposite = (p.sec, p.n_seq - 1 - p.seq, p.dp)
            return [self.remote(own.at[self.cell], self.z_far, 6, opposite)]
        if stage == 5:
            return [self.remote(own.at[self.cell], self.z_one, 5, over_z)]
        return [
            self.remote(source, self.mate, 7, sibling) for source in (own.at[self.cell], self.z_one)
        ]

    def start(self, stage):
        copies = self.copies(stage)
        if stage == 3:
            pl.when(self.at_end)(copies[0].start)
        elif stage in (4, 5):
            pl.when(self.between)(copies[0].start)
        elif stage == 6:
            pl.when(self.between)(copies[0].start)
            pl.when(self.at_end)(copies[1].start)
        else:
            for copy in copies:
                copy.start()

    def add(self, at, other):
        self.own[at] = (self.own[at].astype(f32) + other.astype(f32)).astype(bf16)

    def finish(self, stage):
        copies = self.copies(stage)
        x, y = self.x, self.y
        if stage == 3:
            pl.when(self.at_end)(copies[0].wait_send)

            @pl.when(self.between)
            def _():
                copies[0].wait_recv()
                self.add(self.cell, self.z_one[...])

        elif stage == 4:

            @pl.when(self.between)
            def _():
                copies[0].wait()
                self.add(self.cell, self.z_far[...])

        elif stage == 5:
            pl.when(self.between)(copies[0].wait_send)
            pl.when(self.at_end)(copies[0].wait_recv)
        elif stage == 6:
            copies[0].wait()
            pl.when(self.between)(self.results(self.own.at[self.cell])[0].start)
            pl.when(self.at_end)(self.results(self.z_one)[0].start)
            self.results(self.z_one)[1].start()
        elif stage != HAND:
            for copy in copies:
                copy.wait()
        if stage == 0:

            @pl.loop(0, 4)
            def _(i):
                a, b = lax.div(i, 2), lax.rem(i, 2)
                self.add((a, b), self.core[a, b])

        elif stage == 1:
            for i in range(2):
                self.add((i, x, self.top), self.side_a[i])
                self.add((y, i, self.bottom), self.side_b[i])
        elif stage == 2:
            self.add((y, x, self.top), self.end_a[...])
            self.add((y, x, self.bottom), self.end_b[...])

    def results(self, source):
        copies = []
        for i, (ref, rows) in enumerate(((source, self.mine), (self.mate, self.other))):
            if len(self.target.shape) == 3:
                target = self.target.at[self.to, rows]
            else:
                target = self.target.at[rows, pl.ds(self.to, self.width)]
            copies.append(pltpu.make_async_copy(ref, target, self.sems.at[18 + i]))
        return copies

    def close(self):
        copies = self.results(self.mate) if 6 in self.plan else self.copies(HAND)
        for copy in copies:
            copy.wait()


class Sums:
    def __init__(self, place, sources, targets, chunks, refs):
        self.parts = []
        for plan, begin, source, start, width, target, to in chunks:
            count = len(Summing.names(plan))
            part = Summing(
                place, plan, sources[source], start, width, targets[target], to, refs[:count]
            )
            refs = refs[count:]
            self.parts.append((begin, part))
        self.parts.sort(key=lambda item: -item[0])
        self.last = max([begin + len(part.plan) for begin, part in self.parts], default=-1)
        self.tick = 0

    def step(self):
        if self.tick > self.last:
            return
        for begin, part in self.parts:
            i = self.tick - begin
            if 0 < i <= len(part.plan):
                part.finish(part.plan[i - 1])
            if 0 <= i < len(part.plan):
                part.start(part.plan[i])
        self.tick += 1

    def finish(self):
        while self.tick <= self.last:
            self.step()
        for _, part in self.parts:
            part.close()


def sums_scratch(share, chunks):
    return [ref for chunk in chunks for ref in Summing.scratch(chunk[0], share, chunk[4])]


def count_refs(chunks):
    return sum(len(Summing.names(chunk[0])) for chunk in chunks)


def head_chunks(human_wide):
    size = BLOCK // 2
    pieces = [(0, at) for at in range(0, human_wide, size)] + [(1, 0), (1, size)]
    n_whole = len(pieces) // 2 + 1
    chunks = []
    for k, (source, at) in enumerate(pieces):
        whole = k < n_whole
        to = (k if whole else k - n_whole) * size
        chunks.append((WHOLE if whole else PLANE, k, source, at, size, 0 if whole else 1, to))
    return chunks, n_whole * size, (len(pieces) - n_whole) * size


def split_refs(refs, *counts):
    groups = []
    for count in counts:
        groups.append(refs[:count])
        refs = refs[count:]
    assert not refs
    return groups


def back_high_kernel(shape, n_sums, chunks, *refs):
    (sources, big_in, small_in, targets, d_outs, outs, fixed, sum_refs) = split_refs(
        refs, n_sums, 3, 12, n_sums, 3, 3, 37, count_refs(chunks)
    )
    in_grad, in_u_one, in_u_two = big_in
    (
        act_three,
        branch,
        branch_low,
        branch_high,
        bn_three,
        w_point,
        w_two,
        pooled,
        pooled_low,
        pooled_high,
        bn_two,
        vectors,
    ) = small_in
    grad_ext, sums_three, sums_two = outs
    reduce_three, reduce_two, fixed = fixed[:6], fixed[6:12], fixed[12:]
    (
        grad_summed,
        u_any,
        du_three,
        edge_low,
        edge_high,
        du_low,
        du_high,
        row_low,
        row_high,
        gs_low,
        gs_high,
        local_three,
        grad_branch,
        du_two,
        row_low_two,
        row_high_two,
        dlow_two,
        dhigh_two,
        local_two,
        grad_main,
        d_point,
        d_two,
        d_one,
        halo_sems,
        copy_sems,
    ) = fixed
    place = Place(shape)
    place.greet()
    windows, length, mid = pooled.shape
    small = branch.shape[1]
    pair = 2 * length
    taps = w_two.shape[0] // mid
    scale = 1.0 / (pair * shape[0] * shape[1] * shape[2])
    row = lambda index, width: vectors.at[index : index + 1, :width]
    gain_two, shift_two = row(2, mid), row(3, mid)
    gain_three, shift_three = row(4, small), row(5, small)
    u_two = u_any.at[:, : taps * mid]
    load_grad = pltpu.make_async_copy(in_grad, grad_summed, copy_sems.at[0])
    load_two = pltpu.make_async_copy(in_u_two, u_two, copy_sems.at[1])
    load_one = pltpu.make_async_copy(in_u_one, u_any, copy_sems.at[2])
    save_point, save_two, save_one = [
        pltpu.make_async_copy(a, b, copy_sems.at[3 + i])
        for i, (a, b) in enumerate(((d_point, d_outs[0]), (d_two, d_outs[1]), (d_one, d_outs[2])))
    ]
    load_grad.start()
    load_two.start()
    sums = Sums(place, sources, targets, chunks, sum_refs)
    place.meet()
    sums.step()
    load_grad.wait()

    for m in range(MB):
        at = slice(m * pair, (m + 1) * pair)
        grad = grad_summed[at, :]
        back = dot_nn(grad.astype(bf16), w_point[...])
        xhat = (branch[at, :] - bn_three[m : m + 1, :]) * bn_three[MB + m : MB + m + 1, :]
        du = gelu_slope(xhat * gain_three[...] + shift_three[...]) * back
        du_three[at, :] = du
        local_three[m : m + 1, :] = jnp.sum(du, axis=0, keepdims=True)
        local_three[MB + m : MB + m + 1, :] = jnp.sum(du * xhat, axis=0, keepdims=True)
        for i in range(2):
            w = 2 * m + i
            edge_low[w] = du[i * length : i * length + EDGE]
            edge_high[w] = du[(i + 1) * length - EDGE : (i + 1) * length]
            row_low[w : w + 1, :] = grad[i * length : i * length + 1]
            row_high[w : w + 1, :] = grad[(i + 1) * length - 1 : (i + 1) * length]

    moves = halo_copies(place, (edge_low, edge_high), (du_low, du_high), halo_sems.at[0])
    moves += halo_copies(place, (row_low, row_high), (gs_low, gs_high), halo_sems.at[1])
    place.halos(moves, 0)
    sums_three[...] = reduce_everywhere(
        place, local_three[...], *reduce_three[:2], reduce_three[2:], add_up, sums.step
    )
    d_point[...] = dot_tn(grad_summed[...].astype(bf16), act_three[...]).astype(bf16)
    save_point.start()
    place.halos(moves, 1)
    sums.step()

    for m in range(MB):
        at = slice(m * pair, (m + 1) * pair)
        centre, inverse = bn_three[m : m + 1, :], bn_three[MB + m : MB + m + 1, :]
        factor = gain_three[...] * inverse
        mean_du = sums_three[m : m + 1, :] * scale
        mean_dx = sums_three[MB + m : MB + m + 1, :] * scale

        def back(du, value):
            xhat = (value - centre) * inverse
            return factor * (du - mean_du - xhat * mean_dx)

        main = back(du_three[at, :], branch[at, :])
        grad_branch[at, :] = main.astype(bf16)
        pieces = []
        for i in range(2):
            w = 2 * m + i
            low = jnp.where(place.is_first, 0.0, back(du_low[w], branch_low[w]))
            high = jnp.where(place.is_last, 0.0, back(du_high[w], branch_high[w]))
            pieces += [low, main[i * length : (i + 1) * length], high]
        ext = jnp.concatenate(pieces, axis=0).astype(bf16)
        span = length + 2 * EDGE
        through = [dot_nt(ext, w_two[t * mid : (t + 1) * mid, :]) for t in range(taps)]
        centre_two, inverse_two = bn_two[m : m + 1, :], bn_two[MB + m : MB + m + 1, :]
        total_du = jnp.zeros((1, mid), f32)
        total_dx = jnp.zeros((1, mid), f32)
        for i in range(2):
            w = 2 * m + i
            grad = jnp.zeros((length, mid), f32)
            for t in range(taps):
                whole = through[t][i * span : (i + 1) * span]
                grad = grad + shifted_rows(whole, EDGE - (t - 1) * DILATION, length)
            xhat = (pooled[w].astype(f32) - centre_two) * inverse_two
            du = gelu_slope(xhat * gain_two[...] + shift_two[...]) * grad
            du_two[w] = du
            total_du = total_du + jnp.sum(du, axis=0, keepdims=True)
            total_dx = total_dx + jnp.sum(du * xhat, axis=0, keepdims=True)
            row_low_two[w : w + 1, :] = du[:1]
            row_high_two[w : w + 1, :] = du[length - 1 :]
        local_two[m : m + 1, :] = total_du
        local_two[MB + m : MB + m + 1, :] = total_dx
        if m == 1:
            sums.step()

    moves = halo_copies(
        place, (row_low_two, row_high_two), (dlow_two, dhigh_two), halo_sems.at[2]
    )
    place.halos(moves, 0)
    sums_two[...] = reduce_everywhere(
        place, local_two[...], *reduce_two[:2], reduce_two[2:], add_up, sums.step
    )
    load_two.wait()
    for t in range(taps):
        part = dot_tn(u_two[:, t * mid : (t + 1) * mid], grad_branch[...])
        d_two[:, t * small : (t + 1) * small] = part.astype(bf16)
    save_two.start()
    load_one.start()
    place.halos(moves, 1)
    sums.step()

    for m in range(MB):
        centre, inverse = bn_two[m : m + 1, :], bn_two[MB + m : MB + m + 1, :]
        factor = gain_two[...] * inverse
        mean_du = sums_two[m : m + 1, :] * scale
        mean_dx = sums_two[MB + m : MB + m + 1, :] * scale

        def back(du, value, extra):
            xhat = (value.astype(f32) - centre) * inverse
            return factor * (du - mean_du - xhat * mean_dx) + extra

        edges = []
        for i in range(2):
            w = 2 * m + i
            at = slice(w * length, (w + 1) * length)
            value = back(du_two[w], pooled[w], grad_summed[at, :]).astype(bf16)
            grad_ext[m, i * length : (i + 1) * length, :] = value
            grad_main[at, :] = value
            row = slice(w, w + 1)
            low = back(dlow_two[row, :], pooled_low[w].astype(f32)[EDGE - 1 :], gs_low[row, :])
            high = back(dhigh_two[row, :], pooled_high[w].astype(f32)[:1], gs_high[row, :])
            edges += [jnp.where(place.is_first, 0.0, low), jnp.where(place.is_last, 0.0, high)]
        row = lax.broadcasted_iota(jnp.int32, (EDGE, mid), 0)
        block = jnp.zeros((EDGE, mid), f32)
        for i, edge in enumerate(edges):
            block = jnp.where(row == i, edge, block)
        grad_ext[m, pair : pair + EDGE, :] = block.astype(bf16)
    sums.step()
    load_one.wait()
    columns = d_one.shape[1] // 5
    for t in range(5):
        part = slice(t * columns, (t + 1) * columns)
        d_one[:, part] = dot_tn(grad_main[...], u_any[:, part]).astype(bf16)
        if t in (1, 3):
            sums.step()
    save_one.start()
    sums.finish()
    save_point.wait()
    save_two.wait()
    save_one.wait()


def back_high(shape, sources, grad_summed, u_one, u_two, three, two):
    branch = three[1]
    w_two, pooled = two[0], two[1]
    windows, length, mid = pooled.shape
    rows, small = branch.shape
    share = mid // shape[2]
    chunks, targets = [], []
    if sources:
        chunks, n_whole, n_plane = head_chunks(sources[0].shape[3])
        targets = [((share, n_whole), bf16), ((share // 2, n_plane), bf16)]
    taps = w_two.shape[0] // mid
    d_shapes = [((mid, small), bf16), ((mid, taps * small), bf16), ((mid, u_one.shape[1]), bf16)]
    outs = [
        ((MB, 2 * length + EDGE, mid), bf16),
        ((2 * MB, small), f32),
        ((2 * MB, mid), f32),
    ]
    fixed = reduce_scratch(shape, 2 * MB, small) + reduce_scratch(shape, 2 * MB, mid)
    fixed += [
        pltpu.VMEM(*a)
        for a in [
            ((rows, mid), f32),
            (u_one.shape, bf16),
            ((rows, small), f32),
            ((windows, EDGE, small), f32),
            ((windows, EDGE, small), f32),
            ((windows, EDGE, small), f32),
            ((windows, EDGE, small), f32),
            ((windows, mid), f32),
            ((windows, mid), f32),
            ((windows, mid), f32),
            ((windows, mid), f32),
            ((2 * MB, small), f32),
            ((rows, small), bf16),
            ((windows, length, mid), f32),
            ((windows, mid), f32),
            ((windows, mid), f32),
            ((windows, mid), f32),
            ((windows, mid), f32),
            ((2 * MB, mid), f32),
            ((rows, mid), bf16),
            *d_shapes,
        ]
    ]
    fixed += [pltpu.SemaphoreType.DMA((3, 4)), pltpu.SemaphoreType.DMA((6,))]
    return pl.pallas_call(
        functools.partial(back_high_kernel, shape, len(sources), chunks),
        in_specs=[HBM] * (3 + len(sources)) + [VM] * 12,
        out_specs=[HBM] * (3 + len(sources)) + [VM] * 3,
        out_shape=[jax.ShapeDtypeStruct(*o) for o in targets + d_shapes + outs],
        scratch_shapes=fixed + sums_scratch(share, chunks),
        compiler_params=params(2),
        name="back_high",
    )(*sources, grad_summed, u_one, u_two, *three, *two)


def back_low_kernel(shape, n_sums, chunks, *refs):
    (sources, ins, targets, outs, reduce_one, reduce_b, fixed, sum_refs) = split_refs(
        refs, n_sums, 7, n_sums, 3, 6, 6, 5, count_refs(chunks)
    )
    order, in_one, grad_ext, x2, bn_one, vectors, bias_sums = ins
    grad_input, sums_one, bias_out = outs
    w_one, du_one, local, lanes_buffer, load_sem = fixed
    place = Place(shape)
    place.greet()
    windows, length, wide = x2.shape
    channels = wide // 2
    pair = 2 * length
    gain_one, shift_one = vectors.at[0:1, :wide], vectors.at[1:2, :wide]
    load_one = pltpu.make_async_copy(in_one, w_one, load_sem)
    load_one.start()
    sums = Sums(place, sources, targets, chunks, sum_refs)
    place.meet()
    sums.step()
    load_one.wait()

    for m in range(MB):
        through = [
            dot_nn(grad_ext[m], w_one[:, t * channels : (t + 1) * channels]) for t in range(5)
        ]
        centre, inverse = bn_one[m : m + 1, :], bn_one[MB + m : MB + m + 1, :]
        total_du = jnp.zeros((1, wide), f32)
        total_dx = jnp.zeros((1, wide), f32)
        row = lax.broadcasted_iota(jnp.int32, (length, channels), 0)
        top, bottom = row == 0, row == length - 1
        for i in range(2):
            w = 2 * m + i
            main = [t[i * length : (i + 1) * length] for t in through]
            low = [t[pair + 2 * i : pair + 2 * i + 1] for t in through]
            high = [t[pair + 2 * i + 1 : pair + 2 * i + 2] for t in through]
            later = lambda t: jnp.where(bottom, high[t], pltpu.roll(main[t], length - 1, axis=0))
            earlier = lambda t: jnp.where(top, low[t], pltpu.roll(main[t], 1, axis=0))
            mean = later(0) + main[2] + earlier(4)
            cross = main[1] + earlier(3)
            cross_end = high[1] + main[3][length - 1 :]
            cross_later = jnp.where(bottom, cross_end, pltpu.roll(cross, length - 1, axis=0))
            grad = jnp.concatenate([(mean + cross) * 0.5, (mean + cross_later) * 0.5], axis=1)
            xhat = (x2[w].astype(f32) - centre) * inverse
            du = gelu_slope(xhat * gain_one[...] + shift_one[...]) * grad
            du_one[w] = du
            total_du = total_du + jnp.sum(du, axis=0, keepdims=True)
            total_dx = total_dx + jnp.sum(du * xhat, axis=0, keepdims=True)
        local[m : m + 1, :] = total_du[:, :channels] + total_du[:, channels:]
        local[MB + m : MB + m + 1, :] = total_dx[:, :channels] + total_dx[:, channels:]
        sums.step()

    sums_one[...] = reduce_everywhere(
        place, local[...], *reduce_one[:2], reduce_one[2:], add_up, sums.step
    )
    scale = 1.0 / (4 * length * shape[0] * shape[1] * shape[2])
    lanes = lanes_buffer.shape[0]
    twice = lambda v: jnp.concatenate([v, v], axis=1)

    def write(window):
        w = 0
        for p in range(1, windows):
            w = jnp.where(order[p] == window, p, w)
        m = lax.div(w, 2)
        mean_du = twice(sums_one[pl.ds(m, 1), :]) * scale
        mean_dx = twice(sums_one[pl.ds(MB + m, 1), :]) * scale
        inverse = bn_one[pl.ds(MB + m, 1), :]
        xhat = (x2[w].astype(f32) - bn_one[pl.ds(m, 1), :]) * inverse
        grad = gain_one[...] * inverse * (du_one[w] - mean_du - xhat * mean_dx)
        for odd in range(2):
            for c in range(lanes):
                at = odd * channels + c * LANES
                lanes_buffer[c, pl.ds(odd, length, 2), :] = grad[:, at : at + LANES]
        for c in range(lanes):
            grad_input[window, :, c * LANES : (c + 1) * LANES] = lanes_buffer[c].astype(bf16)

    for half in range(2):
        sums.step()

        @pl.loop(half * windows // 2, (half + 1) * windows // 2)
        def _(window):
            write(window)

    bias_out[...] = reduce_everywhere(
        place, bias_sums[...], *reduce_b[:2], reduce_b[2:], add_up, sums.step
    )
    sums.finish()


def back_low(shape, sources, order, w_one, grad_ext, x2, bn_one, vectors, bias_sums):
    windows, length, wide = x2.shape
    channels = wide // 2
    share = grad_ext.shape[2] // shape[2]
    chunks, targets = [], []
    if sources:
        columns = sources[0].shape[1]
        size = BLOCK // 2
        chunks = [(ALONG, i // 2, 0, i * size, size, 0, i * size) for i in range(columns // size)]
        targets = [((share, columns), bf16)]
        begin = 0
        for i, taps in enumerate((1, 3, w_one.shape[1] // channels), 1):
            width = sources[i].shape[3] // taps
            for t in range(taps):
                begin += width > share * 2
                chunks.append((WHOLE, begin, i, t * width, width, i, t))
            targets.append(((taps, share, width), bf16))
    outs = [((windows, 2 * length, channels), bf16), ((2 * MB, channels), f32)]
    outs += [(bias_sums.shape, f32)]
    scratch = reduce_scratch(shape, 2 * MB, channels) + reduce_scratch(shape, *bias_sums.shape)
    scratch += [
        pltpu.VMEM(w_one.shape, bf16),
        pltpu.VMEM((windows, length, wide), f32),
        pltpu.VMEM((2 * MB, channels), f32),
        pltpu.VMEM((channels // LANES, 2 * length, LANES), f32),
        pltpu.SemaphoreType.DMA,
    ]
    smem = pl.BlockSpec(memory_space=pltpu.SMEM)
    return pl.pallas_call(
        functools.partial(back_low_kernel, shape, len(sources), chunks),
        in_specs=[HBM] * len(sources) + [smem, HBM] + [VM] * 5,
        out_specs=[HBM] * len(sources) + [VM] * 3,
        out_shape=[jax.ShapeDtypeStruct(*o) for o in targets + outs],
        scratch_shapes=scratch + sums_scratch(share, chunks),
        compiler_params=params(3),
        name="back_low",
    )(*sources, order, w_one, grad_ext, x2, bn_one, vectors, bias_sums)


def per_device(
    shape,
    tracks,
    species,
    batch_order,
    conv_one,
    dilated_kernel,
    point_wise,
    head_human,
    head_mouse,
    bias_human,
    bias_mouse,
    gain_one,
    shift_one,
    gain_two,
    shift_two,
    gain_three,
    shift_three,
    cotangent,
):
    sec = lax.axis_index("section").astype(jnp.int32)
    windows, seq_bins, channels = tracks.shape
    half = seq_bins // 2
    length = half // 2
    human_tracks, mouse_tracks = head_human.shape[1], head_mouse.shape[1]
    human_wide = -(-human_tracks // BLOCK) * BLOCK
    share = conv_one.shape[2]
    mid = share * shape[2]

    taps_one = conv_one.shape[0]
    shard_one = jnp.transpose(conv_one, (0, 2, 1))
    shard_point = point_wise.T
    shard_heads = jnp.concatenate(
        [
            jnp.pad(head_human, ((0, 0), (0, human_wide - human_tracks))),
            jnp.pad(head_mouse, ((0, 0), (0, BLOCK - mouse_tracks))),
        ],
        axis=1,
    )
    half_rows = share // shape[0]
    half_heads = lax.dynamic_slice_in_dim(shard_heads, sec * half_rows, half_rows, 0)
    w_heads = lax.all_gather(half_heads, ("dp", "section"), axis=0, tiled=True)
    weights = [shard_one, dilated_kernel, shard_point]
    if shape != (2, 4, 4):
        weights[0] = jnp.transpose(conv_one, (2, 0, 1)).reshape(share, taps_one * channels)
        weights = [lax.all_gather(w, "dp", axis=w.ndim - 2, tiled=True) for w in weights]

    wide = 2 * channels
    vectors = jnp.stack(
        [
            jnp.pad(v, (0, wide - v.shape[0]))
            for v in (
                jnp.tile(gain_one, 2),
                jnp.tile(shift_one, 2),
                gain_two,
                shift_two,
                gain_three,
                shift_three,
            )
        ]
    )
    native = jnp.transpose(cotangent, (2, 0, 1))
    relay = [native] if length % LANES == 0 else []
    (
        u_one,
        u_two,
        pooled,
        pooled_low,
        pooled_high,
        branch,
        branch_low,
        branch_high,
        act_three,
        summed,
        bn_one,
        bn_two,
        bn_three,
        w_one,
        w_two,
        w_point,
        x2,
        *cot,
    ) = forward(shape, mid, batch_order, tracks, vectors, *weights, relay)
    if not cot:
        half_cot = lax.dynamic_slice_in_dim(cotangent, sec * length, length, 1)
        cot = [jnp.pad(half_cot, ((0, 0), (0, 0), (0, human_wide - human_tracks)))]
    w_two = w_two.reshape(-1, w_two.shape[2])

    wide_bias = jnp.concatenate(
        [
            jnp.pad(bias_human, (0, human_wide - human_tracks)),
            jnp.pad(bias_mouse, (0, BLOCK - mouse_tracks)),
        ]
    ).reshape(1, -1)
    predicted, grad_summed, d_human, d_mouse, bias_sums = heads(
        species, batch_order, summed, w_heads, wide_bias, cot[0], human_tracks, mouse_tracks
    )


    def in_kernel(*grads):
        if shape != (2, 4, 4):
            return []
        return [g.reshape(2, 2, -1, g.shape[1]) for g in grads]

    def summed_up(*grads):
        parts = [lax.psum_scatter(g, "dp", scatter_dimension=0, tiled=True) for g in grads]
        return [lax.psum(part, ("section", "seq")) for part in parts]

    def by_tap(grad, taps):
        grad = grad.astype(f32)
        if grad.ndim == 2:
            grad = jnp.transpose(grad.reshape(share, taps, -1), (1, 0, 2))
        return grad

    *heads_summed, d_point, d_two, d_one, grad_ext, sums_three, sums_two = back_high(
        shape,
        in_kernel(d_human, d_mouse),
        grad_summed,
        u_one,
        u_two,
        (act_three, branch, branch_low, branch_high, bn_three, w_point),
        (w_two, pooled, pooled_low, pooled_high, bn_two, vectors),
    )
    *sums_low, grad_input, sums_one, bias_out = back_low(
        shape,
        heads_summed[1:] + in_kernel(d_point, d_two, d_one),
        batch_order,
        w_one,
        grad_ext,
        x2,
        bn_one,
        vectors,
        bias_sums,
    )
    if sums_low:
        rest, r_point, r_two, r_one = sums_low
        all_heads = jnp.concatenate([heads_summed[0], rest], axis=1)
        r_human, r_mouse = all_heads[:, :human_wide], all_heads[:, human_wide:]
    else:
        r_human, r_mouse, r_point, r_two, r_one = summed_up(d_human, d_mouse, d_point, d_two, d_one)
    r_human = r_human[:, :human_tracks].astype(f32)
    r_mouse = r_mouse[:, :mouse_tracks].astype(f32)
    r_point = by_tap(r_point, 1)[0]
    r_two = by_tap(r_two, dilated_kernel.shape[0])
    r_one = by_tap(r_one, taps_one)
    r_point = r_point.T
    r_one = jnp.transpose(r_one, (0, 2, 1))
    bias_human_grad = bias_out[: human_wide // BLOCK].reshape(-1)[:human_tracks]
    bias_mouse_grad = bias_out[human_wide // BLOCK, :mouse_tracks]
    return (
        jnp.transpose(predicted, (1, 2, 0)),
        grad_input,
        r_one,
        r_two,
        r_point,
        r_human,
        r_mouse,
        bias_human_grad,
        bias_mouse_grad,
        jnp.sum(sums_one[MB:], axis=0),
        jnp.sum(sums_one[:MB], axis=0),
        jnp.sum(sums_two[MB:], axis=0),
        jnp.sum(sums_two[:MB], axis=0),
        jnp.sum(sums_three[MB:], axis=0),
        jnp.sum(sums_three[:MB], axis=0),
    )


def solution(mesh):
    shape = (mesh.shape["section"], mesh.shape["seq"], mesh.shape["dp"])
    placed = (
        P("dp", "seq", None),
        P("dp"),
        P(),
        P(None, None, "dp"),
        P(None, "dp", None),
        P(None, "dp"),
        P("dp", None),
        P("dp", None),
    ) + (P(),) * 8 + (P("dp", "seq", None),)
    return jax.shard_map(
        functools.partial(per_device, shape),
        mesh=mesh,
        in_specs=placed,
        out_specs=(
            P("dp", ("seq", "section"), None),
            P("dp", ("seq", "section"), None),
            P(None, None, "dp"),
            P(None, "dp", None),
            P(None, "dp"),
            P("dp", None),
            P("dp", None),
        )
        + (P(),) * 8,
        check_vma=False,
    )
```

```python
import functools
import math

import jax
import jax.numpy as jnp
from jax import lax
from jax.experimental import pallas as pl
from jax.experimental.pallas import tpu as pltpu
from jax.sharding import PartitionSpec as P

MESH = pl.DeviceIdType.MESH
DILATION = 11
MB = 4
EPS = 1e-05
EDGE = 16
BLOCK = 1792
SPLIT = 512
LANES = 128
VMEM_LIMIT = 60 * 1024 * 1024
GELU_K = math.sqrt(2.0 / math.pi)
GELU_C = 0.044715
f32 = jnp.float32
bf16 = jnp.bfloat16
VM = pl.BlockSpec(memory_space=pltpu.VMEM)
HBM = pl.BlockSpec(memory_space=pl.ANY)


def params(collective_id=None, limit=VMEM_LIMIT):
    if collective_id is None:
        return pltpu.CompilerParams(vmem_limit_bytes=limit)
    return pltpu.CompilerParams(
        vmem_limit_bytes=limit, collective_id=collective_id, has_side_effects=True
    )


def gelu(u):
    t = jnp.tanh(u * (GELU_K + (GELU_K * GELU_C) * (u * u)))
    h = 0.5 * u
    return h + h * t


def gelu_slope(u):
    uu = u * u
    t = jnp.tanh(u * (GELU_K + (GELU_K * GELU_C) * uu))
    return 0.5 * (1.0 + t) + (0.5 * u) * (1.0 - t * t) * (GELU_K + (3.0 * GELU_K * GELU_C) * uu)


def dot_nn(a, b):
    return jnp.dot(a, b, preferred_element_type=f32)


def dot_nt(a, b):
    return lax.dot_general(a, b, (((1,), (1,)), ((), ())), preferred_element_type=f32)


def dot_tn(a, b):
    return lax.dot_general(a, b, (((0,), (0,)), ((), ())), preferred_element_type=f32)


class Place:
    def __init__(self, shape):
        self.n_sec, self.n_seq, self.n_dp = shape
        self.n_near = self.n_sec * self.n_dp
        self.sec = lax.axis_index("section")
        self.seq = lax.axis_index("seq")
        self.dp = lax.axis_index("dp")
        self.near = self.sec * self.n_dp + self.dp
        n_bins = self.n_seq * self.n_sec
        bins = self.seq * self.n_sec + self.sec
        self.is_first = bins == 0
        self.is_last = bins == n_bins - 1
        low = lax.rem(bins + n_bins - 1, n_bins)
        high = lax.rem(bins + 1, n_bins)
        self.low = self.bin_device(low)
        self.high = self.bin_device(high)
        across = jnp.where(self.sec == 0, low, high)
        self.across = self.bin_device(across)

    def halos(self, moves, action):
        for up, down in zip(moves[::2], moves[1::2]):
            if action == 0:
                pl.when(jnp.logical_not(self.is_last))(up.start)
                pl.when(jnp.logical_not(self.is_first))(down.start)
            else:
                for first, last in ((up.wait_send, up.wait_recv), (down.wait_recv, down.wait_send)):
                    pl.when(jnp.logical_not(self.is_last))(first)
                    pl.when(jnp.logical_not(self.is_first))(last)

    def bin_device(self, bins):
        return (lax.rem(bins, self.n_sec), lax.div(bins, self.n_sec), self.dp)

    def near_device(self, rank):
        return (lax.div(rank, self.n_dp), self.seq, lax.rem(rank, self.n_dp))

    def greet(self):
        barrier = pltpu.get_barrier_semaphore()
        for k in range(1, self.n_near):
            rank = lax.rem(self.near + k, self.n_near)
            pl.semaphore_signal(
                barrier, inc=1, device_id=self.near_device(rank), device_id_type=MESH
            )
        for k in range(1, self.n_seq):
            seq = lax.rem(self.seq + k, self.n_seq)
            pl.semaphore_signal(
                barrier, inc=1, device_id=(self.sec, seq, self.dp), device_id_type=MESH
            )
        pl.semaphore_signal(barrier, inc=1, device_id=self.across, device_id_type=MESH)

    def meet(self):
        pl.semaphore_wait(pltpu.get_barrier_semaphore(), self.n_near + self.n_seq - 1)


def halo_copies(place, from_self, arrived, sems):
    up = pltpu.make_async_remote_copy(
        src_ref=from_self[1],
        dst_ref=arrived[0],
        send_sem=sems.at[0],
        recv_sem=sems.at[1],
        device_id=place.high,
        device_id_type=MESH,
    )
    down = pltpu.make_async_remote_copy(
        src_ref=from_self[0],
        dst_ref=arrived[1],
        send_sem=sems.at[2],
        recv_sem=sems.at[3],
        device_id=place.low,
        device_id_type=MESH,
    )
    return up, down


def nothing():
    pass


def spread_round(buffer, mine, count, device_of, send, recv, meanwhile=nothing):
    copies = []
    for k in range(1, count):
        rank = lax.rem(mine + k, count)
        copy = pltpu.make_async_remote_copy(
            src_ref=buffer.at[mine],
            dst_ref=buffer.at[mine],
            send_sem=send.at[k],
            recv_sem=recv.at[mine],
            device_id=device_of(rank),
            device_id_type=MESH,
        )
        copy.start()
        copies.append((rank, copy))
    meanwhile()
    for rank, copy in copies:
        pltpu.make_async_remote_copy(
            src_ref=buffer.at[rank],
            dst_ref=buffer.at[rank],
            send_sem=send.at[0],
            recv_sem=recv.at[rank],
            device_id=device_of(rank),
            device_id_type=MESH,
        ).wait_recv()
    for rank, copy in copies:
        copy.wait_send()


def reduce_everywhere(
    place, value, near_buf, far_buf, sems, combine, meanwhile=nothing, then=None
):
    then = meanwhile if then is None else then
    near_send, near_recv, far_send, far_recv = sems
    far_buf[place.seq] = value
    spread_round(
        far_buf,
        place.seq,
        place.n_seq,
        lambda seq: (place.sec, seq, place.dp),
        far_send,
        far_recv,
        meanwhile,
    )
    near_buf[place.near] = combine(far_buf, place.n_seq, 1)
    spread_round(
        near_buf, place.near, place.n_near, place.near_device, near_send, near_recv, then
    )
    return combine(near_buf, place.n_near, place.n_seq)


def add_up(buffer, count, weight):
    total = buffer[0]
    for i in range(1, count):
        total = total + buffer[i]
    return total


def merge_stats(rows, buffer, count, weight):
    means = [buffer[i][:MB] for i in range(count)]
    centre = means[0]
    spread = buffer[0][MB:]
    for i in range(1, count):
        centre = centre + means[i]
        spread = spread + buffer[i][MB:]
    centre = centre * (1.0 / count)
    apart = jnp.square(means[0] - centre)
    for i in range(1, count):
        apart = apart + jnp.square(means[i] - centre)
    return jnp.concatenate([centre, spread + apart * float(rows * weight)], axis=0)


def reduce_scratch(shape, rows, columns):
    n_sec, n_seq, n_dp = shape
    near = n_sec * n_dp
    return [
        pltpu.VMEM((near, rows, columns), f32),
        pltpu.VMEM((n_seq, rows, columns), f32),
        pltpu.SemaphoreType.DMA((near,)),
        pltpu.SemaphoreType.DMA((near,)),
        pltpu.SemaphoreType.DMA((n_seq,)),
        pltpu.SemaphoreType.DMA((n_seq,)),
    ]


def local_stats(value):
    count = value.shape[0]
    centre = jnp.sum(value, axis=0, keepdims=True) * (1.0 / count)
    return centre, jnp.sum(jnp.square(value - centre), axis=0, keepdims=True)


def finish_stats(stats, total):
    return jnp.concatenate(
        [stats[:MB], lax.rsqrt(stats[MB:] * (1.0 / total) + EPS)], axis=0
    )


def prepare(place, order, tracks, pairs, low, high, stats, scratch):
    lanes, half, _ = scratch.shape
    start = pl.multiple_of(place.sec * half, half)

    @pl.loop(0, MB)
    def _(m):
        values = []
        for i in range(2):
            value = tracks[order[2 * m + i], pl.ds(start, half), :].astype(f32)
            values.append(value)
            for c in range(lanes):
                scratch[c] = value[:, c * LANES : (c + 1) * LANES]
            both = jnp.concatenate(
                [scratch[c, pl.ds(odd, half // 2, 2), :] for odd in range(2) for c in range(lanes)],
                axis=1,
            )
            pairs[2 * m + i] = both.astype(bf16)
            low[pl.ds(2 * m + i, 1), :] = both[:1]
            high[pl.ds(2 * m + i, 1), :] = both[half // 2 - 1 :]
        count = 2 * half
        centre = (
            jnp.sum(values[0], axis=0, keepdims=True) + jnp.sum(values[1], axis=0, keepdims=True)
        ) * (1.0 / count)
        spread = jnp.sum(jnp.square(values[0] - centre), axis=0, keepdims=True) + jnp.sum(
            jnp.square(values[1] - centre), axis=0, keepdims=True
        )
        stats[pl.ds(m, 1), :] = centre
        stats[pl.ds(MB + m, 1), :] = spread


class Gathering:
    STAGES = 5

    def __init__(self, place, shard, full, rows_at, sems):
        self.place, self.shard, self.full, self.rows_at, self.sems = place, shard, full, rows_at, sems
        p = place
        x, y, z = lax.rem(p.dp, 2), lax.div(p.dp, 2), lax.rem(p.seq, 2)
        self.share = full.shape[rows_at] // p.n_dp
        self.group = self.share // 6
        g = self.group
        self.dp_x, self.dp_y = p.dp + 1 - 2 * x, p.dp + 2 - 4 * y
        self.dp_xy = 3 - p.dp
        self.sibling = (1 - p.sec, p.seq, p.dp)
        self.over_x, self.over_y = (p.sec, p.seq, self.dp_x), (p.sec, p.seq, self.dp_y)
        self.over_z = (p.sec, p.seq + 1 - 2 * z, p.dp)
        base = p.sec * 3 * g
        self.near, self.middle, self.edge, self.far, self.half = (
            (base + z * g, 2 * g),
            (base + g, g),
            (base + 2 * z * g, g),
            (base + 2 * (1 - z) * g, g),
            (base, 3 * g),
        )

    def at(self, ref, dp, span):
        start, rows = span
        index = pl.ds(pl.multiple_of(dp * self.share + start, self.group), rows)
        return ref.at[:, index] if self.rows_at else ref.at[index]

    def remote(self, dp, span, sem, device, source=None):
        source = self.at(self.full, dp, span) if source is None else source
        return pltpu.make_async_remote_copy(
            src_ref=source,
            dst_ref=self.at(self.full, dp, span),
            send_sem=self.sems.at[2 * sem],
            recv_sem=self.sems.at[2 * sem + 1],
            device_id=device,
            device_id_type=MESH,
        )

    def own_copy(self):
        target = self.at(self.full, self.place.dp, (0, self.share))
        return pltpu.make_async_copy(self.shard, target, self.sems.at[26])

    def copies(self, stage):
        me = self.place.dp
        if stage == 0:
            own = None if self.shard is None else self.at(self.shard, 0, self.near)
            return [
                self.remote(me, self.near, 0, self.over_x, own),
                self.remote(me, self.near, 1, self.over_y, own),
            ]
        if stage == 1:
            return [
                self.remote(self.dp_x, self.middle, 2, self.over_y),
                self.remote(self.dp_y, self.edge, 3, self.over_x),
                self.remote(self.dp_x, self.edge, 4, self.over_z),
                self.remote(self.dp_y, self.edge, 5, self.over_z),
                self.remote(self.dp_x, self.near, 6, self.sibling),
                self.remote(self.dp_y, self.near, 7, self.sibling),
            ]
        if stage == 2:
            return [
                self.remote(self.dp_xy, self.edge, 8, self.over_z),
                self.remote(self.dp_xy, self.near, 9, self.sibling),
            ]
        if stage == 3:
            return [
                self.remote(self.dp_x, self.far, 10, self.sibling),
                self.remote(self.dp_y, self.far, 11, self.sibling),
                self.remote(self.dp_xy, self.far, 12, self.sibling),
            ]
        return []

    def start(self, stage):
        for copy in self.copies(stage):
            copy.start()

    def arrived(self, stage, which, dp, span):
        copy = self.copies(stage)[which]
        pltpu.make_async_remote_copy(
            src_ref=self.at(self.full, dp, span),
            dst_ref=self.at(self.full, dp, span),
            send_sem=self.sems.at[0],
            recv_sem=self.sems.at[2 * {0: 0, 1: 2, 2: 8, 3: 10}[stage] + 2 * which + 1],
            device_id=self.sibling,
            device_id_type=MESH,
        ).wait_recv()

    def advance(self, stage):
        if stage == 0:
            if self.shard is not None:
                self.own_copy().start()
        elif stage == 1:
            self.arrived(0, 0, self.dp_x, self.near)
            self.arrived(0, 1, self.dp_y, self.near)
        elif stage == 2:
            self.arrived(1, 0, self.dp_xy, self.middle)
            self.arrived(1, 1, self.dp_xy, self.edge)
        elif stage == 3:
            self.arrived(1, 2, self.dp_x, self.far)
            self.arrived(1, 3, self.dp_y, self.far)
            self.arrived(2, 0, self.dp_xy, self.far)
        if stage < 4:
            self.start(stage)
            return
        base = (1 - self.place.sec) * 3 * self.group
        z = lax.rem(self.place.seq, 2)
        near = (base + z * self.group, 2 * self.group)
        far = (base + 2 * (1 - z) * self.group, self.group)
        self.arrived(1, 4, self.dp_x, near)
        self.arrived(1, 5, self.dp_y, near)
        self.arrived(2, 1, self.dp_xy, near)
        self.arrived(3, 0, self.dp_x, far)
        self.arrived(3, 1, self.dp_y, far)
        self.arrived(3, 2, self.dp_xy, far)
        if self.shard is not None:
            self.own_copy().wait()
        for stage in range(4):
            for copy in self.copies(stage):
                copy.wait_send()


class Relay:
    TRACKS = 512

    def __init__(self, source, target, first_bin, refs):
        self.source, self.target, self.first = source, target, first_bin
        self.got, self.rows, self.made, self.sems = refs
        self.length = target.shape[1]
        self.count = -(-source.shape[0] // self.TRACKS)
        self.at = 0

    def width(self, i):
        return min(self.TRACKS, self.source.shape[0] - i * self.TRACKS)

    def load(self, i):
        width = self.width(i)
        bins = pl.ds(pl.multiple_of(self.first, self.length), self.length)
        return pltpu.make_async_copy(
            self.source.at[pl.ds(i * self.TRACKS, width), :, bins],
            self.got.at[i % 2, pl.ds(0, width)],
            self.sems.at[i % 2],
        )

    def store(self, i):
        width = min(self.TRACKS, self.target.shape[2] - i * self.TRACKS)
        return pltpu.make_async_copy(
            self.made.at[i % 2, :, :, pl.ds(0, width)],
            self.target.at[:, :, pl.ds(i * self.TRACKS, width)],
            self.sems.at[2 + i % 2],
        )

    def begin(self):
        self.load(0).start()

    def step(self):
        i = self.at
        if i == self.count:
            return
        self.at += 1
        slot, width = i % 2, self.width(i)
        windows = self.got.shape[2]
        self.load(i).wait()
        if i + 1 < self.count:
            self.load(i + 1).start()
        if i > 1:
            self.store(i - 2).wait()
        if width < self.TRACKS:
            self.got[slot, width:] = jnp.zeros((self.TRACKS - width, *self.got.shape[2:]), bf16)
        value = self.got[slot].astype(f32)
        self.rows[...] = value.reshape(self.TRACKS * windows, self.length)
        for w in range(windows):
            self.made[slot, w] = self.rows[pl.ds(w, self.TRACKS, windows), :].astype(bf16).T
        self.store(i).start()

    def finish(self):
        while self.at < self.count:
            self.step()
        for i in range(max(0, self.count - 2), self.count):
            self.store(i).wait()

    @staticmethod
    def scratch(windows, length):
        tracks = Relay.TRACKS
        return [
            pltpu.VMEM((2, tracks, windows, length), bf16),
            pltpu.VMEM((tracks * windows, length), f32),
            pltpu.VMEM((2, windows, length, tracks), bf16),
            pltpu.SemaphoreType.DMA((4,)),
        ]


def shifted_rows(value, offset, length):
    rows = value.shape[0]
    if offset:
        value = pltpu.roll(value, rows - offset, axis=0)
    return value[:length]


def forward_kernel(shape, n_relay, *refs):
    (
        order,
        tracks,
        vectors,
        in_one,
        in_two,
        in_point,
    ) = refs[:6]
    refs = refs[6:]
    in_cot, refs = refs[:n_relay], refs[n_relay:]
    (
        out_u_one,
        out_u_two,
        pooled,
        pooled_low,
        pooled_high,
        branch,
        branch_low,
        branch_high,
        act_three,
        summed,
        bn_one,
        bn_two,
        bn_three,
        out_one,
        out_two,
        out_point,
        x2,
    ) = refs[:17]
    refs = refs[17:]
    out_cot, refs = refs[:n_relay], refs[n_relay:]
    (
        near_one,
        far_one,
        s10,
        s11,
        s12,
        s13,
        near_two,
        far_two,
        s20,
        s21,
        s22,
        s23,
        near_three,
        far_three,
        s30,
        s31,
        s32,
        s33,
        got_low,
        got_high,
        stats_two,
        stats_three,
        halo_sems,
        s_branch_edge_low,
        s_branch_edge_high,
        u_one,
        u_two,
        w_one,
        w_two,
        w_point,
        weight_sems,
        save_sems,
        edge_low,
        edge_high,
        stats_in,
        lanes_buffer,
    ) = refs[:36]
    relay_refs = refs[36:]
    place = Place(shape)
    place.greet()
    windows, length, wide = x2.shape
    channels = wide // 2
    mid = pooled.shape[2]
    small = branch.shape[1]
    parts = shape[0] * shape[1] * shape[2]
    pair = 2 * length
    saves = [
        pltpu.make_async_copy(source, target, save_sems.at[i])
        for i, (source, target) in enumerate(
            ((u_one, out_u_one), (u_two, out_u_two), (w_one, out_one), (w_two, out_two), (w_point, out_point))
        )
    ]
    gathers = []
    own_taps = []
    if len(in_one.shape) == 3:
        taps, share, columns = in_one.shape
        own_rows = pl.ds(pl.multiple_of(place.dp * share, share), share)
        own_taps = [
            pltpu.make_async_copy(
                in_one.at[t],
                w_one.at[own_rows, pl.ds(t * columns, columns)],
                weight_sems.at[0, 27 + t],
            )
            for t in range(taps)
        ]
        for tap in own_taps:
            tap.start()
        columns = w_one.shape[1]
        first = columns // (2 * LANES) * LANES
        pieces = [
            (None, w_one.at[:, part], 0)
            for part in (pl.ds(0, first), pl.ds(first, columns - first))
        ]
        pieces += [(in_two, w_two, 1), (in_point, w_point, 0)]
        gathers = [
            Gathering(place, *piece, weight_sems.at[i]) for i, piece in enumerate(pieces)
        ]
    else:
        loads = [
            pltpu.make_async_copy(source, target, weight_sems.at[i, 0])
            for i, (source, target) in enumerate(
                ((in_one, w_one), (in_two, w_two), (in_point, w_point))
            )
        ]
        for load in loads:
            load.start()
        for load in loads:
            load.wait()

    def advance(*steps):
        for index, stage in steps:
            if index < len(gathers):
                gathers[index].advance(stage)

    mid_rows = lambda index, width: vectors.at[index : index + 1, :width]
    gain_one, shift_one = mid_rows(0, wide), mid_rows(1, wide)
    gain_two, shift_two = mid_rows(2, mid), mid_rows(3, mid)
    gain_three, shift_three = mid_rows(4, small), mid_rows(5, small)
    relay = None
    if n_relay:
        relay = Relay(in_cot[0], out_cot[0], place.sec * length, relay_refs)
        relay.begin()

    def fill(count=1):
        for _ in range(count if relay else 0):
            relay.step()

    prepare(place, order, tracks, x2, edge_low, edge_high, stats_in, lanes_buffer)
    for tap in own_taps:
        tap.wait()
    place.meet()
    advance((0, 0), (1, 0))
    up, down = halo_copies(place, (edge_low, edge_high), (got_low, got_high), halo_sems.at[0])
    place.halos((up, down), 0)
    stats = reduce_everywhere(
        place,
        stats_in[...],
        near_one,
        far_one,
        (s10, s11, s12, s13),
        functools.partial(merge_stats, 4 * length),
        fill,
        lambda: advance((0, 1)),
    )
    stats = finish_stats(stats, 4 * length * parts)
    bn_one[...] = jnp.concatenate([stats, stats], axis=1)
    place.halos((up, down), 1)
    advance((1, 1), (0, 2), (2, 0), (3, 0))

    @pl.loop(0, windows)
    def _(w):
        m = lax.div(w, 2)
        centre = bn_one[pl.ds(m, 1), :]
        scale = bn_one[pl.ds(MB + m, 1), :] * gain_one[...]
        move = shift_one[...]

        def act(value):
            return gelu((value - centre) * scale + move).astype(bf16).astype(f32)

        main = act(x2[w].astype(f32))
        before = jnp.where(place.is_first, 0.0, act(got_low[pl.ds(w, 1), :]))
        after = jnp.where(place.is_last, 0.0, act(got_high[pl.ds(w, 1), :]))
        even, odd = main[:, :channels], main[:, channels:]
        mean = (even + odd) * 0.5
        mean_before = (before[:, :channels] + before[:, channels:]) * 0.5
        mean_after = (after[:, :channels] + after[:, channels:]) * 0.5
        row = lax.broadcasted_iota(jnp.int32, (length, channels), 0)
        top, bottom = row == 0, row == length - 1
        odd_before = jnp.where(top, before[:, channels:], pltpu.roll(odd, 1, axis=0))
        cross = (odd_before + even) * 0.5
        cross_after = (odd[length - 1 :] + after[:, :channels]) * 0.5
        start = pl.multiple_of(w * length, length)
        taps = (
            jnp.where(top, mean_before, pltpu.roll(mean, 1, axis=0)),
            cross,
            mean,
            jnp.where(bottom, cross_after, pltpu.roll(cross, length - 1, axis=0)),
            jnp.where(bottom, mean_after, pltpu.roll(mean, length - 1, axis=0)),
        )
        for t, tap in enumerate(taps):
            u_one[pl.ds(start, length), t * channels : (t + 1) * channels] = tap.astype(bf16)

    saves[0].start()
    advance((1, 2), (0, 3))
    fill(2)
    advance((1, 3), (0, 4))
    fill()
    advance((1, 4), (2, 1), (3, 1))
    saves[2].start()

    @pl.loop(0, MB)
    def _(m):
        start = pl.multiple_of(m * pair, pair)
        value = dot_nt(u_one[pl.ds(start, pair), :], w_one[...]).astype(bf16)
        pooled[pl.ds(2 * m, 2)] = value.reshape(2, length, mid)
        centre, spread = local_stats(value.astype(f32))
        stats_two[pl.ds(m, 1), :] = centre
        stats_two[pl.ds(MB + m, 1), :] = spread

    advance((2, 2), (3, 2))
    up, down = halo_copies(
        place,
        (pooled.at[:, pl.ds(0, EDGE), :], pooled.at[:, pl.ds(length - EDGE, EDGE), :]),
        (pooled_low, pooled_high),
        halo_sems.at[1],
    )
    place.halos((up, down), 0)
    stats = reduce_everywhere(
        place,
        stats_two[...],
        near_two,
        far_two,
        (s20, s21, s22, s23),
        functools.partial(merge_stats, pair),
        fill,
    )
    bn_two[...] = finish_stats(stats, pair * parts)
    place.halos((up, down), 1)
    advance((2, 3), (3, 3))

    @pl.loop(0, windows)
    def _(w):
        m = lax.div(w, 2)
        centre = bn_two[pl.ds(m, 1), :]
        scale = bn_two[pl.ds(MB + m, 1), :] * gain_two[...]
        move = shift_two[...]

        def act(value):
            return gelu((value.astype(f32) - centre) * scale + move)

        ext = jnp.concatenate(
            [
                jnp.where(place.is_first, 0.0, act(pooled_low[w])),
                act(pooled[w]),
                jnp.where(place.is_last, 0.0, act(pooled_high[w])),
            ],
            axis=0,
        )
        start = pl.multiple_of(w * length, length)
        for t in range(3):
            tap = shifted_rows(ext, EDGE + (t - 1) * DILATION, length)
            u_two[pl.ds(start, length), t * mid : (t + 1) * mid] = tap.astype(bf16)

    saves[1].start()
    advance((2, 4), (3, 4))
    saves[3].start()
    saves[4].start()

    @pl.loop(0, MB)
    def _(m):
        start = pl.multiple_of(m * pair, pair)
        value = jnp.zeros((pair, small), f32)
        for t in range(w_two.shape[0]):
            value = value + dot_nn(
                u_two[pl.ds(start, pair), t * mid : (t + 1) * mid], w_two[t]
            )
        branch[pl.ds(start, pair), :] = value
        centre, spread = local_stats(value)
        stats_three[pl.ds(m, 1), :] = centre
        stats_three[pl.ds(MB + m, 1), :] = spread
        for i in range(2):
            s_branch_edge_low[2 * m + i] = value[i * length : i * length + EDGE]
            s_branch_edge_high[2 * m + i] = value[(i + 1) * length - EDGE : (i + 1) * length]

    up, down = halo_copies(
        place,
        (s_branch_edge_low, s_branch_edge_high),
        (branch_low, branch_high),
        halo_sems.at[2],
    )
    place.halos((up, down), 0)
    stats = reduce_everywhere(
        place,
        stats_three[...],
        near_three,
        far_three,
        (s30, s31, s32, s33),
        functools.partial(merge_stats, pair),
        fill,
    )
    bn_three[...] = finish_stats(stats, pair * parts)

    @pl.loop(0, MB)
    def _(m):
        centre = bn_three[pl.ds(m, 1), :]
        scale = bn_three[pl.ds(MB + m, 1), :] * gain_three[...]
        start = pl.multiple_of(m * pair, pair)
        act = gelu((branch[pl.ds(start, pair), :] - centre) * scale + shift_three[...])
        act = act.astype(bf16)
        act_three[pl.ds(start, pair), :] = act
        lifted = dot_nt(act, w_point[...])
        here = pooled[pl.ds(2 * m, 2)].reshape(pair, mid).astype(f32)
        summed[pl.ds(start, pair), :] = (here + lifted).astype(bf16)

    place.halos((up, down), 1)
    if relay:
        relay.finish()
    for save in saves:
        save.wait()


def forward(shape, mid, order, tracks, vectors, w_one, w_two, w_point, cot):
    windows, seq_bins, channels = tracks.shape
    half = seq_bins // shape[0]
    length, wide = half // 2, 2 * channels
    rows = windows * length
    taps_two, _, small = w_two.shape
    big = [
        ((mid, w_one.shape[-1] * (w_one.shape[0] if w_one.ndim == 3 else 1)), bf16),
        ((taps_two, mid, small), bf16),
        ((mid, small), bf16),
    ]
    out = [
        ((rows, big[0][0][1]), bf16),
        ((rows, taps_two * mid), bf16),
        ((windows, length, mid), bf16),
        ((windows, EDGE, mid), bf16),
        ((windows, EDGE, mid), bf16),
        ((rows, small), f32),
        ((windows, EDGE, small), f32),
        ((windows, EDGE, small), f32),
        ((rows, small), bf16),
        ((rows, mid), bf16),
        ((2 * MB, wide), f32),
        ((2 * MB, mid), f32),
        ((2 * MB, small), f32),
    ]
    out_specs = [HBM] * 2 + [VM] * 11 + [HBM] * 3 + [VM] + [HBM] * len(cot)
    out += big + [((windows, length, wide), bf16)]
    out += [((windows, length, -(-c.shape[0] // BLOCK) * BLOCK), bf16) for c in cot]
    scratch = (
        reduce_scratch(shape, 2 * MB, wide // 2)
        + reduce_scratch(shape, 2 * MB, mid)
        + reduce_scratch(shape, 2 * MB, small)
    )
    scratch += [
        pltpu.VMEM((windows, wide), f32),
        pltpu.VMEM((windows, wide), f32),
        pltpu.VMEM((2 * MB, mid), f32),
        pltpu.VMEM((2 * MB, small), f32),
        pltpu.SemaphoreType.DMA((3, 4)),
        pltpu.VMEM((windows, EDGE, small), f32),
        pltpu.VMEM((windows, EDGE, small), f32),
        pltpu.VMEM(*out[0]),
        pltpu.VMEM(*out[1]),
    ]
    scratch += [pltpu.VMEM(*b) for b in big]
    scratch += [
        pltpu.SemaphoreType.DMA((4, 32)),
        pltpu.SemaphoreType.DMA((5,)),
        pltpu.VMEM((windows, wide), f32),
        pltpu.VMEM((windows, wide), f32),
        pltpu.VMEM((2 * MB, channels), f32),
        pltpu.VMEM((channels // LANES, half, LANES), f32),
        *(Relay.scratch(windows, length) if cot else []),
    ]
    return pl.pallas_call(
        functools.partial(forward_kernel, shape, len(cot)),
        in_specs=[pl.BlockSpec(memory_space=pltpu.SMEM), VM, VM] + [HBM] * (3 + len(cot)),
        out_specs=out_specs,
        out_shape=[jax.ShapeDtypeStruct(*o) for o in out],
        scratch_shapes=scratch,
        compiler_params=params(1),
        name="forward",
    )(order, tracks, vectors, w_one, w_two, w_point, *cot)


def heads_kernel(
    human_tracks,
    mouse_tracks,
    species,
    order,
    summed,
    w_human,
    w_mouse,
    b_human,
    b_mouse,
    cot,
    predicted,
    grad_summed,
    d_human,
    d_mouse,
    db,
    rows_sorted,
    grad_sorted,
    grad_pre,
    by_track,
    meta,
):
    j = pl.program_id(0)
    windows, length, block = cot.shape
    pair = 2 * length
    n_pairs = windows // 2
    mid = summed.shape[1]

    @pl.when(j == 0)
    def _():
        grad_sorted[...] = jnp.zeros_like(grad_sorted)
        db[...] = jnp.zeros_like(db)
        found = 0
        for kind in range(2):
            for p in range(windows):
                window = order[p]
                mine = species[window] == kind

                @pl.when(mine)
                def _(found=found, p=p, window=window):
                    meta[found] = p
                    meta[windows + found] = window

                found = found + mine.astype(jnp.int32)
            if kind == 0:
                meta[2 * windows] = found

        @pl.loop(0, windows)
        def _(s):
            source = pl.multiple_of(meta[s] * length, length)
            target = pl.multiple_of(s * length, length)
            rows_sorted[pl.ds(target, length), :] = summed[pl.ds(source, length), :]

    n_human = meta[2 * windows]
    column = lax.broadcasted_iota(jnp.int32, (1, block), 1)

    cuts = [slice(at, min(at + SPLIT, block)) for at in range(0, block, SPLIT)]

    def run(weight, bias, limit, is_mouse, first_pair, last_pair):
        def body(p, carry):
            start = pl.multiple_of(p * pair, pair)
            rows = rows_sorted[pl.ds(start, pair), :]
            mine = [s >= n_human if is_mouse else s < n_human for s in (2 * p, 2 * p + 1)]
            window = [meta[windows + 2 * p], meta[windows + 2 * p + 1]]
            pres = [dot_nn(rows, weight[:, cut]) + bias[:, cut] for cut in cuts]
            back = jnp.zeros((pair, mid), f32)
            for cut, pre in zip(cuts, pres):
                inside = column[:, cut] < limit
                decay = jnp.exp(-jnp.abs(pre))
                whole = 1.0 + decay
                inverse = 1.0 / whole
                sigmoid = jnp.where(pre >= 0, inverse, decay * inverse)
                logs = jnp.where(decay < 2.0**-11, decay, jnp.log(whole))
                output = jnp.where(inside, jnp.maximum(pre, 0.0) + logs, 0.0)
                grads = []
                for i in range(2):
                    part = slice(i * length, (i + 1) * length)
                    grad = cot[window[i], :, cut].astype(f32) * sigmoid[part]
                    grads.append(jnp.where(inside & mine[i], grad, 0.0))
                    here = output[part].T
                    spots = pl.ds(cut.start * windows + window[i], cut.stop - cut.start, windows)
                    if is_mouse:
                        here = jnp.where(mine[i], here, by_track[spots, :])
                    by_track[spots, :] = here
                grad = jnp.concatenate(grads, axis=0).astype(bf16)
                grad_pre[pl.ds(start, pair), cut] = grad
                back = back + dot_nt(grad, weight[:, cut])
            grad_sorted[pl.ds(start, pair), :] += back
            return carry

        lax.fori_loop(first_pair, last_pair, body, 0)

    def weight_grads(n_used, from_end, d_weight, bias_row):
        for n in range(n_pairs + 1):

            @pl.when(n_used == n)
            def _(n=n):
                if n == 0:
                    d_weight[...] = jnp.zeros_like(d_weight)
                else:
                    part = slice((n_pairs - n) * pair, None) if from_end else slice(0, n * pair)
                    grad = grad_pre[part, :]
                    d_weight[...] = dot_tn(rows_sorted[part, :], grad).astype(bf16)
                    total = dot_nn(jnp.ones((8, n * pair), bf16), grad)[:1]
                    db[pl.ds(bias_row, 1), :] = total

    human_pairs = lax.div(n_human + 1, 2)
    run(w_human, b_human, human_tracks - j * block, False, 0, human_pairs)
    weight_grads(human_pairs, False, d_human, j)

    @pl.when(j == 0)
    def _():
        mouse_start = lax.div(n_human, 2)
        run(w_mouse, b_mouse, mouse_tracks, True, mouse_start, n_pairs)
        weight_grads(n_pairs - mouse_start, True, d_mouse, pl.num_programs(0))

    @pl.when(j > 0)
    def _():
        def body(s, carry):
            by_track[pl.ds(meta[windows + s], block, windows), :] = jnp.zeros((block, length), f32)
            return carry

        lax.fori_loop(n_human, windows, body, 0)

    predicted[...] = by_track[...].reshape(block, windows, length).astype(bf16)

    @pl.when(j == pl.num_programs(0) - 1)
    def _():
        @pl.loop(0, windows)
        def _(s):
            source = pl.multiple_of(s * length, length)
            target = pl.multiple_of(meta[s] * length, length)
            grad_summed[pl.ds(target, length), :] = grad_sorted[pl.ds(source, length), :]


def heads(species, order, summed, w_heads, bias, cot, human_tracks, mouse_tracks):
    windows, length, _ = cot.shape
    rows, mid = summed.shape
    blocks = w_heads.shape[1] // BLOCK - 1
    smem = pl.BlockSpec(memory_space=pltpu.SMEM)
    fixed = lambda shape, at=0: pl.BlockSpec(
        shape, lambda j: (0, at), pipeline_mode=pl.Buffered(1)
    )
    return pl.pallas_call(
        functools.partial(heads_kernel, human_tracks, mouse_tracks),
        grid=(blocks,),
        in_specs=[
            smem,
            smem,
            fixed((rows, mid)),
            pl.BlockSpec((mid, BLOCK), lambda j: (0, j)),
            fixed((mid, BLOCK), blocks),
            pl.BlockSpec((1, BLOCK), lambda j: (0, j)),
            fixed((1, BLOCK), blocks),
            pl.BlockSpec((windows, length, BLOCK), lambda j: (0, 0, j)),
        ],
        out_specs=[
            pl.BlockSpec((BLOCK, windows, length), lambda j: (j, 0, 0)),
            pl.BlockSpec((rows, mid), lambda j: (0, 0)),
            pl.BlockSpec((mid, BLOCK), lambda j: (0, j)),
            pl.BlockSpec((mid, BLOCK), lambda j: (0, 0)),
            pl.BlockSpec((8, BLOCK), lambda j: (0, 0)),
        ],
        scratch_shapes=[
            pltpu.VMEM((rows, mid), bf16),
            pltpu.VMEM((rows, mid), f32),
            pltpu.VMEM((rows, BLOCK), bf16),
            pltpu.VMEM((BLOCK * windows, length), f32),
            pltpu.SMEM((2 * windows + 1,), jnp.int32),
        ],
        out_shape=[
            jax.ShapeDtypeStruct((human_tracks, windows, length), bf16),
            jax.ShapeDtypeStruct((rows, mid), f32),
            jax.ShapeDtypeStruct((mid, blocks * BLOCK), bf16),
            jax.ShapeDtypeStruct((mid, BLOCK), bf16),
            jax.ShapeDtypeStruct((8, BLOCK), f32),
        ],
        compiler_params=params(),
        name="heads",
    )(species, order, summed, w_heads, w_heads, bias, bias, cot)


HAND, LOAD = 7, 8
WHOLE = (0, 1, 2, 3, 4, 5, 6)
PLANE = (0, 1, 2, HAND)
ALONG = (LOAD, 3, 4, 5, 6)


class Summing:
    def __init__(self, place, plan, source, start, width, target, to, scratch):
        self.place, self.plan, self.source, self.target = place, plan, source, target
        self.columns = pl.ds(start, width)
        self.width, self.to = width, to
        for name, ref in zip(self.names(plan), scratch):
            setattr(self, name, ref)
        half = self.own.shape[2]
        self.half, self.part = half, half // 2
        self.mine = pl.ds(pl.multiple_of(place.sec * half, half), half)
        self.other = pl.ds(pl.multiple_of((1 - place.sec) * half, half), half)
        self.x, self.y = lax.rem(place.dp, 2), lax.div(place.dp, 2)
        self.cell = (self.y, self.x) if 0 in plan else (0, 0)
        self.top, self.bottom = pl.ds(0, self.part), pl.ds(self.part, self.part)
        self.at_end = (place.seq == 0) | (place.seq == place.n_seq - 1)
        self.between = jnp.logical_not(self.at_end)

    @staticmethod
    def names(plan):
        names = ["own"]
        if 0 in plan:
            names += ["core", "side_a", "side_b", "end_a", "end_b"]
        if 6 in plan:
            names += ["z_one", "z_far", "mate"]
        return names + ["sems"]

    @staticmethod
    def scratch(plan, share, width):
        half = share // 2
        part = half // 2
        cells = 2 if 0 in plan else 1
        shapes = dict(
            own=(cells, cells, half, width),
            core=(2, 2, half, width),
            side_a=(2, part, width),
            side_b=(2, part, width),
            end_a=(part, width),
            end_b=(part, width),
            z_one=(half, width),
            z_far=(half, width),
            mate=(half, width),
        )
        refs = [pltpu.VMEM(shapes[name], bf16) for name in Summing.names(plan)[:-1]]
        return refs + [pltpu.SemaphoreType.DMA((23,))]

    def remote(self, source, target, sem, device):
        return pltpu.make_async_remote_copy(
            src_ref=source,
            dst_ref=target,
            send_sem=self.sems.at[2 * sem],
            recv_sem=self.sems.at[2 * sem + 1],
            device_id=device,
            device_id_type=MESH,
        )

    def copies(self, stage):
        p, own, x, y = self.place, self.own, self.x, self.y
        sibling = (1 - p.sec, p.seq, p.dp)
        over_x = (p.sec, p.seq, p.dp + 1 - 2 * x)
        over_y = (p.sec, p.seq, p.dp + 2 - 4 * y)
        over_z = (p.sec, p.seq + 1 - 2 * lax.rem(p.seq, 2), p.dp)
        if stage == 0:
            return [
                pltpu.make_async_copy(
                    self.source.at[:, :, self.mine, self.columns], own, self.sems.at[16]
                ),
                self.remote(
                    self.source.at[:, :, self.other, self.columns], self.core, 0, sibling
                ),
            ]
        if stage == 1:
            return [
                self.remote(own.at[:, 1 - x, self.top], self.side_a, 1, over_x),
                self.remote(own.at[1 - y, :, self.bottom], self.side_b, 2, over_y),
            ]
        if stage == 2:
            return [
                self.remote(own.at[1 - y, x, self.top], self.end_a, 3, over_y),
                self.remote(own.at[y, 1 - x, self.bottom], self.end_b, 4, over_x),
            ]
        if stage == HAND:
            columns = pl.ds(self.to, self.width)
            return [
                pltpu.make_async_copy(
                    own.at[self.cell], self.target.at[:, columns], self.sems.at[17]
                )
            ]
        if stage == LOAD:
            return [
                pltpu.make_async_copy(
                    self.source.at[:, self.columns], own.at[self.cell], self.sems.at[17]
                )
            ]
        if stage == 3:
            return [self.remote(own.at[self.cell], self.z_one, 5, over_z)]
        if stage == 4:
            opposite = (p.sec, p.n_seq - 1 - p.seq, p.dp)
            return [self.remote(own.at[self.cell], self.z_far, 6, opposite)]
        if stage == 5:
            return [self.remote(own.at[self.cell], self.z_one, 5, over_z)]
        return [
            self.remote(source, self.mate, 7, sibling) for source in (own.at[self.cell], self.z_one)
        ]

    def start(self, stage):
        copies = self.copies(stage)
        if stage == 3:
            pl.when(self.at_end)(copies[0].start)
        elif stage in (4, 5):
            pl.when(self.between)(copies[0].start)
        elif stage == 6:
            pl.when(self.between)(copies[0].start)
            pl.when(self.at_end)(copies[1].start)
        else:
            for copy in copies:
                copy.start()

    def add(self, at, other):
        self.own[at] = (self.own[at].astype(f32) + other.astype(f32)).astype(bf16)

    def finish(self, stage):
        copies = self.copies(stage)
        x, y = self.x, self.y
        if stage == 3:
            pl.when(self.at_end)(copies[0].wait_send)

            @pl.when(self.between)
            def _():
                copies[0].wait_recv()
                self.add(self.cell, self.z_one[...])

        elif stage == 4:

            @pl.when(self.between)
            def _():
                copies[0].wait()
                self.add(self.cell, self.z_far[...])

        elif stage == 5:
            pl.when(self.between)(copies[0].wait_send)
            pl.when(self.at_end)(copies[0].wait_recv)
        elif stage == 6:
            copies[0].wait()
            pl.when(self.between)(self.results(self.own.at[self.cell])[0].start)
            pl.when(self.at_end)(self.results(self.z_one)[0].start)
            self.results(self.z_one)[1].start()
        elif stage != HAND:
            for copy in copies:
                copy.wait()
        if stage == 0:

            @pl.loop(0, 4)
            def _(i):
                a, b = lax.div(i, 2), lax.rem(i, 2)
                self.add((a, b), self.core[a, b])

        elif stage == 1:
            for i in range(2):
                self.add((i, x, self.top), self.side_a[i])
                self.add((y, i, self.bottom), self.side_b[i])
        elif stage == 2:
            self.add((y, x, self.top), self.end_a[...])
            self.add((y, x, self.bottom), self.end_b[...])

    def results(self, source):
        copies = []
        for i, (ref, rows) in enumerate(((source, self.mine), (self.mate, self.other))):
            if len(self.target.shape) == 3:
                target = self.target.at[self.to, rows]
            else:
                target = self.target.at[rows, pl.ds(self.to, self.width)]
            copies.append(pltpu.make_async_copy(ref, target, self.sems.at[18 + i]))
        return copies

    def close(self):
        copies = self.results(self.mate) if 6 in self.plan else self.copies(HAND)
        for copy in copies:
            copy.wait()


class Sums:
    def __init__(self, place, sources, targets, chunks, refs):
        self.parts = []
        for plan, begin, source, start, width, target, to in chunks:
            count = len(Summing.names(plan))
            part = Summing(
                place, plan, sources[source], start, width, targets[target], to, refs[:count]
            )
            refs = refs[count:]
            self.parts.append((begin, part))
        self.parts.sort(key=lambda item: -item[0])
        self.last = max([begin + len(part.plan) for begin, part in self.parts], default=-1)
        self.tick = 0

    def step(self):
        if self.tick > self.last:
            return
        for begin, part in self.parts:
            i = self.tick - begin
            if 0 < i <= len(part.plan):
                part.finish(part.plan[i - 1])
            if 0 <= i < len(part.plan):
                part.start(part.plan[i])
        self.tick += 1

    def finish(self):
        while self.tick <= self.last:
            self.step()
        for _, part in self.parts:
            part.close()


def sums_scratch(share, chunks):
    return [ref for chunk in chunks for ref in Summing.scratch(chunk[0], share, chunk[4])]


def count_refs(chunks):
    return sum(len(Summing.names(chunk[0])) for chunk in chunks)


def head_chunks(human_wide):
    size = BLOCK // 2
    pieces = [(0, at) for at in range(0, human_wide, size)] + [(1, 0), (1, size)]
    n_whole = len(pieces) // 2 + 1
    chunks = []
    for k, (source, at) in enumerate(pieces):
        whole = k < n_whole
        to = (k if whole else k - n_whole) * size
        chunks.append((WHOLE if whole else PLANE, k, source, at, size, 0 if whole else 1, to))
    return chunks, n_whole * size, (len(pieces) - n_whole) * size


def split_refs(refs, *counts):
    groups = []
    for count in counts:
        groups.append(refs[:count])
        refs = refs[count:]
    assert not refs
    return groups


def back_high_kernel(shape, n_sums, chunks, *refs):
    (sources, big_in, small_in, targets, d_outs, outs, fixed, sum_refs) = split_refs(
        refs, n_sums, 3, 12, n_sums, 3, 3, 37, count_refs(chunks)
    )
    in_grad, in_u_one, in_u_two = big_in
    (
        act_three,
        branch,
        branch_low,
        branch_high,
        bn_three,
        w_point,
        w_two,
        pooled,
        pooled_low,
        pooled_high,
        bn_two,
        vectors,
    ) = small_in
    grad_ext, sums_three, sums_two = outs
    reduce_three, reduce_two, fixed = fixed[:6], fixed[6:12], fixed[12:]
    (
        grad_summed,
        u_any,
        du_three,
        edge_low,
        edge_high,
        du_low,
        du_high,
        row_low,
        row_high,
        gs_low,
        gs_high,
        local_three,
        grad_branch,
        du_two,
        row_low_two,
        row_high_two,
        dlow_two,
        dhigh_two,
        local_two,
        grad_main,
        d_point,
        d_two,
        d_one,
        halo_sems,
        copy_sems,
    ) = fixed
    place = Place(shape)
    place.greet()
    windows, length, mid = pooled.shape
    small = branch.shape[1]
    pair = 2 * length
    taps = w_two.shape[0] // mid
    scale = 1.0 / (pair * shape[0] * shape[1] * shape[2])
    row = lambda index, width: vectors.at[index : index + 1, :width]
    gain_two, shift_two = row(2, mid), row(3, mid)
    gain_three, shift_three = row(4, small), row(5, small)
    u_two = u_any.at[:, : taps * mid]
    load_grad = pltpu.make_async_copy(in_grad, grad_summed, copy_sems.at[0])
    load_two = pltpu.make_async_copy(in_u_two, u_two, copy_sems.at[1])
    load_one = pltpu.make_async_copy(in_u_one, u_any, copy_sems.at[2])
    save_point, save_two, save_one = [
        pltpu.make_async_copy(a, b, copy_sems.at[3 + i])
        for i, (a, b) in enumerate(((d_point, d_outs[0]), (d_two, d_outs[1]), (d_one, d_outs[2])))
    ]
    load_grad.start()
    load_two.start()
    sums = Sums(place, sources, targets, chunks, sum_refs)
    place.meet()
    sums.step()
    load_grad.wait()

    for m in range(MB):
        at = slice(m * pair, (m + 1) * pair)
        grad = grad_summed[at, :]
        back = dot_nn(grad.astype(bf16), w_point[...])
        xhat = (branch[at, :] - bn_three[m : m + 1, :]) * bn_three[MB + m : MB + m + 1, :]
        du = gelu_slope(xhat * gain_three[...] + shift_three[...]) * back
        du_three[at, :] = du
        local_three[m : m + 1, :] = jnp.sum(du, axis=0, keepdims=True)
        local_three[MB + m : MB + m + 1, :] = jnp.sum(du * xhat, axis=0, keepdims=True)
        for i in range(2):
            w = 2 * m + i
            edge_low[w] = du[i * length : i * length + EDGE]
            edge_high[w] = du[(i + 1) * length - EDGE : (i + 1) * length]
            row_low[w : w + 1, :] = grad[i * length : i * length + 1]
            row_high[w : w + 1, :] = grad[(i + 1) * length - 1 : (i + 1) * length]

    moves = halo_copies(place, (edge_low, edge_high), (du_low, du_high), halo_sems.at[0])
    moves += halo_copies(place, (row_low, row_high), (gs_low, gs_high), halo_sems.at[1])
    place.halos(moves, 0)
    sums_three[...] = reduce_everywhere(
        place, local_three[...], *reduce_three[:2], reduce_three[2:], add_up, sums.step
    )
    d_point[...] = dot_tn(grad_summed[...].astype(bf16), act_three[...]).astype(bf16)
    save_point.start()
    place.halos(moves, 1)
    sums.step()

    for m in range(MB):
        at = slice(m * pair, (m + 1) * pair)
        centre, inverse = bn_three[m : m + 1, :], bn_three[MB + m : MB + m + 1, :]
        factor = gain_three[...] * inverse
        mean_du = sums_three[m : m + 1, :] * scale
        mean_dx = sums_three[MB + m : MB + m + 1, :] * scale

        def back(du, value):
            xhat = (value - centre) * inverse
            return factor * (du - mean_du - xhat * mean_dx)

        main = back(du_three[at, :], branch[at, :])
        grad_branch[at, :] = main.astype(bf16)
        pieces = []
        for i in range(2):
            w = 2 * m + i
            low = jnp.where(place.is_first, 0.0, back(du_low[w], branch_low[w]))
            high = jnp.where(place.is_last, 0.0, back(du_high[w], branch_high[w]))
            pieces += [low, main[i * length : (i + 1) * length], high]
        ext = jnp.concatenate(pieces, axis=0).astype(bf16)
        span = length + 2 * EDGE
        through = [dot_nt(ext, w_two[t * mid : (t + 1) * mid, :]) for t in range(taps)]
        centre_two, inverse_two = bn_two[m : m + 1, :], bn_two[MB + m : MB + m + 1, :]
        total_du = jnp.zeros((1, mid), f32)
        total_dx = jnp.zeros((1, mid), f32)
        for i in range(2):
            w = 2 * m + i
            grad = jnp.zeros((length, mid), f32)
            for t in range(taps):
                whole = through[t][i * span : (i + 1) * span]
                grad = grad + shifted_rows(whole, EDGE - (t - 1) * DILATION, length)
            xhat = (pooled[w].astype(f32) - centre_two) * inverse_two
            du = gelu_slope(xhat * gain_two[...] + shift_two[...]) * grad
            du_two[w] = du
            total_du = total_du + jnp.sum(du, axis=0, keepdims=True)
            total_dx = total_dx + jnp.sum(du * xhat, axis=0, keepdims=True)
            row_low_two[w : w + 1, :] = du[:1]
            row_high_two[w : w + 1, :] = du[length - 1 :]
        local_two[m : m + 1, :] = total_du
        local_two[MB + m : MB + m + 1, :] = total_dx
        if m == 1:
            sums.step()

    moves = halo_copies(
        place, (row_low_two, row_high_two), (dlow_two, dhigh_two), halo_sems.at[2]
    )
    place.halos(moves, 0)
    sums_two[...] = reduce_everywhere(
        place, local_two[...], *reduce_two[:2], reduce_two[2:], add_up, sums.step
    )
    load_two.wait()
    for t in range(taps):
        part = dot_tn(u_two[:, t * mid : (t + 1) * mid], grad_branch[...])
        d_two[:, t * small : (t + 1) * small] = part.astype(bf16)
    save_two.start()
    load_one.start()
    place.halos(moves, 1)
    sums.step()

    for m in range(MB):
        centre, inverse = bn_two[m : m + 1, :], bn_two[MB + m : MB + m + 1, :]
        factor = gain_two[...] * inverse
        mean_du = sums_two[m : m + 1, :] * scale
        mean_dx = sums_two[MB + m : MB + m + 1, :] * scale

        def back(du, value, extra):
            xhat = (value.astype(f32) - centre) * inverse
            return factor * (du - mean_du - xhat * mean_dx) + extra

        edges = []
        for i in range(2):
            w = 2 * m + i
            at = slice(w * length, (w + 1) * length)
            value = back(du_two[w], pooled[w], grad_summed[at, :]).astype(bf16)
            grad_ext[m, i * length : (i + 1) * length, :] = value
            grad_main[at, :] = value
            row = slice(w, w + 1)
            low = back(dlow_two[row, :], pooled_low[w].astype(f32)[EDGE - 1 :], gs_low[row, :])
            high = back(dhigh_two[row, :], pooled_high[w].astype(f32)[:1], gs_high[row, :])
            edges += [jnp.where(place.is_first, 0.0, low), jnp.where(place.is_last, 0.0, high)]
        row = lax.broadcasted_iota(jnp.int32, (EDGE, mid), 0)
        block = jnp.zeros((EDGE, mid), f32)
        for i, edge in enumerate(edges):
            block = jnp.where(row == i, edge, block)
        grad_ext[m, pair : pair + EDGE, :] = block.astype(bf16)
    sums.step()
    load_one.wait()
    columns = d_one.shape[1] // 5
    for t in range(5):
        part = slice(t * columns, (t + 1) * columns)
        d_one[:, part] = dot_tn(grad_main[...], u_any[:, part]).astype(bf16)
        if t in (1, 3):
            sums.step()
    save_one.start()
    sums.finish()
    save_point.wait()
    save_two.wait()
    save_one.wait()


def back_high(shape, sources, grad_summed, u_one, u_two, three, two):
    branch = three[1]
    w_two, pooled = two[0], two[1]
    windows, length, mid = pooled.shape
    rows, small = branch.shape
    share = mid // shape[2]
    chunks, targets = [], []
    if sources:
        chunks, n_whole, n_plane = head_chunks(sources[0].shape[3])
        targets = [((share, n_whole), bf16), ((share // 2, n_plane), bf16)]
    taps = w_two.shape[0] // mid
    d_shapes = [((mid, small), bf16), ((mid, taps * small), bf16), ((mid, u_one.shape[1]), bf16)]
    outs = [
        ((MB, 2 * length + EDGE, mid), bf16),
        ((2 * MB, small), f32),
        ((2 * MB, mid), f32),
    ]
    fixed = reduce_scratch(shape, 2 * MB, small) + reduce_scratch(shape, 2 * MB, mid)
    fixed += [
        pltpu.VMEM(*a)
        for a in [
            ((rows, mid), f32),
            (u_one.shape, bf16),
            ((rows, small), f32),
            ((windows, EDGE, small), f32),
            ((windows, EDGE, small), f32),
            ((windows, EDGE, small), f32),
            ((windows, EDGE, small), f32),
            ((windows, mid), f32),
            ((windows, mid), f32),
            ((windows, mid), f32),
            ((windows, mid), f32),
            ((2 * MB, small), f32),
            ((rows, small), bf16),
            ((windows, length, mid), f32),
            ((windows, mid), f32),
            ((windows, mid), f32),
            ((windows, mid), f32),
            ((windows, mid), f32),
            ((2 * MB, mid), f32),
            ((rows, mid), bf16),
            *d_shapes,
        ]
    ]
    fixed += [pltpu.SemaphoreType.DMA((3, 4)), pltpu.SemaphoreType.DMA((6,))]
    return pl.pallas_call(
        functools.partial(back_high_kernel, shape, len(sources), chunks),
        in_specs=[HBM] * (3 + len(sources)) + [VM] * 12,
        out_specs=[HBM] * (3 + len(sources)) + [VM] * 3,
        out_shape=[jax.ShapeDtypeStruct(*o) for o in targets + d_shapes + outs],
        scratch_shapes=fixed + sums_scratch(share, chunks),
        compiler_params=params(2),
        name="back_high",
    )(*sources, grad_summed, u_one, u_two, *three, *two)


def back_low_kernel(shape, n_sums, chunks, *refs):
    (sources, ins, targets, outs, reduce_one, reduce_b, fixed, sum_refs) = split_refs(
        refs, n_sums, 7, n_sums, 3, 6, 6, 5, count_refs(chunks)
    )
    order, in_one, grad_ext, x2, bn_one, vectors, bias_sums = ins
    grad_input, sums_one, bias_out = outs
    w_one, du_one, local, lanes_buffer, load_sem = fixed
    place = Place(shape)
    place.greet()
    windows, length, wide = x2.shape
    channels = wide // 2
    pair = 2 * length
    gain_one, shift_one = vectors.at[0:1, :wide], vectors.at[1:2, :wide]
    load_one = pltpu.make_async_copy(in_one, w_one, load_sem)
    load_one.start()
    sums = Sums(place, sources, targets, chunks, sum_refs)
    place.meet()
    sums.step()
    load_one.wait()

    for m in range(MB):
        through = [
            dot_nn(grad_ext[m], w_one[:, t * channels : (t + 1) * channels]) for t in range(5)
        ]
        centre, inverse = bn_one[m : m + 1, :], bn_one[MB + m : MB + m + 1, :]
        total_du = jnp.zeros((1, wide), f32)
        total_dx = jnp.zeros((1, wide), f32)
        row = lax.broadcasted_iota(jnp.int32, (length, channels), 0)
        top, bottom = row == 0, row == length - 1
        for i in range(2):
            w = 2 * m + i
            main = [t[i * length : (i + 1) * length] for t in through]
            low = [t[pair + 2 * i : pair + 2 * i + 1] for t in through]
            high = [t[pair + 2 * i + 1 : pair + 2 * i + 2] for t in through]
            later = lambda t: jnp.where(bottom, high[t], pltpu.roll(main[t], length - 1, axis=0))
            earlier = lambda t: jnp.where(top, low[t], pltpu.roll(main[t], 1, axis=0))
            mean = later(0) + main[2] + earlier(4)
            cross = main[1] + earlier(3)
            cross_end = high[1] + main[3][length - 1 :]
            cross_later = jnp.where(bottom, cross_end, pltpu.roll(cross, length - 1, axis=0))
            grad = jnp.concatenate([(mean + cross) * 0.5, (mean + cross_later) * 0.5], axis=1)
            xhat = (x2[w].astype(f32) - centre) * inverse
            du = gelu_slope(xhat * gain_one[...] + shift_one[...]) * grad
            du_one[w] = du
            total_du = total_du + jnp.sum(du, axis=0, keepdims=True)
            total_dx = total_dx + jnp.sum(du * xhat, axis=0, keepdims=True)
        local[m : m + 1, :] = total_du[:, :channels] + total_du[:, channels:]
        local[MB + m : MB + m + 1, :] = total_dx[:, :channels] + total_dx[:, channels:]
        sums.step()

    sums_one[...] = reduce_everywhere(
        place, local[...], *reduce_one[:2], reduce_one[2:], add_up, sums.step
    )
    scale = 1.0 / (4 * length * shape[0] * shape[1] * shape[2])
    lanes = lanes_buffer.shape[0]
    twice = lambda v: jnp.concatenate([v, v], axis=1)

    def write(window):
        w = 0
        for p in range(1, windows):
            w = jnp.where(order[p] == window, p, w)
        m = lax.div(w, 2)
        mean_du = twice(sums_one[pl.ds(m, 1), :]) * scale
        mean_dx = twice(sums_one[pl.ds(MB + m, 1), :]) * scale
        inverse = bn_one[pl.ds(MB + m, 1), :]
        xhat = (x2[w].astype(f32) - bn_one[pl.ds(m, 1), :]) * inverse
        grad = gain_one[...] * inverse * (du_one[w] - mean_du - xhat * mean_dx)
        for odd in range(2):
            for c in range(lanes):
                at = odd * channels + c * LANES
                lanes_buffer[c, pl.ds(odd, length, 2), :] = grad[:, at : at + LANES]
        for c in range(lanes):
            grad_input[window, :, c * LANES : (c + 1) * LANES] = lanes_buffer[c].astype(bf16)

    for half in range(2):
        sums.step()

        @pl.loop(half * windows // 2, (half + 1) * windows // 2)
        def _(window):
            write(window)

    bias_out[...] = reduce_everywhere(
        place, bias_sums[...], *reduce_b[:2], reduce_b[2:], add_up, sums.step
    )
    sums.finish()


def back_low(shape, sources, order, w_one, grad_ext, x2, bn_one, vectors, bias_sums):
    windows, length, wide = x2.shape
    channels = wide // 2
    share = grad_ext.shape[2] // shape[2]
    chunks, targets = [], []
    if sources:
        columns = sources[0].shape[1]
        size = BLOCK // 2
        chunks = [(ALONG, i // 2, 0, i * size, size, 0, i * size) for i in range(columns // size)]
        targets = [((share, columns), bf16)]
        begin = 0
        for i, taps in enumerate((1, 3, w_one.shape[1] // channels), 1):
            width = sources[i].shape[3] // taps
            for t in range(taps):
                begin += width > share * 2
                chunks.append((WHOLE, begin, i, t * width, width, i, t))
            targets.append(((taps, share, width), bf16))
    outs = [((windows, 2 * length, channels), bf16), ((2 * MB, channels), f32)]
    outs += [(bias_sums.shape, f32)]
    scratch = reduce_scratch(shape, 2 * MB, channels) + reduce_scratch(shape, *bias_sums.shape)
    scratch += [
        pltpu.VMEM(w_one.shape, bf16),
        pltpu.VMEM((windows, length, wide), f32),
        pltpu.VMEM((2 * MB, channels), f32),
        pltpu.VMEM((channels // LANES, 2 * length, LANES), f32),
        pltpu.SemaphoreType.DMA,
    ]
    smem = pl.BlockSpec(memory_space=pltpu.SMEM)
    return pl.pallas_call(
        functools.partial(back_low_kernel, shape, len(sources), chunks),
        in_specs=[HBM] * len(sources) + [smem, HBM] + [VM] * 5,
        out_specs=[HBM] * len(sources) + [VM] * 3,
        out_shape=[jax.ShapeDtypeStruct(*o) for o in targets + outs],
        scratch_shapes=scratch + sums_scratch(share, chunks),
        compiler_params=params(3),
        name="back_low",
    )(*sources, order, w_one, grad_ext, x2, bn_one, vectors, bias_sums)


def per_device(
    shape,
    tracks,
    species,
    batch_order,
    conv_one,
    dilated_kernel,
    point_wise,
    head_human,
    head_mouse,
    bias_human,
    bias_mouse,
    gain_one,
    shift_one,
    gain_two,
    shift_two,
    gain_three,
    shift_three,
    cotangent,
):
    sec = lax.axis_index("section").astype(jnp.int32)
    windows, seq_bins, channels = tracks.shape
    half = seq_bins // 2
    length = half // 2
    human_tracks, mouse_tracks = head_human.shape[1], head_mouse.shape[1]
    human_wide = -(-human_tracks // BLOCK) * BLOCK
    share = conv_one.shape[2]
    mid = share * shape[2]

    taps_one = conv_one.shape[0]
    shard_one = jnp.transpose(conv_one, (0, 2, 1))
    shard_point = point_wise.T
    shard_heads = jnp.concatenate(
        [
            jnp.pad(head_human, ((0, 0), (0, human_wide - human_tracks))),
            jnp.pad(head_mouse, ((0, 0), (0, BLOCK - mouse_tracks))),
        ],
        axis=1,
    )
    half_rows = share // shape[0]
    half_heads = lax.dynamic_slice_in_dim(shard_heads, sec * half_rows, half_rows, 0)
    w_heads = lax.all_gather(half_heads, ("dp", "section"), axis=0, tiled=True)
    weights = [shard_one, dilated_kernel, shard_point]
    if shape != (2, 4, 4):
        weights[0] = jnp.transpose(conv_one, (2, 0, 1)).reshape(share, taps_one * channels)
        weights = [lax.all_gather(w, "dp", axis=w.ndim - 2, tiled=True) for w in weights]

    wide = 2 * channels
    vectors = jnp.stack(
        [
            jnp.pad(v, (0, wide - v.shape[0]))
            for v in (
                jnp.tile(gain_one, 2),
                jnp.tile(shift_one, 2),
                gain_two,
                shift_two,
                gain_three,
                shift_three,
            )
        ]
    )
    native = jnp.transpose(cotangent, (2, 0, 1))
    relay = [native] if length % LANES == 0 else []
    (
        u_one,
        u_two,
        pooled,
        pooled_low,
        pooled_high,
        branch,
        branch_low,
        branch_high,
        act_three,
        summed,
        bn_one,
        bn_two,
        bn_three,
        w_one,
        w_two,
        w_point,
        x2,
        *cot,
    ) = forward(shape, mid, batch_order, tracks, vectors, *weights, relay)
    if not cot:
        half_cot = lax.dynamic_slice_in_dim(cotangent, sec * length, length, 1)
        cot = [jnp.pad(half_cot, ((0, 0), (0, 0), (0, human_wide - human_tracks)))]
    w_two = w_two.reshape(-1, w_two.shape[2])

    wide_bias = jnp.concatenate(
        [
            jnp.pad(bias_human, (0, human_wide - human_tracks)),
            jnp.pad(bias_mouse, (0, BLOCK - mouse_tracks)),
        ]
    ).reshape(1, -1)
    predicted, grad_summed, d_human, d_mouse, bias_sums = heads(
        species, batch_order, summed, w_heads, wide_bias, cot[0], human_tracks, mouse_tracks
    )


    def in_kernel(*grads):
        if shape != (2, 4, 4):
            return []
        return [g.reshape(2, 2, -1, g.shape[1]) for g in grads]

    def summed_up(*grads):
        parts = [lax.psum_scatter(g, "dp", scatter_dimension=0, tiled=True) for g in grads]
        return [lax.psum(part, ("section", "seq")) for part in parts]

    def by_tap(grad, taps):
        grad = grad.astype(f32)
        if grad.ndim == 2:
            grad = jnp.transpose(grad.reshape(share, taps, -1), (1, 0, 2))
        return grad

    *heads_summed, d_point, d_two, d_one, grad_ext, sums_three, sums_two = back_high(
        shape,
        in_kernel(d_human, d_mouse),
        grad_summed,
        u_one,
        u_two,
        (act_three, branch, branch_low, branch_high, bn_three, w_point),
        (w_two, pooled, pooled_low, pooled_high, bn_two, vectors),
    )
    *sums_low, grad_input, sums_one, bias_out = back_low(
        shape,
        heads_summed[1:] + in_kernel(d_point, d_two, d_one),
        batch_order,
        w_one,
        grad_ext,
        x2,
        bn_one,
        vectors,
        bias_sums,
    )
    if sums_low:
        rest, r_point, r_two, r_one = sums_low
        done = heads_summed[0].shape[1]
        r_human = jnp.concatenate([heads_summed[0], rest[:, : human_tracks - done]], axis=1)
        r_mouse = rest[:, human_wide - done :]
    else:
        r_human, r_mouse, r_point, r_two, r_one = summed_up(d_human, d_mouse, d_point, d_two, d_one)
    r_human = r_human[:, :human_tracks].astype(f32)
    r_mouse = r_mouse[:, :mouse_tracks].astype(f32)
    r_point = by_tap(r_point, 1)[0]
    r_two = by_tap(r_two, dilated_kernel.shape[0])
    r_one = by_tap(r_one, taps_one)
    r_point = r_point.T
    r_one = jnp.transpose(r_one, (0, 2, 1))
    bias_human_grad = bias_out[: human_wide // BLOCK].reshape(-1)[:human_tracks]
    bias_mouse_grad = bias_out[human_wide // BLOCK, :mouse_tracks]
    return (
        jnp.transpose(predicted, (1, 2, 0)),
        grad_input,
        r_one,
        r_two,
        r_point,
        r_human,
        r_mouse,
        bias_human_grad,
        bias_mouse_grad,
        jnp.sum(sums_one[MB:], axis=0),
        jnp.sum(sums_one[:MB], axis=0),
        jnp.sum(sums_two[MB:], axis=0),
        jnp.sum(sums_two[:MB], axis=0),
        jnp.sum(sums_three[MB:], axis=0),
        jnp.sum(sums_three[:MB], axis=0),
    )


def solution(mesh):
    shape = (mesh.shape["section"], mesh.shape["seq"], mesh.shape["dp"])
    placed = (
        P("dp", "seq", None),
        P("dp"),
        P(),
        P(None, None, "dp"),
        P(None, "dp", None),
        P(None, "dp"),
        P("dp", None),
        P("dp", None),
    ) + (P(),) * 8 + (P("dp", "seq", None),)
    return jax.shard_map(
        functools.partial(per_device, shape),
        mesh=mesh,
        in_specs=placed,
        out_specs=(
            P("dp", ("seq", "section"), None),
            P("dp", ("seq", "section"), None),
            P(None, None, "dp"),
            P(None, "dp", None),
            P(None, "dp"),
            P("dp", None),
            P("dp", None),
        )
        + (P(),) * 8,
        check_vma=False,
    )
```
